32 devices in a mesh: dp: 4 (over y, x), seq: 8 (over z, core).
Axes of the slice: x: 2, y: 2, z: 4, core: 2. Of those that a mesh axis runs over, the one named last changes fastest.
Arguments:
- inputs: bfloat16 [8, 1024, 1024], P('dp', 'seq'), may hold values from -6 to 6
- lengths: int32 [8, 2], P('dp'), may hold values from 0 to 1024, as said below
- infill: int32 [8, 1024], P('dp', 'seq'), may hold values 0 or 1
- cotangent: bfloat16 [8, 1024, 1024], P('dp', 'seq'), may hold values from -6 to 6
- w_qkv: bfloat16 [1024, 3072], P(('dp', 'seq')), may hold values from -0.1875 to 0.1875
- w_out: bfloat16 [1024, 1024], P(('dp', 'seq')), may hold values from -0.75 to 0.75
- w_up: bfloat16 [1024, 4096], P(('dp', 'seq')), may hold values from -0.1875 to 0.1875
- w_down: bfloat16 [4096, 1024], P(('dp', 'seq')), may hold values from -0.09375 to 0.09375
- gain_one: bfloat16 [1024], P(('dp', 'seq')), may hold values from 0.25 to 1.75
- shift_one: bfloat16 [1024], P(('dp', 'seq')), may hold values from -3 to 3
- gain_two: bfloat16 [1024], P(('dp', 'seq')), may hold values from 0.25 to 1.75
- shift_two: bfloat16 [1024], P(('dp', 'seq')), may hold values from -3 to 3
Outputs:
- output: bfloat16 [8, 1024, 1024], P('dp', 'seq')
- input_grad: bfloat16 [8, 1024, 1024], P('dp', 'seq')
- grad_w_qkv: float32 [1024, 3072], P(('dp', 'seq'))
- grad_w_out: float32 [1024, 1024], P(('dp', 'seq'))
- grad_w_up: float32 [1024, 4096], P(('dp', 'seq'))
- grad_w_down: float32 [4096, 1024], P(('dp', 'seq'))
- grad_gain_one: float32 [1024], P(('dp', 'seq'))
- grad_shift_one: float32 [1024], P(('dp', 'seq'))
- grad_gain_two: float32 [1024], P(('dp', 'seq'))
- grad_shift_two: float32 [1024], P(('dp', 'seq'))
The draws below stay inside these ranges and needn't reach their ends.
Inputs may be any that keep to these rules, and one draw needn't show every extreme that they name: Each row lists the utterance lengths of one stream in order and sums to 1024. In each group of 2 rows on one index of dp, one row, which one varies, is a single utterance of 1024 frames followed by zeros; the other rows hold 2 utterances of positive length.
All inputs are finite; a program needn't handle non-finite values. No bound on the sum of `infill` on one device may be relied on, other than what follows from the above.
Results may differ from the reference program's by a relative error of at most 0.017.
Values may be sent and summed in bfloat16 or wider, within the bound.
A program may use at most 320 MiB of HBM per device.

```python
import jax
import jax.numpy as jnp
from jax import lax

D = 1024
HEADS = 16
HEAD_DIM = 64
FF = 4096
STREAMS = 2
STREAM_LEN = 1024
BATCH = 8
NSEG = 2


def draw_lengths(key, part):
    key = jax.random.fold_in(key, 11)
    key_pick, key_cut = jax.random.split(key)
    step_len = STREAM_LEN // NSEG
    jitter = jax.random.randint(key_cut, (BATCH, NSEG - 1), -(step_len // 3), step_len // 3 + 1)
    cuts = (jnp.arange(1, NSEG, dtype=jnp.int32) * step_len)[None, :] + jitter
    edges = jnp.concatenate([jnp.zeros((BATCH, 1), jnp.int32), cuts.astype(jnp.int32), jnp.full((BATCH, 1), STREAM_LEN, jnp.int32)], axis=1)
    ragged = edges[:, 1:] - edges[:, :-1]
    groups = BATCH // STREAMS
    picked = jax.random.randint(key_pick, (groups, 1), 0, STREAMS)
    slot_ids = jnp.arange(STREAMS, dtype=jnp.int32)[None, :]
    whole_row = (slot_ids == picked).reshape(BATCH, 1)
    single = jnp.concatenate([jnp.full((BATCH, 1), STREAM_LEN, jnp.int32), jnp.zeros((BATCH, NSEG - 1), jnp.int32)], axis=1)
    return jnp.where(whole_row, single, ragged).astype(jnp.int32)


def with_ends(result, rng, low, high):
    extent = result.shape
    place = [jax.random.randint(jax.random.fold_in(rng, axis), (), 0, extent[axis]) for axis in range(len(extent))]
    result = result.at[tuple(place)].set(low)
    longest = extent.index(max(extent))
    place[longest] = (place[longest] + 1) % extent[longest]
    return result.at[tuple(place)].set(high)


def shard_levels(key, dims, shards, least, high):
    factor_of, own = 1.0, jax.random.fold_in(key, 6)
    for position, shards_of in shards:
        steps = jnp.exp(jax.random.uniform(jax.random.fold_in(own, position), (shards_of,), jnp.float32, least / len(shards), high / len(shards)))
        factor_of = factor_of * jnp.repeat(steps, dims[position] // shards_of).reshape([-1 if axis == position else 1 for axis in range(len(dims))])
    return factor_of


def centred(stream_key, shape, width, limit, cuts=(), kind=jnp.bfloat16):
    entries = jax.random.normal(stream_key, shape, jnp.float32) * width
    if len(cuts) > 0:
        entries = shard_levels(stream_key, shape, cuts, -0.22, 0.18) * entries
    return jnp.clip(entries, min=-limit, max=limit).astype(kind)


def setup_inputs(seed: int = 0) -> dict:
    arg_keys = jax.random.split(jax.random.key(seed), 13)
    inputs = centred(arg_keys[0], (BATCH, STREAM_LEN, D), 1.0, 6.0, ((0, 4), (1, 8)))
    lengths = draw_lengths(jax.random.fold_in(arg_keys[12], 71), 0)
    infill = with_ends((jax.random.randint(arg_keys[2], (BATCH, STREAM_LEN), 0, 20) < 17).astype(jnp.int32), jax.random.fold_in(arg_keys[2], 1), 0, 1)
    cotangent = centred(arg_keys[3], (BATCH, STREAM_LEN, D), 1.0, 6.0, ((0, 4), (1, 8)))
    w_qkv = centred(arg_keys[4], (D, 3 * D), D ** -0.5, 0.1875, ((0, 32),))
    w_out = centred(arg_keys[5], (D, D), (D // 16) ** -0.5, 0.75, ((0, 32),))
    w_up = centred(arg_keys[6], (D, FF), D ** -0.5, 0.1875, ((0, 32),))
    w_down = centred(arg_keys[7], (FF, D), FF ** -0.5, 0.09375, ((0, 32),))
    gain_one = jnp.clip(1.0 + 0.15 * jax.random.normal(arg_keys[8], (D,), jnp.float32), 0.25, 1.75).astype(jnp.bfloat16)
    shift_one = centred(arg_keys[9], (D,), 0.5, 3.0, ((0, 32),))
    gain_two = jnp.clip(1.0 + 0.15 * jax.random.normal(arg_keys[10], (D,), jnp.float32), 0.25, 1.75).astype(jnp.bfloat16)
    shift_two = centred(arg_keys[11], (D,), 0.5, 3.0, ((0, 32),))
    return {"inputs": inputs, "lengths": lengths, "infill": infill, "cotangent": cotangent, "w_qkv": w_qkv, "w_out": w_out, "w_up": w_up, "w_down": w_down, "gain_one": gain_one, "shift_one": shift_one, "gain_two": gain_two, "shift_two": shift_two}


@jax.custom_vjp
def low(v):
    return lax.optimization_barrier(v.astype(jnp.bfloat16)).astype(jnp.float32)

@jax.custom_vjp
def low_back(v):
    return v

def low_keep(v):
    return (low(v), None)

def low_pass(kept, grad):
    return (grad,)

def back_keep(v):
    return (v, None)

def back_low(kept, grad):
    return (low(grad),)
low.defvjp(low_keep, low_pass)
low_back.defvjp(back_keep, back_low)
norm_eps = 1e-05
masked_score = -1e+30

def layer_norm(features, gain_vec, shift_vec):
    row_mean = lax.optimization_barrier(jnp.mean(features, axis=-1, keepdims=True))
    centered = features - row_mean
    spread = lax.optimization_barrier(jnp.mean(centered * centered, axis=-1, keepdims=True))
    return centered * lax.rsqrt(spread + norm_eps) * gain_vec + shift_vec

def mix(left_arr, right_arr):
    return jnp.dot(left_arr, right_arr, precision=lax.Precision.HIGHEST, preferred_element_type=jnp.float32)

def slope_table(head_count, stream_len):
    return 2.0 ** (-8.0 * (jnp.arange(head_count, dtype=jnp.float32) + 1.0) / head_count) * (256.0 / stream_len)

def stream_layer(features, segments, params):
    w_qkv, w_out, w_up, w_down, gain_one, shift_one, gain_two, shift_two = params
    normed_one = low(layer_norm(features, gain_one, shift_one))
    packed = low(low_back(mix(normed_one, w_qkv)))
    queries = packed[:, :D].reshape(STREAM_LEN, HEADS, HEAD_DIM)
    key_heads = packed[:, D:2 * D].reshape(STREAM_LEN, HEADS, HEAD_DIM)
    values = packed[:, 2 * D:].reshape(STREAM_LEN, HEADS, HEAD_DIM)
    positions = jnp.arange(STREAM_LEN, dtype=jnp.int32)
    slopes = slope_table(HEADS, STREAM_LEN)
    block_rows = min(512, STREAM_LEN)

    def attend(first_row):
        query_blk = lax.dynamic_slice_in_dim(queries, first_row, block_rows, 0)
        query_pos = lax.dynamic_slice_in_dim(positions, first_row, block_rows, 0)
        query_seg = lax.dynamic_slice_in_dim(segments, first_row, block_rows, 0)
        raw_scores = jnp.einsum('qhc,khc->hqk', query_blk, key_heads, precision=lax.Precision.HIGHEST)
        distance = jnp.abs(query_pos[:, None] - positions[None, :]).astype(jnp.float32)
        scores = low_back(raw_scores * HEAD_DIM ** (-0.5) - slopes[:, None, None] * distance[None])
        same_utt = query_seg[:, None] == segments[None, :]
        scores = jnp.where(same_utt[None], scores, masked_score)
        top_score = lax.optimization_barrier(jnp.max(scores, axis=2, keepdims=True))
        weights_blk = jnp.exp(scores - top_score)
        probs = weights_blk / lax.optimization_barrier(jnp.sum(weights_blk, axis=2, keepdims=True))
        return jnp.einsum('hqk,khc->qhc', low(probs), values, precision=lax.Precision.HIGHEST)
    starts = jnp.arange(STREAM_LEN // block_rows, dtype=jnp.int32) * block_rows
    attended = lax.map(jax.checkpoint(attend), starts).reshape(STREAM_LEN, D)
    attn_low = low(low_back(attended))
    hidden = features + low_back(mix(attn_low, w_out))
    normed_two = low(layer_norm(hidden, gain_two, shift_two))
    upward = low_back(mix(normed_two, w_up))
    active = low(jax.nn.gelu(upward))
    return hidden + mix(active, w_down)

def reference(inputs, lengths, infill, cotangent, w_qkv, w_out, w_up, w_down, gain_one, shift_one, gain_two, shift_two):
    params = (w_qkv.astype(jnp.float32), w_out.astype(jnp.float32), w_up.astype(jnp.float32), w_down.astype(jnp.float32), gain_one.astype(jnp.float32), shift_one.astype(jnp.float32), gain_two.astype(jnp.float32), shift_two.astype(jnp.float32))
    positions = jnp.arange(STREAM_LEN, dtype=jnp.int32)
    bounds = jnp.cumsum(lengths, axis=1).astype(jnp.int32)
    segments = lax.optimization_barrier(jnp.sum((positions[None, :, None] >= bounds[:, None, :]).astype(jnp.int32), axis=2))

    def whole(stacked, weights):

        def one_stream(items):
            return jax.checkpoint(stream_layer)(items[0], items[1], weights)
        return lax.map(one_stream, (stacked, segments))
    outputs, pullback = jax.vjp(whole, inputs.astype(jnp.float32), params)
    grad_seed = cotangent.astype(jnp.float32) * infill.astype(jnp.float32)[:, :, None]
    input_grad, weight_grads = pullback(grad_seed)
    return (outputs.astype(jnp.bfloat16), input_grad.astype(jnp.bfloat16), weight_grads[0], weight_grads[1], weight_grads[2], weight_grads[3], weight_grads[4], weight_grads[5], weight_grads[6], weight_grads[7])
```

```python
import jax
import jax.numpy as jnp
from jax import lax
from jax.experimental import pallas as pl
from jax.experimental.pallas import tpu as pltpu

from jax.sharding import PartitionSpec as P

HEADS = 16
HEAD_DIM = 64

norm_eps = 1e-05
masked_score = -1e30
MESH_ID = pl.DeviceIdType.MESH
F32 = jnp.float32
BF16 = jnp.bfloat16
far = 1e33
q_block = 256


def place():
    dp, sq = lax.axis_index("dp"), lax.axis_index("seq")
    return dp, sq, dp // 2, dp % 2, sq // 2, sq % 2


def dot_nt(a, b):
    return lax.dot_general(a, b, (((1,), (1,)), ((), ())), preferred_element_type=F32)


def dot_nn(a, b):
    return lax.dot_general(a, b, (((1,), (0,)), ((), ())), preferred_element_type=F32)


class Link:
    def __init__(self, src, dst, landing, sems, index, target, when_send=None, when_recv=None):
        send, recv = sems
        self.copy = pltpu.make_async_remote_copy(
            src_ref=src,
            dst_ref=dst,
            send_sem=send.at[index],
            recv_sem=recv.at[index],
            device_id=target,
            device_id_type=MESH_ID,
        )
        self.back = pltpu.make_async_remote_copy(
            src_ref=landing,
            dst_ref=landing,
            send_sem=send.at[index],
            recv_sem=recv.at[index],
            device_id=target,
            device_id_type=MESH_ID,
        )
        self.when_send, self.when_recv = when_send, when_recv

    def start(self):
        if self.when_send is None:
            self.copy.start()
        else:
            pl.when(self.when_send)(self.copy.start)

    def wait(self):
        if self.when_recv is None:
            self.back.wait_recv()
        else:
            pl.when(self.when_recv)(self.back.wait_recv)

    def wait_sent(self):
        if self.when_send is None:
            self.copy.wait_send()
        else:
            pl.when(self.when_send)(self.copy.wait_send)


def greet(dp, sq, n_seq, n_dp):
    barrier = pltpu.get_barrier_semaphore()
    for k in range(1, n_seq):
        pl.semaphore_signal(
            barrier, inc=1, device_id=(dp, lax.rem(sq + k, n_seq)), device_id_type=MESH_ID
        )
    for m in range(1, n_dp):
        other = lax.rem(dp + m, n_dp)
        pl.semaphore_signal(barrier, inc=1, device_id=(other, sq), device_id_type=MESH_ID)
    pl.semaphore_wait(barrier, n_seq - 1 + n_dp - 1)


def distance_block(dist, len_ref, stream, first, rows, width):
    slots = len_ref.shape[1]
    key_pos = lax.broadcasted_iota(jnp.int32, (rows, 1), 0)
    query_pos = lax.broadcasted_iota(jnp.int32, (1, width), 1) + first
    key_seg = jnp.zeros((rows, 1), jnp.int32)
    query_seg = jnp.zeros((1, width), jnp.int32)
    bound = 0
    for k in range(slots):
        bound = bound + len_ref[stream, k]
        key_seg = key_seg + (key_pos >= bound).astype(jnp.int32)
        query_seg = query_seg + (query_pos >= bound).astype(jnp.int32)
    gap = jnp.abs(key_pos - query_pos).astype(F32)
    dist[...] = jnp.where(key_seg == query_seg, gap, far)


def gather_kernel(
    x_ref, wq_ref, wo_ref, wu_ref, wd_ref, par_ref, len_ref, slope_ref,
    wo_all, wu_all, wd_all, par_out, attn, qkv_out, ot_out, lse_out, xh_out, wt_out,
    xg, xh, wqb, wt, pbuf, pown, par, qkv, vt, obuf, ot, lse, dist,
    z_send, z_recv, w_send, w_recv, x_send, x_recv, s_send, s_recv, loc,
):
    dp, sq, y, x, z, c = place()
    streams, tok_rows, width = x_ref.shape
    n_seq, n_dp = lax.axis_size("seq"), lax.axis_size("dp")
    nz = n_seq // 2
    total = n_seq * tok_rows
    own_rows = par_ref.shape[0]
    x_nbr, y_nbr = (y * 2 + (1 - x), sq), ((1 - y) * 2 + x, sq)
    sibling = (dp, z * 2 + (1 - c))
    up, down = (dp, sq + 2), (dp, sq - 2)
    greet(dp, sq, n_seq, n_dp)
    links = []

    def keep(link):
        link.start()
        links.append(link)
        return link

    locals_ = []

    def local(src, dst):
        copy = pltpu.make_async_copy(src, dst, loc.at[len(locals_)])
        copy.start()
        locals_.append(copy)
        return copy

    cp_x = local(x_ref, xg.at[:, sq])
    cp_wq = local(wq_ref.at[sq], wqb.at[pl.ds(pl.multiple_of(sq * 32 + dp * 32 * n_seq, 32), 32), :])
    cp_w = [
        local(src, dst.at[y, x, z, c])
        for src, dst in ((wo_ref, wo_all), (wu_ref, wu_all), (wd_ref, wd_all))
    ]

    par_links, wq_links = [], []
    for k in range(1, n_seq):
        other = lax.rem(sq + k, n_seq)
        source = lax.rem(sq + n_seq - k, n_seq)
        par_links.append(
            keep(Link(par_ref, pbuf.at[k - 1], pbuf.at[k - 1], (s_send, s_recv), k - 1, (dp, other)))
        )
        mine = wqb.at[pl.ds(pl.multiple_of(sq * 32 + dp * 32 * n_seq, 32), 32), :]
        theirs = wqb.at[pl.ds(pl.multiple_of(source * 32 + dp * 32 * n_seq, 32), 32), :]
        wq_links.append(
            keep(Link(wq_ref.at[other], mine, theirs, (s_send, s_recv), 7 + k - 1, (dp, other)))
        )
    half = wu_ref.shape[2] // 2
    half_d = wd_ref.shape[2] // 2
    chunks = [
        (wo_ref, wo_all, 0, wo_ref.shape[2]),
        (wu_ref, wu_all, 0, half),
        (wu_ref, wu_all, half, half),
        (wd_ref, wd_all, 0, half_d),
        (wd_ref, wd_all, half_d, half_d),
    ]
    pending = {}

    def z_hop(i, h):
        own, full, first, cols = chunks[i]
        cut = pl.ds(first, cols)
        out = []
        for way, target, block, landing, ok_send, ok_recv in (
            (0, up, z - (h - 1), z - h, (z >= h - 1) & (z <= nz - 2), z >= h),
            (1, down, z + (h - 1), z + h, (z + h - 1 <= nz - 1) & (z >= 1), z + h <= nz - 1),
        ):
            there = full.at[y, x, block, c, :, :, cut]
            src = own.at[:, :, cut] if h == 1 else there
            land = full.at[y, x, landing, c, :, :, cut]
            index = (i * 3 + h - 1) * 2 + way
            out.append(keep(Link(src, there, land, (w_send, w_recv), index, target, ok_send, ok_recv)))
        pending[("z", i, h)] = out

    def plane(i, tag, pairs):
        full, first, cols = chunks[i][1:]
        cut = pl.ds(first, cols)
        out = []
        for name, target, where, landing in pairs:
            slot = {"x1a": 0, "x1b": 1, "x2a": 2, "x2b": 3, "c0": 4, "c1a": 5, "c1b": 6, "c2a": 7, "c2b": 8}[name]
            src = full.at[where + (slice(None), cut)]
            land = full.at[landing + (slice(None), cut)]
            out.append(keep(Link(src, src, land, (x_send, x_recv), i * 9 + slot, target)))
        pending[(tag, i)] = out

    every = slice(None)

    def cross_one(i):
        plane(i, "x1", [
            ("x1a", x_nbr, (y, x, every, c, 0), (y, 1 - x, every, c, 0)),
            ("x1b", y_nbr, (y, x, every, c, 1), (1 - y, x, every, c, 1)),
        ])
        plane(i, "c0", [("c0", sibling, (y, x, every, c, every), (y, x, every, 1 - c, every))])

    def cross_two(i):
        wait("x1", i)
        plane(i, "x2", [
            ("x2a", y_nbr, (y, every, every, c, 0), (1 - y, every, every, c, 0)),
            ("x2b", x_nbr, (every, x, every, c, 1), (every, 1 - x, every, c, 1)),
        ])
        plane(i, "c1", [
            ("c1a", sibling, (y, 1 - x, every, c, 0), (y, 1 - x, every, 1 - c, 0)),
            ("c1b", sibling, (1 - y, x, every, c, 1), (1 - y, x, every, 1 - c, 1)),
        ])

    def cross_last(i):
        wait("x2", i)
        plane(i, "c2", [
            ("c2a", sibling, (1 - y, every, every, c, 0), (1 - y, every, every, 1 - c, 0)),
            ("c2b", sibling, (every, 1 - x, every, c, 1), (every, 1 - x, every, 1 - c, 1)),
        ])

    def wait(*key):
        for link in pending.pop(key):
            link.wait()

    def x_hop(h):
        out = []
        for way, target, block, landing, ok_send, ok_recv in (
            (0, up, z - (h - 1), z - h, (z >= h - 1) & (z <= nz - 2), z >= h),
            (1, down, z + (h - 1), z + h, (z + h - 1 <= nz - 1) & (z >= 1), z + h <= nz - 1),
        ):
            there = xg.at[:, block * 2 + c]
            src = x_ref if h == 1 else there
            index = (h - 1) * 2 + way
            out.append(
                keep(Link(src, there, xg.at[:, landing * 2 + c], (z_send, z_recv), index, target, ok_send, ok_recv))
            )
        pending[("x", h)] = out

    def x_pass(h):
        out = []
        for way, block, ok in ((0, z - h, z >= h), (1, z + h, z + h <= nz - 1)):
            src = xg.at[:, block * 2 + c]
            land = xg.at[:, block * 2 + (1 - c)]
            out.append(
                keep(Link(src, src, land, (z_send, z_recv), 6 + (h - 1) * 2 + way, sibling, ok, ok))
            )
        pending[("xc", h)] = out

    sib_x = keep(Link(x_ref, xg.at[:, sq], xg.at[:, z * 2 + (1 - c)], (z_send, z_recv), 12, sibling))
    z_hop(0, 1)
    z_hop(1, 1)
    for link in par_links:
        link.wait()
    pown[...] = par_ref[...] + pbuf[0]
    for k in range(1, n_seq - 1):
        pown[...] += pbuf[k]
    par_dp = []
    for m in range(1, n_dp):
        par_dp.append(
            keep(Link(pown, pbuf.at[n_seq - 2 + m], pbuf.at[n_seq - 2 + m], (s_send, s_recv), 14 + m - 1, (lax.rem(dp + m, n_dp), sq)))
        )
    for link in wq_links:
        link.wait()
    cp_wq.wait()
    wq_dp = []
    rows_dp = 32 * n_seq
    for m in range(1, n_dp):
        mine = wqb.at[pl.ds(pl.multiple_of(dp * rows_dp, 32), rows_dp), :]
        source = lax.rem(dp + n_dp - m, n_dp)
        theirs = wqb.at[pl.ds(pl.multiple_of(source * rows_dp, 32), rows_dp), :]
        wq_dp.append(
            keep(Link(mine, mine, theirs, (s_send, s_recv), 17 + m - 1, (lax.rem(dp + m, n_dp), sq)))
        )
    wait("z", 0, 1)
    wait("z", 1, 1)
    z_hop(0, 2)
    z_hop(1, 2)
    for link in par_dp:
        link.wait()
    par[...] = pown[...] + pbuf[n_seq - 1] + pbuf[n_seq] + pbuf[n_seq + 1]
    wait("z", 0, 2)
    wait("z", 1, 2)
    z_hop(0, 3)
    z_hop(1, 3)
    x_hop(1)
    wait("z", 0, 3)
    wait("z", 1, 3)
    for copy in cp_w:
        copy.wait()
    cross_one(0)
    cross_one(1)
    for link in wq_dp:
        link.wait()
    step = 256
    for r in range(width // step):
        wt[:, r * step:(r + 1) * step] = jnp.transpose(
            wqb[r * step:(r + 1) * step, :].astype(F32)
        ).astype(BF16)
    put_wt = local(wt, wt_out)
    put_par = local(par, par_out)

    lanes = width // 8

    def vector(row):
        block = par[row * 8:(row + 1) * 8, :].astype(F32)
        return jnp.concatenate([block[r:r + 1, :] for r in range(8)], axis=1)

    gain, shift = vector(0), vector(1)
    scale = 0.125

    def process(s):
        def one(b, carry):
            v = xg[b, s].astype(F32)
            mean = jnp.mean(v, axis=1, keepdims=True)
            v = v - mean
            spread = jnp.mean(v * v, axis=1, keepdims=True)
            n = v * lax.rsqrt(spread + 1e-5)
            xh[b, s] = n.astype(BF16)
            normed = (n * gain + shift).astype(BF16)
            packed = dot_nt(normed, wt[...])
            row = pl.ds(pl.multiple_of(s * tok_rows, tok_rows), tok_rows)
            qkv[b, row, 0:128] = (packed[:, 0:128] * scale).astype(BF16)
            qkv[b, row, 128:384] = packed[:, 128:384].astype(BF16)
            return carry
        lax.fori_loop(0, streams, one, 0)

    def process_hop(h):
        def one(j, carry):
            way, core = j // 2, j % 2
            block = jnp.where(way == 0, z - h, z + h)
            ok = jnp.where(way == 0, (z >= h).astype(jnp.int32), (z + h <= nz - 1).astype(jnp.int32))

            @pl.when(ok == 1)
            def _():
                process(block * 2 + core)
            return carry
        lax.fori_loop(0, 4, one, 0)

    wait("x", 1)
    z_hop(2, 1)
    x_pass(1)
    cross_two(0)
    cross_two(1)
    cp_x.wait()
    sib_x.wait()

    def first_two(j, carry):
        process(z * 2 + j)
        return carry
    lax.fori_loop(0, 2, first_two, 0)
    wait("z", 2, 1)
    z_hop(2, 2)
    wait("xc", 1)
    process_hop(1)
    wait("z", 2, 2)
    z_hop(2, 3)
    wait("z", 2, 3)
    x_hop(2)
    cross_one(2)
    cross_last(0)
    cross_last(1)
    wait("x", 2)
    z_hop(3, 1)
    x_pass(2)
    wait("xc", 2)
    process_hop(2)
    wait("z", 3, 1)
    z_hop(3, 2)
    wait("z", 3, 2)
    z_hop(3, 3)
    wait("z", 3, 3)
    x_hop(3)
    cross_one(3)
    cross_two(2)
    wait("x", 3)
    z_hop(4, 1)
    x_pass(3)
    wait("xc", 3)
    process_hop(3)
    put_xh = local(xh, xh_out)
    put_qkv = local(qkv, qkv_out)

    def turn(j, carry):
        b, r = j // (total // step), j % (total // step)
        row = pl.ds(pl.multiple_of(r * step, step), step)
        vt[b, :, row] = jnp.transpose(qkv[b, row, 256:384].astype(F32)).astype(BF16)
        return carry
    lax.fori_loop(0, streams * (total // step), turn, 0)
    blocks = total // q_block

    def attend(j, carry):
        b, qb = j // blocks, j % blocks
        row = pl.ds(pl.multiple_of(qb * q_block, q_block), q_block)
        distance_block(dist, len_ref, b, qb * q_block, total, q_block)
        queries = qkv[b, row, 0:128]
        lane = lax.broadcasted_iota(jnp.int32, (q_block, 128), 1)
        for h in range(2):
            own = jnp.where((lane < 64) == (h == 0), queries, jnp.zeros_like(queries))
            s = dot_nt(qkv[b, :, 128:256], own) - slope_ref[0, h] * dist[...]
            top = jnp.max(s, axis=0, keepdims=True)
            p = jnp.exp(s - top)
            weight = jnp.sum(p, axis=0, keepdims=True)
            o = dot_nn(vt[b, h * 64:(h + 1) * 64, :], p.astype(BF16))
            ot[b, h * 64:(h + 1) * 64, row] = o / weight
            lse[b, h:h + 1, row] = top + jnp.log(weight)
        obuf[b, row, :] = jnp.transpose(ot[b, :, row]).astype(BF16)
        return carry

    def send_rows(b):
        out = []
        for k in range(1, n_seq):
            other = lax.rem(sq + k, n_seq)
            source = lax.rem(sq + n_seq - k, n_seq)
            src = obuf.at[b, pl.ds(pl.multiple_of(other * tok_rows, tok_rows), tok_rows), :]
            dst = attn.at[b, :, pl.ds(pl.multiple_of(sq * 128, 128), 128)]
            land = attn.at[b, :, pl.ds(pl.multiple_of(source * 128, 128), 128)]
            out.append(keep(Link(src, dst, land, (s_send, s_recv), 20 + b * 7 + k - 1, (dp, other))))
        pending[("o", b)] = out
        local(
            obuf.at[b, pl.ds(pl.multiple_of(sq * tok_rows, tok_rows), tok_rows), :],
            attn.at[b, :, pl.ds(pl.multiple_of(sq * 128, 128), 128)],
        )

    def attend_some(first, last):
        lax.fori_loop(first, last, attend, 0)

    cross_last(2)
    attend_some(0, 1)
    wait("z", 4, 1)
    z_hop(4, 2)
    attend_some(1, 2)
    cross_two(3)
    wait("z", 4, 2)
    z_hop(4, 3)
    attend_some(2, 3)
    wait("z", 4, 3)
    cross_one(4)
    attend_some(3, 4)
    send_rows(0)
    attend_some(4, 6)
    cross_last(3)
    attend_some(6, 8)
    send_rows(1)
    put_ot = local(ot, ot_out)
    put_lse = local(lse, lse_out)
    cross_two(4)
    cross_last(4)
    for key in list(pending):
        wait(*key)
    for copy in locals_[5:]:
        copy.wait()
    for link in links:
        link.wait_sent()


def gather_call(inputs, wq_blocks, w_out, w_up, w_down, params, lengths, slopes):
    streams, tok_rows, width = inputs.shape
    n_seq, n_dp = lax.axis_size("seq"), lax.axis_size("dp")
    nz, total = n_seq // 2, n_seq * tok_rows
    any_space = pl.BlockSpec(memory_space=pl.ANY)
    vmem = pl.BlockSpec(memory_space=pltpu.VMEM)
    smem = pl.BlockSpec(memory_space=pltpu.SMEM)

    def halves(w):
        return w.reshape(2, w.shape[0] // 2, w.shape[1])

    own = [halves(w) for w in (w_out, w_up, w_down)]
    full = [jax.ShapeDtypeStruct((2, n_dp // 2, nz, 2) + w.shape, BF16) for w in own]
    cols = wq_blocks.shape[2]
    outs = full + [
        jax.ShapeDtypeStruct(params.shape, BF16),
        jax.ShapeDtypeStruct((streams, tok_rows, width), BF16),
        jax.ShapeDtypeStruct((streams, total, cols), BF16),
        jax.ShapeDtypeStruct((streams, 128, total), F32),
        jax.ShapeDtypeStruct((streams, 8, total), F32),
        jax.ShapeDtypeStruct((streams, n_seq, tok_rows, width), BF16),
        jax.ShapeDtypeStruct((cols, width), BF16),
    ]
    dma = pltpu.SemaphoreType.DMA
    scratch = [
        pltpu.VMEM((streams, n_seq, tok_rows, width), BF16),
        pltpu.VMEM((streams, n_seq, tok_rows, width), BF16),
        pltpu.VMEM((width, cols), BF16),
        pltpu.VMEM((cols, width), BF16),
        pltpu.VMEM((n_seq - 1 + n_dp - 1,) + params.shape, BF16),
        pltpu.VMEM(params.shape, BF16),
        pltpu.VMEM(params.shape, BF16),
        pltpu.VMEM((streams, total, cols), BF16),
        pltpu.VMEM((streams, 128, total), BF16),
        pltpu.VMEM((streams, total, 128), BF16),
        pltpu.VMEM((streams, 128, total), F32),
        pltpu.VMEM((streams, 8, total), F32),
        pltpu.VMEM((total, q_block), F32),
        dma((13,)), dma((13,)), dma((30,)), dma((30,)), dma((45,)), dma((45,)), dma((34,)), dma((34,)),
        dma((16,)),
    ]
    return pl.pallas_call(
        gather_kernel,
        out_shape=outs,
        in_specs=[any_space, any_space, any_space, any_space, any_space, vmem, smem, smem],
        out_specs=[any_space] * len(outs),
        scratch_shapes=scratch,
        compiler_params=pltpu.CompilerParams(
            collective_id=0, has_side_effects=True, vmem_limit_bytes=56 * 2**20
        ),
        name="gather_attend",
    )(inputs, wq_blocks, *own, params, lengths, slopes)


def scatter_kernel(
    ga_ref, po_ref, pu_ref, pd_ref, qkv_ref, ot_ref, lse_ref, xh_ref, wt_ref, par_ref, two_ref,
    len_ref, slope_ref,
    gx_out, go_out, gu_out, gd_out, gq_out, pg_out,
    acc_o, acc_u0, acc_u1, acc_d0, acc_d1, sib_o, sib_u0, sib_u1, sib_d0, sib_d1,
    ra_o, ra_u0, ra_u1, ra_d0, ra_d1, rb_o, rb_u0, rb_u1, rb_d0, rb_d1,
    sa_o, sa_u0, sa_u1, sa_d0, sa_d1, sb_o, sb_u0, sb_u1, sb_d0, sb_d1,
    zr_o, zr_u0, zr_u1, zr_d0, zr_d1, fin_o, fin_u, fin_d,
    do, qkv, ot, lse, xh, wt, kt, dot_t, delta, dist, dk, dv, dqt, dqkv, dqkvt,
    gp, gs, gz, gfin, gt, dqs, dqr, dqsum, pgp, pr1, psum, pr2, pgo,
    o_send, o_recv, x_send, x_recv, zw_send, zw_recv, zg_send, zg_recv, s_send, s_recv, loc,
):
    dp, sq, y, x, z, c = place()
    streams, tok_rows, width = ga_ref.shape
    n_seq, n_dp = lax.axis_size("seq"), lax.axis_size("dp")
    nz = n_seq // 2
    total = n_seq * tok_rows
    x_nbr, y_nbr = (y * 2 + (1 - x), sq), ((1 - y) * 2 + x, sq)
    sibling = (dp, z * 2 + (1 - c))
    up, down = (dp, sq + 2), (dp, sq - 2)
    greet(dp, sq, n_seq, n_dp)
    links, locals_ = [], []
    every = slice(None)

    def keep(link):
        link.start()
        links.append(link)
        return link

    def local(src, dst):
        copy = pltpu.make_async_copy(src, dst, loc.at[len(locals_)])
        copy.start()
        locals_.append(copy)
        return copy

    def loop(n, body):
        def step(j, carry):
            body(j)
            return carry
        lax.fori_loop(0, n, step, 0)

    grad_links = []
    for b in range(streams):
        out = []
        for k in range(1, n_seq):
            other = lax.rem(sq + k, n_seq)
            source = lax.rem(sq + n_seq - k, n_seq)
            src = ga_ref.at[b, :, pl.ds(pl.multiple_of(other * 128, 128), 128)]
            dst = do.at[b, pl.ds(pl.multiple_of(sq * tok_rows, tok_rows), tok_rows), :]
            land = do.at[b, pl.ds(pl.multiple_of(source * tok_rows, tok_rows), tok_rows), :]
            out.append(keep(Link(src, dst, land, (o_send, o_recv), b * 7 + k - 1, (dp, other))))
        grad_links.append(out)
    own_do = [
        local(
            ga_ref.at[b, :, pl.ds(pl.multiple_of(sq * 128, 128), 128)],
            do.at[b, pl.ds(pl.multiple_of(sq * tok_rows, tok_rows), tok_rows), :],
        )
        for b in range(streams)
    ]
    half, half_d = pu_ref.shape[6] // 2, pd_ref.shape[6] // 2
    chunks = [
        (pu_ref, 0, half, acc_u0, sib_u0, ra_u0, rb_u0, sa_u0, sb_u0, zr_u0, fin_u, gu_out),
        (pu_ref, half, half, acc_u1, sib_u1, ra_u1, rb_u1, sa_u1, sb_u1, zr_u1, fin_u, gu_out),
        (pd_ref, 0, half_d, acc_d0, sib_d0, ra_d0, rb_d0, sa_d0, sb_d0, zr_d0, fin_d, gd_out),
        (pd_ref, half_d, half_d, acc_d1, sib_d1, ra_d1, rb_d1, sa_d1, sb_d1, zr_d1, fin_d, gd_out),
        (po_ref, 0, po_ref.shape[6], acc_o, sib_o, ra_o, rb_o, sa_o, sb_o, zr_o, fin_o, go_out),
    ]
    pending, loads = {}, {}

    def wait(*key):
        for link in pending.pop(key):
            link.wait()

    def load(i):
        part, first, cols, acc, sib = chunks[i][:5]
        cut = pl.ds(first, cols)
        loads[i] = local(part.at[:, :, :, c, :, :, cut], acc)
        pending[("c", i)] = [
            keep(Link(part.at[:, :, :, 1 - c, :, :, cut], sib, sib, (x_send, x_recv), i * 5, sibling))
        ]

    def f32(v):
        return v.astype(F32)

    def cross_one(i):
        acc, sib, ra, rb = chunks[i][3:7]
        loads[i].wait()
        wait("c", i)

        def add(j):
            w, b = j // nz, j % nz
            acc[1 - y, w, b, 0] = (f32(acc[1 - y, w, b, 0]) + f32(sib[1 - y, w, b, 0])).astype(BF16)
            acc[w, 1 - x, b, 1] = (f32(acc[w, 1 - x, b, 1]) + f32(sib[w, 1 - x, b, 1])).astype(BF16)
        loop(2 * nz, add)
        pending[("x1", i)] = [
            keep(Link(acc.at[1 - y, :, :, 0], ra, ra, (x_send, x_recv), i * 5 + 1, y_nbr)),
            keep(Link(acc.at[:, 1 - x, :, 1], rb, rb, (x_send, x_recv), i * 5 + 2, x_nbr)),
        ]

    def cross_two(i):
        acc, sib, ra, rb, sa, sb = chunks[i][3:9]
        wait("x1", i)

        def add(b):
            acc[y, 1 - x, b, 0] = (
                f32(acc[y, 1 - x, b, 0]) + f32(sib[y, 1 - x, b, 0]) + f32(ra[1 - x, b])
            ).astype(BF16)
            acc[1 - y, x, b, 1] = (
                f32(acc[1 - y, x, b, 1]) + f32(sib[1 - y, x, b, 1]) + f32(rb[1 - y, b])
            ).astype(BF16)
        loop(nz, add)
        pending[("x2", i)] = [
            keep(Link(acc.at[y, 1 - x, :, 0], sa, sa, (x_send, x_recv), i * 5 + 3, x_nbr)),
            keep(Link(acc.at[1 - y, x, :, 1], sb, sb, (x_send, x_recv), i * 5 + 4, y_nbr)),
        ]

    def ways(t):
        return (
            (0, up, nz - t + z, (z <= t - 1) & (z <= nz - 2), nz - t + z - 1, (z >= 1) & (z <= t)),
            (1, down, z - nz + t, (z >= 1) & (z >= nz - t), z + 1 - nz + t, (z <= nz - 2) & (z >= nz - 1 - t)),
        )

    def z_send(i, t):
        acc, zr = chunks[i][3], chunks[i][9]
        pending[("z", i, t)] = [
            keep(Link(
                acc.at[y, x, block], zr.at[t - 1, way], zr.at[t - 1, way], (zw_send, zw_recv),
                (i * 3 + t - 1) * 2 + way, target, ok_send, ok_recv,
            ))
            for way, target, block, ok_send, _, ok_recv in ways(t)
        ]

    def cross_last(i):
        acc, sib, ra, rb, sa, sb = chunks[i][3:9]
        wait("x2", i)

        def add(b):
            acc[y, x, b, 0] = (
                f32(acc[y, x, b, 0]) + f32(sib[y, x, b, 0]) + f32(ra[x, b]) + f32(sa[b])
            ).astype(BF16)
            acc[y, x, b, 1] = (
                f32(acc[y, x, b, 1]) + f32(sib[y, x, b, 1]) + f32(rb[y, b]) + f32(sb[b])
            ).astype(BF16)
        loop(nz, add)
        z_send(i, 1)

    def z_pass(i, t):
        first, cols, acc = chunks[i][1:4]
        zr, fin, out = chunks[i][9:]
        wait("z", i, t)
        if t < nz - 1:
            for way, _, _, _, block, ok in ways(t):
                @pl.when(ok)
                def _():
                    for h in range(2):
                        acc[y, x, block, h] = (f32(acc[y, x, block, h]) + f32(zr[t - 1, way, h])).astype(BF16)
            z_send(i, t + 1)
            return
        cut = pl.ds(first, cols)
        fin[:, :, cut] = f32(acc[y, x, z])
        for way, ok in ((0, z >= 1), (1, z <= nz - 2)):
            @pl.when(ok)
            def _():
                fin[:, :, cut] += f32(zr[t - 1, way])
        local(fin.at[:, :, cut], out.at[:, :, cut])

    load(0)
    copies = [local(qkv_ref, qkv), local(ot_ref, ot), local(lse_ref, lse), local(wt_ref, wt)]
    load(1)
    load(2)
    load(3)
    load(4)
    copy_xh = local(xh_ref, xh)
    cross_one(0)
    for copy in copies:
        copy.wait()
    step = 256
    blocks = total // q_block

    def turn(j):
        b, r = j // (total // step), j % (total // step)
        row = pl.ds(pl.multiple_of(r * step, step), step)
        kt[b, :, row] = jnp.transpose(f32(qkv[b, row, 128:256])).astype(BF16)
    loop(streams * (total // step), turn)

    def prepare(b):
        own_do[b].wait()
        for link in grad_links[b]:
            link.wait()

        def one(r):
            row = pl.ds(pl.multiple_of(r * step, step), step)
            both = jnp.transpose(f32(do[b, row, :])) * ot[b, :, row]
            for h in range(2):
                delta[h:h + 1, row] = jnp.sum(both[h * 64:(h + 1) * 64], axis=0, keepdims=True)
        loop(total // step, one)
        dk[...] = jnp.zeros_like(dk)
        dv[...] = jnp.zeros_like(dv)

    tile = 256

    def attend(b, qb):
        row = pl.ds(pl.multiple_of(qb * q_block, q_block), q_block)
        distance_block(dist, len_ref, b, qb * q_block, total, q_block)
        lane = lax.broadcasted_iota(jnp.int32, (q_block, 128), 1)
        queries, grads = qkv[b, row, 0:128], do[b, row, :]
        for h in range(2):
            mine = (lane < 64) == (h == 0)
            own = jnp.where(mine, queries, jnp.zeros_like(queries))
            own_grad = jnp.where(mine, grads, jnp.zeros_like(grads))
            total_row, delta_row = lse[b, h:h + 1, row], delta[h:h + 1, row]
            slope = slope_ref[0, h]
            part = jnp.zeros((64, q_block), F32)
            for r in range(total // tile):
                keys = slice(r * tile, (r + 1) * tile)
                s = dot_nt(qkv[b, keys, 128:256], own) - slope * dist[keys, :]
                p = jnp.exp(s - total_row)
                gp_t = dot_nt(qkv[b, keys, 256:384], own_grad)
                ds = (p * (gp_t - delta_row)).astype(BF16)
                dv[keys, :] += dot_nn(p.astype(BF16), own_grad)
                dk[keys, :] += dot_nn(ds, own)
                part = part + dot_nn(kt[b, h * 64:(h + 1) * 64, keys], ds)
            dqt[h * 64:(h + 1) * 64, row] = part * 0.125

    def attend_some(b, first, last):
        def one(qb, carry):
            attend(b, qb)
            return carry
        lax.fori_loop(first, last, one, 0)

    def finish_stream(b):
        def one(r):
            row = pl.ds(pl.multiple_of(r * step, step), step)
            low = dqt[:, row].astype(BF16)
            dqkvt[b, 0:128, row] = low
            dqkv[row, 0:128] = jnp.transpose(f32(low)).astype(BF16)
            for first, grad in ((128, dk), (256, dv)):
                low = grad[row, :].astype(BF16)
                dqkv[row, first:first + 128] = low
                dqkvt[b, first:first + 128, row] = jnp.transpose(f32(low)).astype(BF16)
        loop(total // step, one)

        def product(s):
            row = pl.ds(pl.multiple_of(s * tok_rows, tok_rows), tok_rows)
            gp[b, s // 2, s % 2] = dot_nn(dqkv[row, :], wt[...]).astype(BF16)
        loop(n_seq, product)
        pending[("gc", b)] = [
            keep(Link(gp.at[b, :, 1 - c], gs.at[b], gs.at[b], (zg_send, zg_recv), b * 7, sibling))
        ]

    def g_send(b, t):
        pending[("g", b, t)] = [
            keep(Link(
                gp.at[b, block, c], gz.at[b, t - 1, way], gz.at[b, t - 1, way], (zg_send, zg_recv),
                b * 7 + 1 + (t - 1) * 2 + way, target, ok_send, ok_recv,
            ))
            for way, target, block, ok_send, _, ok_recv in ways(t)
        ]

    def g_first(b):
        wait("gc", b)

        def add(j):
            gp[b, j, c] = (f32(gp[b, j, c]) + f32(gs[b, j])).astype(BF16)
        loop(nz, add)
        g_send(b, 1)

    def g_pass(b, t):
        wait("g", b, t)
        if t < nz - 1:
            for way, _, _, _, block, ok in ways(t):
                @pl.when(ok)
                def _():
                    gp[b, block, c] = (f32(gp[b, block, c]) + f32(gz[b, t - 1, way])).astype(BF16)
            g_send(b, t + 1)
            return
        gfin[b] = f32(gp[b, z, c])
        for way, ok in ((0, z >= 1), (1, z <= nz - 2)):
            @pl.when(ok)
            def _():
                gfin[b] += f32(gz[b, t - 1, way])
        local(gfin.at[b], gx_out.at[b])

    def vector(row):
        block = f32(par_ref[row * 8:(row + 1) * 8, :])
        return jnp.concatenate([block[r:r + 1, :] for r in range(8)], axis=1)

    rows_dp = 32 * n_seq

    def weight_grad():
        copy_xh.wait()
        for r in range(width // step):
            cols = slice(r * step, (r + 1) * step)
            gt[:, cols] = dot_nn(dqkvt[0], xh[0, :, cols])
            for b in range(1, streams):
                gt[:, cols] += dot_nn(dqkvt[b], xh[b, :, cols])
        sums = jnp.sum(f32(dqkvt[0]), axis=1, keepdims=True)
        for b in range(1, streams):
            sums = sums + jnp.sum(f32(dqkvt[b]), axis=1, keepdims=True)
        pgp[...] = two_ref[...]
        gain, shift = vector(0), vector(1)
        for r in range(width // step):
            cols = slice(r * step, (r + 1) * step)
            weight, raw = f32(wt[:, cols]), gt[:, cols]
            pgp[0:1, cols] = jnp.sum(raw * weight, axis=0, keepdims=True)
            pgp[1:2, cols] = jnp.sum(sums * weight, axis=0, keepdims=True)
            grad = raw * gain[:, cols] + sums * shift[:, cols]
            dqs[cols, :] = jnp.transpose(grad).astype(BF16)
        out = []
        for m in range(1, n_dp):
            other = lax.rem(dp + m, n_dp)
            src = dqs.at[pl.ds(pl.multiple_of(other * rows_dp, rows_dp), rows_dp), :]
            out.append(keep(Link(src, dqr.at[m - 1], dqr.at[m - 1], (s_send, s_recv), m - 1, (other, sq))))
            src = pgp.at[:, pl.ds(pl.multiple_of(other * rows_dp, rows_dp), rows_dp)]
            out.append(keep(Link(src, pr1.at[m - 1], pr1.at[m - 1], (s_send, s_recv), 3 + m - 1, (other, sq))))
        pending["qd",] = out

    def weight_grad_two():
        wait("qd")
        mine = pl.ds(pl.multiple_of(dp * rows_dp, rows_dp), rows_dp)
        part = f32(dqs[mine, :])
        small = pgp[:, mine]
        for m in range(n_dp - 1):
            part = part + f32(dqr[m])
            small = small + pr1[m]
        dqsum[...] = part.astype(BF16)
        psum[...] = small
        out = []
        for k in range(1, n_seq):
            other = lax.rem(sq + k, n_seq)
            source = lax.rem(sq + n_seq - k, n_seq)
            src = dqsum.at[pl.ds(pl.multiple_of(other * 32, 32), 32), :]
            out.append(keep(Link(src, gq_out.at[sq], gq_out.at[source], (s_send, s_recv), 6 + k - 1, (dp, other))))
            src = psum.at[:, pl.ds(pl.multiple_of(other // 4 * 128, 128), 128)]
            out.append(keep(Link(src, pr2.at[k - 1], pr2.at[k - 1], (s_send, s_recv), 13 + k - 1, (dp, other))))
        local(dqsum.at[pl.ds(pl.multiple_of(sq * 32, 32), 32), :], gq_out.at[sq])
        pending["qs",] = out

    def weight_grad_last():
        wait("qs")
        small = psum[:, pl.ds(pl.multiple_of(sq // 4 * 128, 128), 128)]
        for k in range(n_seq - 1):
            small = small + pr2[k]
        pgo[...] = small
        local(pgo, pg_out)

    prepare(0)
    attend_some(0, 0, 1)
    cross_two(0)
    cross_one(1)
    attend_some(0, 1, 3)
    cross_last(0)
    attend_some(0, 3, 4)
    z_pass(0, 1)
    finish_stream(0)
    prepare(1)
    g_first(0)
    z_pass(0, 2)
    attend_some(1, 0, 1)
    cross_two(1)
    cross_one(2)
    z_pass(0, 3)
    attend_some(1, 1, 2)
    g_pass(0, 1)
    cross_last(1)
    attend_some(1, 2, 4)
    z_pass(1, 1)
    g_pass(0, 2)
    finish_stream(1)
    cross_two(2)
    cross_one(3)
    g_first(1)
    z_pass(1, 2)
    weight_grad()
    g_pass(0, 3)
    z_pass(1, 3)
    cross_last(2)
    g_pass(1, 1)
    z_pass(2, 1)
    cross_two(3)
    cross_one(4)
    g_pass(1, 2)
    z_pass(2, 2)
    weight_grad_two()
    cross_last(3)
    z_pass(2, 3)
    g_pass(1, 3)
    z_pass(3, 1)
    cross_two(4)
    z_pass(3, 2)
    weight_grad_last()
    cross_last(4)
    z_pass(3, 3)
    z_pass(4, 1)
    z_pass(4, 2)
    z_pass(4, 3)
    waited = [own_do[0], own_do[1], copy_xh, *copies, *loads.values()]
    for copy in locals_:
        if not any(copy is other for other in waited):
            copy.wait()
    for link in links:
        link.wait_sent()


def scatter_call(grad_attn, parts, qkv, ot, lse, xh, wt, params, two, lengths, slopes):
    streams, tok_rows, width = grad_attn.shape
    n_seq, n_dp = lax.axis_size("seq"), lax.axis_size("dp")
    nz, total = n_seq // 2, n_seq * tok_rows
    cols = qkv.shape[2]
    any_space = pl.BlockSpec(memory_space=pl.ANY)
    vmem = pl.BlockSpec(memory_space=pltpu.VMEM)
    smem = pl.BlockSpec(memory_space=pltpu.SMEM)
    dma = pltpu.SemaphoreType.DMA
    po, pu, pd = parts
    sizes = []
    for part, cuts in ((po, 1), (pu, 2), (pd, 2)):
        sizes += [(part.shape[5], part.shape[6] // cuts)] * cuts

    def buffers(*lead):
        return [pltpu.VMEM(lead + size, BF16) for size in sizes]

    scratch = buffers(2, 2, nz, 2) + buffers(2, 2, nz, 2) + buffers(2, nz) + buffers(2, nz)
    scratch += buffers(nz) + buffers(nz) + buffers(nz - 1, 2, 2)
    scratch += [pltpu.VMEM((2,) + part.shape[5:], F32) for part in parts]
    scratch += [
        pltpu.VMEM((streams, total, 128), BF16),
        pltpu.VMEM(qkv.shape, BF16),
        pltpu.VMEM(ot.shape, F32),
        pltpu.VMEM(lse.shape, F32),
        pltpu.VMEM(xh.shape, BF16),
        pltpu.VMEM(wt.shape, BF16),
        pltpu.VMEM((streams, 128, total), BF16),
        pltpu.VMEM((8, 128), F32),
        pltpu.VMEM((8, total), F32),
        pltpu.VMEM((total, q_block), F32),
        pltpu.VMEM((total, 128), F32),
        pltpu.VMEM((total, 128), F32),
        pltpu.VMEM((128, total), F32),
        pltpu.VMEM((total, cols), BF16),
        pltpu.VMEM((streams, cols, total), BF16),
        pltpu.VMEM((streams, nz, 2, tok_rows, width), BF16),
        pltpu.VMEM((streams, nz, tok_rows, width), BF16),
        pltpu.VMEM((streams, nz - 1, 2, tok_rows, width), BF16),
        pltpu.VMEM((streams, tok_rows, width), F32),
        pltpu.VMEM((cols, width), F32),
        pltpu.VMEM((width, cols), BF16),
        pltpu.VMEM((n_dp - 1, width // n_dp, cols), BF16),
        pltpu.VMEM((width // n_dp, cols), BF16),
        pltpu.VMEM((8, width), F32),
        pltpu.VMEM((n_dp - 1, 8, width // n_dp), F32),
        pltpu.VMEM((8, width // n_dp), F32),
        pltpu.VMEM((n_seq - 1, 8, 128), F32),
        pltpu.VMEM((8, 128), F32),
        dma((14,)), dma((14,)), dma((25,)), dma((25,)), dma((30,)), dma((30,)), dma((14,)), dma((14,)),
        dma((20,)), dma((20,)), dma((24,)),
    ]
    outs = [
        jax.ShapeDtypeStruct((streams, tok_rows, width), F32),
        *[jax.ShapeDtypeStruct((2,) + part.shape[5:], F32) for part in parts],
        jax.ShapeDtypeStruct((n_seq, width // (n_dp * n_seq), cols), BF16),
        jax.ShapeDtypeStruct((8, 128), F32),
    ]
    return pl.pallas_call(
        scatter_kernel,
        out_shape=outs,
        in_specs=[any_space] * 9 + [vmem, vmem, smem, smem],
        out_specs=[any_space] * len(outs),
        scratch_shapes=scratch,
        compiler_params=pltpu.CompilerParams(
            collective_id=1, has_side_effects=True, vmem_limit_bytes=62 * 2**20
        ),
        name="scatter_attend",
    )(grad_attn, po, pu, pd, qkv, ot, lse, xh, wt, params, two, lengths, slopes)


def gelu_both(v):
    inner = 0.7978845608028654 * (v + 0.044715 * v * v * v)
    th = jnp.tanh(inner)
    half = 0.5 * (1.0 + th)
    slope = half + 0.5 * v * (1.0 - th * th) * 0.7978845608028654 * (1.0 + 3 * 0.044715 * v * v)
    return v * half, slope


def norm_parts(v):
    mean = jnp.mean(v, axis=-1, keepdims=True)
    centered = v - mean
    rstd = lax.rsqrt(jnp.mean(centered * centered, axis=-1, keepdims=True) + norm_eps)
    return centered * rstd, rstd


def norm_back(n, rstd, e):
    return rstd * (
        e - jnp.mean(e, axis=-1, keepdims=True) - n * jnp.mean(e * n, axis=-1, keepdims=True)
    )


def by_heads(
    inputs, lengths, infill, cotangent, w_qkv, w_out, w_up, w_down,
    gain_one, shift_one, gain_two, shift_two,
):
    streams, tok_rows, width = inputs.shape
    n_seq, n_dp = lax.axis_size("seq"), lax.axis_size("dp")
    sq, rank = lax.axis_index("seq"), lax.axis_index("dp") * n_seq + lax.axis_index("seq")
    stream_len, tokens = tok_rows * n_seq, streams * tok_rows
    own_rows = w_qkv.shape[0]
    wq_blocks = w_qkv.reshape(own_rows, 3, n_seq, 128).transpose(2, 0, 1, 3)
    wq_blocks = wq_blocks.reshape(n_seq, own_rows, 384)
    mine = jnp.stack([gain_one, shift_one, gain_two, shift_two])
    params = lax.dynamic_update_slice(jnp.zeros((4, width), BF16), mine, (0, rank * own_rows))
    slopes = lax.dynamic_slice(slope_table(HEADS, stream_len), (sq * 2,), (2,)).reshape(1, 2)
    full_out, full_up, full_down, params, attn, qkv, ot, lse, xh, wt = gather_call(
        inputs, wq_blocks, w_out, w_up, w_down, params.reshape(32, 128), lengths, slopes
    )
    full_out = full_out.reshape(width, width)
    full_up = full_up.reshape(width, -1)
    full_down = full_down.reshape(-1, width)
    gain_two_f, shift_two_f = params.reshape(4, width)[2:].astype(F32)
    inputs_f = inputs.reshape(tokens, width).astype(F32)
    attn = attn.reshape(tokens, width)
    hidden = inputs_f + dot_nn(attn, full_out)
    n_two, r_two = norm_parts(hidden)
    normed_two = (n_two * gain_two_f + shift_two_f).astype(BF16)
    upward = dot_nn(normed_two, full_up)
    active_f, slope = gelu_both(upward)
    active = active_f.astype(BF16)
    output = (hidden + dot_nn(active, full_down)).astype(BF16)
    grad_output = (
        cotangent.reshape(tokens, width).astype(F32) * infill.reshape(tokens, 1).astype(F32)
    ).astype(BF16)
    grad_upward = (dot_nt(grad_output, full_down) * slope).astype(BF16)
    grad_norm_two = dot_nt(grad_upward, full_up)
    grad_hidden = grad_output.astype(F32) + norm_back(n_two, r_two, grad_norm_two * gain_two_f)
    grad_branch = grad_hidden.astype(BF16)
    grad_attn = dot_nt(grad_branch, full_out).astype(BF16)
    two = jnp.stack([jnp.sum(grad_norm_two * n_two, axis=0), jnp.sum(grad_norm_two, axis=0)])
    two = jnp.pad(two, ((2, 4), (0, 0)))

    def term(a, b):
        return lax.dot_general(
            a, b, (((0,), (0,)), ((), ())), preferred_element_type=F32
        ).astype(BF16)

    def split(v):
        return v.reshape(2, n_dp // 2, n_seq // 2, 2, 2, v.shape[0] // (n_dp * n_seq * 2), v.shape[1])

    parts = [
        split(term(attn, grad_branch)),
        split(term(normed_two, grad_upward)),
        split(term(active, grad_output)),
    ]
    grad_norm_one, grad_out, grad_up, grad_down, grad_qkv, small = scatter_call(
        grad_attn.reshape(inputs.shape), parts, qkv, ot, lse, xh.reshape(streams, stream_len, width),
        wt, params, two, lengths, slopes,
    )
    gain_one_f = params.reshape(4, width)[0].astype(F32)
    n_one, r_one = norm_parts(inputs_f)
    grad_in = norm_back(n_one, r_one, grad_norm_one.reshape(tokens, width) * gain_one_f)
    input_grad = (grad_hidden + grad_in).astype(BF16)
    grad_qkv = grad_qkv.reshape(n_seq, own_rows, 3, 128).transpose(1, 2, 0, 3)
    small = lax.dynamic_slice(small, (0, sq % (128 // own_rows) * own_rows), (4, own_rows))
    return (
        output.reshape(inputs.shape),
        input_grad.reshape(inputs.shape),
        grad_qkv.reshape(own_rows, 3 * width).astype(F32),
        grad_out.reshape(w_out.shape),
        grad_up.reshape(w_up.shape),
        grad_down.reshape(w_down.shape),
        small[0], small[1], small[2], small[3],
    )


def layer_norm(features, gain_vec, shift_vec):
    row_mean = jnp.mean(features, axis=-1, keepdims=True)
    centered = features - row_mean
    spread = jnp.mean(centered * centered, axis=-1, keepdims=True)
    return centered * lax.rsqrt(spread + norm_eps) * gain_vec + shift_vec


def segment_of(bounds, positions):
    return jnp.sum((positions[None, :, None] >= bounds[:, None, :]).astype(jnp.int32), axis=2)


def slope_table(head_count, stream_len):
    return 2.0 ** (-8.0 * (jnp.arange(head_count, dtype=jnp.float32) + 1.0) / head_count) * (
        256.0 / stream_len
    )


def block_scores(queries, key_heads, query_pos, key_pos, query_seg, key_seg, slopes):
    raw_scores = jnp.einsum(
        "sqhc,skhc->shqk", queries, key_heads, preferred_element_type=jnp.float32
    )
    distance = jnp.abs(query_pos[:, None] - key_pos[None, :]).astype(jnp.float32)
    scores = (
        raw_scores * queries.shape[3] ** (-0.5) - slopes[None, :, None, None] * distance[None, None]
    )
    same_utt = query_seg[:, None, :, None] == key_seg[:, None, None, :]
    return jnp.where(same_utt, scores, masked_score)


def score_grads(
    queries,
    grad_heads,
    log_total,
    delta,
    key_heads,
    values,
    query_pos,
    key_pos,
    query_seg,
    key_seg,
    slopes,
):
    scores = block_scores(queries, key_heads, query_pos, key_pos, query_seg, key_seg, slopes)
    probs = jnp.exp(scores - log_total[..., None])
    grad_probs = jnp.einsum(
        "sqhc,skhc->shqk", grad_heads, values, preferred_element_type=jnp.float32
    )
    grad_scores = (probs * (grad_probs - delta[..., None])).astype(jnp.bfloat16)
    return (probs.astype(jnp.bfloat16), grad_scores)


def by_frames(
    inputs,
    lengths,
    infill,
    cotangent,
    w_qkv,
    w_out,
    w_up,
    w_down,
    gain_one,
    shift_one,
    gain_two,
    shift_two,
):
    w_qkv, w_out, w_up, w_down, gain_one, shift_one, gain_two, shift_two = (
        lax.all_gather(w_qkv, ("dp", "seq"), axis=0, tiled=True),
        lax.all_gather(w_out, ("dp", "seq"), axis=0, tiled=True),
        lax.all_gather(w_up, ("dp", "seq"), axis=0, tiled=True),
        lax.all_gather(w_down, ("dp", "seq"), axis=0, tiled=True),
        lax.all_gather(gain_one, ("dp", "seq"), axis=0, tiled=True),
        lax.all_gather(shift_one, ("dp", "seq"), axis=0, tiled=True),
        lax.all_gather(gain_two, ("dp", "seq"), axis=0, tiled=True),
        lax.all_gather(shift_two, ("dp", "seq"), axis=0, tiled=True),
    )
    streams, tok_rows, model_width = inputs.shape
    head_count = HEADS
    head_size = HEAD_DIM
    stream_len = tok_rows * lax.axis_size("seq")
    score_scale = head_size ** (-0.5)
    slopes = slope_table(head_count, stream_len)
    bounds = jnp.cumsum(lengths, axis=1)
    own_pos = lax.axis_index("seq") * tok_rows + jnp.arange(tok_rows, dtype=jnp.int32)
    own_seg = segment_of(bounds, own_pos)
    gain_one_f = gain_one.astype(jnp.float32)
    shift_one_f = shift_one.astype(jnp.float32)
    gain_two_f = gain_two.astype(jnp.float32)
    shift_two_f = shift_two.astype(jnp.float32)
    inputs_f = inputs.astype(jnp.float32)
    normed_one = layer_norm(inputs_f, gain_one_f, shift_one_f).astype(jnp.bfloat16)
    packed = jnp.einsum(
        "std,de->ste", normed_one, w_qkv, preferred_element_type=jnp.float32
    ).astype(jnp.bfloat16)
    query_low = packed[:, :, :model_width]
    key_value = packed[:, :, model_width:]
    query_heads = query_low.reshape(streams, tok_rows, head_count, head_size)
    start_state = (
        jnp.full((streams, head_count, tok_rows), masked_score, jnp.float32),
        jnp.zeros((streams, head_count, tok_rows), jnp.float32),
        jnp.zeros((streams, head_count, tok_rows, head_size), jnp.float32),
    )
    shard_piece = lax.all_gather(key_value, "seq", axis=1, tiled=True)
    key_count = shard_piece.shape[1]
    visit_block_len = 256

    def one_block(carried, offset):
        top_score, weight_sum, weighted = carried
        key_part = lax.dynamic_slice_in_dim(shard_piece, offset, visit_block_len, 1)
        key_pos = offset + jnp.arange(visit_block_len, dtype=jnp.int32)
        key_seg = segment_of(bounds, key_pos)
        key_heads = key_part[:, :, :model_width].reshape(
            streams, visit_block_len, head_count, head_size
        )
        values = key_part[:, :, model_width:].reshape(
            streams, visit_block_len, head_count, head_size
        )
        scores = block_scores(query_heads, key_heads, own_pos, key_pos, own_seg, key_seg, slopes)
        new_top = jnp.maximum(top_score, jnp.max(scores, axis=3))
        rescale = jnp.exp(top_score - new_top)
        weights_blk = jnp.exp(scores - new_top[..., None])
        weight_sum = weight_sum * rescale + jnp.sum(weights_blk, axis=3)
        weighted = weighted * rescale[..., None] + jnp.einsum(
            "shqk,skhc->shqc",
            weights_blk.astype(jnp.bfloat16),
            values,
            preferred_element_type=jnp.float32,
        )
        return ((new_top, weight_sum, weighted), None)

    offsets = jnp.arange(key_count // visit_block_len, dtype=jnp.int32) * visit_block_len
    finished, _ = lax.scan(one_block, start_state, offsets)
    top_score, weight_sum, weighted = finished
    attn_heads = weighted / weight_sum[..., None]
    log_total = top_score + jnp.log(weight_sum)
    attn_rows = jnp.transpose(attn_heads, (0, 2, 1, 3)).reshape(streams, tok_rows, model_width)
    attn_low = attn_rows.astype(jnp.bfloat16)
    hidden = inputs_f + jnp.einsum(
        "std,de->ste", attn_low, w_out, preferred_element_type=jnp.float32
    )
    normed_two_f, ln_two_pull = jax.vjp(layer_norm, hidden, gain_two_f, shift_two_f)
    normed_two = normed_two_f.astype(jnp.bfloat16)
    upward = jnp.einsum("std,df->stf", normed_two, w_up, preferred_element_type=jnp.float32)
    active_f, gelu_pull = jax.vjp(jax.nn.gelu, upward)
    active = active_f.astype(jnp.bfloat16)
    output = (
        hidden + jnp.einsum("stf,fd->std", active, w_down, preferred_element_type=jnp.float32)
    ).astype(jnp.bfloat16)
    grad_output = (cotangent.astype(jnp.float32) * infill.astype(jnp.float32)[:, :, None]).astype(
        jnp.bfloat16
    )
    grad_active = jnp.einsum("ste,fe->stf", grad_output, w_down, preferred_element_type=jnp.float32)
    grad_upward = gelu_pull(grad_active)[0].astype(jnp.bfloat16)
    grad_norm_two = jnp.einsum("stf,df->std", grad_upward, w_up, preferred_element_type=jnp.float32)
    grad_in_two, grad_gain_two, grad_shift_two = ln_two_pull(grad_norm_two)
    grad_hidden = grad_output.astype(jnp.float32) + grad_in_two
    grad_branch = grad_hidden.astype(jnp.bfloat16)
    grad_attn = jnp.einsum(
        "ste,de->std", grad_branch, w_out, preferred_element_type=jnp.float32
    ).astype(jnp.bfloat16)
    grad_heads = grad_attn.reshape(streams, tok_rows, head_count, head_size)
    delta = jnp.einsum("sqhc,shqc->shq", grad_heads.astype(jnp.float32), attn_heads)
    every_kv = lax.all_gather(key_value, "seq", axis=1, tiled=True)
    total_len = every_kv.shape[1]
    block_len = 256
    offsets = jnp.arange(total_len // block_len, dtype=jnp.int32) * block_len
    grad_start = jnp.zeros((streams, tok_rows, head_count, head_size), jnp.float32)

    def key_step(grad_query, offset):
        key_part = lax.dynamic_slice_in_dim(every_kv, offset, block_len, 1)
        key_pos = offset + jnp.arange(block_len, dtype=jnp.int32)
        key_seg = segment_of(bounds, key_pos)
        key_heads = key_part[:, :, :model_width].reshape(streams, block_len, head_count, head_size)
        values = key_part[:, :, model_width:].reshape(streams, block_len, head_count, head_size)
        probs_low, grad_scores = score_grads(
            query_heads,
            grad_heads,
            log_total,
            delta,
            key_heads,
            values,
            own_pos,
            key_pos,
            own_seg,
            key_seg,
            slopes,
        )
        grad_query = (
            grad_query
            + jnp.einsum(
                "shqk,skhc->sqhc", grad_scores, key_heads, preferred_element_type=jnp.float32
            )
            * score_scale
        )
        grad_keys = (
            jnp.einsum(
                "shqk,sqhc->kshc", grad_scores, query_heads, preferred_element_type=jnp.float32
            )
            * score_scale
        )
        grad_values = jnp.einsum(
            "shqk,sqhc->kshc", probs_low, grad_heads, preferred_element_type=jnp.float32
        )
        key_terms = jnp.concatenate(
            [
                grad_keys.reshape(block_len, streams, model_width),
                grad_values.reshape(block_len, streams, model_width),
            ],
            axis=2,
        )
        return (grad_query, key_terms)

    grad_query, key_terms = lax.scan(key_step, grad_start, offsets)
    key_terms = key_terms.reshape(total_len, streams, 2 * model_width)
    own_kv_grad = lax.psum_scatter(
        key_terms.astype(jnp.bfloat16), "seq", scatter_dimension=0, tiled=True
    ).astype(jnp.float32)
    grad_kv = jnp.transpose(own_kv_grad, (1, 0, 2))
    grad_packed = jnp.concatenate(
        [grad_query.reshape(streams, tok_rows, model_width), grad_kv], axis=2
    ).astype(jnp.bfloat16)
    grad_norm_one = jnp.einsum(
        "ste,de->std", grad_packed, w_qkv, preferred_element_type=jnp.float32
    )
    _, ln_one_pull = jax.vjp(layer_norm, inputs_f, gain_one_f, shift_one_f)
    grad_in_one, grad_gain_one, grad_shift_one = ln_one_pull(grad_norm_one)
    input_grad = (grad_hidden + grad_in_one).astype(jnp.bfloat16)
    weight_terms = (
        jnp.einsum("std,ste->de", normed_one, grad_packed, preferred_element_type=jnp.float32),
        jnp.einsum("std,ste->de", attn_low, grad_branch, preferred_element_type=jnp.float32),
        jnp.einsum("std,stf->df", normed_two, grad_upward, preferred_element_type=jnp.float32),
        jnp.einsum("stf,std->fd", active, grad_output, preferred_element_type=jnp.float32),
        grad_gain_one,
        grad_shift_one,
        grad_gain_two,
        grad_shift_two,
    )
    summed = (
        lax.psum_scatter(weight_terms[0], ("dp", "seq"), scatter_dimension=0, tiled=True),
        lax.psum_scatter(weight_terms[1], ("dp", "seq"), scatter_dimension=0, tiled=True),
        lax.psum_scatter(weight_terms[2], ("dp", "seq"), scatter_dimension=0, tiled=True),
        lax.psum_scatter(weight_terms[3], ("dp", "seq"), scatter_dimension=0, tiled=True),
        lax.psum_scatter(weight_terms[4], ("dp", "seq"), scatter_dimension=0, tiled=True),
        lax.psum_scatter(weight_terms[5], ("dp", "seq"), scatter_dimension=0, tiled=True),
        lax.psum_scatter(weight_terms[6], ("dp", "seq"), scatter_dimension=0, tiled=True),
        lax.psum_scatter(weight_terms[7], ("dp", "seq"), scatter_dimension=0, tiled=True),
    )
    return (
        output,
        input_grad,
        summed[0],
        summed[1],
        summed[2],
        summed[3],
        summed[4],
        summed[5],
        summed[6],
        summed[7],
    )


def solution(mesh):
    in_specs = (
        P("dp", "seq", None),
        P("dp", None),
        P("dp", "seq"),
        P("dp", "seq", None),
        P(("dp", "seq"), None),
        P(("dp", "seq"), None),
        P(("dp", "seq"), None),
        P(("dp", "seq"), None),
        P(("dp", "seq")),
        P(("dp", "seq")),
        P(("dp", "seq")),
        P(("dp", "seq")),
    )
    out_specs = (
        P("dp", "seq", None),
        P("dp", "seq", None),
        P(("dp", "seq"), None),
        P(("dp", "seq"), None),
        P(("dp", "seq"), None),
        P(("dp", "seq"), None),
        P(("dp", "seq")),
        P(("dp", "seq")),
        P(("dp", "seq")),
        P(("dp", "seq")),
    )
    grid = (mesh.shape["dp"], mesh.shape["seq"])
    local = by_heads if grid == (4, HEADS // 2) else by_frames
    return jax.shard_map(local, mesh=mesh, in_specs=in_specs, out_specs=out_specs, check_vma=False)
```

```python
import jax
import jax.numpy as jnp
from jax import lax
from jax.experimental import pallas as pl
from jax.experimental.pallas import tpu as pltpu

from jax.sharding import PartitionSpec as P

HEADS = 16
HEAD_DIM = 64

norm_eps = 1e-05
masked_score = -1e30
MESH_ID = pl.DeviceIdType.MESH
F32 = jnp.float32
BF16 = jnp.bfloat16
far = 1e33
q_block = 256


def place():
    dp, sq = lax.axis_index("dp"), lax.axis_index("seq")
    return dp, sq, dp // 2, dp % 2, sq // 2, sq % 2


def dot_nt(a, b):
    return lax.dot_general(a, b, (((1,), (1,)), ((), ())), preferred_element_type=F32)


def dot_nn(a, b):
    return lax.dot_general(a, b, (((1,), (0,)), ((), ())), preferred_element_type=F32)


class Link:
    def __init__(self, src, dst, landing, sems, index, target, when_send=None, when_recv=None):
        self.sems, self.index, self.target = sems, index, target
        self.src, self.dst, self.landing = src, dst, landing
        self.when_send, self.when_recv = when_send, when_recv

    def copy(self, src, dst):
        send, recv = self.sems
        return pltpu.make_async_remote_copy(
            src_ref=src,
            dst_ref=dst,
            send_sem=send.at[self.index],
            recv_sem=recv.at[self.index],
            device_id=self.target,
            device_id_type=MESH_ID,
        )

    def run(self, when, action):
        if when is None:
            action()
        else:
            pl.when(when)(action)

    def start(self):
        self.run(self.when_send, lambda: self.copy(self.src, self.dst).start())

    def wait(self):
        self.run(self.when_recv, lambda: self.copy(self.landing, self.landing).wait_recv())

    def wait_sent(self):
        self.run(self.when_send, lambda: self.copy(self.src, self.dst).wait_send())


def greet(dp, sq, n_seq, n_dp):
    barrier = pltpu.get_barrier_semaphore()
    for k in range(1, n_seq):
        pl.semaphore_signal(
            barrier, inc=1, device_id=(dp, lax.rem(sq + k, n_seq)), device_id_type=MESH_ID
        )
    for m in range(1, n_dp):
        other = lax.rem(dp + m, n_dp)
        pl.semaphore_signal(barrier, inc=1, device_id=(other, sq), device_id_type=MESH_ID)
    pl.semaphore_wait(barrier, n_seq - 1 + n_dp - 1)


def distance(len_ref, stream, first_key, keys, first_query, queries):
    key_pos = lax.broadcasted_iota(jnp.int32, (keys, 1), 0) + first_key
    query_pos = lax.broadcasted_iota(jnp.int32, (1, queries), 1) + first_query
    key_seg = jnp.zeros((keys, 1), jnp.int32)
    query_seg = jnp.zeros((1, queries), jnp.int32)
    bound = 0
    for k in range(len_ref.shape[1]):
        bound = bound + len_ref[stream, k]
        key_seg = key_seg + (key_pos >= bound).astype(jnp.int32)
        query_seg = query_seg + (query_pos >= bound).astype(jnp.int32)
    gap = jnp.abs(key_pos - query_pos).astype(F32)
    return jnp.where(key_seg == query_seg, gap, far)


def gather_kernel(
    x_ref, wq_ref, wo_ref, wu_ref, wd_ref, par_ref, len_ref, slope_ref,
    wo_all, wu_all, wd_all, par_out, attn, qkv_out, ot_out, lse_out, xh_out, wt_out,
    xg, xh, wqb, wt, pbuf, pown, par, qkv, vt, obuf, ot, lse, dist,
    z_send, z_recv, w_send, w_recv, x_send, x_recv, s_send, s_recv, loc,
):
    dp, sq, y, x, z, c = place()
    streams, tok_rows, width = x_ref.shape
    n_seq, n_dp = lax.axis_size("seq"), lax.axis_size("dp")
    nz = n_seq // 2
    total = n_seq * tok_rows
    own_rows = par_ref.shape[0]
    x_nbr, y_nbr = (y * 2 + (1 - x), sq), ((1 - y) * 2 + x, sq)
    sibling = (dp, z * 2 + (1 - c))
    up, down = (dp, sq + 2), (dp, sq - 2)
    greet(dp, sq, n_seq, n_dp)
    links = []

    def keep(link):
        link.start()
        links.append(link)
        return link

    locals_ = []

    def local(src, dst):
        copy = pltpu.make_async_copy(src, dst, loc.at[len(locals_)])
        copy.start()
        locals_.append(copy)
        return copy

    cp_x = local(x_ref, xg.at[:, sq])
    cp_wq = local(wq_ref.at[sq], wqb.at[pl.ds(pl.multiple_of(sq * 32 + dp * 32 * n_seq, 32), 32), :])
    cp_w = [
        local(src, dst.at[y, x, z, c])
        for src, dst in ((wo_ref, wo_all), (wu_ref, wu_all), (wd_ref, wd_all))
    ]

    par_links, wq_links = [], []
    for k in range(1, n_seq):
        other = lax.rem(sq + k, n_seq)
        source = lax.rem(sq + n_seq - k, n_seq)
        par_links.append(
            keep(Link(par_ref, pbuf.at[k - 1], pbuf.at[k - 1], (s_send, s_recv), k - 1, (dp, other)))
        )
        mine = wqb.at[pl.ds(pl.multiple_of(sq * 32 + dp * 32 * n_seq, 32), 32), :]
        theirs = wqb.at[pl.ds(pl.multiple_of(source * 32 + dp * 32 * n_seq, 32), 32), :]
        wq_links.append(
            keep(Link(wq_ref.at[other], mine, theirs, (s_send, s_recv), 7 + k - 1, (dp, other)))
        )
    arrays = [(wo_ref, wo_all), (wu_ref, wu_all), (wd_ref, wd_all)]
    groups = [(0, 1), (2,)]
    pending = {}
    every = slice(None)

    def wait(*key):
        for link in pending.pop(key):
            link.wait()

    def blocks_of(h):
        if h == 0:
            return [(0, z, None)]
        return [(2 * h - 1, z - h, z >= h), (2 * h, z + h, z + h <= nz - 1)]

    def z_hop(g, h):
        out = []
        for i in groups[g]:
            own, full = arrays[i]
            for way, target, block, landing, ok_send, ok_recv in (
                (0, up, z - (h - 1), z - h, (z >= h - 1) & (z <= nz - 2), z >= h),
                (1, down, z + (h - 1), z + h, (z + h - 1 <= nz - 1) & (z >= 1), z + h <= nz - 1),
            ):
                there = full.at[y, x, block, c]
                src = own if h == 1 else there
                index = (i * 3 + h - 1) * 2 + way
                out.append(keep(Link(
                    src, there, full.at[y, x, landing, c], (w_send, w_recv), index, target, ok_send, ok_recv
                )))
        pending[("z", g, h)] = out

    def plane(tag, g, h, pairs):
        out = []
        for i in groups[g]:
            own, full = arrays[i]
            for slot, block, ok in blocks_of(h):
                for kind, target, where, landing, own_half in pairs(block):
                    here = full.at[where]
                    src = own.at[own_half] if own_half is not None and h == 0 else here
                    out.append(keep(Link(
                        src, here, full.at[landing], (x_send, x_recv), (i * 7 + slot) * 5 + kind, target, ok, ok
                    )))
        pending[(tag, g, h)] = out

    def cross_one(g, h):
        plane("x1", g, h, lambda b: [
            (0, x_nbr, (y, x, b, c, 0), (y, 1 - x, b, c, 0), 0),
            (1, y_nbr, (y, x, b, c, 1), (1 - y, x, b, c, 1), 1),
        ])

    def cross_two(g, h):
        wait("x1", g, h)
        plane("x2", g, h, lambda b: [
            (2, y_nbr, (y, every, b, c, 0), (1 - y, every, b, c, 0), None),
            (3, x_nbr, (every, x, b, c, 1), (every, 1 - x, b, c, 1), None),
        ])

    def cross_core(g, h):
        wait("x2", g, h)
        plane("c", g, h, lambda b: [
            (4, sibling, (every, every, b, c), (every, every, b, 1 - c), None),
        ])

    def x_hop(h):
        out = []
        for way, target, block, landing, ok_send, ok_recv in (
            (0, up, z - (h - 1), z - h, (z >= h - 1) & (z <= nz - 2), z >= h),
            (1, down, z + (h - 1), z + h, (z + h - 1 <= nz - 1) & (z >= 1), z + h <= nz - 1),
        ):
            there = xg.at[:, block * 2 + c]
            src = x_ref if h == 1 else there
            index = (h - 1) * 2 + way
            out.append(
                keep(Link(src, there, xg.at[:, landing * 2 + c], (z_send, z_recv), index, target, ok_send, ok_recv))
            )
        pending[("x", h)] = out

    def x_pass(h):
        out = []
        for way, block, ok in ((0, z - h, z >= h), (1, z + h, z + h <= nz - 1)):
            src = xg.at[:, block * 2 + c]
            land = xg.at[:, block * 2 + (1 - c)]
            out.append(
                keep(Link(src, src, land, (z_send, z_recv), 6 + (h - 1) * 2 + way, sibling, ok, ok))
            )
        pending[("xc", h)] = out

    z_hop(0, 1)
    cross_one(0, 0)
    sib_x = keep(Link(x_ref, xg.at[:, sq], xg.at[:, z * 2 + (1 - c)], (z_send, z_recv), 12, sibling))
    x_hop(1)
    for link in par_links:
        link.wait()
    pown[...] = par_ref[...] + pbuf[0]
    for k in range(1, n_seq - 1):
        pown[...] += pbuf[k]
    par_dp = []
    for m in range(1, n_dp):
        par_dp.append(
            keep(Link(pown, pbuf.at[n_seq - 2 + m], pbuf.at[n_seq - 2 + m], (s_send, s_recv), 14 + m - 1, (lax.rem(dp + m, n_dp), sq)))
        )
    for link in wq_links:
        link.wait()
    cp_wq.wait()
    wq_dp = []
    rows_dp = 32 * n_seq
    for m in range(1, n_dp):
        mine = wqb.at[pl.ds(pl.multiple_of(dp * rows_dp, 32), rows_dp), :]
        source = lax.rem(dp + n_dp - m, n_dp)
        theirs = wqb.at[pl.ds(pl.multiple_of(source * rows_dp, 32), rows_dp), :]
        wq_dp.append(
            keep(Link(mine, mine, theirs, (s_send, s_recv), 17 + m - 1, (lax.rem(dp + m, n_dp), sq)))
        )
    for copy in cp_w:
        copy.wait()
    cross_two(0, 0)
    wait("z", 0, 1)
    z_hop(0, 2)
    cross_one(0, 1)
    for link in par_dp:
        link.wait()
    par[...] = pown[...] + pbuf[n_seq - 1] + pbuf[n_seq] + pbuf[n_seq + 1]
    for link in wq_dp:
        link.wait()
    step = 256
    for r in range(width // step):
        wt[:, r * step:(r + 1) * step] = jnp.transpose(
            wqb[r * step:(r + 1) * step, :].astype(F32)
        ).astype(BF16)
    put_wt = local(wt, wt_out)
    put_par = local(par, par_out)

    lanes = width // 8

    def vector(row):
        block = par[row * 8:(row + 1) * 8, :].astype(F32)
        return jnp.concatenate([block[r:r + 1, :] for r in range(8)], axis=1)

    gain, shift = vector(0), vector(1)
    scale = 0.125

    def process(s):
        def one(b, carry):
            v = xg[b, s].astype(F32)
            mean = jnp.mean(v, axis=1, keepdims=True)
            v = v - mean
            spread = jnp.mean(v * v, axis=1, keepdims=True)
            n = v * lax.rsqrt(spread + 1e-5)
            xh[b, s] = n.astype(BF16)
            normed = (n * gain + shift).astype(BF16)
            packed = dot_nt(normed, wt[...])
            row = pl.ds(pl.multiple_of(s * tok_rows, tok_rows), tok_rows)
            qkv[b, row, 0:128] = (packed[:, 0:128] * scale).astype(BF16)
            qkv[b, row, 128:384] = packed[:, 128:384].astype(BF16)
            return carry
        lax.fori_loop(0, streams, one, 0)

    def process_hop(h):
        def one(j, carry):
            way, core = j // 2, j % 2
            block = jnp.where(way == 0, z - h, z + h)
            ok = jnp.where(way == 0, (z >= h).astype(jnp.int32), (z + h <= nz - 1).astype(jnp.int32))

            @pl.when(ok == 1)
            def _():
                process(block * 2 + core)
            return carry
        lax.fori_loop(0, 4, one, 0)

    wait("x", 1)
    x_hop(2)
    x_pass(1)
    cp_x.wait()
    sib_x.wait()

    def first_two(j, carry):
        process(z * 2 + j)
        return carry
    lax.fori_loop(0, 2, first_two, 0)
    cross_core(0, 0)
    cross_two(0, 1)
    wait("z", 0, 2)
    z_hop(0, 3)
    cross_one(0, 2)
    wait("xc", 1)
    process_hop(1)
    wait("x", 2)
    x_hop(3)
    x_pass(2)
    z_hop(1, 1)
    cross_core(0, 1)
    cross_two(0, 2)
    cross_one(1, 0)
    wait("xc", 2)
    process_hop(2)
    wait("z", 0, 3)
    cross_one(0, 3)
    wait("z", 1, 1)
    z_hop(1, 2)
    cross_one(1, 1)
    wait("x", 3)
    x_pass(3)
    cross_core(0, 2)
    cross_two(0, 3)
    cross_two(1, 0)
    wait("xc", 3)
    process_hop(3)
    put_xh = local(xh, xh_out)
    put_qkv = local(qkv, qkv_out)

    def turn(j, carry):
        b, r = j // (total // step), j % (total // step)
        row = pl.ds(pl.multiple_of(r * step, step), step)
        vt[b, :, row] = jnp.transpose(qkv[b, row, 256:384].astype(F32)).astype(BF16)
        return carry
    lax.fori_loop(0, streams * (total // step), turn, 0)
    blocks = total // q_block

    def attend(j, carry):
        b, qb = j // blocks, j % blocks
        row = pl.ds(pl.multiple_of(qb * q_block, q_block), q_block)
        dist[...] = distance(len_ref, b, 0, total, qb * q_block, q_block)
        queries = qkv[b, row, 0:128]
        lane = lax.broadcasted_iota(jnp.int32, (q_block, 128), 1)
        for h in range(2):
            own = jnp.where((lane < 64) == (h == 0), queries, jnp.zeros_like(queries))
            s = dot_nt(qkv[b, :, 128:256], own) - slope_ref[0, h] * dist[...]
            top = jnp.max(s, axis=0, keepdims=True)
            p = jnp.exp(s - top)
            weight = jnp.sum(p, axis=0, keepdims=True)
            o = dot_nn(vt[b, h * 64:(h + 1) * 64, :], p.astype(BF16))
            ot[b, h * 64:(h + 1) * 64, row] = o / weight
            lse[b, h:h + 1, row] = top + jnp.log(weight)
        obuf[b, row, :] = jnp.transpose(ot[b, :, row]).astype(BF16)
        return carry

    def send_rows(b):
        out = []
        for k in range(1, n_seq):
            other = lax.rem(sq + k, n_seq)
            source = lax.rem(sq + n_seq - k, n_seq)
            src = obuf.at[b, pl.ds(pl.multiple_of(other * tok_rows, tok_rows), tok_rows), :]
            dst = attn.at[b, :, pl.ds(pl.multiple_of(sq * 128, 128), 128)]
            land = attn.at[b, :, pl.ds(pl.multiple_of(source * 128, 128), 128)]
            out.append(keep(Link(src, dst, land, (s_send, s_recv), 20 + b * 7 + k - 1, (dp, other))))
        pending[("o", b)] = out
        local(
            obuf.at[b, pl.ds(pl.multiple_of(sq * tok_rows, tok_rows), tok_rows), :],
            attn.at[b, :, pl.ds(pl.multiple_of(sq * 128, 128), 128)],
        )

    def attend_some(first, last):
        lax.fori_loop(first, last, attend, 0)

    attend_some(0, 2)
    wait("z", 1, 2)
    z_hop(1, 3)
    cross_one(1, 2)
    cross_two(1, 1)
    attend_some(2, 4)
    send_rows(0)
    cross_core(0, 3)
    cross_core(1, 0)
    attend_some(4, 6)
    wait("z", 1, 3)
    cross_one(1, 3)
    cross_two(1, 2)
    cross_core(1, 1)
    attend_some(6, 8)
    send_rows(1)
    put_ot = local(ot, ot_out)
    put_lse = local(lse, lse_out)
    cross_two(1, 3)
    cross_core(1, 2)
    cross_core(1, 3)
    for key in list(pending):
        wait(*key)
    for copy in locals_[5:]:
        copy.wait()
    for link in links:
        link.wait_sent()


def gather_call(inputs, wq_blocks, w_out, w_up, w_down, params, lengths, slopes):
    streams, tok_rows, width = inputs.shape
    n_seq, n_dp = lax.axis_size("seq"), lax.axis_size("dp")
    nz, total = n_seq // 2, n_seq * tok_rows
    any_space = pl.BlockSpec(memory_space=pl.ANY)
    vmem = pl.BlockSpec(memory_space=pltpu.VMEM)
    smem = pl.BlockSpec(memory_space=pltpu.SMEM)

    def halves(w):
        return w.reshape(2, w.shape[0] // 2, w.shape[1])

    own = [halves(w) for w in (w_out, w_up, w_down)]
    full = [jax.ShapeDtypeStruct((2, n_dp // 2, nz, 2) + w.shape, BF16) for w in own]
    cols = wq_blocks.shape[2]
    outs = full + [
        jax.ShapeDtypeStruct(params.shape, BF16),
        jax.ShapeDtypeStruct((streams, tok_rows, width), BF16),
        jax.ShapeDtypeStruct((streams, total, cols), BF16),
        jax.ShapeDtypeStruct((streams, 128, total), F32),
        jax.ShapeDtypeStruct((streams, 8, total), F32),
        jax.ShapeDtypeStruct((streams, n_seq, tok_rows, width), BF16),
        jax.ShapeDtypeStruct((cols, width), BF16),
    ]
    dma = pltpu.SemaphoreType.DMA
    scratch = [
        pltpu.VMEM((streams, n_seq, tok_rows, width), BF16),
        pltpu.VMEM((streams, n_seq, tok_rows, width), BF16),
        pltpu.VMEM((width, cols), BF16),
        pltpu.VMEM((cols, width), BF16),
        pltpu.VMEM((n_seq - 1 + n_dp - 1,) + params.shape, BF16),
        pltpu.VMEM(params.shape, BF16),
        pltpu.VMEM(params.shape, BF16),
        pltpu.VMEM((streams, total, cols), BF16),
        pltpu.VMEM((streams, 128, total), BF16),
        pltpu.VMEM((streams, total, 128), BF16),
        pltpu.VMEM((streams, 128, total), F32),
        pltpu.VMEM((streams, 8, total), F32),
        pltpu.VMEM((total, q_block), F32),
        dma((13,)), dma((13,)), dma((18,)), dma((18,)), dma((105,)), dma((105,)), dma((34,)), dma((34,)),
        dma((16,)),
    ]
    return pl.pallas_call(
        gather_kernel,
        out_shape=outs,
        in_specs=[vmem, vmem, vmem, vmem, vmem, vmem, smem, smem],
        out_specs=[any_space] * len(outs),
        scratch_shapes=scratch,
        compiler_params=pltpu.CompilerParams(
            collective_id=0, has_side_effects=True, vmem_limit_bytes=56 * 2**20
        ),
        name="gather_attend",
    )(inputs, wq_blocks, *own, params, lengths, slopes)


def gelu_both(v):
    square = v * v
    th = jnp.tanh(v * (0.7978845608028654 + 0.7978845608028654 * 0.044715 * square))
    half = 0.5 * (1.0 + th)
    bend = v * (0.5 - 0.5 * th * th)
    return v * half, half + bend * (0.7978845608028654 + 0.7978845608028654 * 0.134145 * square)


def norm_parts(v):
    mean = jnp.mean(v, axis=-1, keepdims=True)
    centered = v - mean
    rstd = lax.rsqrt(jnp.mean(centered * centered, axis=-1, keepdims=True) + norm_eps)
    return centered * rstd, rstd


def norm_back(n, rstd, e):
    return rstd * (
        e - jnp.mean(e, axis=-1, keepdims=True) - n * jnp.mean(e * n, axis=-1, keepdims=True)
    )


def scatter_kernel(
    x_ref, fill_ref, par_ref, cot_ref, attn_ref, wo_ref, wu_ref, wd_ref,
    qkv_ref, ot_ref, lse_ref, xh_ref, wt_ref, len_ref, slope_ref,
    y_out, gx_out, go_out, gu_out, gd_out, gq_out, pg_out,
    hidden, n_two, r_two, low_two, grad_two, gout2, gb2, act2, acto, n2s2, n2o, at2, ato, wo_v, wu_t, wd_t, gab,
    acc_o, acc_u, acc_d, ra_o, ra_u, ra_d, rb_o, rb_u, rb_d, sa_o, sa_u, sa_d, sb_o, sb_u, sb_d,
    zr_o, zr_u, zr_d, fin_o, fin_u, fin_d,
    do, qkv, ot, lse, xh, wt, kt, delta, dk, dv, dqt, dqkv, dqkvt,
    gp, gz_one, dqr, dqsum, pgp, pr1, psum, pr2, pgo,
    c_send, c_recv, o_send, o_recv, x_send, x_recv, zw_send, zw_recv, zg_send, zg_recv, s_send, s_recv,
    tile_sem, loc,
):
    dp, sq, y, x, z, c = place()
    streams, tok_rows, width = gab.shape
    tokens = streams * tok_rows
    n_seq, n_dp = lax.axis_size("seq"), lax.axis_size("dp")
    nz = n_seq // 2
    total = n_seq * tok_rows
    x_nbr, y_nbr = (y * 2 + (1 - x), sq), ((1 - y) * 2 + x, sq)
    sibling = (dp, z * 2 + (1 - c))
    up, down = (dp, sq + 2), (dp, sq - 2)
    greet(dp, sq, n_seq, n_dp)
    links, locals_ = [], []
    every = slice(None)

    def keep(link):
        link.start()
        links.append(link)
        return link

    def local(src, dst):
        copy = pltpu.make_async_copy(src, dst, loc.at[len(locals_)])
        copy.start()
        locals_.append(copy)
        return copy

    def loop(n, body):
        def step(j, carry):
            body(j)
            return carry
        lax.fori_loop(0, n, step, 0)

    pending = {}

    def wait(*key):
        for link in pending.pop(key):
            link.wait()

    def f32(v):
        return v.astype(F32)

    def vector(row):
        block = f32(par_ref[row * 8:(row + 1) * 8, :])
        return jnp.concatenate([block[r:r + 1, :] for r in range(8)], axis=1)

    def to_sibling(src, dst, index):
        return keep(Link(src, dst, dst, (c_send, c_recv), index, sibling))

    cols = wu_t.shape[2]
    tiles = wu_ref.shape[1] // cols
    near = 1 - z // 2

    def tile_place(i):
        k = i % 4
        ty = y + (1 - 2 * y) * (1 - k // 2)
        tx = x + (1 - 2 * x) * (1 - k % 2)
        return ty, tx, near + (1 - 2 * near) * (i // 4)

    def tile_copies(i):
        ty, tx, pair = tile_place(i)
        first = pl.multiple_of(((ty * 2 + tx) * 2 + pair) * cols, cols)
        slot = i % 2
        return (
            pltpu.make_async_copy(wu_ref.at[:, pl.ds(first, cols)], wu_t.at[slot], tile_sem.at[slot]),
            pltpu.make_async_copy(wd_ref.at[pl.ds(((ty * 2 + tx) * 2 + pair) * 4, 4)], wd_t.at[slot], tile_sem.at[2 + slot]),
        )

    load_cot, load_attn = local(cot_ref, gab), local(attn_ref, low_two)
    load_out = local(wo_ref, wo_v)
    for copy in tile_copies(0):
        copy.start()
    copies = [local(qkv_ref, qkv), local(ot_ref, ot), local(lse_ref, lse), local(wt_ref, wt)]
    copy_xh = [local(xh_ref.at[:, :, 0:cols], xh)]
    load_cot.wait()
    for b in range(streams):
        rows = slice(b * tok_rows, (b + 1) * tok_rows)
        gout2[rows] = (f32(gab[b]) * fill_ref[rows]).astype(BF16)
    gout_link = to_sibling(gout2.at[0:tokens], gout2.at[tokens:2 * tokens], 0)

    def chosen(parity):
        j = lax.broadcasted_iota(jnp.int32, (1, width // 2), 1)
        column = ((((j & 127) >> 5) * n_seq + (j >> 7) * 2 + parity) << 5) + (j & 31)
        return (lax.broadcasted_iota(jnp.int32, (width, 1), 0) == column).astype(F32).astype(BF16)

    ours, others = chosen(c), chosen(1 - c)

    def pick(v, mine, theirs, index):
        here, there = dot_nn(v, ours).astype(BF16), dot_nn(v, others).astype(BF16)
        for b in range(nz):
            mine[b, 0:tokens] = here[:, b * 128:(b + 1) * 128]
            theirs[b] = there[:, b * 128:(b + 1) * 128]
        return to_sibling(theirs, mine.at[:, tokens:2 * tokens], index)

    load_attn.wait()
    attn_link = pick(low_two[...], at2, ato, 1)
    load_out.wait()
    for r in range(0, width, 512):
        hidden[:, r:r + 512] = f32(x_ref[:, r:r + 512]) + dot_nn(
            low_two[...], wo_v[:, :, r:r + 512].reshape(width, 512)
        )
    gain_two, shift_two = vector(2), vector(3)
    for r in range(0, tokens, 128):
        n, rstd = norm_parts(hidden[r:r + 128])
        n_two[r:r + 128] = n
        r_two[r:r + 128] = jnp.broadcast_to(rstd, (128, 128))
        low_two[r:r + 128] = (n * gain_two + shift_two).astype(BF16)
    norm_link = pick(low_two[...], n2s2, n2o, 2)
    grad_two[...] = jnp.zeros_like(grad_two)

    def tile_links(i, make):
        ty, tx, pair = tile_place(i)
        group = pl.ds((ty * 2 + tx) * 4 + pair * 2, 2)
        cut = pl.ds(pl.multiple_of(pair * cols, cols), cols)
        return (
            make(acto.at[group], act2.at[group, tokens:2 * tokens], 4 + i * 2),
            make(gp.at[ty, tx * 2, :, :, cut], gp.at[ty, tx * 2 + 1, :, :, cut], 5 + i * 2),
        )

    def tile_link(src, dst, index):
        return Link(src, dst, dst, (c_send, c_recv), index, sibling)

    def one_tile(i, carry):
        slot = i % 2
        for copy in tile_copies(i):
            copy.wait()

        @pl.when(i + 1 < tiles)
        def _():
            for copy in tile_copies(i + 1):
                copy.start()
        ty, tx, pair = tile_place(i)
        up_f = dot_nn(low_two[...], wu_t[slot])
        act_f, bend = gelu_both(up_f)
        act = act_f.astype(BF16)
        group = (ty * 2 + tx) * 4 + pair * 2
        for j in range(2):
            lo, hi = act[:, j * 256:j * 256 + 128], act[:, j * 256 + 128:j * 256 + 256]
            act2[group + j, 0:tokens] = jnp.where(c == 0, lo, hi)
            acto[group + j] = jnp.where(c == 0, hi, lo)
        down = wd_t[slot].reshape(cols, width)
        hidden[...] += dot_nn(act, down)
        grad_up = (dot_nt(gout2[0:tokens], down) * bend).astype(BF16)
        cut = pl.ds(pl.multiple_of(pair * cols, cols), cols)
        gp[ty, tx * 2, :, :, cut] = grad_up.reshape(streams, tok_rows, cols)
        grad_two[...] += dot_nt(grad_up, wu_t[slot])
        for link in tile_links(i, tile_link):
            link.start()
        return carry

    arrays = [
        (acc_o, ra_o, rb_o, sa_o, sb_o, zr_o, fin_o, go_out),
        (acc_u, ra_u, rb_u, sa_u, sb_u, zr_u, fin_u, gu_out),
        (acc_d, ra_d, rb_d, sa_d, sb_d, zr_d, fin_d, gd_out),
    ]
    groups = [(1, 0), (2,)]
    U, D = 0, 1
    plane_of = [near * 3, 1 + near, z + 1 - 2 * (z % 2), z]

    def cross_one(g, p):
        t = plane_of[p]
        out = []
        for i in groups[g]:
            acc, ra, rb = arrays[i][:3]
            out.append(keep(Link(acc.at[1 - y, :, t, 0], ra.at[p], ra.at[p], (x_send, x_recv), (i * 4 + p) * 4, y_nbr)))
            out.append(keep(Link(acc.at[:, 1 - x, t, 1], rb.at[p], rb.at[p], (x_send, x_recv), (i * 4 + p) * 4 + 1, x_nbr)))
        pending[("x1", g, p)] = out

    def cross_two(g, p):
        t = plane_of[p]
        wait("x1", g, p)
        out = []
        for i in groups[g]:
            acc, ra, rb, sa, sb = arrays[i][:5]
            acc[y, 1 - x, t, 0] = (f32(acc[y, 1 - x, t, 0]) + f32(ra[p, 1 - x])).astype(BF16)
            acc[1 - y, x, t, 1] = (f32(acc[1 - y, x, t, 1]) + f32(rb[p, 1 - y])).astype(BF16)
            out.append(keep(Link(acc.at[y, 1 - x, t, 0], sa.at[p], sa.at[p], (x_send, x_recv), (i * 4 + p) * 4 + 2, x_nbr)))
            out.append(keep(Link(acc.at[1 - y, x, t, 1], sb.at[p], sb.at[p], (x_send, x_recv), (i * 4 + p) * 4 + 3, y_nbr)))
        pending[("x2", g, p)] = out

    def cross_three(g, p):
        t = plane_of[p]
        wait("x2", g, p)
        for i in groups[g]:
            acc, ra, rb, sa, sb = arrays[i][:5]
            acc[y, x, t, 0] = (f32(acc[y, x, t, 0]) + f32(ra[p, x]) + f32(sa[p])).astype(BF16)
            acc[y, x, t, 1] = (f32(acc[y, x, t, 1]) + f32(rb[p, y]) + f32(sb[p])).astype(BF16)

    def ways(t):
        return (
            (0, up, nz - t + z, (z <= t - 1) & (z <= nz - 2), nz - t + z - 1, (z >= 1) & (z <= t)),
            (1, down, z - nz + t, (z >= 1) & (z >= nz - t), z + 1 - nz + t, (z <= nz - 2) & (z >= nz - 1 - t)),
        )

    def z_send(g, t):
        pending[("z", g, t)] = [
            keep(Link(
                arrays[i][0].at[y, x, block], arrays[i][5].at[t - 1, way], arrays[i][5].at[t - 1, way],
                (zw_send, zw_recv), (i * 3 + t - 1) * 2 + way, target, ok_send, ok_recv,
            ))
            for i in groups[g]
            for way, target, block, ok_send, _, ok_recv in ways(t)
        ]

    def z_pass(g, t):
        wait("z", g, t)
        for i in groups[g]:
            acc, zr, fin, out = arrays[i][0], *arrays[i][5:]
            if t < nz - 1:
                for way, _, _, _, block, ok in ways(t):
                    @pl.when(ok)
                    def _():
                        for h in range(2):
                            acc[y, x, block, h] = (f32(acc[y, x, block, h]) + f32(zr[t - 1, way, h])).astype(BF16)
                continue
            fin[...] = f32(acc[y, x, z])
            for way, ok in ((0, z >= 1), (1, z <= nz - 2)):
                @pl.when(ok)
                def _():
                    fin[...] += f32(zr[t - 1, way])
            local(fin, out)
        if t < nz - 1:
            z_send(g, t + 1)

    def dot_tn(a, b):
        return lax.dot_general(a, b, (((0,), (0,)), ((), ())), preferred_element_type=F32)

    def down_terms(pair):
        def one(d):
            left = jnp.concatenate([act2[d * 4 + pair * 2], act2[d * 4 + pair * 2 + 1]], axis=1)
            rows = acc_d.shape[4]
            for r in range(0, width, 512):
                terms = dot_tn(left, gout2[:, r:r + 512]).astype(BF16)
                for j in range(4):
                    acc_d[d // 2, d % 2, pair * 2 + j // 2, j % 2, :, r:r + 512] = terms[j * rows:(j + 1) * rows]
        loop(n_dp, one)

    def narrow_terms(source, pair, acc, right, where):
        left = jnp.concatenate([source[pair * 2], source[pair * 2 + 1]], axis=1)
        terms = dot_tn(left, right).astype(BF16)
        for j in range(16):
            d = j % 8 // 2
            acc[d // 2, d % 2, pair * 2 + j // 8, j % 2, :, where] = terms[j * 16:(j + 1) * 16]

    def up_terms(pair):
        def one(i):
            d, part = i // 2, i % 2
            cut = pl.ds(pl.multiple_of(part * cols, cols), cols)
            right = gp[d // 2, pl.ds(d % 2 * 2, 2), :, :, cut].reshape(2 * tokens, cols)
            where = pl.ds(pl.multiple_of(i * cols, cols), cols)
            narrow_terms(n2s2, pair, acc_u, right, where)
        loop(tiles, one)
        for r in range(0, width, 512):
            narrow_terms(at2, pair, acc_o, gb2[:, r:r + 512], slice(r, r + 512))

    def wait_tiles(first, last, which):
        def one(j):
            tile_links(first + j, tile_link)[which].wait()
        loop(last - first, one)

    lax.fori_loop(0, tiles // 2, one_tile, 0)
    gout_link.wait()
    wait_tiles(0, tiles // 2, 0)
    down_terms(near)
    cross_one(D, 0)
    cross_one(D, 1)
    lax.fori_loop(tiles // 2, tiles, one_tile, 0)
    low_two[...] = hidden[...].astype(BF16)
    put_y = local(low_two, y_out)
    for r in range(0, tokens, 128):
        rows = slice(r, r + 128)
        back = norm_back(n_two[rows], r_two[rows, 0:1], grad_two[rows] * gain_two)
        grad = f32(gout2[rows]) + back
        hidden[rows] = grad
        gb2[rows] = grad.astype(BF16)
    branch_link = to_sibling(gb2.at[0:tokens], gb2.at[tokens:2 * tokens], 3)
    for r in range(0, width, 512):
        grad = dot_nt(gb2[0:tokens], wo_v[r // 128:r // 128 + 4].reshape(512, width)).astype(BF16)
        gab[:, :, r:r + 512] = grad.reshape(streams, tok_rows, 512)
    grad_links = []
    for b in range(streams):
        out = []
        for k in range(1, n_seq):
            other = lax.rem(sq + k, n_seq)
            source = lax.rem(sq + n_seq - k, n_seq)
            src = gab.at[b, :, pl.ds(pl.multiple_of(other * 128, 128), 128)]
            dst = do.at[b, pl.ds(pl.multiple_of(sq * tok_rows, tok_rows), tok_rows), :]
            land = do.at[b, pl.ds(pl.multiple_of(source * tok_rows, tok_rows), tok_rows), :]
            out.append(keep(Link(src, dst, land, (o_send, o_recv), b * 7 + k - 1, (dp, other))))
        grad_links.append(out)
    copy_xh.append(local(xh_ref.at[:, :, cols:width], wu_t))
    own_do = [
        local(
            gab.at[b, :, pl.ds(pl.multiple_of(sq * 128, 128), 128)],
            do.at[b, pl.ds(pl.multiple_of(sq * tok_rows, tok_rows), tok_rows), :],
        )
        for b in range(streams)
    ]
    pgp[...] = jnp.zeros_like(pgp)
    pgp[2:3, :] = jnp.sum(grad_two[...] * n_two[...], axis=0, keepdims=True)
    pgp[3:4, :] = jnp.sum(grad_two[...], axis=0, keepdims=True)
    wait_tiles(tiles // 2, tiles, 0)
    down_terms(1 - near)
    for copy in copies:
        copy.wait()
    step = 256
    blocks = total // q_block

    def turn(j):
        b, r = j // (total // step), j % (total // step)
        row = pl.ds(pl.multiple_of(r * step, step), step)
        kt[b, :, row] = jnp.transpose(f32(qkv[b, row, 128:256])).astype(BF16)
    loop(streams * (total // step), turn)

    def prepare(b):
        own_do[b].wait()
        for link in grad_links[b]:
            link.wait()

        def one(r):
            row = pl.ds(pl.multiple_of(r * step, step), step)
            both = jnp.transpose(f32(do[b, row, :])) * ot[b, :, row]
            for h in range(2):
                delta[h:h + 1, row] = jnp.sum(both[h * 64:(h + 1) * 64], axis=0, keepdims=True)
        loop(total // step, one)
        dk[...] = jnp.zeros_like(dk)
        dv[...] = jnp.zeros_like(dv)

    tile = 256

    def attend(b, qb):
        row = pl.ds(pl.multiple_of(qb * q_block, q_block), q_block)
        lane = lax.broadcasted_iota(jnp.int32, (q_block, 128), 1)
        queries, grads = qkv[b, row, 0:128], do[b, row, :]
        none = jnp.zeros_like(queries)
        own = [jnp.where((lane < 64) == (h == 0), queries, none) for h in range(2)]
        own_grad = [jnp.where((lane < 64) == (h == 0), grads, none) for h in range(2)]
        part = [jnp.zeros((64, q_block), F32)] * 2
        for r in range(total // tile):
            keys = slice(r * tile, (r + 1) * tile)
            gap = distance(len_ref, b, r * tile, tile, qb * q_block, q_block)
            grad_v = grad_k = 0
            for h in range(2):
                s = dot_nt(qkv[b, keys, 128:256], own[h]) - slope_ref[0, h] * gap
                p = jnp.exp(s - lse[b, h:h + 1, row])
                gp_t = dot_nt(qkv[b, keys, 256:384], own_grad[h])
                ds = (p * (gp_t - delta[h:h + 1, row])).astype(BF16)
                grad_v = grad_v + dot_nn(p.astype(BF16), own_grad[h])
                grad_k = grad_k + dot_nn(ds, own[h])
                part[h] = part[h] + dot_nn(kt[b, h * 64:(h + 1) * 64, keys], ds)
            dv[keys, :] += grad_v
            dk[keys, :] += grad_k
        for h in range(2):
            dqt[h * 64:(h + 1) * 64, row] = part[h] * 0.125

    def attend_some(b, first, last):
        def one(qb, carry):
            attend(b, qb)
            return carry
        lax.fori_loop(first, last, one, 0)

    def gs(b):
        return wo_v.at[b * nz:(b + 1) * nz]

    def gz(b, t, way):
        index = t * 2 + way
        return wd_t.at[index // 4, index % 4] if b == 0 else gz_one.at[index]

    def finish_stream(b):
        def one(r):
            row = pl.ds(pl.multiple_of(r * step, step), step)
            low = dqt[:, row].astype(BF16)
            dqkvt[b, 0:128, row] = low
            dqkv[row, 0:128] = jnp.transpose(f32(low)).astype(BF16)
            for first, grad in ((128, dk), (256, dv)):
                low = grad[row, :].astype(BF16)
                dqkv[row, first:first + 128] = low
                dqkvt[b, first:first + 128, row] = jnp.transpose(f32(low)).astype(BF16)
        loop(total // step, one)

        def product(s):
            row = pl.ds(pl.multiple_of(s * tok_rows, tok_rows), tok_rows)
            gp[b, s // 2, s % 2] = dot_nn(dqkv[row, :], wt[...]).astype(BF16)
        loop(n_seq, product)
        pending[("gc", b)] = [
            keep(Link(gp.at[b, :, 1 - c], gs(b), gs(b), (zg_send, zg_recv), b * 7, sibling))
        ]

    def g_send(b, t):
        pending[("g", b, t)] = [
            keep(Link(
                gp.at[b, block, c], gz(b, t - 1, way), gz(b, t - 1, way), (zg_send, zg_recv),
                b * 7 + 1 + (t - 1) * 2 + way, target, ok_send, ok_recv,
            ))
            for way, target, block, ok_send, _, ok_recv in ways(t)
        ]

    def g_first(b):
        wait("gc", b)

        def add(j):
            gp[b, j, c] = (f32(gp[b, j, c]) + f32(wo_v[b * nz + j])).astype(BF16)
        loop(nz, add)
        g_send(b, 1)

    def gt_first(b):
        return grad_two.at[b * tok_rows:(b + 1) * tok_rows]

    def g_pass(b, t):
        wait("g", b, t)
        if t < nz - 1:
            for way, _, _, _, block, ok in ways(t):
                @pl.when(ok)
                def _():
                    gp[b, block, c] = (f32(gp[b, block, c]) + f32(gz(b, t - 1, way)[...])).astype(BF16)
            g_send(b, t + 1)
            return
        own = gt_first(b)
        own[...] = f32(gp[b, z, c])
        for way, ok in ((0, z >= 1), (1, z <= nz - 2)):
            @pl.when(ok)
            def _():
                own[...] += f32(gz(b, t - 1, way)[...])
        rows = slice(b * tok_rows, (b + 1) * tok_rows)
        n, rstd = norm_parts(f32(x_ref[rows]))
        low_two[rows] = (hidden[rows] + norm_back(n, rstd, own[...] * vector(0))).astype(BF16)
        local(low_two.at[rows], gx_out.at[b])

    rows_dp = 32 * n_seq

    def weight_grad():
        for copy in copy_xh:
            copy.wait()
        sums = jnp.sum(f32(dqkvt[0]), axis=1, keepdims=True)
        for b in range(1, streams):
            sums = sums + jnp.sum(f32(dqkvt[b]), axis=1, keepdims=True)
        gain, shift = vector(0), vector(1)
        for r in range(width // step):
            cols = slice(r * step, (r + 1) * step)
            weight = f32(wt[:, cols])
            n = xh if r < 2 else wu_t
            there = slice(r % 2 * step, (r % 2 + 1) * step)
            raw = dot_nn(dqkvt[0], n[0, :, there])
            for b in range(1, streams):
                raw = raw + dot_nn(dqkvt[b], n[b, :, there])
            pgp[0:1, cols] = jnp.sum(raw * weight, axis=0, keepdims=True)
            pgp[1:2, cols] = jnp.sum(sums * weight, axis=0, keepdims=True)
            grad = raw * gain[:, cols] + sums * shift[:, cols]
            dqkv[cols, :] = jnp.transpose(grad).astype(BF16)
        out = []
        for m in range(1, n_dp):
            other = lax.rem(dp + m, n_dp)
            src = dqkv.at[pl.ds(pl.multiple_of(other * rows_dp, rows_dp), rows_dp), :]
            out.append(keep(Link(src, dqr.at[m - 1], dqr.at[m - 1], (s_send, s_recv), m - 1, (other, sq))))
            src = pgp.at[:, pl.ds(pl.multiple_of(other * rows_dp, rows_dp), rows_dp)]
            out.append(keep(Link(src, pr1.at[m - 1], pr1.at[m - 1], (s_send, s_recv), 3 + m - 1, (other, sq))))
        pending["qd",] = out

    def weight_grad_two():
        wait("qd")
        mine = pl.ds(pl.multiple_of(dp * rows_dp, rows_dp), rows_dp)
        part = f32(dqkv[mine, :])
        small = pgp[:, mine]
        for m in range(n_dp - 1):
            part = part + f32(dqr[m])
            small = small + pr1[m]
        dqsum[...] = part.astype(BF16)
        psum[...] = small
        out = []
        for k in range(1, n_seq):
            other = lax.rem(sq + k, n_seq)
            source = lax.rem(sq + n_seq - k, n_seq)
            src = dqsum.at[pl.ds(pl.multiple_of(other * 32, 32), 32), :]
            out.append(keep(Link(src, gq_out.at[sq], gq_out.at[source], (s_send, s_recv), 6 + k - 1, (dp, other))))
            src = psum.at[:, pl.ds(pl.multiple_of(other // 4 * 128, 128), 128)]
            out.append(keep(Link(src, pr2.at[k - 1], pr2.at[k - 1], (s_send, s_recv), 13 + k - 1, (dp, other))))
        local(dqsum.at[pl.ds(pl.multiple_of(sq * 32, 32), 32), :], gq_out.at[sq])
        pending["qs",] = out

    def weight_grad_last():
        wait("qs")
        small = psum[:, pl.ds(pl.multiple_of(sq // 4 * 128, 128), 128)]
        for k in range(n_seq - 1):
            small = small + pr2[k]
        pgo[...] = small
        local(pgo, pg_out)

    cross_two(D, 0)
    cross_one(D, 2)
    cross_two(D, 1)
    cross_one(D, 3)
    attn_link.wait()
    norm_link.wait()
    branch_link.wait()
    wait_tiles(0, tiles, 1)
    up_terms(near)
    cross_one(U, 0)
    cross_three(D, 0)
    z_send(D, 1)
    cross_three(D, 1)
    up_terms(1 - near)
    cross_two(D, 2)
    cross_one(U, 1)
    put_y.wait()
    prepare(0)
    attend_some(0, 0, 1)
    z_pass(D, 1)
    cross_two(D, 3)
    cross_one(U, 2)
    attend_some(0, 1, 2)
    cross_three(D, 2)
    z_pass(D, 2)
    attend_some(0, 2, 3)
    cross_two(U, 0)
    cross_one(U, 3)
    attend_some(0, 3, 4)
    cross_three(D, 3)
    cross_three(U, 0)
    z_send(U, 1)
    z_pass(D, 3)

    def sent(i):
        for link in tile_links(i, tile_link):
            link.wait_sent()
    loop(tiles, sent)
    finish_stream(0)
    prepare(1)
    cross_two(U, 1)
    attend_some(1, 0, 1)
    g_first(0)
    cross_three(U, 1)
    z_pass(U, 1)
    attend_some(1, 1, 2)
    cross_two(U, 2)
    attend_some(1, 2, 3)
    g_pass(0, 1)
    cross_three(U, 2)
    z_pass(U, 2)
    attend_some(1, 3, 4)
    finish_stream(1)
    cross_two(U, 3)
    g_pass(0, 2)
    g_first(1)
    weight_grad()
    g_pass(0, 3)
    g_pass(1, 1)
    cross_three(U, 3)
    z_pass(U, 3)
    weight_grad_two()
    g_pass(1, 2)
    g_pass(1, 3)
    weight_grad_last()
    waited = [load_cot, load_attn, load_out, put_y, *copy_xh, *own_do, *copies]
    for copy in locals_:
        if not any(copy is other for other in waited):
            copy.wait()
    for link in links:
        link.wait_sent()


def scatter_call(inputs, cotangent, infill, attn, params, weights, qkv, ot, lse, xh, wt, lengths, slopes):
    streams, total = qkv.shape[:2]
    tokens, width = inputs.shape
    tok_rows = tokens // streams
    n_seq, n_dp = lax.axis_size("seq"), lax.axis_size("dp")
    nz = n_seq // 2
    cols = qkv.shape[2]
    any_space = pl.BlockSpec(memory_space=pl.ANY)
    vmem = pl.BlockSpec(memory_space=pltpu.VMEM)
    smem = pl.BlockSpec(memory_space=pltpu.SMEM)
    dma = pltpu.SemaphoreType.DMA
    sizes = [(w.shape[0] // (2 * n_dp * n_seq), w.shape[1]) for w in weights]
    tile = weights[1].shape[1] // 8

    def buffers(*lead):
        return [pltpu.VMEM(lead + size, BF16) for size in sizes]

    def low(*shape):
        return pltpu.VMEM(shape, BF16)

    def full(*shape):
        return pltpu.VMEM(shape, F32)

    half = width // 2 // nz
    scratch = [
        full(tokens, width), full(tokens, width), full(tokens, 128), low(tokens, width), full(tokens, width),
        low(2 * tokens, width), low(2 * tokens, width),
        low(16, 2 * tokens, 128), low(16, tokens, 128),
        low(nz, 2 * tokens, half), low(nz, tokens, half), low(nz, 2 * tokens, half), low(nz, tokens, half),
        low(width // 128, 128, width), low(2, width, tile), low(2, tile // 128, 128, width), low(streams, tok_rows, width),
    ]
    scratch += buffers(2, 2, nz, 2) + buffers(nz, 2) + buffers(nz, 2) + buffers(nz) + buffers(nz)
    scratch += buffers(nz - 1, 2, 2)
    scratch += [pltpu.VMEM((2,) + size, F32) for size in sizes]
    scratch += [
        low(streams, total, 128), low(*qkv.shape), full(*ot.shape), full(*lse.shape), low(streams, total, tile), low(*wt.shape),
        low(streams, 128, total), full(8, total), full(total, 128), full(total, 128),
        full(128, total), low(total, cols), low(streams, cols, total),
        low(streams, nz, 2, tok_rows, width), low((nz - 1) * 2, tok_rows, width),
        low(n_dp - 1, width // n_dp, cols), low(width // n_dp, cols),
        full(8, width), full(n_dp - 1, 8, width // n_dp), full(8, width // n_dp), full(n_seq - 1, 8, 128), full(8, 128),
        dma((20,)), dma((20,)), dma((14,)), dma((14,)), dma((48,)), dma((48,)), dma((18,)), dma((18,)),
        dma((14,)), dma((14,)), dma((20,)), dma((20,)), dma((4,)), dma((24,)),
    ]
    outs = [
        jax.ShapeDtypeStruct((tokens, width), BF16),
        jax.ShapeDtypeStruct((streams, tok_rows, width), BF16),
        *[jax.ShapeDtypeStruct((2,) + size, F32) for size in sizes],
        jax.ShapeDtypeStruct((n_seq, width // (n_dp * n_seq), cols), BF16),
        jax.ShapeDtypeStruct((8, 128), F32),
    ]
    return pl.pallas_call(
        scatter_kernel,
        out_shape=outs,
        in_specs=[vmem] * 3 + [any_space] * 10 + [smem] * 2,
        out_specs=[any_space] * len(outs),
        scratch_shapes=scratch,
        compiler_params=pltpu.CompilerParams(
            collective_id=1, has_side_effects=True, vmem_limit_bytes=63 * 2**20
        ),
        name="scatter_attend",
    )(
        inputs, infill, params, cotangent, attn, weights[0].reshape(-1, 128, width), weights[1],
        weights[2].reshape(-1, 128, width), qkv, ot, lse, xh, wt, lengths, slopes,
    )


def by_heads(
    inputs, lengths, infill, cotangent, w_qkv, w_out, w_up, w_down,
    gain_one, shift_one, gain_two, shift_two,
):
    streams, tok_rows, width = inputs.shape
    n_seq, n_dp = lax.axis_size("seq"), lax.axis_size("dp")
    sq, rank = lax.axis_index("seq"), lax.axis_index("dp") * n_seq + lax.axis_index("seq")
    stream_len, tokens = tok_rows * n_seq, streams * tok_rows
    own_rows = w_qkv.shape[0]
    wq_blocks = w_qkv.reshape(own_rows, 3, n_seq, 128).transpose(2, 0, 1, 3)
    wq_blocks = wq_blocks.reshape(n_seq, own_rows, 384)
    mine = jnp.stack([gain_one, shift_one, gain_two, shift_two])
    params = lax.dynamic_update_slice(jnp.zeros((4, width), BF16), mine, (0, rank * own_rows))
    slopes = lax.dynamic_slice(slope_table(HEADS, stream_len), (sq * 2,), (2,)).reshape(1, 2)
    full_out, full_up, full_down, params, attn, qkv, ot, lse, xh, wt = gather_call(
        inputs, wq_blocks, w_out, w_up, w_down, params.reshape(32, 128), lengths, slopes
    )
    weights = (
        full_out.reshape(width, width), full_up.reshape(width, -1), full_down.reshape(-1, width)
    )
    output, input_grad, grad_out, grad_up, grad_down, grad_qkv, small = scatter_call(
        inputs.reshape(tokens, width), cotangent,
        infill.reshape(tokens, 1).astype(F32), attn.reshape(tokens, width), params, weights,
        qkv, ot, lse, xh.reshape(streams, stream_len, width), wt, lengths, slopes,
    )
    grad_qkv = grad_qkv.reshape(n_seq, own_rows, 3, 128).transpose(1, 2, 0, 3)
    small = lax.dynamic_slice(small, (0, sq % (128 // own_rows) * own_rows), (4, own_rows))
    return (
        output.reshape(inputs.shape),
        input_grad,
        grad_qkv.reshape(own_rows, 3 * width).astype(F32),
        grad_out.reshape(w_out.shape),
        grad_up.reshape(w_up.shape),
        grad_down.reshape(w_down.shape),
        small[0], small[1], small[2], small[3],
    )


def layer_norm(features, gain_vec, shift_vec):
    row_mean = jnp.mean(features, axis=-1, keepdims=True)
    centered = features - row_mean
    spread = jnp.mean(centered * centered, axis=-1, keepdims=True)
    return centered * lax.rsqrt(spread + norm_eps) * gain_vec + shift_vec


def segment_of(bounds, positions):
    return jnp.sum((positions[None, :, None] >= bounds[:, None, :]).astype(jnp.int32), axis=2)


def slope_table(head_count, stream_len):
    return 2.0 ** (-8.0 * (jnp.arange(head_count, dtype=jnp.float32) + 1.0) / head_count) * (
        256.0 / stream_len
    )


def block_scores(queries, key_heads, query_pos, key_pos, query_seg, key_seg, slopes):
    raw_scores = jnp.einsum(
        "sqhc,skhc->shqk", queries, key_heads, preferred_element_type=jnp.float32
    )
    distance = jnp.abs(query_pos[:, None] - key_pos[None, :]).astype(jnp.float32)
    scores = (
        raw_scores * queries.shape[3] ** (-0.5) - slopes[None, :, None, None] * distance[None, None]
    )
    same_utt = query_seg[:, None, :, None] == key_seg[:, None, None, :]
    return jnp.where(same_utt, scores, masked_score)


def score_grads(
    queries,
    grad_heads,
    log_total,
    delta,
    key_heads,
    values,
    query_pos,
    key_pos,
    query_seg,
    key_seg,
    slopes,
):
    scores = block_scores(queries, key_heads, query_pos, key_pos, query_seg, key_seg, slopes)
    probs = jnp.exp(scores - log_total[..., None])
    grad_probs = jnp.einsum(
        "sqhc,skhc->shqk", grad_heads, values, preferred_element_type=jnp.float32
    )
    grad_scores = (probs * (grad_probs - delta[..., None])).astype(jnp.bfloat16)
    return (probs.astype(jnp.bfloat16), grad_scores)


def by_frames(
    inputs,
    lengths,
    infill,
    cotangent,
    w_qkv,
    w_out,
    w_up,
    w_down,
    gain_one,
    shift_one,
    gain_two,
    shift_two,
):
    w_qkv, w_out, w_up, w_down, gain_one, shift_one, gain_two, shift_two = (
        lax.all_gather(w_qkv, ("dp", "seq"), axis=0, tiled=True),
        lax.all_gather(w_out, ("dp", "seq"), axis=0, tiled=True),
        lax.all_gather(w_up, ("dp", "seq"), axis=0, tiled=True),
        lax.all_gather(w_down, ("dp", "seq"), axis=0, tiled=True),
        lax.all_gather(gain_one, ("dp", "seq"), axis=0, tiled=True),
        lax.all_gather(shift_one, ("dp", "seq"), axis=0, tiled=True),
        lax.all_gather(gain_two, ("dp", "seq"), axis=0, tiled=True),
        lax.all_gather(shift_two, ("dp", "seq"), axis=0, tiled=True),
    )
    streams, tok_rows, model_width = inputs.shape
    head_count = HEADS
    head_size = HEAD_DIM
    stream_len = tok_rows * lax.axis_size("seq")
    score_scale = head_size ** (-0.5)
    slopes = slope_table(head_count, stream_len)
    bounds = jnp.cumsum(lengths, axis=1)
    own_pos = lax.axis_index("seq") * tok_rows + jnp.arange(tok_rows, dtype=jnp.int32)
    own_seg = segment_of(bounds, own_pos)
    gain_one_f = gain_one.astype(jnp.float32)
    shift_one_f = shift_one.astype(jnp.float32)
    gain_two_f = gain_two.astype(jnp.float32)
    shift_two_f = shift_two.astype(jnp.float32)
    inputs_f = inputs.astype(jnp.float32)
    normed_one = layer_norm(inputs_f, gain_one_f, shift_one_f).astype(jnp.bfloat16)
    packed = jnp.einsum(
        "std,de->ste", normed_one, w_qkv, preferred_element_type=jnp.float32
    ).astype(jnp.bfloat16)
    query_low = packed[:, :, :model_width]
    key_value = packed[:, :, model_width:]
    query_heads = query_low.reshape(streams, tok_rows, head_count, head_size)
    start_state = (
        jnp.full((streams, head_count, tok_rows), masked_score, jnp.float32),
        jnp.zeros((streams, head_count, tok_rows), jnp.float32),
        jnp.zeros((streams, head_count, tok_rows, head_size), jnp.float32),
    )
    shard_piece = lax.all_gather(key_value, "seq", axis=1, tiled=True)
    key_count = shard_piece.shape[1]
    visit_block_len = 256

    def one_block(carried, offset):
        top_score, weight_sum, weighted = carried
        key_part = lax.dynamic_slice_in_dim(shard_piece, offset, visit_block_len, 1)
        key_pos = offset + jnp.arange(visit_block_len, dtype=jnp.int32)
        key_seg = segment_of(bounds, key_pos)
        key_heads = key_part[:, :, :model_width].reshape(
            streams, visit_block_len, head_count, head_size
        )
        values = key_part[:, :, model_width:].reshape(
            streams, visit_block_len, head_count, head_size
        )
        scores = block_scores(query_heads, key_heads, own_pos, key_pos, own_seg, key_seg, slopes)
        new_top = jnp.maximum(top_score, jnp.max(scores, axis=3))
        rescale = jnp.exp(top_score - new_top)
        weights_blk = jnp.exp(scores - new_top[..., None])
        weight_sum = weight_sum * rescale + jnp.sum(weights_blk, axis=3)
        weighted = weighted * rescale[..., None] + jnp.einsum(
            "shqk,skhc->shqc",
            weights_blk.astype(jnp.bfloat16),
            values,
            preferred_element_type=jnp.float32,
        )
        return ((new_top, weight_sum, weighted), None)

    offsets = jnp.arange(key_count // visit_block_len, dtype=jnp.int32) * visit_block_len
    finished, _ = lax.scan(one_block, start_state, offsets)
    top_score, weight_sum, weighted = finished
    attn_heads = weighted / weight_sum[..., None]
    log_total = top_score + jnp.log(weight_sum)
    attn_rows = jnp.transpose(attn_heads, (0, 2, 1, 3)).reshape(streams, tok_rows, model_width)
    attn_low = attn_rows.astype(jnp.bfloat16)
    hidden = inputs_f + jnp.einsum(
        "std,de->ste", attn_low, w_out, preferred_element_type=jnp.float32
    )
    normed_two_f, ln_two_pull = jax.vjp(layer_norm, hidden, gain_two_f, shift_two_f)
    normed_two = normed_two_f.astype(jnp.bfloat16)
    upward = jnp.einsum("std,df->stf", normed_two, w_up, preferred_element_type=jnp.float32)
    active_f, gelu_pull = jax.vjp(jax.nn.gelu, upward)
    active = active_f.astype(jnp.bfloat16)
    output = (
        hidden + jnp.einsum("stf,fd->std", active, w_down, preferred_element_type=jnp.float32)
    ).astype(jnp.bfloat16)
    grad_output = (cotangent.astype(jnp.float32) * infill.astype(jnp.float32)[:, :, None]).astype(
        jnp.bfloat16
    )
    grad_active = jnp.einsum("ste,fe->stf", grad_output, w_down, preferred_element_type=jnp.float32)
    grad_upward = gelu_pull(grad_active)[0].astype(jnp.bfloat16)
    grad_norm_two = jnp.einsum("stf,df->std", grad_upward, w_up, preferred_element_type=jnp.float32)
    grad_in_two, grad_gain_two, grad_shift_two = ln_two_pull(grad_norm_two)
    grad_hidden = grad_output.astype(jnp.float32) + grad_in_two
    grad_branch = grad_hidden.astype(jnp.bfloat16)
    grad_attn = jnp.einsum(
        "ste,de->std", grad_branch, w_out, preferred_element_type=jnp.float32
    ).astype(jnp.bfloat16)
    grad_heads = grad_attn.reshape(streams, tok_rows, head_count, head_size)
    delta = jnp.einsum("sqhc,shqc->shq", grad_heads.astype(jnp.float32), attn_heads)
    every_kv = lax.all_gather(key_value, "seq", axis=1, tiled=True)
    total_len = every_kv.shape[1]
    block_len = 256
    offsets = jnp.arange(total_len // block_len, dtype=jnp.int32) * block_len
    grad_start = jnp.zeros((streams, tok_rows, head_count, head_size), jnp.float32)

    def key_step(grad_query, offset):
        key_part = lax.dynamic_slice_in_dim(every_kv, offset, block_len, 1)
        key_pos = offset + jnp.arange(block_len, dtype=jnp.int32)
        key_seg = segment_of(bounds, key_pos)
        key_heads = key_part[:, :, :model_width].reshape(streams, block_len, head_count, head_size)
        values = key_part[:, :, model_width:].reshape(streams, block_len, head_count, head_size)
        probs_low, grad_scores = score_grads(
            query_heads,
            grad_heads,
            log_total,
            delta,
            key_heads,
            values,
            own_pos,
            key_pos,
            own_seg,
            key_seg,
            slopes,
        )
        grad_query = (
            grad_query
            + jnp.einsum(
                "shqk,skhc->sqhc", grad_scores, key_heads, preferred_element_type=jnp.float32
            )
            * score_scale
        )
        grad_keys = (
            jnp.einsum(
                "shqk,sqhc->kshc", grad_scores, query_heads, preferred_element_type=jnp.float32
            )
            * score_scale
        )
        grad_values = jnp.einsum(
            "shqk,sqhc->kshc", probs_low, grad_heads, preferred_element_type=jnp.float32
        )
        key_terms = jnp.concatenate(
            [
                grad_keys.reshape(block_len, streams, model_width),
                grad_values.reshape(block_len, streams, model_width),
            ],
            axis=2,
        )
        return (grad_query, key_terms)

    grad_query, key_terms = lax.scan(key_step, grad_start, offsets)
    key_terms = key_terms.reshape(total_len, streams, 2 * model_width)
    own_kv_grad = lax.psum_scatter(
        key_terms.astype(jnp.bfloat16), "seq", scatter_dimension=0, tiled=True
    ).astype(jnp.float32)
    grad_kv = jnp.transpose(own_kv_grad, (1, 0, 2))
    grad_packed = jnp.concatenate(
        [grad_query.reshape(streams, tok_rows, model_width), grad_kv], axis=2
    ).astype(jnp.bfloat16)
    grad_norm_one = jnp.einsum(
        "ste,de->std", grad_packed, w_qkv, preferred_element_type=jnp.float32
    )
    _, ln_one_pull = jax.vjp(layer_norm, inputs_f, gain_one_f, shift_one_f)
    grad_in_one, grad_gain_one, grad_shift_one = ln_one_pull(grad_norm_one)
    input_grad = (grad_hidden + grad_in_one).astype(jnp.bfloat16)
    weight_terms = (
        jnp.einsum("std,ste->de", normed_one, grad_packed, preferred_element_type=jnp.float32),
        jnp.einsum("std,ste->de", attn_low, grad_branch, preferred_element_type=jnp.float32),
        jnp.einsum("std,stf->df", normed_two, grad_upward, preferred_element_type=jnp.float32),
        jnp.einsum("stf,std->fd", active, grad_output, preferred_element_type=jnp.float32),
        grad_gain_one,
        grad_shift_one,
        grad_gain_two,
        grad_shift_two,
    )
    summed = (
        lax.psum_scatter(weight_terms[0], ("dp", "seq"), scatter_dimension=0, tiled=True),
        lax.psum_scatter(weight_terms[1], ("dp", "seq"), scatter_dimension=0, tiled=True),
        lax.psum_scatter(weight_terms[2], ("dp", "seq"), scatter_dimension=0, tiled=True),
        lax.psum_scatter(weight_terms[3], ("dp", "seq"), scatter_dimension=0, tiled=True),
        lax.psum_scatter(weight_terms[4], ("dp", "seq"), scatter_dimension=0, tiled=True),
        lax.psum_scatter(weight_terms[5], ("dp", "seq"), scatter_dimension=0, tiled=True),
        lax.psum_scatter(weight_terms[6], ("dp", "seq"), scatter_dimension=0, tiled=True),
        lax.psum_scatter(weight_terms[7], ("dp", "seq"), scatter_dimension=0, tiled=True),
    )
    return (
        output,
        input_grad,
        summed[0],
        summed[1],
        summed[2],
        summed[3],
        summed[4],
        summed[5],
        summed[6],
        summed[7],
    )


def solution(mesh):
    in_specs = (
        P("dp", "seq", None),
        P("dp", None),
        P("dp", "seq"),
        P("dp", "seq", None),
        P(("dp", "seq"), None),
        P(("dp", "seq"), None),
        P(("dp", "seq"), None),
        P(("dp", "seq"), None),
        P(("dp", "seq")),
        P(("dp", "seq")),
        P(("dp", "seq")),
        P(("dp", "seq")),
    )
    out_specs = (
        P("dp", "seq", None),
        P("dp", "seq", None),
        P(("dp", "seq"), None),
        P(("dp", "seq"), None),
        P(("dp", "seq"), None),
        P(("dp", "seq"), None),
        P(("dp", "seq")),
        P(("dp", "seq")),
        P(("dp", "seq")),
        P(("dp", "seq")),
    )
    grid = (mesh.shape["dp"], mesh.shape["seq"])
    local = by_heads if grid == (4, HEADS // 2) else by_frames
    return jax.shard_map(local, mesh=mesh, in_specs=in_specs, out_specs=out_specs, check_vma=False)
```

```python
import functools

import jax
import jax.numpy as jnp
from jax import lax
from jax.experimental import pallas as pl
from jax.experimental.pallas import tpu as pltpu

from jax.sharding import PartitionSpec as P

HEADS = 16
HEAD_DIM = 64

norm_eps = 1e-05
masked_score = -1e30
MESH_ID = pl.DeviceIdType.MESH
F32 = jnp.float32
BF16 = jnp.bfloat16
far = 1e33
gather_order = (
    "xh1", "x110", "xs", "seq", "x100", "x210", "zh11", "zh02", "xh2", "wq", "x111", "zh01",
    "x200", "x211", "xp2", "xp1", "xh3", "x102", "wt", "cc10", "p2", "x101", "x202", "cc11", "p0",
    "p1", "x201", "zh03", "xp3", "p3", "zh12", "vt", "a0", "a1", "a2", "cc00", "x103", "a3", "a4",
    "cc01", "x203", "zh13", "cc02", "a5", "x112", "a6", "o0", "a7", "x212", "x113", "cc03", "o1",
    "c0", "x213", "hid", "cc12", "u0", "u1", "cc13", "u2", "u3",
)
scatter_order = (
    "DT0", "c1D0", "c1D1", "pkA", "LN", "DT1", "T0", "T1", "c1D2", "T2", "T3", "LNB", "c2D0",
    "pkN", "UT0", "c1U0", "zfD", "c2D2", "UT1", "P0", "c2D1", "ztD", "A00", "c2U0", "zsD", "A01",
    "c1U1", "zfU", "A02", "A03", "F0", "P1", "A10", "c2U1", "gf0", "A11", "c1D3", "A12", "zsU",
    "A13", "F1", "c2D3", "WG", "c1U2", "gf1", "gs0", "c2U2", "W2", "ztU", "c1U3", "gs1", "W3",
    "zlD", "gl0", "c2U3", "gl1", "zlU",
)
q_block = 256


def place():
    dp, sq = lax.axis_index("dp"), lax.axis_index("seq")
    return dp, sq, dp // 2, dp % 2, sq // 2, sq % 2


def planes(z, nz):
    z1 = z + 1 - 2 * (z % 2)
    return z1, (z + 2) % nz, (z1 + 2) % nz


def dot_nt(a, b):
    return lax.dot_general(a, b, (((1,), (1,)), ((), ())), preferred_element_type=F32)


def dot_nn(a, b):
    return lax.dot_general(a, b, (((1,), (0,)), ((), ())), preferred_element_type=F32)


def runs(order, counted):
    out = []
    for name in order:
        kind = name[:-1]
        if kind in counted:
            number = int(name[-1])
            if out and out[-1][0] == kind and out[-1][2] == number:
                out[-1] = (kind, out[-1][1], number + 1)
            else:
                out.append((kind, number, number + 1))
        else:
            out.append((name, 0, 0))
    return out


class Link:
    def __init__(self, src, dst, landing, sems, index, target, when_send=None, when_recv=None):
        self.sems, self.index, self.target = sems, index, target
        self.src, self.dst, self.landing = src, dst, landing
        self.when_send, self.when_recv = when_send, when_recv

    def copy(self, src, dst):
        send, recv = self.sems
        return pltpu.make_async_remote_copy(
            src_ref=src,
            dst_ref=dst,
            send_sem=send.at[self.index],
            recv_sem=recv.at[self.index],
            device_id=self.target,
            device_id_type=MESH_ID,
        )

    def run(self, when, action):
        if when is None:
            action()
        else:
            pl.when(when)(action)

    def start(self):
        self.run(self.when_send, lambda: self.copy(self.src, self.dst).start())

    def wait(self):
        self.run(self.when_recv, lambda: self.copy(self.landing, self.landing).wait_recv())

    def wait_sent(self):
        self.run(self.when_send, lambda: self.copy(self.src, self.dst).wait_send())


def greet(dp, sq, n_seq, n_dp):
    barrier = pltpu.get_barrier_semaphore()
    for k in range(1, n_seq):
        pl.semaphore_signal(
            barrier, inc=1, device_id=(dp, lax.rem(sq + k, n_seq)), device_id_type=MESH_ID
        )
    for m in range(1, n_dp):
        other = lax.rem(dp + m, n_dp)
        pl.semaphore_signal(barrier, inc=1, device_id=(other, sq), device_id_type=MESH_ID)
    pl.semaphore_wait(barrier, n_seq - 1 + n_dp - 1)


def distance(len_ref, stream, first_key, keys, first_query, queries):
    key_pos = lax.broadcasted_iota(jnp.int32, (keys, 1), 0) + first_key
    query_pos = lax.broadcasted_iota(jnp.int32, (1, queries), 1) + first_query
    key_seg = jnp.zeros((keys, 1), jnp.int32)
    query_seg = jnp.zeros((1, queries), jnp.int32)
    bound = 0
    for k in range(len_ref.shape[1]):
        bound = bound + len_ref[stream, k]
        key_seg = key_seg + (key_pos >= bound).astype(jnp.int32)
        query_seg = query_seg + (query_pos >= bound).astype(jnp.int32)
    gap = jnp.abs(key_pos - query_pos).astype(F32)
    return jnp.where(key_seg == query_seg, gap, far)


def gelu_both(v):
    square = v * v
    th = jnp.tanh(v * (0.7978845608028654 + 0.7978845608028654 * 0.044715 * square))
    half = 0.5 * (1.0 + th)
    bend = v * (0.5 - 0.5 * th * th)
    return v * half, half + bend * (0.7978845608028654 + 0.7978845608028654 * 0.134145 * square)


def norm_parts(v):
    mean = jnp.mean(v, axis=-1, keepdims=True)
    centered = v - mean
    rstd = lax.rsqrt(jnp.mean(centered * centered, axis=-1, keepdims=True) + norm_eps)
    return centered * rstd, rstd


def norm_back(n, rstd, e):
    return rstd * (
        e - jnp.mean(e, axis=-1, keepdims=True) - n * jnp.mean(e * n, axis=-1, keepdims=True)
    )


def own_slopes(sq, n_seq, total):
    out = []
    for h in range(2):
        value = 0.0
        for q in range(n_seq):
            slope = 2.0 ** (-8.0 * (2 * q + h + 1) / (2 * n_seq)) * (256.0 / total)
            value = jnp.where(sq == q, jnp.float32(slope), value)
        out.append(value)
    return out


def gather_kernel(
    x_ref, w_ref, wo_ref, wu_ref, wd_ref, vec_ref, len_ref,
    wo_all, wu_all, wd_all, par_out, attn, qkv_out, ot_out, lse_out, xh_out, wt_out, hid_out, act_out, bend_out,
    xg, xh, wqb, wt, wq_ref, par_ref, pbuf, pown, par, qkv, vt, obuf, ot, lse, dist, wo_v, wu_t, av, hid, low_two, act_v, bend_v,
    z_send, z_recv, w_send, w_recv, x_send, x_recv, s_send, s_recv, tile_sem, loc,
):
    dp, sq, y, x, z, c = place()
    streams, tok_rows, width = x_ref.shape
    n_seq, n_dp = lax.axis_size("seq"), lax.axis_size("dp")
    nz = n_seq // 2
    total = n_seq * tok_rows
    own_rows = w_ref.shape[0]
    slopes = own_slopes(sq, n_seq, total)
    x_nbr, y_nbr = (y * 2 + (1 - x), sq), ((1 - y) * 2 + x, sq)
    sibling = (dp, z * 2 + (1 - c))
    z1, z2, z3 = planes(z, nz)
    near_dev, far_dev = (dp, z1 * 2 + c), (dp, z2 * 2 + c)
    rank = dp * n_seq + sq
    row = lax.broadcasted_iota(jnp.int32, (8, 128), 0)
    lane = lax.broadcasted_iota(jnp.int32, (8, 128), 1)
    mine = (row == rank // 4) & ((lane >> 5) == rank % 4)
    vecs = vec_ref[...].astype(F32)
    par_ref[...] = jnp.concatenate(
        [jnp.where(mine, jnp.broadcast_to(vecs[i:i + 1], (8, 128)), 0.0) for i in range(4)], axis=0
    ).astype(BF16)
    for q in range(n_seq):
        for j in range(3):
            wq_ref[q, :, j * 128:(j + 1) * 128] = w_ref[:, j * width + q * 128:j * width + (q + 1) * 128]
    greet(dp, sq, n_seq, n_dp)
    links = []

    def keep(link):
        link.start()
        links.append(link)
        return link

    locals_ = []

    def local(src, dst):
        copy = pltpu.make_async_copy(src, dst, loc.at[len(locals_)])
        copy.start()
        locals_.append(copy)
        return copy

    cp_x = local(x_ref, xg.at[:, sq])
    cp_wq = local(wq_ref.at[sq], wqb.at[pl.ds(pl.multiple_of(sq * 32 + dp * 32 * n_seq, 32), 32), :])
    cp_w = [
        local(src, dst.at[y, x, z, c])
        for src, dst in ((wo_ref, wo_all), (wu_ref, wu_all), (wd_ref, wd_all))
    ]

    arrays = [(wo_ref, wo_all), (wu_ref, wu_all), (wd_ref, wd_all)]
    groups = [(0, 1), (2,)]
    pending = {}
    every = slice(None)

    arrived = set()

    def wait(*key):
        if key not in arrived:
            arrived.add(key)
            for link in pending[key]:
                link.wait()

    where = [z, z1, z2, z3]

    def z_hop(g, h):
        out = []
        for i in groups[g]:
            own, full = arrays[i]
            there = full.at[y, x, z if h < 3 else z2, c]
            land = full.at[y, x, where[h], c]
            src = own if h < 3 else there
            target = far_dev if h == 2 else near_dev
            out.append(keep(Link(src, there, land, (w_send, w_recv), i * 3 + h - 1, target)))
        pending[("z", g, h)] = out

    def plane(tag, g, h, pairs):
        out = []
        for i in groups[g]:
            own, full = arrays[i]
            for kind, target, src_at, land_at, own_half in pairs(where[h]):
                here = full.at[src_at]
                src = own.at[own_half] if own_half is not None and h == 0 else here
                out.append(keep(Link(
                    src, here, full.at[land_at], (x_send, x_recv), (i * 4 + h) * 5 + kind, target
                )))
        pending[(tag, g, h)] = out

    def cross_one(g, h):
        plane("x1", g, h, lambda b: [
            (0, x_nbr, (y, x, b, c, 0), (y, 1 - x, b, c, 0), 0),
            (1, y_nbr, (y, x, b, c, 1), (1 - y, x, b, c, 1), 1),
        ])

    def cross_two(g, h):
        wait("x1", g, h)
        plane("x2", g, h, lambda b: [
            (2, y_nbr, (y, every, b, c, 0), (1 - y, every, b, c, 0), None),
            (3, x_nbr, (every, x, b, c, 1), (every, 1 - x, b, c, 1), None),
        ])

    def cross_core(g, h):
        wait("x2", g, h)
        plane("c", g, h, lambda b: [
            (4, sibling, (every, every, b, c), (every, every, b, 1 - c), None),
        ])

    def x_hop(h):
        there = xg.at[:, (z if h < 3 else z2) * 2 + c]
        land = xg.at[:, where[h] * 2 + c]
        target = far_dev if h == 2 else near_dev
        pending[("x", h)] = [keep(Link(x_ref if h < 3 else there, there, land, (z_send, z_recv), h - 1, target))]

    def x_pass(h):
        src = xg.at[:, where[h] * 2 + c]
        land = xg.at[:, where[h] * 2 + (1 - c)]
        pending[("xc", h)] = [keep(Link(src, src, land, (z_send, z_recv), 3 + h - 1, sibling))]

    rows_dp = 32 * n_seq

    def shard_rows(d, q):
        return wqb.at[pl.ds(pl.multiple_of((d * n_seq + q) * 32, 32), 32), :]

    def plane_rows(d):
        return wqb.at[pl.ds(pl.multiple_of(d * rows_dp, 32), rows_dp), :]

    def along_seq():
        small, wide = [], []
        for k in range(1, n_seq):
            other = lax.rem(sq + k, n_seq)
            source = lax.rem(sq + n_seq - k, n_seq)
            slot = pbuf.at[k - 1]
            small.append(keep(Link(par_ref, slot, slot, (s_send, s_recv), k - 1, (dp, other))))
            wide.append(keep(Link(
                wq_ref.at[other], shard_rows(dp, sq), shard_rows(dp, source), (s_send, s_recv), 7 + k - 1, (dp, other)
            )))
        pending["ps",], pending["ws",] = small, wide

    def along_dp():
        wait("ps")
        pown[...] = par_ref[...] + pbuf[0]
        for k in range(1, n_seq - 1):
            pown[...] += pbuf[k]
        pending["pd",] = []
        for m in range(1, n_dp):
            slot = pbuf.at[n_seq - 2 + m]
            pending["pd",].append(
                keep(Link(pown, slot, slot, (s_send, s_recv), 14 + m - 1, (lax.rem(dp + m, n_dp), sq)))
            )
        wait("ws")
        cp_wq.wait()
        pending["wd",] = []
        for m in range(1, n_dp):
            other, source = lax.rem(dp + m, n_dp), lax.rem(dp + n_dp - m, n_dp)
            pending["wd",].append(keep(Link(
                plane_rows(dp), plane_rows(dp), plane_rows(source), (s_send, s_recv), 17 + m - 1, (other, sq)
            )))

    step = 256
    rows_of = {}

    def columns():
        wait("pd")
        par[...] = pown[...] + pbuf[n_seq - 1] + pbuf[n_seq] + pbuf[n_seq + 1]
        wait("wd")
        for r in range(width // step):
            wt[:, r * step:(r + 1) * step] = jnp.transpose(
                wqb[r * step:(r + 1) * step, :].astype(F32)
            ).astype(BF16)
        local(wt, wt_out)
        local(par, par_out)

    def vector(row):
        block = par[row * 8:(row + 1) * 8, :].astype(F32)
        return jnp.concatenate([block[r:r + 1, :] for r in range(8)], axis=1)

    scale = 0.125

    def process(s):
        gain, shift = vector(0), vector(1)

        def one(b, carry):
            v = xg[b, s].astype(F32)
            mean = jnp.mean(v, axis=1, keepdims=True)
            v = v - mean
            spread = jnp.mean(v * v, axis=1, keepdims=True)
            n = v * lax.rsqrt(spread + 1e-5)
            xh[b, s] = n.astype(BF16)
            normed = (n * gain + shift).astype(BF16)
            packed = dot_nt(normed, wt[...])
            row = pl.ds(pl.multiple_of(s * tok_rows, tok_rows), tok_rows)
            qkv[b, row, 0:128] = (packed[:, 0:128] * scale).astype(BF16)
            qkv[b, row, 128:384] = packed[:, 128:384].astype(BF16)
            return carry
        lax.fori_loop(0, streams, one, 0)

    def process_hop(h):
        def one(j, carry):
            process(where[h] * 2 + j)
            return carry
        lax.fori_loop(0, 2, one, 0)

    def turn(j, carry):
        b, r = j // (total // step), j % (total // step)
        row = pl.ds(pl.multiple_of(r * step, step), step)
        vt[b, :, row] = jnp.transpose(qkv[b, row, 256:384].astype(F32)).astype(BF16)
        return carry
    def values():
        local(xh, xh_out)
        local(qkv, qkv_out)
        lax.fori_loop(0, streams * (total // step), turn, 0)

    blocks = total // q_block
    cols = bend_v.shape[2]
    tiles = bend_v.shape[0]

    def tile_copies(i):
        cut = pl.ds(pl.multiple_of(i * cols, cols), cols)
        return [
            pltpu.make_async_copy(
                wu_all.at[:, :, :, :, :, :, cut], wu_t.at[i % 2], tile_sem.at[i % 2]
            )
        ]


    def attend(j, carry):
        b, qb = j // blocks, j % blocks
        row = pl.ds(pl.multiple_of(qb * q_block, q_block), q_block)
        dist[...] = distance(len_ref, b, 0, total, qb * q_block, q_block)
        queries = qkv[b, row, 0:128]
        lane = lax.broadcasted_iota(jnp.int32, (q_block, 128), 1)
        for h in range(2):
            own = jnp.where((lane < 64) == (h == 0), queries, jnp.zeros_like(queries))
            s = dot_nt(qkv[b, :, 128:256], own) - slopes[h] * dist[...]
            top = jnp.max(s, axis=0, keepdims=True)
            p = jnp.exp(s - top)
            weight = jnp.sum(p, axis=0, keepdims=True)
            o = dot_nn(vt[b, h * 64:(h + 1) * 64, :], p.astype(BF16))
            ot[b, h * 64:(h + 1) * 64, row] = o / weight
            lse[b, h:h + 1, row] = top + jnp.log(weight)
        obuf[b, row, :] = jnp.transpose(ot[b, :, row]).astype(BF16)
        return carry

    def send_rows(b):
        out = []
        for k in range(1, n_seq):
            other = lax.rem(sq + k, n_seq)
            source = lax.rem(sq + n_seq - k, n_seq)
            src = obuf.at[b, pl.ds(pl.multiple_of(other * tok_rows, tok_rows), tok_rows), :]
            dst = attn.at[b, :, pl.ds(pl.multiple_of(sq * 128, 128), 128)]
            land = attn.at[b, :, pl.ds(pl.multiple_of(source * 128, 128), 128)]
            out.append(keep(Link(src, dst, land, (s_send, s_recv), 20 + b * 7 + k - 1, (dp, other))))
        pending[("o", b)] = out
        own_rows.append(local(
            obuf.at[b, pl.ds(pl.multiple_of(sq * tok_rows, tok_rows), tok_rows), :],
            attn.at[b, :, pl.ds(pl.multiple_of(sq * 128, 128), 128)],
        ))

    own_rows = []

    def attend_some(first, last):
        lax.fori_loop(first, last, attend, 0)

    tokens = streams * tok_rows
    late = []

    def residual():
        wait("o", 0)
        wait("o", 1)
        for copy in own_rows:
            copy.wait()
        load_attn = local(attn, av)
        late.append(load_attn)
        load_attn.wait()
        late[0].wait()
        out_w = wo_v[...].reshape(width, width)
        for r in range(0, width, 512):
            hid[:, r:r + 512] = x_ref[...].reshape(tokens, width)[:, r:r + 512].astype(F32) + dot_nn(
                av[...].reshape(tokens, width), out_w[:, r:r + 512]
            )
        local(hid, hid_out)
        gain_two, shift_two = vector(2), vector(3)
        for r in range(0, tokens, 128):
            n, _ = norm_parts(hid[r:r + 128])
            low_two[r:r + 128] = (n * gain_two + shift_two).astype(BF16)

    def one_tile(i, carry):
        for copy in tile_copies(i):
            copy.wait()

        @pl.when(i + 1 < tiles)
        def _():
            for copy in tile_copies(i + 1):
                copy.start()
        act_f, bend = gelu_both(dot_nn(low_two[...], wu_t[i % 2].reshape(width, cols)))
        act = act_f.astype(BF16)
        for j in range(4):
            act_v[i * 2 + j // 2, j % 2] = act[:, j * 128:(j + 1) * 128]
        bend_v[i] = bend.astype(BF16)
        return carry

    def some_tiles(first, last):
        lax.fori_loop(first * tiles // 4, last * tiles // 4, one_tile, 0)

    def first_group():
        for h in range(4):
            wait("c", 0, h)
        late.append(local(wo_all, wo_v))
        for copy in tile_copies(0):
            copy.start()

    def x_arrived(h):
        wait("x", h)
        x_pass(h)

    def own_x():
        pending["xc", 0] = [
            keep(Link(x_ref, xg.at[:, sq], xg.at[:, z * 2 + (1 - c)], (z_send, z_recv), 6, sibling))
        ]

    def block_done(h):
        if h == 0:
            cp_x.wait()
        wait("xc", h)
        process_hop(h)

    def hop_x(h):
        if h == 3:
            wait("x", 2)
        x_hop(h)

    def hop(g, h):
        if h == 3:
            wait("z", g, 2)
        z_hop(g, h)

    def cross_begin(g, h):
        if h > 0:
            wait("z", g, h)
        cross_one(g, h)

    def cross_next(g, h):
        if h == 0:
            for i in groups[g]:
                cp_w[i].wait()
        cross_two(g, h)

    def stream_out(b):
        send_rows(b)
        if b == 1:
            local(ot, ot_out)
            local(lse, lse_out)

    steps = {
        "seq": along_seq, "wq": along_dp, "wt": columns, "xs": own_x, "vt": values,
        "c0": first_group, "hid": residual,
    }
    for h in range(4):
        steps["p%d" % h] = functools.partial(block_done, h)
        for g in range(2):
            steps["x1%d%d" % (g, h)] = functools.partial(cross_begin, g, h)
            steps["x2%d%d" % (g, h)] = functools.partial(cross_next, g, h)
            steps["cc%d%d" % (g, h)] = functools.partial(cross_core, g, h)
            if h > 0:
                steps["zh%d%d" % (g, h)] = functools.partial(hop, g, h)
        if h > 0:
            steps["xh%d" % h] = functools.partial(hop_x, h)
            steps["xp%d" % h] = functools.partial(x_arrived, h)
    for b in range(streams):
        steps["o%d" % b] = functools.partial(stream_out, b)
    for name, first, last in runs(gather_order, ("a", "u")):
        if name == "a":
            attend_some(first, last)
        elif name == "u":
            some_tiles(first, last)
        else:
            steps[name]()
    local(act_v, act_out)
    local(bend_v, bend_out)
    for key in pending:
        wait(*key)
    waited = [cp_x, cp_wq, *cp_w, *own_rows, *late]
    for copy in locals_:
        if not any(copy is other for other in waited):
            copy.wait()
    for link in links:
        link.wait_sent()


def gather_call(inputs, w_qkv, w_out, w_up, w_down, vectors, lengths):
    streams, tok_rows, width = inputs.shape
    n_seq, n_dp = lax.axis_size("seq"), lax.axis_size("dp")
    nz, total = n_seq // 2, n_seq * tok_rows
    any_space = pl.BlockSpec(memory_space=pl.ANY)
    vmem = pl.BlockSpec(memory_space=pltpu.VMEM)
    smem = pl.BlockSpec(memory_space=pltpu.SMEM)

    def halves(w):
        return w.reshape(2, w.shape[0] // 2, w.shape[1])

    own = [halves(w) for w in (w_out, w_up, w_down)]
    full = [jax.ShapeDtypeStruct((2, n_dp // 2, nz, 2) + w.shape, BF16) for w in own]
    cols = w_qkv.shape[1] // n_seq
    outs = full + [
        jax.ShapeDtypeStruct((32, 128), BF16),
        jax.ShapeDtypeStruct((streams, tok_rows, width), BF16),
        jax.ShapeDtypeStruct((streams, total, cols), BF16),
        jax.ShapeDtypeStruct((streams, 128, total), F32),
        jax.ShapeDtypeStruct((streams, 8, total), F32),
        jax.ShapeDtypeStruct((streams, n_seq, tok_rows, width), BF16),
        jax.ShapeDtypeStruct((cols, width), BF16),
        jax.ShapeDtypeStruct((streams * tok_rows, width), F32),
        jax.ShapeDtypeStruct((n_dp * nz, 2, streams * tok_rows, 128), BF16),
        jax.ShapeDtypeStruct((8, streams * tok_rows, w_up.shape[1] // 8), BF16),
    ]
    dma = pltpu.SemaphoreType.DMA
    scratch = [
        pltpu.VMEM((streams, n_seq, tok_rows, width), BF16),
        pltpu.VMEM((streams, n_seq, tok_rows, width), BF16),
        pltpu.VMEM((width, cols), BF16),
        pltpu.VMEM((cols, width), BF16),
        pltpu.VMEM((n_seq, w_qkv.shape[0], cols), BF16),
        pltpu.VMEM((32, 128), BF16),
        pltpu.VMEM((n_seq - 1 + n_dp - 1, 32, 128), BF16),
        pltpu.VMEM((32, 128), BF16),
        pltpu.VMEM((32, 128), BF16),
        pltpu.VMEM((streams, total, cols), BF16),
        pltpu.VMEM((streams, 128, total), BF16),
        pltpu.VMEM((streams, total, 128), BF16),
        pltpu.VMEM((streams, 128, total), F32),
        pltpu.VMEM((streams, 8, total), F32),
        pltpu.VMEM((total, q_block), F32),
        pltpu.VMEM(full[0].shape, BF16),
        pltpu.VMEM((2,) + full[1].shape[:-1] + (w_up.shape[1] // 8,), BF16),
        pltpu.VMEM((streams, tok_rows, width), BF16),
        pltpu.VMEM((streams * tok_rows, width), F32),
        pltpu.VMEM((streams * tok_rows, width), BF16),
        pltpu.VMEM(outs[11].shape, BF16),
        pltpu.VMEM(outs[12].shape, BF16),
        dma((7,)), dma((7,)), dma((9,)), dma((9,)), dma((60,)), dma((60,)), dma((34,)), dma((34,)),
        dma((2,)), dma((20,)),
    ]
    return pl.pallas_call(
        gather_kernel,
        out_shape=outs,
        in_specs=[vmem] * 6 + [smem],
        out_specs=[any_space] * len(outs),
        scratch_shapes=scratch,
        compiler_params=pltpu.CompilerParams(
            collective_id=0, has_side_effects=True, vmem_limit_bytes=56 * 2**20
        ),
        name="gather_attend",
    )(inputs, w_qkv, *own, vectors, lengths)


def scatter_kernel(
    x_ref, fill_ref, par_ref, cot_ref, attn_ref, hid_ref, act_ref, bend_ref, wo_ref, wu_ref, wd_ref,
    qkv_ref, ot_ref, lse_ref, xh_ref, wt_ref, len_ref,
    y_out, gx_out, go_out, gu_out, gd_out, gq_out, pg_out,
    hidden, n_two, r_two, low_two, grad_two, yb, gout2, gb2, act_v, act_s, bend_t, n2s2, n2o, at2, ato, wo_v, wu_t, wd_t, gab,
    acc_o, acc_u, acc_d, ra_o, ra_u, ra_d, rb_o, rb_u, rb_d, sa_o, sa_u, sa_d, sb_o, sb_u, sb_d,
    zr_o, zr_u, zr_d, fin_o, fin_u, fin_d,
    do, qkv, ot, lse, xh, wt, kt, delta, dk, dv, dqt, dqkv, dqkvt,
    gp, dqr, dqsum, pgp, pr1, psum, pr2, pgo,
    c_send, c_recv, o_send, o_recv, x_send, x_recv, zw_send, zw_recv, zg_send, zg_recv, s_send, s_recv,
    tile_sem, loc,
):
    dp, sq, y, x, z, c = place()
    streams, tok_rows, width = gab.shape
    tokens = streams * tok_rows
    slopes = own_slopes(lax.axis_index("seq"), lax.axis_size("seq"), qkv.shape[1])
    n_seq, n_dp = lax.axis_size("seq"), lax.axis_size("dp")
    nz = n_seq // 2
    total = n_seq * tok_rows
    x_nbr, y_nbr = (y * 2 + (1 - x), sq), ((1 - y) * 2 + x, sq)
    sibling = (dp, z * 2 + (1 - c))
    z1, z2, z3 = planes(z, nz)
    near_dev, far_dev = (dp, z1 * 2 + c), (dp, z2 * 2 + c)
    greet(dp, sq, n_seq, n_dp)
    links, locals_ = [], []
    every = slice(None)

    def keep(link):
        link.start()
        links.append(link)
        return link

    def local(src, dst):
        copy = pltpu.make_async_copy(src, dst, loc.at[len(locals_)])
        copy.start()
        locals_.append(copy)
        return copy

    def loop(n, body):
        def step(j, carry):
            body(j)
            return carry
        lax.fori_loop(0, n, step, 0)

    pending = {}

    arrived = set()

    def wait(*key):
        if key not in arrived:
            arrived.add(key)
            for link in pending[key]:
                link.wait()

    def f32(v):
        return v.astype(F32)

    def vector(row):
        block = f32(par_ref[row * 8:(row + 1) * 8, :])
        return jnp.concatenate([block[r:r + 1, :] for r in range(8)], axis=1)

    def to_sibling(src, dst, index):
        return keep(Link(src, dst, dst, (c_send, c_recv), index, sibling))

    cols = wu_t.shape[2]
    tiles = wu_ref.shape[1] // cols

    def tile_copies(i):
        slot, first = i % 2, pl.multiple_of(i * cols, cols)
        return (
            pltpu.make_async_copy(wu_ref.at[:, pl.ds(first, cols)], wu_t.at[slot], tile_sem.at[slot]),
            pltpu.make_async_copy(wd_ref.at[pl.ds(i * 4, 4)], wd_t.at[slot], tile_sem.at[2 + slot]),
            pltpu.make_async_copy(bend_ref.at[i], bend_t.at[slot], tile_sem.at[4 + slot]),
        )

    load_cot, load_act = local(cot_ref, gab), local(act_ref, act_v)
    act_link = to_sibling(act_ref.at[:, 1 - c], act_s, 1)
    load_hid = local(hid_ref, hidden)
    for copy in tile_copies(0):
        copy.start()
    load_attn, load_out = local(attn_ref, low_two), local(wo_ref, wo_v)
    copies = [local(qkv_ref, qkv), local(ot_ref, ot), local(lse_ref, lse), local(wt_ref, wt)]
    copy_xh = [local(xh_ref.at[:, :, 0:cols], xh)]
    load_cot.wait()
    for b in range(streams):
        rows = slice(b * tok_rows, (b + 1) * tok_rows)
        fill = jnp.broadcast_to(f32(fill_ref[b:b + 1, :]), (128, tok_rows))
        gout2[rows] = (f32(gab[b]) * jnp.transpose(fill)[:, 0:1]).astype(BF16)
    gout_link = to_sibling(gout2.at[0:tokens], gout2.at[tokens:2 * tokens], 0)

    def chosen(parity):
        j = lax.broadcasted_iota(jnp.int32, (1, width // 2), 1)
        column = ((((j & 127) >> 5) * n_seq + (j >> 7) * 2 + parity) << 5) + (j & 31)
        return (lax.broadcasted_iota(jnp.int32, (width, 1), 0) == column).astype(F32).astype(BF16)

    def pick(v, mine, theirs, index):
        here, there = dot_nn(v, chosen(c)).astype(BF16), dot_nn(v, chosen(1 - c)).astype(BF16)
        for b in range(nz):
            mine[b, 0:tokens] = here[:, b * 128:(b + 1) * 128]
            theirs[b] = there[:, b * 128:(b + 1) * 128]
        return to_sibling(theirs, mine.at[:, tokens:2 * tokens], index)

    gain_two, shift_two = vector(2), vector(3)

    def tile_grad(i):
        cut = pl.ds(pl.multiple_of(i % 2 * cols, cols), cols)
        return gp.at[i // 4, i // 2 % 2 * 2, :, :, cut], gp.at[i // 4, i // 2 % 2 * 2 + 1, :, :, cut]

    def tile_link(i):
        src, dst = tile_grad(i)
        return Link(src, dst, dst, (c_send, c_recv), 4 + i, sibling)

    def one_tile(i, carry):
        slot = i % 2
        for copy in tile_copies(i):
            copy.wait()

        @pl.when(i + 1 < tiles)
        def _():
            for copy in tile_copies(i + 1):
                copy.start()
        down = wd_t[slot].reshape(cols, width)
        act = jnp.concatenate([act_v[i * 2 + j // 2, j % 2] for j in range(4)], axis=1)
        hidden[...] += dot_nn(act, down)
        grad_up = (dot_nt(gout2[0:tokens], down) * f32(bend_t[slot])).astype(BF16)
        tile_grad(i)[0][...] = grad_up.reshape(streams, tok_rows, cols)
        grad_two[...] += dot_nt(grad_up, wu_t[slot])
        tile_link(i).start()
        return carry

    arrays = [
        (acc_o, ra_o, rb_o, sa_o, sb_o, zr_o, fin_o, go_out),
        (acc_u, ra_u, rb_u, sa_u, sb_u, zr_u, fin_u, gu_out),
        (acc_d, ra_d, rb_d, sa_d, sb_d, zr_d, fin_d, gd_out),
    ]
    groups = [(1, 0), (2,)]
    U, D = 0, 1
    near = 1 - z // 2
    plane_of = [z3, z2, z1, z]

    def cross_one(g, p):
        t = plane_of[p]
        out = []
        for i in groups[g]:
            acc, ra, rb = arrays[i][:3]
            out.append(keep(Link(acc.at[1 - y, :, t, 0], ra.at[p], ra.at[p], (x_send, x_recv), (i * 4 + p) * 4, y_nbr)))
            out.append(keep(Link(acc.at[:, 1 - x, t, 1], rb.at[p], rb.at[p], (x_send, x_recv), (i * 4 + p) * 4 + 1, x_nbr)))
        pending[("x1", g, p)] = out

    def cross_two(g, p):
        t = plane_of[p]
        wait("x1", g, p)
        out = []
        for i in groups[g]:
            acc, ra, rb, sa, sb = arrays[i][:5]
            acc[y, 1 - x, t, 0] = (f32(acc[y, 1 - x, t, 0]) + f32(ra[p, 1 - x])).astype(BF16)
            acc[1 - y, x, t, 1] = (f32(acc[1 - y, x, t, 1]) + f32(rb[p, 1 - y])).astype(BF16)
            out.append(keep(Link(acc.at[y, 1 - x, t, 0], sa.at[p], sa.at[p], (x_send, x_recv), (i * 4 + p) * 4 + 2, x_nbr)))
            out.append(keep(Link(acc.at[1 - y, x, t, 1], sb.at[p], sb.at[p], (x_send, x_recv), (i * 4 + p) * 4 + 3, y_nbr)))
        pending[("x2", g, p)] = out

    def cross_three(g, p):
        t = plane_of[p]
        wait("x2", g, p)
        for i in groups[g]:
            acc, ra, rb, sa, sb = arrays[i][:5]
            acc[y, x, t, 0] = (f32(acc[y, x, t, 0]) + f32(ra[p, x]) + f32(sa[p])).astype(BF16)
            acc[y, x, t, 1] = (f32(acc[y, x, t, 1]) + f32(rb[p, y]) + f32(sb[p])).astype(BF16)

    def z_one(g, step, target):
        pending[("z", g, step)] = [
            keep(Link(
                arrays[i][0].at[y, x, plane_of[step]], arrays[i][5].at[step], arrays[i][5].at[step],
                (zw_send, zw_recv), i * 3 + step, target,
            ))
            for i in groups[g]
        ]

    def z_first(g):
        cross_three(g, 0)
        z_one(g, 0, near_dev)

    def z_second(g):
        cross_three(g, 1)
        wait("z", g, 0)
        for i in groups[g]:
            acc, zr = arrays[i][0], arrays[i][5]
            for h in range(2):
                acc[y, x, z2, h] = (f32(acc[y, x, z2, h]) + f32(zr[0, h])).astype(BF16)
        z_one(g, 1, far_dev)

    def z_third(g):
        cross_three(g, 2)
        z_one(g, 2, near_dev)

    def z_last(g):
        cross_three(g, 3)
        wait("z", g, 1)
        wait("z", g, 2)
        for i in groups[g]:
            acc, zr, fin, out = arrays[i][0], *arrays[i][5:]
            fin[...] = f32(acc[y, x, z]) + f32(zr[1]) + f32(zr[2])
            local(fin, out)

    def dot_tn(a, b):
        return lax.dot_general(a, b, (((0,), (0,)), ((), ())), preferred_element_type=F32)

    def down_terms(pair):
        def one(d):
            first = d * 4 + pair * 2
            left = jnp.concatenate([
                jnp.concatenate([act_v[first, c], act_v[first + 1, c]], axis=1),
                jnp.concatenate([act_s[first], act_s[first + 1]], axis=1),
            ], axis=0)
            rows = acc_d.shape[4]
            for r in range(0, width, 512):
                terms = dot_tn(left, gout2[:, r:r + 512]).astype(BF16)
                for j in range(4):
                    acc_d[d // 2, d % 2, pair * 2 + j // 2, j % 2, :, r:r + 512] = terms[j * rows:(j + 1) * rows]
        loop(n_dp, one)

    def narrow_terms(source, pair, acc, right, where):
        left = jnp.concatenate([source[pair * 2], source[pair * 2 + 1]], axis=1)
        terms = dot_tn(left, right).astype(BF16)
        for j in range(16):
            d = j % 8 // 2
            acc[d // 2, d % 2, pair * 2 + j // 8, j % 2, :, where] = terms[j * 16:(j + 1) * 16]

    def up_terms(pair):
        def one(i):
            d, part = i // 2, i % 2
            cut = pl.ds(pl.multiple_of(part * cols, cols), cols)
            right = gp[d // 2, pl.ds(d % 2 * 2, 2), :, :, cut].reshape(2 * tokens, cols)
            where = pl.ds(pl.multiple_of(i * cols, cols), cols)
            narrow_terms(n2s2, pair, acc_u, right, where)
        loop(tiles, one)
        for r in range(0, width, 512):
            narrow_terms(at2, pair, acc_o, gb2[:, r:r + 512], slice(r, r + 512))

    def down_first():
        for copy in (load_act, load_hid, load_attn):
            copy.wait()
        gout_link.wait()
        act_link.wait()
        down_terms(near)

    def pick_attn():
        pending["attn",] = [pick(low_two[...], at2, ato, 2)]

    def pick_norm():
        pending["norm",] = [pick(low_two[...], n2s2, n2o, 3)]

    def second_norm():
        for r in range(0, tokens, 128):
            n, rstd = norm_parts(hidden[r:r + 128])
            n_two[r:r + 128] = n
            r_two[r:r + 128] = jnp.broadcast_to(rstd, (128, 128))
            low_two[r:r + 128] = (n * gain_two + shift_two).astype(BF16)
        grad_two[...] = jnp.zeros_like(grad_two)

    def some_tiles(first, last):
        lax.fori_loop(first * tiles // 4, last * tiles // 4, one_tile, 0)

    grad_links, own_do = [], []

    def branch():
        yb[...] = hidden[...].astype(BF16)
        local(yb, y_out)
        for r in range(0, tokens, 128):
            rows = slice(r, r + 128)
            back = norm_back(n_two[rows], r_two[rows, 0:1], grad_two[rows] * gain_two)
            grad = f32(gout2[rows]) + back
            hidden[rows] = grad
            gb2[rows] = grad.astype(BF16)
        load_out.wait()
        pending["branch",] = [to_sibling(gb2.at[0:tokens], gb2.at[tokens:2 * tokens], 12)]
        for r in range(0, width, 512):
            grad = dot_nt(gb2[0:tokens], wo_v[r // 128:r // 128 + 4].reshape(512, width)).astype(BF16)
            gab[:, :, r:r + 512] = grad.reshape(streams, tok_rows, 512)
        for b in range(streams):
            out = []
            for k in range(1, n_seq):
                other = lax.rem(sq + k, n_seq)
                source = lax.rem(sq + n_seq - k, n_seq)
                src = gab.at[b, :, pl.ds(pl.multiple_of(other * 128, 128), 128)]
                dst = do.at[b, pl.ds(pl.multiple_of(sq * tok_rows, tok_rows), tok_rows), :]
                land = do.at[b, pl.ds(pl.multiple_of(source * tok_rows, tok_rows), tok_rows), :]
                out.append(keep(Link(src, dst, land, (o_send, o_recv), b * 7 + k - 1, (dp, other))))
            grad_links.append(out)
        copy_xh.append(local(xh_ref.at[:, :, cols:width], wu_t))
        own_do.extend(
            local(
                gab.at[b, :, pl.ds(pl.multiple_of(sq * 128, 128), 128)],
                do.at[b, pl.ds(pl.multiple_of(sq * tok_rows, tok_rows), tok_rows), :],
            )
            for b in range(streams)
        )
        pgp[...] = jnp.zeros_like(pgp)
        pgp[2:3, :] = jnp.sum(grad_two[...] * n_two[...], axis=0, keepdims=True)
        pgp[3:4, :] = jnp.sum(grad_two[...], axis=0, keepdims=True)

    def up_first():
        for key in ("attn", "norm", "branch"):
            wait(key)

        def wait_tile(i):
            tile_link(i).wait()
        loop(tiles, wait_tile)
        up_terms(near)

    step = 256
    blocks = total // q_block

    def turn(j):
        b, r = j // (total // step), j % (total // step)
        row = pl.ds(pl.multiple_of(r * step, step), step)
        kt[b, :, row] = jnp.transpose(f32(qkv[b, row, 128:256])).astype(BF16)
    def keys_turned():
        for copy in copies:
            copy.wait()
        loop(streams * (total // step), turn)


    def prepare(b):
        own_do[b].wait()
        for link in grad_links[b]:
            link.wait()

        def one(r):
            row = pl.ds(pl.multiple_of(r * step, step), step)
            both = jnp.transpose(f32(do[b, row, :])) * ot[b, :, row]
            for h in range(2):
                delta[h:h + 1, row] = jnp.sum(both[h * 64:(h + 1) * 64], axis=0, keepdims=True)
        loop(total // step, one)
        dk[...] = jnp.zeros_like(dk)
        dv[...] = jnp.zeros_like(dv)

    tile = 256

    def attend(b, qb):
        row = pl.ds(pl.multiple_of(qb * q_block, q_block), q_block)
        lane = lax.broadcasted_iota(jnp.int32, (q_block, 128), 1)
        queries, grads = qkv[b, row, 0:128], do[b, row, :]
        none = jnp.zeros_like(queries)
        own = [jnp.where((lane < 64) == (h == 0), queries, none) for h in range(2)]
        own_grad = [jnp.where((lane < 64) == (h == 0), grads, none) for h in range(2)]
        part = [jnp.zeros((64, q_block), F32)] * 2
        for r in range(total // tile):
            keys = slice(r * tile, (r + 1) * tile)
            gap = distance(len_ref, b, r * tile, tile, qb * q_block, q_block)
            grad_v = grad_k = 0
            for h in range(2):
                s = dot_nt(qkv[b, keys, 128:256], own[h]) - slopes[h] * gap
                p = jnp.exp(s - lse[b, h:h + 1, row])
                gp_t = dot_nt(qkv[b, keys, 256:384], own_grad[h])
                ds = (p * (gp_t - delta[h:h + 1, row])).astype(BF16)
                grad_v = grad_v + dot_nn(p.astype(BF16), own_grad[h])
                grad_k = grad_k + dot_nn(ds, own[h])
                part[h] = part[h] + dot_nn(kt[b, h * 64:(h + 1) * 64, keys], ds)
            dv[keys, :] += grad_v
            dk[keys, :] += grad_k
        for h in range(2):
            dqt[h * 64:(h + 1) * 64, row] = part[h] * 0.125

    def attend_some(b, first, last):
        def one(qb, carry):
            attend(b, qb)
            return carry
        lax.fori_loop(first, last, one, 0)

    def gs(b):
        return wo_v.at[b * nz:(b + 1) * nz]

    def gz(b, step):
        return wd_t.at[b, step]

    def finish_stream(b):
        def one(r):
            row = pl.ds(pl.multiple_of(r * step, step), step)
            low = dqt[:, row].astype(BF16)
            dqkvt[b, 0:128, row] = low
            dqkv[row, 0:128] = jnp.transpose(f32(low)).astype(BF16)
            for first, grad in ((128, dk), (256, dv)):
                low = grad[row, :].astype(BF16)
                dqkv[row, first:first + 128] = low
                dqkvt[b, first:first + 128, row] = jnp.transpose(f32(low)).astype(BF16)
        loop(total // step, one)

        def product(s):
            row = pl.ds(pl.multiple_of(s * tok_rows, tok_rows), tok_rows)
            gp[b, s // 2, s % 2] = dot_nn(dqkv[row, :], wt[...]).astype(BF16)
        loop(n_seq, product)
        pending[("gc", b)] = [
            keep(Link(gp.at[b, :, 1 - c], gs(b), gs(b), (zg_send, zg_recv), b * 4, sibling))
        ]

    def g_one(b, step, target):
        pending[("g", b, step)] = [
            keep(Link(gp.at[b, plane_of[step], c], gz(b, step), gz(b, step), (zg_send, zg_recv), b * 4 + 1 + step, target))
        ]

    def g_first(b):
        wait("gc", b)

        def add(j):
            gp[b, j, c] = (f32(gp[b, j, c]) + f32(wo_v[b * nz + j])).astype(BF16)
        loop(nz, add)
        g_one(b, 0, near_dev)
        g_one(b, 2, near_dev)

    def g_second(b):
        wait("g", b, 0)
        gp[b, z2, c] = (f32(gp[b, z2, c]) + f32(gz(b, 0)[...])).astype(BF16)
        g_one(b, 1, far_dev)

    def g_last(b):
        wait("g", b, 1)
        wait("g", b, 2)
        own = f32(gp[b, z, c]) + f32(gz(b, 1)[...]) + f32(gz(b, 2)[...])
        rows = slice(b * tok_rows, (b + 1) * tok_rows)
        n, rstd = norm_parts(f32(x_ref[rows]))
        low_two[rows] = (hidden[rows] + norm_back(n, rstd, own * vector(0))).astype(BF16)
        local(low_two.at[rows], gx_out.at[b])

    rows_dp = 32 * n_seq

    def weight_grad():
        for copy in copy_xh:
            copy.wait()
        sums = jnp.sum(f32(dqkvt[0]), axis=1, keepdims=True)
        for b in range(1, streams):
            sums = sums + jnp.sum(f32(dqkvt[b]), axis=1, keepdims=True)
        gain, shift = vector(0), vector(1)
        for r in range(width // step):
            cols = slice(r * step, (r + 1) * step)
            weight = f32(wt[:, cols])
            n = xh if r < 2 else wu_t
            there = slice(r % 2 * step, (r % 2 + 1) * step)
            raw = dot_nn(dqkvt[0], n[0, :, there])
            for b in range(1, streams):
                raw = raw + dot_nn(dqkvt[b], n[b, :, there])
            pgp[0:1, cols] = jnp.sum(raw * weight, axis=0, keepdims=True)
            pgp[1:2, cols] = jnp.sum(sums * weight, axis=0, keepdims=True)
            grad = raw * gain[:, cols] + sums * shift[:, cols]
            dqkv[cols, :] = jnp.transpose(grad).astype(BF16)
        out = []
        for m in range(1, n_dp):
            other = lax.rem(dp + m, n_dp)
            src = dqkv.at[pl.ds(pl.multiple_of(other * rows_dp, rows_dp), rows_dp), :]
            out.append(keep(Link(src, dqr.at[m - 1], dqr.at[m - 1], (s_send, s_recv), m - 1, (other, sq))))
            src = pgp.at[:, pl.ds(pl.multiple_of(other * rows_dp, rows_dp), rows_dp)]
            out.append(keep(Link(src, pr1.at[m - 1], pr1.at[m - 1], (s_send, s_recv), 3 + m - 1, (other, sq))))
        pending["qd",] = out

    def weight_grad_two():
        wait("qd")
        mine = pl.ds(pl.multiple_of(dp * rows_dp, rows_dp), rows_dp)
        part = f32(dqkv[mine, :])
        small = pgp[:, mine]
        for m in range(n_dp - 1):
            part = part + f32(dqr[m])
            small = small + pr1[m]
        dqsum[...] = part.astype(BF16)
        psum[...] = small
        out = []
        for k in range(1, n_seq):
            other = lax.rem(sq + k, n_seq)
            source = lax.rem(sq + n_seq - k, n_seq)
            src = dqsum.at[pl.ds(pl.multiple_of(other * 32, 32), 32), :]
            out.append(keep(Link(src, gq_out.at[sq], gq_out.at[source], (s_send, s_recv), 6 + k - 1, (dp, other))))
            src = psum.at[:, pl.ds(pl.multiple_of(other // 4 * 128, 128), 128)]
            out.append(keep(Link(src, pr2.at[k - 1], pr2.at[k - 1], (s_send, s_recv), 13 + k - 1, (dp, other))))
        local(dqsum.at[pl.ds(pl.multiple_of(sq * 32, 32), 32), :], gq_out.at[sq])
        pending["qs",] = out

    def weight_grad_last():
        wait("qs")
        small = psum[:, pl.ds(pl.multiple_of(sq // 4 * 128, 128), 128)]
        for k in range(n_seq - 1):
            small = small + pr2[k]
        pgo[...] = small
        local(pgo, pg_out)

    def first_frames():
        keys_turned()
        prepare(0)

    def first_done():
        def sent(i):
            tile_link(i).wait_sent()
        loop(tiles, sent)
        finish_stream(0)

    steps = {
        "DT0": down_first, "DT1": functools.partial(down_terms, 1 - near), "pkA": pick_attn, "pkN": pick_norm,
        "LN": second_norm, "LNB": branch, "UT0": up_first, "UT1": functools.partial(up_terms, 1 - near),
        "P0": first_frames, "P1": functools.partial(prepare, 1),
        "F0": first_done, "F1": functools.partial(finish_stream, 1),
        "WG": weight_grad, "W2": weight_grad_two, "W3": weight_grad_last,
    }
    for name, action in (("gf", g_first), ("gs", g_second), ("gl", g_last)):
        for b in range(streams):
            steps[name + str(b)] = functools.partial(action, b)
    for letter, g in (("U", U), ("D", D)):
        for name, action in (("zf", z_first), ("zs", z_second), ("zt", z_third), ("zl", z_last)):
            steps[name + letter] = functools.partial(action, g)
        for p in range(nz):
            steps["c1%s%d" % (letter, p)] = functools.partial(cross_one, g, p)
            steps["c2%s%d" % (letter, p)] = functools.partial(cross_two, g, p)
    for name, first, last in runs(scatter_order, ("A0", "A1", "T")):
        if name in ("A0", "A1"):
            attend_some(int(name[1]), first, last)
        elif name == "T":
            some_tiles(first, last)
        else:
            steps[name]()
    for key in pending:
        wait(*key)
    waited = [load_cot, load_act, load_hid, load_attn, load_out, *copy_xh, *own_do, *copies]
    for copy in locals_:
        if not any(copy is other for other in waited):
            copy.wait()
    for link in links:
        link.wait_sent()


def scatter_call(
    inputs, cotangent, infill, attn, hidden, act, bend, params, weights, qkv, ot, lse, xh, wt, lengths,
):
    streams, total = qkv.shape[:2]
    tokens, width = inputs.shape
    tok_rows = tokens // streams
    n_seq, n_dp = lax.axis_size("seq"), lax.axis_size("dp")
    nz = n_seq // 2
    cols = qkv.shape[2]
    any_space = pl.BlockSpec(memory_space=pl.ANY)
    vmem = pl.BlockSpec(memory_space=pltpu.VMEM)
    smem = pl.BlockSpec(memory_space=pltpu.SMEM)
    dma = pltpu.SemaphoreType.DMA
    sizes = [(w.shape[0] // (2 * n_dp * n_seq), w.shape[1]) for w in weights]
    tile = weights[1].shape[1] // 8

    def buffers(*lead):
        return [pltpu.VMEM(lead + size, BF16) for size in sizes]

    def low(*shape):
        return pltpu.VMEM(shape, BF16)

    def full(*shape):
        return pltpu.VMEM(shape, F32)

    half = width // 2 // nz
    scratch = [
        full(tokens, width), full(tokens, width), full(tokens, 128), low(tokens, width), full(tokens, width),
        low(tokens, width), low(2 * tokens, width), low(2 * tokens, width),
        low(*act.shape), low(act.shape[0], tokens, 128), low(2, *bend.shape[1:]),
        low(nz, 2 * tokens, half), low(nz, tokens, half), low(nz, 2 * tokens, half), low(nz, tokens, half),
        low(width // 128, 128, width), low(2, width, tile), low(2, tile // 128, 128, width), low(streams, tok_rows, width),
    ]
    scratch += buffers(2, 2, nz, 2) + buffers(nz, 2) + buffers(nz, 2) + buffers(nz) + buffers(nz)
    scratch += buffers(nz - 1, 2)
    scratch += [pltpu.VMEM((2,) + size, F32) for size in sizes]
    scratch += [
        low(streams, total, 128), low(*qkv.shape), full(*ot.shape), full(*lse.shape), low(streams, total, tile), low(*wt.shape),
        low(streams, 128, total), full(8, total), full(total, 128), full(total, 128),
        full(128, total), low(total, cols), low(streams, cols, total),
        low(streams, nz, 2, tok_rows, width),
        low(n_dp - 1, width // n_dp, cols), low(width // n_dp, cols),
        full(8, width), full(n_dp - 1, 8, width // n_dp), full(8, width // n_dp), full(n_seq - 1, 8, 128), full(8, 128),
        dma((13,)), dma((13,)), dma((14,)), dma((14,)), dma((48,)), dma((48,)), dma((9,)), dma((9,)),
        dma((8,)), dma((8,)), dma((20,)), dma((20,)), dma((6,)), dma((24,)),
    ]
    outs = [
        jax.ShapeDtypeStruct((tokens, width), BF16),
        jax.ShapeDtypeStruct((streams, tok_rows, width), BF16),
        *[jax.ShapeDtypeStruct((2,) + size, F32) for size in sizes],
        jax.ShapeDtypeStruct((n_seq, width // (n_dp * n_seq), cols), BF16),
        jax.ShapeDtypeStruct((8, 128), F32),
    ]
    return pl.pallas_call(
        scatter_kernel,
        out_shape=outs,
        in_specs=[vmem] * 3 + [any_space] * 13 + [smem],
        out_specs=[any_space] * len(outs),
        scratch_shapes=scratch,
        compiler_params=pltpu.CompilerParams(
            collective_id=1, has_side_effects=True, vmem_limit_bytes=63 * 2**20
        ),
        name="scatter_attend",
    )(
        inputs, infill, params, cotangent, attn, hidden, act, bend, weights[0].reshape(-1, 128, width), weights[1],
        weights[2].reshape(-1, 128, width), qkv, ot, lse, xh, wt, lengths,
    )


def finish_kernel(y, gx, go, gu, gd, gq, y_out, gx_out, go_out, gu_out, gd_out, gq_out, wide, sems):
    width = gq_out.shape[1] // 3
    pairs = ((y, y_out), (gx, gx_out), (go, go_out), (gu, gu_out), (gd, gd_out), (wide, gq_out))
    copies = [pltpu.make_async_copy(src, dst, sems.at[i]) for i, (src, dst) in enumerate(pairs)]
    for copy in copies[:-1]:
        copy.start()
    for q in range(gq.shape[0]):
        for j in range(3):
            wide[:, j * width + q * 128:j * width + (q + 1) * 128] = gq[q, :, j * 128:(j + 1) * 128].astype(F32)
    copies[-1].start()
    for copy in copies:
        copy.wait()


def finish_call(*parts):
    gq = parts[-1]
    vmem = pl.BlockSpec(memory_space=pltpu.VMEM)
    outs = [jax.ShapeDtypeStruct(part.shape, part.dtype) for part in parts[:-1]]
    outs.append(jax.ShapeDtypeStruct((gq.shape[1], gq.shape[0] * gq.shape[2]), F32))
    return pl.pallas_call(
        finish_kernel,
        out_shape=outs,
        in_specs=[vmem] * len(parts),
        out_specs=[pl.BlockSpec(memory_space=pltpu.HBM)] * len(outs),
        scratch_shapes=[pltpu.VMEM(outs[-1].shape, F32), pltpu.SemaphoreType.DMA((len(outs),))],
        compiler_params=pltpu.CompilerParams(vmem_limit_bytes=32 * 2**20),
        name="finish",
    )(*parts)


def by_heads(
    inputs, lengths, infill, cotangent, w_qkv, w_out, w_up, w_down,
    gain_one, shift_one, gain_two, shift_two,
):
    streams, tok_rows, width = inputs.shape
    n_seq = lax.axis_size("seq")
    sq = lax.axis_index("seq")
    stream_len, tokens = tok_rows * n_seq, streams * tok_rows
    own_rows = w_qkv.shape[0]
    vectors = jnp.tile(jnp.stack([gain_one, shift_one, gain_two, shift_two]), (1, 128 // own_rows))
    (
        full_out, full_up, full_down, params, attn, qkv, ot, lse, xh, wt, hidden, act, bend
    ) = gather_call(inputs, w_qkv, w_out, w_up, w_down, vectors, lengths)
    weights = (
        full_out.reshape(width, width), full_up.reshape(width, -1), full_down.reshape(-1, width)
    )
    output, input_grad, grad_out, grad_up, grad_down, grad_qkv, small = scatter_call(
        inputs.reshape(tokens, width), cotangent,
        infill, attn.reshape(tokens, width), hidden, act, bend,
        params, weights,
        qkv, ot, lse, xh.reshape(streams, stream_len, width), wt, lengths,
    )
    output, input_grad, grad_out, grad_up, grad_down, grad_qkv = finish_call(
        output, input_grad, grad_out, grad_up, grad_down, grad_qkv
    )
    small = lax.dynamic_slice(small, (0, sq % (128 // own_rows) * own_rows), (4, own_rows))
    return (
        output.reshape(inputs.shape),
        input_grad,
        grad_qkv,
        grad_out.reshape(w_out.shape),
        grad_up.reshape(w_up.shape),
        grad_down.reshape(w_down.shape),
        small[0], small[1], small[2], small[3],
    )


def layer_norm(features, gain_vec, shift_vec):
    row_mean = jnp.mean(features, axis=-1, keepdims=True)
    centered = features - row_mean
    spread = jnp.mean(centered * centered, axis=-1, keepdims=True)
    return centered * lax.rsqrt(spread + norm_eps) * gain_vec + shift_vec


def segment_of(bounds, positions):
    return jnp.sum((positions[None, :, None] >= bounds[:, None, :]).astype(jnp.int32), axis=2)


def slope_table(head_count, stream_len):
    return 2.0 ** (-8.0 * (jnp.arange(head_count, dtype=jnp.float32) + 1.0) / head_count) * (
        256.0 / stream_len
    )


def block_scores(queries, key_heads, query_pos, key_pos, query_seg, key_seg, slopes):
    raw_scores = jnp.einsum(
        "sqhc,skhc->shqk", queries, key_heads, preferred_element_type=jnp.float32
    )
    distance = jnp.abs(query_pos[:, None] - key_pos[None, :]).astype(jnp.float32)
    scores = (
        raw_scores * queries.shape[3] ** (-0.5) - slopes[None, :, None, None] * distance[None, None]
    )
    same_utt = query_seg[:, None, :, None] == key_seg[:, None, None, :]
    return jnp.where(same_utt, scores, masked_score)


def score_grads(
    queries,
    grad_heads,
    log_total,
    delta,
    key_heads,
    values,
    query_pos,
    key_pos,
    query_seg,
    key_seg,
    slopes,
):
    scores = block_scores(queries, key_heads, query_pos, key_pos, query_seg, key_seg, slopes)
    probs = jnp.exp(scores - log_total[..., None])
    grad_probs = jnp.einsum(
        "sqhc,skhc->shqk", grad_heads, values, preferred_element_type=jnp.float32
    )
    grad_scores = (probs * (grad_probs - delta[..., None])).astype(jnp.bfloat16)
    return (probs.astype(jnp.bfloat16), grad_scores)


def by_frames(
    inputs,
    lengths,
    infill,
    cotangent,
    w_qkv,
    w_out,
    w_up,
    w_down,
    gain_one,
    shift_one,
    gain_two,
    shift_two,
):
    w_qkv, w_out, w_up, w_down, gain_one, shift_one, gain_two, shift_two = (
        lax.all_gather(w_qkv, ("dp", "seq"), axis=0, tiled=True),
        lax.all_gather(w_out, ("dp", "seq"), axis=0, tiled=True),
        lax.all_gather(w_up, ("dp", "seq"), axis=0, tiled=True),
        lax.all_gather(w_down, ("dp", "seq"), axis=0, tiled=True),
        lax.all_gather(gain_one, ("dp", "seq"), axis=0, tiled=True),
        lax.all_gather(shift_one, ("dp", "seq"), axis=0, tiled=True),
        lax.all_gather(gain_two, ("dp", "seq"), axis=0, tiled=True),
        lax.all_gather(shift_two, ("dp", "seq"), axis=0, tiled=True),
    )
    streams, tok_rows, model_width = inputs.shape
    head_count = HEADS
    head_size = HEAD_DIM
    stream_len = tok_rows * lax.axis_size("seq")
    score_scale = head_size ** (-0.5)
    slopes = slope_table(head_count, stream_len)
    bounds = jnp.cumsum(lengths, axis=1)
    own_pos = lax.axis_index("seq") * tok_rows + jnp.arange(tok_rows, dtype=jnp.int32)
    own_seg = segment_of(bounds, own_pos)
    gain_one_f = gain_one.astype(jnp.float32)
    shift_one_f = shift_one.astype(jnp.float32)
    gain_two_f = gain_two.astype(jnp.float32)
    shift_two_f = shift_two.astype(jnp.float32)
    inputs_f = inputs.astype(jnp.float32)
    normed_one = layer_norm(inputs_f, gain_one_f, shift_one_f).astype(jnp.bfloat16)
    packed = jnp.einsum(
        "std,de->ste", normed_one, w_qkv, preferred_element_type=jnp.float32
    ).astype(jnp.bfloat16)
    query_low = packed[:, :, :model_width]
    key_value = packed[:, :, model_width:]
    query_heads = query_low.reshape(streams, tok_rows, head_count, head_size)
    start_state = (
        jnp.full((streams, head_count, tok_rows), masked_score, jnp.float32),
        jnp.zeros((streams, head_count, tok_rows), jnp.float32),
        jnp.zeros((streams, head_count, tok_rows, head_size), jnp.float32),
    )
    shard_piece = lax.all_gather(key_value, "seq", axis=1, tiled=True)
    key_count = shard_piece.shape[1]
    visit_block_len = 256

    def one_block(carried, offset):
        top_score, weight_sum, weighted = carried
        key_part = lax.dynamic_slice_in_dim(shard_piece, offset, visit_block_len, 1)
        key_pos = offset + jnp.arange(visit_block_len, dtype=jnp.int32)
        key_seg = segment_of(bounds, key_pos)
        key_heads = key_part[:, :, :model_width].reshape(
            streams, visit_block_len, head_count, head_size
        )
        values = key_part[:, :, model_width:].reshape(
            streams, visit_block_len, head_count, head_size
        )
        scores = block_scores(query_heads, key_heads, own_pos, key_pos, own_seg, key_seg, slopes)
        new_top = jnp.maximum(top_score, jnp.max(scores, axis=3))
        rescale = jnp.exp(top_score - new_top)
        weights_blk = jnp.exp(scores - new_top[..., None])
        weight_sum = weight_sum * rescale + jnp.sum(weights_blk, axis=3)
        weighted = weighted * rescale[..., None] + jnp.einsum(
            "shqk,skhc->shqc",
            weights_blk.astype(jnp.bfloat16),
            values,
            preferred_element_type=jnp.float32,
        )
        return ((new_top, weight_sum, weighted), None)

    offsets = jnp.arange(key_count // visit_block_len, dtype=jnp.int32) * visit_block_len
    finished, _ = lax.scan(one_block, start_state, offsets)
    top_score, weight_sum, weighted = finished
    attn_heads = weighted / weight_sum[..., None]
    log_total = top_score + jnp.log(weight_sum)
    attn_rows = jnp.transpose(attn_heads, (0, 2, 1, 3)).reshape(streams, tok_rows, model_width)
    attn_low = attn_rows.astype(jnp.bfloat16)
    hidden = inputs_f + jnp.einsum(
        "std,de->ste", attn_low, w_out, preferred_element_type=jnp.float32
    )
    normed_two_f, ln_two_pull = jax.vjp(layer_norm, hidden, gain_two_f, shift_two_f)
    normed_two = normed_two_f.astype(jnp.bfloat16)
    upward = jnp.einsum("std,df->stf", normed_two, w_up, preferred_element_type=jnp.float32)
    active_f, gelu_pull = jax.vjp(jax.nn.gelu, upward)
    active = active_f.astype(jnp.bfloat16)
    output = (
        hidden + jnp.einsum("stf,fd->std", active, w_down, preferred_element_type=jnp.float32)
    ).astype(jnp.bfloat16)
    grad_output = (cotangent.astype(jnp.float32) * infill.astype(jnp.float32)[:, :, None]).astype(
        jnp.bfloat16
    )
    grad_active = jnp.einsum("ste,fe->stf", grad_output, w_down, preferred_element_type=jnp.float32)
    grad_upward = gelu_pull(grad_active)[0].astype(jnp.bfloat16)
    grad_norm_two = jnp.einsum("stf,df->std", grad_upward, w_up, preferred_element_type=jnp.float32)
    grad_in_two, grad_gain_two, grad_shift_two = ln_two_pull(grad_norm_two)
    grad_hidden = grad_output.astype(jnp.float32) + grad_in_two
    grad_branch = grad_hidden.astype(jnp.bfloat16)
    grad_attn = jnp.einsum(
        "ste,de->std", grad_branch, w_out, preferred_element_type=jnp.float32
    ).astype(jnp.bfloat16)
    grad_heads = grad_attn.reshape(streams, tok_rows, head_count, head_size)
    delta = jnp.einsum("sqhc,shqc->shq", grad_heads.astype(jnp.float32), attn_heads)
    every_kv = lax.all_gather(key_value, "seq", axis=1, tiled=True)
    total_len = every_kv.shape[1]
    block_len = 256
    offsets = jnp.arange(total_len // block_len, dtype=jnp.int32) * block_len
    grad_start = jnp.zeros((streams, tok_rows, head_count, head_size), jnp.float32)

    def key_step(grad_query, offset):
        key_part = lax.dynamic_slice_in_dim(every_kv, offset, block_len, 1)
        key_pos = offset + jnp.arange(block_len, dtype=jnp.int32)
        key_seg = segment_of(bounds, key_pos)
        key_heads = key_part[:, :, :model_width].reshape(streams, block_len, head_count, head_size)
        values = key_part[:, :, model_width:].reshape(streams, block_len, head_count, head_size)
        probs_low, grad_scores = score_grads(
            query_heads,
            grad_heads,
            log_total,
            delta,
            key_heads,
            values,
            own_pos,
            key_pos,
            own_seg,
            key_seg,
            slopes,
        )
        grad_query = (
            grad_query
            + jnp.einsum(
                "shqk,skhc->sqhc", grad_scores, key_heads, preferred_element_type=jnp.float32
            )
            * score_scale
        )
        grad_keys = (
            jnp.einsum(
                "shqk,sqhc->kshc", grad_scores, query_heads, preferred_element_type=jnp.float32
            )
            * score_scale
        )
        grad_values = jnp.einsum(
            "shqk,sqhc->kshc", probs_low, grad_heads, preferred_element_type=jnp.float32
        )
        key_terms = jnp.concatenate(
            [
                grad_keys.reshape(block_len, streams, model_width),
                grad_values.reshape(block_len, streams, model_width),
            ],
            axis=2,
        )
        return (grad_query, key_terms)

    grad_query, key_terms = lax.scan(key_step, grad_start, offsets)
    key_terms = key_terms.reshape(total_len, streams, 2 * model_width)
    own_kv_grad = lax.psum_scatter(
        key_terms.astype(jnp.bfloat16), "seq", scatter_dimension=0, tiled=True
    ).astype(jnp.float32)
    grad_kv = jnp.transpose(own_kv_grad, (1, 0, 2))
    grad_packed = jnp.concatenate(
        [grad_query.reshape(streams, tok_rows, model_width), grad_kv], axis=2
    ).astype(jnp.bfloat16)
    grad_norm_one = jnp.einsum(
        "ste,de->std", grad_packed, w_qkv, preferred_element_type=jnp.float32
    )
    _, ln_one_pull = jax.vjp(layer_norm, inputs_f, gain_one_f, shift_one_f)
    grad_in_one, grad_gain_one, grad_shift_one = ln_one_pull(grad_norm_one)
    input_grad = (grad_hidden + grad_in_one).astype(jnp.bfloat16)
    weight_terms = (
        jnp.einsum("std,ste->de", normed_one, grad_packed, preferred_element_type=jnp.float32),
        jnp.einsum("std,ste->de", attn_low, grad_branch, preferred_element_type=jnp.float32),
        jnp.einsum("std,stf->df", normed_two, grad_upward, preferred_element_type=jnp.float32),
        jnp.einsum("stf,std->fd", active, grad_output, preferred_element_type=jnp.float32),
        grad_gain_one,
        grad_shift_one,
        grad_gain_two,
        grad_shift_two,
    )
    summed = (
        lax.psum_scatter(weight_terms[0], ("dp", "seq"), scatter_dimension=0, tiled=True),
        lax.psum_scatter(weight_terms[1], ("dp", "seq"), scatter_dimension=0, tiled=True),
        lax.psum_scatter(weight_terms[2], ("dp", "seq"), scatter_dimension=0, tiled=True),
        lax.psum_scatter(weight_terms[3], ("dp", "seq"), scatter_dimension=0, tiled=True),
        lax.psum_scatter(weight_terms[4], ("dp", "seq"), scatter_dimension=0, tiled=True),
        lax.psum_scatter(weight_terms[5], ("dp", "seq"), scatter_dimension=0, tiled=True),
        lax.psum_scatter(weight_terms[6], ("dp", "seq"), scatter_dimension=0, tiled=True),
        lax.psum_scatter(weight_terms[7], ("dp", "seq"), scatter_dimension=0, tiled=True),
    )
    return (
        output,
        input_grad,
        summed[0],
        summed[1],
        summed[2],
        summed[3],
        summed[4],
        summed[5],
        summed[6],
        summed[7],
    )


def solution(mesh):
    in_specs = (
        P("dp", "seq", None),
        P("dp", None),
        P("dp", "seq"),
        P("dp", "seq", None),
        P(("dp", "seq"), None),
        P(("dp", "seq"), None),
        P(("dp", "seq"), None),
        P(("dp", "seq"), None),
        P(("dp", "seq")),
        P(("dp", "seq")),
        P(("dp", "seq")),
        P(("dp", "seq")),
    )
    out_specs = (
        P("dp", "seq", None),
        P("dp", "seq", None),
        P(("dp", "seq"), None),
        P(("dp", "seq"), None),
        P(("dp", "seq"), None),
        P(("dp", "seq"), None),
        P(("dp", "seq")),
        P(("dp", "seq")),
        P(("dp", "seq")),
        P(("dp", "seq")),
    )
    grid = (mesh.shape["dp"], mesh.shape["seq"])
    local = by_heads if grid == (4, HEADS // 2) else by_frames
    return jax.shard_map(local, mesh=mesh, in_specs=in_specs, out_specs=out_specs, check_vma=False)
```

```python
import functools

import jax
import jax.numpy as jnp
from jax import lax
from jax.experimental import pallas as pl
from jax.experimental.pallas import tpu as pltpu

from jax.sharding import PartitionSpec as P

HEADS = 16
HEAD_DIM = 64

norm_eps = 1e-05
masked_score = -1e30
MESH_ID = pl.DeviceIdType.MESH
F32 = jnp.float32
BF16 = jnp.bfloat16
far = 1e33
gather_order = (
    "zh02", "xs", "zh11", "x110", "x210", "x100", "xh2", "zh01", "cc10", "x200", "xh1", "x111",
    "seq", "x102", "x211", "zh03", "x202", "wq", "xp2", "x101", "cc00", "xh3", "wt", "xp1", "p0",
    "x103", "p2", "cc11", "p1", "x203", "zh12", "xp3", "x201", "p3", "vt", "a0", "a1", "zh13",
    "a2", "x112", "cc03", "a3", "a4", "o0", "a5", "a6", "x212", "cc02", "x113", "cc01", "a7", "o1",
    "c0", "x213", "hid", "u0", "cc12", "u1", "cc13", "u2", "u3",
)
scatter_order = (
    "DT0", "c1D0", "DT1", "c1D2", "c1D1", "pkA", "LN", "T0", "T1", "T2", "T3", "LNB", "c2D0",
    "pkN", "UT0", "c1U0", "zfD", "c2D2", "UT1", "ztD", "c2D1", "P0", "c2U0", "A00", "zsD", "A01",
    "c1U1", "zfU", "A02", "A03", "F0", "c2U1", "P1", "gf0", "c1U3", "A10", "A11", "zsU", "A12",
    "c1D3", "A13", "F1", "c1U2", "WG", "gf1", "gs0", "W2", "c2U2", "ztU", "gs1", "W3", "gl0",
    "c2D3", "zlD", "c2U3", "gl1", "zlU",
)
q_block = 256


def place():
    dp, sq = lax.axis_index("dp"), lax.axis_index("seq")
    return dp, sq, dp // 2, dp % 2, sq // 2, sq % 2


def planes(z, nz):
    z1 = z + 1 - 2 * (z % 2)
    return z1, (z + 2) % nz, (z1 + 2) % nz


def dot_nt(a, b):
    return lax.dot_general(a, b, (((1,), (1,)), ((), ())), preferred_element_type=F32)


def dot_nn(a, b):
    return lax.dot_general(a, b, (((1,), (0,)), ((), ())), preferred_element_type=F32)


def runs(order, counted):
    out = []
    for name in order:
        kind = name[:-1]
        if kind in counted:
            number = int(name[-1])
            if out and out[-1][0] == kind and out[-1][2] == number:
                out[-1] = (kind, out[-1][1], number + 1)
            else:
                out.append((kind, number, number + 1))
        else:
            out.append((name, 0, 0))
    return out


class Link:
    def __init__(self, src, dst, landing, sems, index, target, when_send=None, when_recv=None):
        self.sems, self.index, self.target = sems, index, target
        self.src, self.dst, self.landing = src, dst, landing
        self.when_send, self.when_recv = when_send, when_recv

    def copy(self, src, dst):
        send, recv = self.sems
        return pltpu.make_async_remote_copy(
            src_ref=src,
            dst_ref=dst,
            send_sem=send.at[self.index],
            recv_sem=recv.at[self.index],
            device_id=self.target,
            device_id_type=MESH_ID,
        )

    def run(self, when, action):
        if when is None:
            action()
        else:
            pl.when(when)(action)

    def start(self):
        self.run(self.when_send, lambda: self.copy(self.src, self.dst).start())

    def wait(self):
        self.run(self.when_recv, lambda: self.copy(self.landing, self.landing).wait_recv())

    def wait_sent(self):
        self.run(self.when_send, lambda: self.copy(self.src, self.dst).wait_send())


def greet(dp, sq, n_seq, n_dp):
    barrier = pltpu.get_barrier_semaphore()
    for k in range(1, n_seq):
        pl.semaphore_signal(
            barrier, inc=1, device_id=(dp, lax.rem(sq + k, n_seq)), device_id_type=MESH_ID
        )
    for m in range(1, n_dp):
        other = lax.rem(dp + m, n_dp)
        pl.semaphore_signal(barrier, inc=1, device_id=(other, sq), device_id_type=MESH_ID)
    pl.semaphore_wait(barrier, n_seq - 1 + n_dp - 1)


def distance(len_ref, stream, first_key, keys, first_query, queries):
    key_pos = lax.broadcasted_iota(jnp.int32, (keys, 1), 0) + first_key
    query_pos = lax.broadcasted_iota(jnp.int32, (1, queries), 1) + first_query
    key_seg = jnp.zeros((keys, 1), jnp.int32)
    query_seg = jnp.zeros((1, queries), jnp.int32)
    bound = 0
    for k in range(len_ref.shape[1]):
        bound = bound + len_ref[stream, k]
        key_seg = key_seg + (key_pos >= bound).astype(jnp.int32)
        query_seg = query_seg + (query_pos >= bound).astype(jnp.int32)
    gap = jnp.abs(key_pos - query_pos).astype(F32)
    return jnp.where(key_seg == query_seg, gap, far)


def gelu_both(v):
    square = v * v
    th = jnp.tanh(v * (0.7978845608028654 + 0.7978845608028654 * 0.044715 * square))
    half = 0.5 * (1.0 + th)
    bend = v * (0.5 - 0.5 * th * th)
    return v * half, half + bend * (0.7978845608028654 + 0.7978845608028654 * 0.134145 * square)


def norm_parts(v):
    mean = jnp.mean(v, axis=-1, keepdims=True)
    centered = v - mean
    rstd = lax.rsqrt(jnp.mean(centered * centered, axis=-1, keepdims=True) + norm_eps)
    return centered * rstd, rstd


def norm_back(n, rstd, e):
    return rstd * (
        e - jnp.mean(e, axis=-1, keepdims=True) - n * jnp.mean(e * n, axis=-1, keepdims=True)
    )


def own_slopes(sq, n_seq, total):
    out = []
    for h in range(2):
        value = 0.0
        for q in range(n_seq):
            slope = 2.0 ** (-8.0 * (2 * q + h + 1) / (2 * n_seq)) * (256.0 / total)
            value = jnp.where(sq == q, jnp.float32(slope), value)
        out.append(value)
    return out


def gather_kernel(
    x_ref, w_ref, wo_ref, wu_ref, wd_ref, vec_ref, len_ref,
    wo_all, wu_all, wd_all, par_out, attn, qkv_out, ot_out, lse_out, xh_out, wt_out, hid_out, act_out, bend_out,
    xg, xh, wqb, wt, wq_ref, par_ref, pbuf, pown, par, qkv, vt, obuf, ot, lse, dist, wo_v, wu_t, av, hid, low_two, act_v, bend_v,
    z_send, z_recv, w_send, w_recv, x_send, x_recv, s_send, s_recv, tile_sem, store_sem, loc,
):
    dp, sq, y, x, z, c = place()
    streams, tok_rows, width = x_ref.shape
    n_seq, n_dp = lax.axis_size("seq"), lax.axis_size("dp")
    nz = n_seq // 2
    total = n_seq * tok_rows
    own_rows = w_ref.shape[0]
    slopes = own_slopes(sq, n_seq, total)
    x_nbr, y_nbr = (y * 2 + (1 - x), sq), ((1 - y) * 2 + x, sq)
    sibling = (dp, z * 2 + (1 - c))
    z1, z2, z3 = planes(z, nz)
    near_dev, far_dev = (dp, z1 * 2 + c), (dp, z2 * 2 + c)
    rank = dp * n_seq + sq
    row = lax.broadcasted_iota(jnp.int32, (8, 128), 0)
    lane = lax.broadcasted_iota(jnp.int32, (8, 128), 1)
    mine = (row == rank // 4) & ((lane >> 5) == rank % 4)
    vecs = vec_ref[...].astype(F32)
    par_ref[...] = jnp.concatenate(
        [jnp.where(mine, jnp.broadcast_to(vecs[i:i + 1], (8, 128)), 0.0) for i in range(4)], axis=0
    ).astype(BF16)
    for q in range(n_seq):
        for j in range(3):
            wq_ref[q, :, j * 128:(j + 1) * 128] = w_ref[:, j * width + q * 128:j * width + (q + 1) * 128]
    greet(dp, sq, n_seq, n_dp)
    links = []

    def keep(link):
        link.start()
        links.append(link)
        return link

    locals_ = []

    def local(src, dst):
        copy = pltpu.make_async_copy(src, dst, loc.at[len(locals_)])
        copy.start()
        locals_.append(copy)
        return copy

    cp_x = local(x_ref, xg.at[:, sq])
    cp_wq = local(wq_ref.at[sq], wqb.at[pl.ds(pl.multiple_of(sq * 32 + dp * 32 * n_seq, 32), 32), :])
    cp_w = [
        local(src, dst.at[y, x, z, c])
        for src, dst in ((wo_ref, wo_all), (wu_ref, wu_all), (wd_ref, wd_all))
    ]

    arrays = [(wo_ref, wo_all), (wu_ref, wu_all), (wd_ref, wd_all)]
    groups = [(0, 1), (2,)]
    pending = {}
    every = slice(None)

    arrived = set()

    def wait(*key):
        if key not in arrived:
            arrived.add(key)
            for link in pending[key]:
                link.wait()

    where = [z, z1, z2, z3]

    def z_hop(g, h):
        out = []
        for i in groups[g]:
            own, full = arrays[i]
            there = full.at[y, x, z if h < 3 else z2, c]
            land = full.at[y, x, where[h], c]
            src = own if h < 3 else there
            target = far_dev if h == 2 else near_dev
            out.append(keep(Link(src, there, land, (w_send, w_recv), i * 3 + h - 1, target)))
        pending[("z", g, h)] = out

    def plane(tag, g, h, pairs):
        out = []
        for i in groups[g]:
            own, full = arrays[i]
            for kind, target, src_at, land_at, own_half in pairs(where[h]):
                here = full.at[src_at]
                src = own.at[own_half] if own_half is not None and h == 0 else here
                out.append(keep(Link(
                    src, here, full.at[land_at], (x_send, x_recv), (i * 4 + h) * 5 + kind, target
                )))
        pending[(tag, g, h)] = out

    def cross_one(g, h):
        plane("x1", g, h, lambda b: [
            (0, x_nbr, (y, x, b, c, 0), (y, 1 - x, b, c, 0), 0),
            (1, y_nbr, (y, x, b, c, 1), (1 - y, x, b, c, 1), 1),
        ])

    def cross_two(g, h):
        wait("x1", g, h)
        plane("x2", g, h, lambda b: [
            (2, y_nbr, (y, every, b, c, 0), (1 - y, every, b, c, 0), None),
            (3, x_nbr, (every, x, b, c, 1), (every, 1 - x, b, c, 1), None),
        ])

    def cross_core(g, h):
        wait("x2", g, h)
        plane("c", g, h, lambda b: [
            (4, sibling, (every, every, b, c), (every, every, b, 1 - c), None),
        ])

    def x_hop(h):
        there = xg.at[:, (z if h < 3 else z2) * 2 + c]
        land = xg.at[:, where[h] * 2 + c]
        target = far_dev if h == 2 else near_dev
        pending[("x", h)] = [keep(Link(x_ref if h < 3 else there, there, land, (z_send, z_recv), h - 1, target))]

    def x_pass(h):
        src = xg.at[:, where[h] * 2 + c]
        land = xg.at[:, where[h] * 2 + (1 - c)]
        pending[("xc", h)] = [keep(Link(src, src, land, (z_send, z_recv), 3 + h - 1, sibling))]

    rows_dp = 32 * n_seq

    def shard_rows(d, q):
        return wqb.at[pl.ds(pl.multiple_of((d * n_seq + q) * 32, 32), 32), :]

    def plane_rows(d):
        return wqb.at[pl.ds(pl.multiple_of(d * rows_dp, 32), rows_dp), :]

    def along_seq():
        small, wide = [], []
        for k in range(1, n_seq):
            other = lax.rem(sq + k, n_seq)
            source = lax.rem(sq + n_seq - k, n_seq)
            slot = pbuf.at[k - 1]
            small.append(keep(Link(par_ref, slot, slot, (s_send, s_recv), k - 1, (dp, other))))
            wide.append(keep(Link(
                wq_ref.at[other], shard_rows(dp, sq), shard_rows(dp, source), (s_send, s_recv), 7 + k - 1, (dp, other)
            )))
        pending["ps",], pending["ws",] = small, wide

    def along_dp():
        wait("ps")
        pown[...] = par_ref[...] + pbuf[0]
        for k in range(1, n_seq - 1):
            pown[...] += pbuf[k]
        pending["pd",] = []
        for m in range(1, n_dp):
            slot = pbuf.at[n_seq - 2 + m]
            pending["pd",].append(
                keep(Link(pown, slot, slot, (s_send, s_recv), 14 + m - 1, (lax.rem(dp + m, n_dp), sq)))
            )
        wait("ws")
        cp_wq.wait()
        pending["wd",] = []
        for m in range(1, n_dp):
            other, source = lax.rem(dp + m, n_dp), lax.rem(dp + n_dp - m, n_dp)
            pending["wd",].append(keep(Link(
                plane_rows(dp), plane_rows(dp), plane_rows(source), (s_send, s_recv), 17 + m - 1, (other, sq)
            )))

    step = 256
    rows_of = {}

    def columns():
        wait("pd")
        par[...] = pown[...] + pbuf[n_seq - 1] + pbuf[n_seq] + pbuf[n_seq + 1]
        wait("wd")
        for r in range(width // step):
            wt[:, r * step:(r + 1) * step] = jnp.transpose(
                wqb[r * step:(r + 1) * step, :].astype(F32)
            ).astype(BF16)
        local(wt, wt_out)
        local(par, par_out)

    def vector(row):
        block = par[row * 8:(row + 1) * 8, :].astype(F32)
        return jnp.concatenate([block[r:r + 1, :] for r in range(8)], axis=1)

    scale = 0.125

    def process(s):
        gain, shift = vector(0), vector(1)

        def one(b, carry):
            v = xg[b, s].astype(F32)
            mean = jnp.mean(v, axis=1, keepdims=True)
            v = v - mean
            spread = jnp.mean(v * v, axis=1, keepdims=True)
            n = v * lax.rsqrt(spread + 1e-5)
            xh[b, s] = n.astype(BF16)
            normed = (n * gain + shift).astype(BF16)
            packed = dot_nt(normed, wt[...])
            row = pl.ds(pl.multiple_of(s * tok_rows, tok_rows), tok_rows)
            qkv[b, row, 0:128] = (packed[:, 0:128] * scale).astype(BF16)
            qkv[b, row, 128:384] = packed[:, 128:384].astype(BF16)
            return carry
        lax.fori_loop(0, streams, one, 0)

    def process_hop(h):
        def one(j, carry):
            process(where[h] * 2 + j)
            return carry
        lax.fori_loop(0, 2, one, 0)

    def turn(j, carry):
        b, r = j // (total // step), j % (total // step)
        row = pl.ds(pl.multiple_of(r * step, step), step)
        vt[b, :, row] = jnp.transpose(qkv[b, row, 256:384].astype(F32)).astype(BF16)
        return carry
    def values():
        local(xh, xh_out)
        local(qkv, qkv_out)
        lax.fori_loop(0, streams * (total // step), turn, 0)

    blocks = total // q_block
    cols = bend_v.shape[2]
    tiles = bend_v.shape[0]

    def tile_copies(i):
        cut = pl.ds(pl.multiple_of(i * cols, cols), cols)
        return [
            pltpu.make_async_copy(
                wu_all.at[part // 2, part % 2, :, :, :, :, cut], wu_t.at[i, part // 2, part % 2], tile_sem.at[i, part]
            )
            for part in range(4)
        ]

    def tile_stores(i):
        return (
            pltpu.make_async_copy(act_v.at[pl.ds(i * 2, 2)], act_out.at[pl.ds(i * 2, 2)], store_sem.at[i, 0]),
            pltpu.make_async_copy(bend_v.at[i], bend_out.at[i], store_sem.at[i, 1]),
        )


    def attend(j, carry):
        b, qb = j // blocks, j % blocks
        row = pl.ds(pl.multiple_of(qb * q_block, q_block), q_block)
        dist[...] = distance(len_ref, b, 0, total, qb * q_block, q_block)
        queries = qkv[b, row, 0:128]
        lane = lax.broadcasted_iota(jnp.int32, (q_block, 128), 1)
        for h in range(2):
            own = jnp.where((lane < 64) == (h == 0), queries, jnp.zeros_like(queries))
            s = dot_nt(qkv[b, :, 128:256], own) - slopes[h] * dist[...]
            top = jnp.max(s, axis=0, keepdims=True)
            p = jnp.exp(s - top)
            weight = jnp.sum(p, axis=0, keepdims=True)
            o = dot_nn(vt[b, h * 64:(h + 1) * 64, :], p.astype(BF16))
            ot[b, h * 64:(h + 1) * 64, row] = o / weight
            lse[b, h:h + 1, row] = top + jnp.log(weight)
        obuf[b, row, :] = jnp.transpose(ot[b, :, row]).astype(BF16)
        return carry

    def send_rows(b):
        out = []
        for k in range(1, n_seq):
            other = lax.rem(sq + k, n_seq)
            source = lax.rem(sq + n_seq - k, n_seq)
            src = obuf.at[b, pl.ds(pl.multiple_of(other * tok_rows, tok_rows), tok_rows), :]
            dst = attn.at[b, :, pl.ds(pl.multiple_of(sq * 128, 128), 128)]
            land = attn.at[b, :, pl.ds(pl.multiple_of(source * 128, 128), 128)]
            out.append(keep(Link(src, dst, land, (s_send, s_recv), 20 + b * 7 + k - 1, (dp, other))))
        pending[("o", b)] = out
        own_rows.append(local(
            obuf.at[b, pl.ds(pl.multiple_of(sq * tok_rows, tok_rows), tok_rows), :],
            attn.at[b, :, pl.ds(pl.multiple_of(sq * 128, 128), 128)],
        ))

    own_rows = []

    def attend_some(first, last):
        lax.fori_loop(first, last, attend, 0)

    tokens = streams * tok_rows
    late = []

    def residual():
        wait("o", 0)
        wait("o", 1)
        for copy in own_rows:
            copy.wait()
        load_attn = local(attn, av)
        late.append(load_attn)
        load_attn.wait()
        late[0].wait()
        out_w = wo_v[...].reshape(width, width)
        for r in range(0, width, 512):
            hid[:, r:r + 512] = x_ref[...].reshape(tokens, width)[:, r:r + 512].astype(F32) + dot_nn(
                av[...].reshape(tokens, width), out_w[:, r:r + 512]
            )
        local(hid, hid_out)
        gain_two, shift_two = vector(2), vector(3)
        for r in range(0, tokens, 128):
            n, _ = norm_parts(hid[r:r + 128])
            low_two[r:r + 128] = (n * gain_two + shift_two).astype(BF16)

    def one_tile(i, carry):
        for copy in tile_copies(i):
            copy.wait()
        act_f, bend = gelu_both(dot_nn(low_two[...], wu_t[i].reshape(width, cols)))
        act = act_f.astype(BF16)
        for j in range(4):
            act_v[i * 2 + j // 2, j % 2] = act[:, j * 128:(j + 1) * 128]
        bend_v[i] = bend.astype(BF16)
        for copy in tile_stores(i):
            copy.start()
        return carry

    def some_tiles(first, last):
        lax.fori_loop(first * tiles // 4, last * tiles // 4, one_tile, 0)

    def first_group():
        for h in range(4):
            wait("c", 0, h)
        late.append(local(wo_all, wo_v))

        def load(i, carry):
            for copy in tile_copies(i):
                copy.start()
            return carry
        lax.fori_loop(0, tiles, load, 0)

    def x_arrived(h):
        wait("x", h)
        x_pass(h)

    def own_x():
        pending["xc", 0] = [
            keep(Link(x_ref, xg.at[:, sq], xg.at[:, z * 2 + (1 - c)], (z_send, z_recv), 6, sibling))
        ]

    def block_done(h):
        if h == 0:
            cp_x.wait()
        wait("xc", h)
        process_hop(h)

    def hop_x(h):
        if h == 3:
            wait("x", 2)
        x_hop(h)

    def hop(g, h):
        if h == 3:
            wait("z", g, 2)
        z_hop(g, h)

    def cross_begin(g, h):
        if h > 0:
            wait("z", g, h)
        cross_one(g, h)

    def cross_next(g, h):
        if h == 0:
            for i in groups[g]:
                cp_w[i].wait()
        cross_two(g, h)

    def stream_out(b):
        send_rows(b)
        if b == 1:
            local(ot, ot_out)
            local(lse, lse_out)

    steps = {
        "seq": along_seq, "wq": along_dp, "wt": columns, "xs": own_x, "vt": values,
        "c0": first_group, "hid": residual,
    }
    for h in range(4):
        steps["p%d" % h] = functools.partial(block_done, h)
        for g in range(2):
            steps["x1%d%d" % (g, h)] = functools.partial(cross_begin, g, h)
            steps["x2%d%d" % (g, h)] = functools.partial(cross_next, g, h)
            steps["cc%d%d" % (g, h)] = functools.partial(cross_core, g, h)
            if h > 0:
                steps["zh%d%d" % (g, h)] = functools.partial(hop, g, h)
        if h > 0:
            steps["xh%d" % h] = functools.partial(hop_x, h)
            steps["xp%d" % h] = functools.partial(x_arrived, h)
    for b in range(streams):
        steps["o%d" % b] = functools.partial(stream_out, b)
    for name, first, last in runs(gather_order, ("a", "u")):
        if name == "a":
            attend_some(first, last)
        elif name == "u":
            some_tiles(first, last)
        else:
            steps[name]()

    def stored(i, carry):
        for copy in tile_stores(i):
            copy.wait()
        return carry
    lax.fori_loop(0, tiles, stored, 0)
    for key in pending:
        wait(*key)
    waited = [cp_x, cp_wq, *cp_w, *own_rows, *late]
    for copy in locals_:
        if not any(copy is other for other in waited):
            copy.wait()
    for link in links:
        link.wait_sent()


def gather_call(inputs, w_qkv, w_out, w_up, w_down, vectors, lengths):
    streams, tok_rows, width = inputs.shape
    n_seq, n_dp = lax.axis_size("seq"), lax.axis_size("dp")
    nz, total = n_seq // 2, n_seq * tok_rows
    any_space = pl.BlockSpec(memory_space=pl.ANY)
    vmem = pl.BlockSpec(memory_space=pltpu.VMEM)
    smem = pl.BlockSpec(memory_space=pltpu.SMEM)

    def halves(w):
        return w.reshape(2, w.shape[0] // 2, w.shape[1])

    own = [halves(w) for w in (w_out, w_up, w_down)]
    full = [jax.ShapeDtypeStruct((2, n_dp // 2, nz, 2) + w.shape, BF16) for w in own]
    cols = w_qkv.shape[1] // n_seq
    outs = full + [
        jax.ShapeDtypeStruct((32, 128), BF16),
        jax.ShapeDtypeStruct((streams, tok_rows, width), BF16),
        jax.ShapeDtypeStruct((streams, total, cols), BF16),
        jax.ShapeDtypeStruct((streams, 128, total), F32),
        jax.ShapeDtypeStruct((streams, 8, total), F32),
        jax.ShapeDtypeStruct((streams, n_seq, tok_rows, width), BF16),
        jax.ShapeDtypeStruct((cols, width), BF16),
        jax.ShapeDtypeStruct((streams * tok_rows, width), F32),
        jax.ShapeDtypeStruct((n_dp * nz, 2, streams * tok_rows, 128), BF16),
        jax.ShapeDtypeStruct((8, streams * tok_rows, w_up.shape[1] // 8), BF16),
    ]
    dma = pltpu.SemaphoreType.DMA
    scratch = [
        pltpu.VMEM((streams, n_seq, tok_rows, width), BF16),
        pltpu.VMEM((streams, n_seq, tok_rows, width), BF16),
        pltpu.VMEM((width, cols), BF16),
        pltpu.VMEM((cols, width), BF16),
        pltpu.VMEM((n_seq, w_qkv.shape[0], cols), BF16),
        pltpu.VMEM((32, 128), BF16),
        pltpu.VMEM((n_seq - 1 + n_dp - 1, 32, 128), BF16),
        pltpu.VMEM((32, 128), BF16),
        pltpu.VMEM((32, 128), BF16),
        pltpu.VMEM((streams, total, cols), BF16),
        pltpu.VMEM((streams, 128, total), BF16),
        pltpu.VMEM((streams, total, 128), BF16),
        pltpu.VMEM((streams, 128, total), F32),
        pltpu.VMEM((streams, 8, total), F32),
        pltpu.VMEM((total, q_block), F32),
        pltpu.VMEM(full[0].shape, BF16),
        pltpu.VMEM((8,) + full[1].shape[:-1] + (w_up.shape[1] // 8,), BF16),
        pltpu.VMEM((streams, tok_rows, width), BF16),
        pltpu.VMEM((streams * tok_rows, width), F32),
        pltpu.VMEM((streams * tok_rows, width), BF16),
        pltpu.VMEM(outs[11].shape, BF16),
        pltpu.VMEM(outs[12].shape, BF16),
        dma((7,)), dma((7,)), dma((9,)), dma((9,)), dma((60,)), dma((60,)), dma((34,)), dma((34,)),
        dma((8, 4)), dma((8, 2)), dma((20,)),
    ]
    return pl.pallas_call(
        gather_kernel,
        out_shape=outs,
        in_specs=[vmem] * 6 + [smem],
        out_specs=[any_space] * len(outs),
        scratch_shapes=scratch,
        compiler_params=pltpu.CompilerParams(
            collective_id=0, has_side_effects=True, vmem_limit_bytes=56 * 2**20
        ),
        name="gather_attend",
    )(inputs, w_qkv, *own, vectors, lengths)


def scatter_kernel(
    x_ref, fill_ref, par_ref, cot_ref, attn_ref, hid_ref, act_ref, bend_ref, wo_ref, wu_ref, wd_ref,
    qkv_ref, ot_ref, lse_ref, xh_ref, wt_ref, len_ref,
    y_out, gx_out, go_out, gu_out, gd_out, gq_out, pg_out,
    hidden, n_two, r_two, low_two, grad_two, yb, gout2, gb2, act_v, act_s, bend_t, n2s2, n2o, at2, ato, wo_v, wu_t, wd_t, gab,
    acc_o, acc_u, acc_d, ra_o, ra_u, ra_d, rb_o, rb_u, rb_d, sa_o, sa_u, sa_d, sb_o, sb_u, sb_d,
    zr_o, zr_u, zr_d, fin_o, fin_u, fin_d,
    do, qkv, ot, lse, xh, wt, kt, delta, dk, dv, dqt, dqkv, dqkvt,
    gp, dqr, dqsum, pgp, pr1, psum, pr2, pgo,
    c_send, c_recv, o_send, o_recv, x_send, x_recv, zw_send, zw_recv, zg_send, zg_recv, s_send, s_recv,
    tile_sem, loc,
):
    dp, sq, y, x, z, c = place()
    streams, tok_rows, width = gab.shape
    tokens = streams * tok_rows
    slopes = own_slopes(lax.axis_index("seq"), lax.axis_size("seq"), qkv.shape[1])
    n_seq, n_dp = lax.axis_size("seq"), lax.axis_size("dp")
    nz = n_seq // 2
    total = n_seq * tok_rows
    x_nbr, y_nbr = (y * 2 + (1 - x), sq), ((1 - y) * 2 + x, sq)
    sibling = (dp, z * 2 + (1 - c))
    z1, z2, z3 = planes(z, nz)
    near_dev, far_dev = (dp, z1 * 2 + c), (dp, z2 * 2 + c)
    greet(dp, sq, n_seq, n_dp)
    links, locals_ = [], []
    every = slice(None)

    def keep(link):
        link.start()
        links.append(link)
        return link

    def local(src, dst):
        copy = pltpu.make_async_copy(src, dst, loc.at[len(locals_)])
        copy.start()
        locals_.append(copy)
        return copy

    def loop(n, body):
        def step(j, carry):
            body(j)
            return carry
        lax.fori_loop(0, n, step, 0)

    pending = {}

    arrived = set()

    def wait(*key):
        if key not in arrived:
            arrived.add(key)
            for link in pending[key]:
                link.wait()

    def f32(v):
        return v.astype(F32)

    def vector(row):
        block = f32(par_ref[row * 8:(row + 1) * 8, :])
        return jnp.concatenate([block[r:r + 1, :] for r in range(8)], axis=1)

    def to_sibling(src, dst, index):
        return keep(Link(src, dst, dst, (c_send, c_recv), index, sibling))

    cols = wu_t.shape[2]
    tiles = wu_ref.shape[1] // cols

    def tile_copies(i):
        slot, first = i % 2, pl.multiple_of(i * cols, cols)
        out = [pltpu.make_async_copy(bend_ref.at[i], bend_t.at[slot], tile_sem.at[8, slot])]
        for part in range(4):
            rows = slice(part * 256, (part + 1) * 256)
            out.append(pltpu.make_async_copy(
                wu_ref.at[rows, pl.ds(first, cols)], wu_t.at[slot, rows], tile_sem.at[part, slot]
            ))
            out.append(pltpu.make_async_copy(
                wd_ref.at[i * 4 + part], wd_t.at[slot, part], tile_sem.at[4 + part, slot]
            ))
        return out

    load_cot, load_act = local(cot_ref, gab), local(act_ref, act_v)
    act_link = to_sibling(act_ref.at[:, 1 - c], act_s, 1)
    load_hid = local(hid_ref, hidden)
    for copy in tile_copies(0):
        copy.start()
    load_attn, load_out = local(attn_ref, low_two), local(wo_ref, wo_v)
    copies = [local(qkv_ref, qkv), local(ot_ref, ot), local(lse_ref, lse), local(wt_ref, wt)]
    copy_xh = [local(xh_ref.at[:, :, 0:cols], xh)]
    load_cot.wait()
    for b in range(streams):
        rows = slice(b * tok_rows, (b + 1) * tok_rows)
        fill = jnp.broadcast_to(f32(fill_ref[b:b + 1, :]), (128, tok_rows))
        gout2[rows] = (f32(gab[b]) * jnp.transpose(fill)[:, 0:1]).astype(BF16)
    gout_link = to_sibling(gout2.at[0:tokens], gout2.at[tokens:2 * tokens], 0)

    def chosen(parity):
        j = lax.broadcasted_iota(jnp.int32, (1, width // 2), 1)
        column = ((((j & 127) >> 5) * n_seq + (j >> 7) * 2 + parity) << 5) + (j & 31)
        return (lax.broadcasted_iota(jnp.int32, (width, 1), 0) == column).astype(F32).astype(BF16)

    def pick(v, mine, theirs, index):
        here, there = dot_nn(v, chosen(c)).astype(BF16), dot_nn(v, chosen(1 - c)).astype(BF16)
        for b in range(nz):
            mine[b, 0:tokens] = here[:, b * 128:(b + 1) * 128]
            theirs[b] = there[:, b * 128:(b + 1) * 128]
        return to_sibling(theirs, mine.at[:, tokens:2 * tokens], index)

    gain_two, shift_two = vector(2), vector(3)

    def tile_grad(i):
        cut = pl.ds(pl.multiple_of(i % 2 * cols, cols), cols)
        return gp.at[i // 4, i // 2 % 2 * 2, :, :, cut], gp.at[i // 4, i // 2 % 2 * 2 + 1, :, :, cut]

    def tile_link(i):
        src, dst = tile_grad(i)
        return Link(src, dst, dst, (c_send, c_recv), 4 + i, sibling)

    def one_tile(i, carry):
        slot = i % 2
        for copy in tile_copies(i):
            copy.wait()

        @pl.when(i + 1 < tiles)
        def _():
            for copy in tile_copies(i + 1):
                copy.start()
        down = wd_t[slot].reshape(cols, width)
        act = jnp.concatenate([act_v[i * 2 + j // 2, j % 2] for j in range(4)], axis=1)
        hidden[...] += dot_nn(act, down)
        grad_up = (dot_nt(gout2[0:tokens], down) * f32(bend_t[slot])).astype(BF16)
        tile_grad(i)[0][...] = grad_up.reshape(streams, tok_rows, cols)
        grad_two[...] += dot_nt(grad_up, wu_t[slot])
        tile_link(i).start()
        return carry

    arrays = [
        (acc_o, ra_o, rb_o, sa_o, sb_o, zr_o, fin_o, go_out),
        (acc_u, ra_u, rb_u, sa_u, sb_u, zr_u, fin_u, gu_out),
        (acc_d, ra_d, rb_d, sa_d, sb_d, zr_d, fin_d, gd_out),
    ]
    groups = [(1, 0), (2,)]
    U, D = 0, 1
    near = 1 - z // 2
    plane_of = [z3, z2, z1, z]

    def cross_one(g, p):
        t = plane_of[p]
        out = []
        for i in groups[g]:
            acc, ra, rb = arrays[i][:3]
            out.append(keep(Link(acc.at[1 - y, :, t, 0], ra.at[p], ra.at[p], (x_send, x_recv), (i * 4 + p) * 4, y_nbr)))
            out.append(keep(Link(acc.at[:, 1 - x, t, 1], rb.at[p], rb.at[p], (x_send, x_recv), (i * 4 + p) * 4 + 1, x_nbr)))
        pending[("x1", g, p)] = out

    def cross_two(g, p):
        t = plane_of[p]
        wait("x1", g, p)
        out = []
        for i in groups[g]:
            acc, ra, rb, sa, sb = arrays[i][:5]
            acc[y, 1 - x, t, 0] = (f32(acc[y, 1 - x, t, 0]) + f32(ra[p, 1 - x])).astype(BF16)
            acc[1 - y, x, t, 1] = (f32(acc[1 - y, x, t, 1]) + f32(rb[p, 1 - y])).astype(BF16)
            out.append(keep(Link(acc.at[y, 1 - x, t, 0], sa.at[p], sa.at[p], (x_send, x_recv), (i * 4 + p) * 4 + 2, x_nbr)))
            out.append(keep(Link(acc.at[1 - y, x, t, 1], sb.at[p], sb.at[p], (x_send, x_recv), (i * 4 + p) * 4 + 3, y_nbr)))
        pending[("x2", g, p)] = out

    def cross_three(g, p):
        t = plane_of[p]
        wait("x2", g, p)
        for i in groups[g]:
            acc, ra, rb, sa, sb = arrays[i][:5]
            acc[y, x, t, 0] = (f32(acc[y, x, t, 0]) + f32(ra[p, x]) + f32(sa[p])).astype(BF16)
            acc[y, x, t, 1] = (f32(acc[y, x, t, 1]) + f32(rb[p, y]) + f32(sb[p])).astype(BF16)

    def z_one(g, step, target):
        pending[("z", g, step)] = [
            keep(Link(
                arrays[i][0].at[y, x, plane_of[step]], arrays[i][5].at[step], arrays[i][5].at[step],
                (zw_send, zw_recv), i * 3 + step, target,
            ))
            for i in groups[g]
        ]

    def z_first(g):
        cross_three(g, 0)
        z_one(g, 0, near_dev)

    def z_second(g):
        cross_three(g, 1)
        wait("z", g, 0)
        for i in groups[g]:
            acc, zr = arrays[i][0], arrays[i][5]
            for h in range(2):
                acc[y, x, z2, h] = (f32(acc[y, x, z2, h]) + f32(zr[0, h])).astype(BF16)
        z_one(g, 1, far_dev)

    def z_third(g):
        cross_three(g, 2)
        z_one(g, 2, near_dev)

    def z_last(g):
        cross_three(g, 3)
        wait("z", g, 1)
        wait("z", g, 2)
        for i in groups[g]:
            acc, zr, fin, out = arrays[i][0], *arrays[i][5:]
            fin[...] = f32(acc[y, x, z]) + f32(zr[1]) + f32(zr[2])
            local(fin, out)

    def dot_tn(a, b):
        return lax.dot_general(a, b, (((0,), (0,)), ((), ())), preferred_element_type=F32)

    def down_terms(pair):
        def one(d):
            first = d * 4 + pair * 2
            left = jnp.concatenate([
                jnp.concatenate([act_v[first, c], act_v[first + 1, c]], axis=1),
                jnp.concatenate([act_s[first], act_s[first + 1]], axis=1),
            ], axis=0)
            rows = acc_d.shape[4]
            for r in range(0, width, 512):
                terms = dot_tn(left, gout2[:, r:r + 512]).astype(BF16)
                for j in range(4):
                    acc_d[d // 2, d % 2, pair * 2 + j // 2, j % 2, :, r:r + 512] = terms[j * rows:(j + 1) * rows]
        loop(n_dp, one)

    def narrow_terms(source, pair, acc, right, where):
        left = jnp.concatenate([source[pair * 2], source[pair * 2 + 1]], axis=1)
        terms = dot_tn(left, right).astype(BF16)
        for j in range(16):
            d = j % 8 // 2
            acc[d // 2, d % 2, pair * 2 + j // 8, j % 2, :, where] = terms[j * 16:(j + 1) * 16]

    def up_terms(pair):
        def one(i):
            d, part = i // 2, i % 2
            cut = pl.ds(pl.multiple_of(part * cols, cols), cols)
            right = gp[d // 2, pl.ds(d % 2 * 2, 2), :, :, cut].reshape(2 * tokens, cols)
            where = pl.ds(pl.multiple_of(i * cols, cols), cols)
            narrow_terms(n2s2, pair, acc_u, right, where)
        loop(tiles, one)
        for r in range(0, width, 512):
            narrow_terms(at2, pair, acc_o, gb2[:, r:r + 512], slice(r, r + 512))

    def down_first():
        for copy in (load_act, load_hid, load_attn):
            copy.wait()
        gout_link.wait()
        act_link.wait()
        down_terms(near)

    def pick_attn():
        pending["attn",] = [pick(low_two[...], at2, ato, 2)]

    def pick_norm():
        pending["norm",] = [pick(low_two[...], n2s2, n2o, 3)]

    def second_norm():
        for r in range(0, tokens, 128):
            n, rstd = norm_parts(hidden[r:r + 128])
            n_two[r:r + 128] = n
            r_two[r:r + 128] = jnp.broadcast_to(rstd, (128, 128))
            low_two[r:r + 128] = (n * gain_two + shift_two).astype(BF16)
        grad_two[...] = jnp.zeros_like(grad_two)

    def some_tiles(first, last):
        lax.fori_loop(first * tiles // 4, last * tiles // 4, one_tile, 0)

    grad_links, own_do = [], []

    def branch():
        yb[...] = hidden[...].astype(BF16)
        local(yb, y_out)
        for r in range(0, tokens, 128):
            rows = slice(r, r + 128)
            back = norm_back(n_two[rows], r_two[rows, 0:1], grad_two[rows] * gain_two)
            grad = f32(gout2[rows]) + back
            hidden[rows] = grad
            gb2[rows] = grad.astype(BF16)
        load_out.wait()
        pending["branch",] = [to_sibling(gb2.at[0:tokens], gb2.at[tokens:2 * tokens], 12)]
        for r in range(0, width, 512):
            grad = dot_nt(gb2[0:tokens], wo_v[r // 128:r // 128 + 4].reshape(512, width)).astype(BF16)
            gab[:, :, r:r + 512] = grad.reshape(streams, tok_rows, 512)
        for b in range(streams):
            out = []
            for k in range(1, n_seq):
                other = lax.rem(sq + k, n_seq)
                source = lax.rem(sq + n_seq - k, n_seq)
                src = gab.at[b, :, pl.ds(pl.multiple_of(other * 128, 128), 128)]
                dst = do.at[b, pl.ds(pl.multiple_of(sq * tok_rows, tok_rows), tok_rows), :]
                land = do.at[b, pl.ds(pl.multiple_of(source * tok_rows, tok_rows), tok_rows), :]
                out.append(keep(Link(src, dst, land, (o_send, o_recv), b * 7 + k - 1, (dp, other))))
            grad_links.append(out)
        copy_xh.append(local(xh_ref.at[:, :, cols:width], wu_t))
        own_do.extend(
            local(
                gab.at[b, :, pl.ds(pl.multiple_of(sq * 128, 128), 128)],
                do.at[b, pl.ds(pl.multiple_of(sq * tok_rows, tok_rows), tok_rows), :],
            )
            for b in range(streams)
        )
        pgp[...] = jnp.zeros_like(pgp)
        pgp[2:3, :] = jnp.sum(grad_two[...] * n_two[...], axis=0, keepdims=True)
        pgp[3:4, :] = jnp.sum(grad_two[...], axis=0, keepdims=True)

    def up_first():
        for key in ("attn", "norm", "branch"):
            wait(key)

        def wait_tile(i):
            tile_link(i).wait()
        loop(tiles, wait_tile)
        up_terms(near)

    step = 256
    blocks = total // q_block

    def turn(j):
        b, r = j // (total // step), j % (total // step)
        row = pl.ds(pl.multiple_of(r * step, step), step)
        kt[b, :, row] = jnp.transpose(f32(qkv[b, row, 128:256])).astype(BF16)
    def keys_turned():
        for copy in copies:
            copy.wait()
        loop(streams * (total // step), turn)


    def prepare(b):
        own_do[b].wait()
        for link in grad_links[b]:
            link.wait()

        def one(r):
            row = pl.ds(pl.multiple_of(r * step, step), step)
            both = jnp.transpose(f32(do[b, row, :])) * ot[b, :, row]
            for h in range(2):
                delta[h:h + 1, row] = jnp.sum(both[h * 64:(h + 1) * 64], axis=0, keepdims=True)
        loop(total // step, one)
        dk[...] = jnp.zeros_like(dk)
        dv[...] = jnp.zeros_like(dv)

    tile = 256

    def attend(b, qb):
        row = pl.ds(pl.multiple_of(qb * q_block, q_block), q_block)
        lane = lax.broadcasted_iota(jnp.int32, (q_block, 128), 1)
        queries, grads = qkv[b, row, 0:128], do[b, row, :]
        none = jnp.zeros_like(queries)
        own = [jnp.where((lane < 64) == (h == 0), queries, none) for h in range(2)]
        own_grad = [jnp.where((lane < 64) == (h == 0), grads, none) for h in range(2)]
        part = [jnp.zeros((64, q_block), F32)] * 2
        for r in range(total // tile):
            keys = slice(r * tile, (r + 1) * tile)
            gap = distance(len_ref, b, r * tile, tile, qb * q_block, q_block)
            grad_v = grad_k = 0
            for h in range(2):
                s = dot_nt(qkv[b, keys, 128:256], own[h]) - slopes[h] * gap
                p = jnp.exp(s - lse[b, h:h + 1, row])
                gp_t = dot_nt(qkv[b, keys, 256:384], own_grad[h])
                ds = (p * (gp_t - delta[h:h + 1, row])).astype(BF16)
                grad_v = grad_v + dot_nn(p.astype(BF16), own_grad[h])
                grad_k = grad_k + dot_nn(ds, own[h])
                part[h] = part[h] + dot_nn(kt[b, h * 64:(h + 1) * 64, keys], ds)
            dv[keys, :] += grad_v
            dk[keys, :] += grad_k
        for h in range(2):
            dqt[h * 64:(h + 1) * 64, row] = part[h] * 0.125

    def attend_some(b, first, last):
        def one(qb, carry):
            attend(b, qb)
            return carry
        lax.fori_loop(first, last, one, 0)

    def gs(b):
        return wo_v.at[b * nz:(b + 1) * nz]

    def gz(b, step):
        return wd_t.at[b, step]

    def finish_stream(b):
        def one(r):
            row = pl.ds(pl.multiple_of(r * step, step), step)
            low = dqt[:, row].astype(BF16)
            dqkvt[b, 0:128, row] = low
            dqkv[row, 0:128] = jnp.transpose(f32(low)).astype(BF16)
            for first, grad in ((128, dk), (256, dv)):
                low = grad[row, :].astype(BF16)
                dqkv[row, first:first + 128] = low
                dqkvt[b, first:first + 128, row] = jnp.transpose(f32(low)).astype(BF16)
        loop(total // step, one)

        def product(s):
            row = pl.ds(pl.multiple_of(s * tok_rows, tok_rows), tok_rows)
            gp[b, s // 2, s % 2] = dot_nn(dqkv[row, :], wt[...]).astype(BF16)
        loop(n_seq, product)
        pending[("gc", b)] = [
            keep(Link(gp.at[b, :, 1 - c], gs(b), gs(b), (zg_send, zg_recv), b * 4, sibling))
        ]

    def g_one(b, step, target):
        pending[("g", b, step)] = [
            keep(Link(gp.at[b, plane_of[step], c], gz(b, step), gz(b, step), (zg_send, zg_recv), b * 4 + 1 + step, target))
        ]

    def g_first(b):
        wait("gc", b)

        def add(j):
            gp[b, j, c] = (f32(gp[b, j, c]) + f32(wo_v[b * nz + j])).astype(BF16)
        loop(nz, add)
        g_one(b, 0, near_dev)
        g_one(b, 2, near_dev)

    def g_second(b):
        wait("g", b, 0)
        gp[b, z2, c] = (f32(gp[b, z2, c]) + f32(gz(b, 0)[...])).astype(BF16)
        g_one(b, 1, far_dev)

    def g_last(b):
        wait("g", b, 1)
        wait("g", b, 2)
        own = f32(gp[b, z, c]) + f32(gz(b, 1)[...]) + f32(gz(b, 2)[...])
        rows = slice(b * tok_rows, (b + 1) * tok_rows)
        n, rstd = norm_parts(f32(x_ref[rows]))
        low_two[rows] = (hidden[rows] + norm_back(n, rstd, own * vector(0))).astype(BF16)
        local(low_two.at[rows], gx_out.at[b])

    rows_dp = 32 * n_seq

    def weight_grad():
        for copy in copy_xh:
            copy.wait()
        sums = jnp.sum(f32(dqkvt[0]), axis=1, keepdims=True)
        for b in range(1, streams):
            sums = sums + jnp.sum(f32(dqkvt[b]), axis=1, keepdims=True)
        gain, shift = vector(0), vector(1)
        for r in range(width // step):
            cols = slice(r * step, (r + 1) * step)
            weight = f32(wt[:, cols])
            n = xh if r < 2 else wu_t
            there = slice(r % 2 * step, (r % 2 + 1) * step)
            raw = dot_nn(dqkvt[0], n[0, :, there])
            for b in range(1, streams):
                raw = raw + dot_nn(dqkvt[b], n[b, :, there])
            pgp[0:1, cols] = jnp.sum(raw * weight, axis=0, keepdims=True)
            pgp[1:2, cols] = jnp.sum(sums * weight, axis=0, keepdims=True)
            grad = raw * gain[:, cols] + sums * shift[:, cols]
            dqkv[cols, :] = jnp.transpose(grad).astype(BF16)
        out = []
        for m in range(1, n_dp):
            other = lax.rem(dp + m, n_dp)
            src = dqkv.at[pl.ds(pl.multiple_of(other * rows_dp, rows_dp), rows_dp), :]
            out.append(keep(Link(src, dqr.at[m - 1], dqr.at[m - 1], (s_send, s_recv), m - 1, (other, sq))))
            src = pgp.at[:, pl.ds(pl.multiple_of(other * rows_dp, rows_dp), rows_dp)]
            out.append(keep(Link(src, pr1.at[m - 1], pr1.at[m - 1], (s_send, s_recv), 3 + m - 1, (other, sq))))
        pending["qd",] = out

    def weight_grad_two():
        wait("qd")
        mine = pl.ds(pl.multiple_of(dp * rows_dp, rows_dp), rows_dp)
        part = f32(dqkv[mine, :])
        small = pgp[:, mine]
        for m in range(n_dp - 1):
            part = part + f32(dqr[m])
            small = small + pr1[m]
        dqsum[...] = part.astype(BF16)
        psum[...] = small
        out = []
        for k in range(1, n_seq):
            other = lax.rem(sq + k, n_seq)
            source = lax.rem(sq + n_seq - k, n_seq)
            src = dqsum.at[pl.ds(pl.multiple_of(other * 32, 32), 32), :]
            out.append(keep(Link(src, gq_out.at[sq], gq_out.at[source], (s_send, s_recv), 6 + k - 1, (dp, other))))
            src = psum.at[:, pl.ds(pl.multiple_of(other // 4 * 128, 128), 128)]
            out.append(keep(Link(src, pr2.at[k - 1], pr2.at[k - 1], (s_send, s_recv), 13 + k - 1, (dp, other))))
        local(dqsum.at[pl.ds(pl.multiple_of(sq * 32, 32), 32), :], gq_out.at[sq])
        pending["qs",] = out

    def weight_grad_last():
        wait("qs")
        small = psum[:, pl.ds(pl.multiple_of(sq // 4 * 128, 128), 128)]
        for k in range(n_seq - 1):
            small = small + pr2[k]
        pgo[...] = small
        local(pgo, pg_out)

    def first_frames():
        keys_turned()
        prepare(0)

    def first_done():
        def sent(i):
            tile_link(i).wait_sent()
        loop(tiles, sent)
        finish_stream(0)

    steps = {
        "DT0": down_first, "DT1": functools.partial(down_terms, 1 - near), "pkA": pick_attn, "pkN": pick_norm,
        "LN": second_norm, "LNB": branch, "UT0": up_first, "UT1": functools.partial(up_terms, 1 - near),
        "P0": first_frames, "P1": functools.partial(prepare, 1),
        "F0": first_done, "F1": functools.partial(finish_stream, 1),
        "WG": weight_grad, "W2": weight_grad_two, "W3": weight_grad_last,
    }
    for name, action in (("gf", g_first), ("gs", g_second), ("gl", g_last)):
        for b in range(streams):
            steps[name + str(b)] = functools.partial(action, b)
    for letter, g in (("U", U), ("D", D)):
        for name, action in (("zf", z_first), ("zs", z_second), ("zt", z_third), ("zl", z_last)):
            steps[name + letter] = functools.partial(action, g)
        for p in range(nz):
            steps["c1%s%d" % (letter, p)] = functools.partial(cross_one, g, p)
            steps["c2%s%d" % (letter, p)] = functools.partial(cross_two, g, p)
    for name, first, last in runs(scatter_order, ("A0", "A1", "T")):
        if name in ("A0", "A1"):
            attend_some(int(name[1]), first, last)
        elif name == "T":
            some_tiles(first, last)
        else:
            steps[name]()
    for key in pending:
        wait(*key)
    waited = [load_cot, load_act, load_hid, load_attn, load_out, *copy_xh, *own_do, *copies]
    for copy in locals_:
        if not any(copy is other for other in waited):
            copy.wait()
    for link in links:
        link.wait_sent()


def scatter_call(
    inputs, cotangent, infill, attn, hidden, act, bend, params, weights, qkv, ot, lse, xh, wt, lengths,
):
    streams, total = qkv.shape[:2]
    tokens, width = inputs.shape
    tok_rows = tokens // streams
    n_seq, n_dp = lax.axis_size("seq"), lax.axis_size("dp")
    nz = n_seq // 2
    cols = qkv.shape[2]
    any_space = pl.BlockSpec(memory_space=pl.ANY)
    vmem = pl.BlockSpec(memory_space=pltpu.VMEM)
    smem = pl.BlockSpec(memory_space=pltpu.SMEM)
    dma = pltpu.SemaphoreType.DMA
    sizes = [(w.shape[0] // (2 * n_dp * n_seq), w.shape[1]) for w in weights]
    tile = weights[1].shape[1] // 8

    def buffers(*lead):
        return [pltpu.VMEM(lead + size, BF16) for size in sizes]

    def low(*shape):
        return pltpu.VMEM(shape, BF16)

    def full(*shape):
        return pltpu.VMEM(shape, F32)

    half = width // 2 // nz
    scratch = [
        full(tokens, width), full(tokens, width), full(tokens, 128), low(tokens, width), full(tokens, width),
        low(tokens, width), low(2 * tokens, width), low(2 * tokens, width),
        low(*act.shape), low(act.shape[0], tokens, 128), low(2, *bend.shape[1:]),
        low(nz, 2 * tokens, half), low(nz, tokens, half), low(nz, 2 * tokens, half), low(nz, tokens, half),
        low(width // 128, 128, width), low(2, width, tile), low(2, tile // 128, 128, width), low(streams, tok_rows, width),
    ]
    scratch += buffers(2, 2, nz, 2) + buffers(nz, 2) + buffers(nz, 2) + buffers(nz) + buffers(nz)
    scratch += buffers(nz - 1, 2)
    scratch += [pltpu.VMEM((2,) + size, F32) for size in sizes]
    scratch += [
        low(streams, total, 128), low(*qkv.shape), full(*ot.shape), full(*lse.shape), low(streams, total, tile), low(*wt.shape),
        low(streams, 128, total), full(8, total), full(total, 128), full(total, 128),
        full(128, total), low(total, cols), low(streams, cols, total),
        low(streams, nz, 2, tok_rows, width),
        low(n_dp - 1, width // n_dp, cols), low(width // n_dp, cols),
        full(8, width), full(n_dp - 1, 8, width // n_dp), full(8, width // n_dp), full(n_seq - 1, 8, 128), full(8, 128),
        dma((13,)), dma((13,)), dma((14,)), dma((14,)), dma((48,)), dma((48,)), dma((9,)), dma((9,)),
        dma((8,)), dma((8,)), dma((20,)), dma((20,)), dma((9, 2)), dma((24,)),
    ]
    outs = [
        jax.ShapeDtypeStruct((tokens, width), BF16),
        jax.ShapeDtypeStruct((streams, tok_rows, width), BF16),
        *[jax.ShapeDtypeStruct((2,) + size, F32) for size in sizes],
        jax.ShapeDtypeStruct((n_seq, width // (n_dp * n_seq), cols), BF16),
        jax.ShapeDtypeStruct((8, 128), F32),
    ]
    return pl.pallas_call(
        scatter_kernel,
        out_shape=outs,
        in_specs=[vmem] * 3 + [any_space] * 13 + [smem],
        out_specs=[any_space] * len(outs),
        scratch_shapes=scratch,
        compiler_params=pltpu.CompilerParams(
            collective_id=1, has_side_effects=True, vmem_limit_bytes=63 * 2**20
        ),
        name="scatter_attend",
    )(
        inputs, infill, params, cotangent, attn, hidden, act, bend, weights[0].reshape(-1, 128, width), weights[1],
        weights[2].reshape(-1, 128, width), qkv, ot, lse, xh, wt, lengths,
    )


def finish_kernel(*refs):
    n = 6
    parts, outs, held, wide, sems = refs[:n], refs[n:2 * n], refs[2 * n:3 * n], refs[3 * n], refs[3 * n + 1]
    loads = [pltpu.make_async_copy(src, dst, sems.at[i]) for i, (src, dst) in enumerate(zip(parts, held))]
    sources = (*held[:-1], wide)
    stores = [pltpu.make_async_copy(src, dst, sems.at[n + i]) for i, (src, dst) in enumerate(zip(sources, outs))]
    for load in reversed(loads):
        load.start()
    loads[-1].wait()
    gq = held[-1]
    width = wide.shape[1] // 3
    for q in range(gq.shape[0]):
        for j in range(3):
            wide[:, j * width + q * 128:j * width + (q + 1) * 128] = gq[q, :, j * 128:(j + 1) * 128].astype(F32)
    stores[-1].start()
    for load, store in zip(loads[:-1], stores[:-1]):
        load.wait()
        store.start()
    for store in stores:
        store.wait()


def finish_call(*parts):
    gq = parts[-1]
    hbm = pl.BlockSpec(memory_space=pltpu.HBM)
    outs = [jax.ShapeDtypeStruct(part.shape, part.dtype) for part in parts[:-1]]
    outs.append(jax.ShapeDtypeStruct((gq.shape[1], gq.shape[0] * gq.shape[2]), F32))
    return pl.pallas_call(
        finish_kernel,
        out_shape=outs,
        in_specs=[hbm] * len(parts),
        out_specs=[hbm] * len(outs),
        scratch_shapes=[pltpu.VMEM(part.shape, part.dtype) for part in parts]
        + [pltpu.VMEM(outs[-1].shape, F32), pltpu.SemaphoreType.DMA((2 * len(outs),))],
        compiler_params=pltpu.CompilerParams(vmem_limit_bytes=63 * 2**20),
        name="finish",
    )(*parts)


def by_heads(
    inputs, lengths, infill, cotangent, w_qkv, w_out, w_up, w_down,
    gain_one, shift_one, gain_two, shift_two,
):
    streams, tok_rows, width = inputs.shape
    n_seq = lax.axis_size("seq")
    sq = lax.axis_index("seq")
    stream_len, tokens = tok_rows * n_seq, streams * tok_rows
    own_rows = w_qkv.shape[0]
    vectors = jnp.tile(jnp.stack([gain_one, shift_one, gain_two, shift_two]), (1, 128 // own_rows))
    (
        full_out, full_up, full_down, params, attn, qkv, ot, lse, xh, wt, hidden, act, bend
    ) = gather_call(inputs, w_qkv, w_out, w_up, w_down, vectors, lengths)
    weights = (
        full_out.reshape(width, width), full_up.reshape(width, -1), full_down.reshape(-1, width)
    )
    output, input_grad, grad_out, grad_up, grad_down, grad_qkv, small = scatter_call(
        inputs.reshape(tokens, width), cotangent,
        infill, attn.reshape(tokens, width), hidden, act, bend,
        params, weights,
        qkv, ot, lse, xh.reshape(streams, stream_len, width), wt, lengths,
    )
    output, input_grad, grad_out, grad_up, grad_down, grad_qkv = finish_call(
        output, input_grad, grad_out, grad_up, grad_down, grad_qkv
    )
    small = lax.dynamic_slice(small, (0, sq % (128 // own_rows) * own_rows), (4, own_rows))
    return (
        output.reshape(inputs.shape),
        input_grad,
        grad_qkv,
        grad_out.reshape(w_out.shape),
        grad_up.reshape(w_up.shape),
        grad_down.reshape(w_down.shape),
        small[0], small[1], small[2], small[3],
    )


def layer_norm(features, gain_vec, shift_vec):
    row_mean = jnp.mean(features, axis=-1, keepdims=True)
    centered = features - row_mean
    spread = jnp.mean(centered * centered, axis=-1, keepdims=True)
    return centered * lax.rsqrt(spread + norm_eps) * gain_vec + shift_vec


def segment_of(bounds, positions):
    return jnp.sum((positions[None, :, None] >= bounds[:, None, :]).astype(jnp.int32), axis=2)


def slope_table(head_count, stream_len):
    return 2.0 ** (-8.0 * (jnp.arange(head_count, dtype=jnp.float32) + 1.0) / head_count) * (
        256.0 / stream_len
    )


def block_scores(queries, key_heads, query_pos, key_pos, query_seg, key_seg, slopes):
    raw_scores = jnp.einsum(
        "sqhc,skhc->shqk", queries, key_heads, preferred_element_type=jnp.float32
    )
    distance = jnp.abs(query_pos[:, None] - key_pos[None, :]).astype(jnp.float32)
    scores = (
        raw_scores * queries.shape[3] ** (-0.5) - slopes[None, :, None, None] * distance[None, None]
    )
    same_utt = query_seg[:, None, :, None] == key_seg[:, None, None, :]
    return jnp.where(same_utt, scores, masked_score)


def score_grads(
    queries,
    grad_heads,
    log_total,
    delta,
    key_heads,
    values,
    query_pos,
    key_pos,
    query_seg,
    key_seg,
    slopes,
):
    scores = block_scores(queries, key_heads, query_pos, key_pos, query_seg, key_seg, slopes)
    probs = jnp.exp(scores - log_total[..., None])
    grad_probs = jnp.einsum(
        "sqhc,skhc->shqk", grad_heads, values, preferred_element_type=jnp.float32
    )
    grad_scores = (probs * (grad_probs - delta[..., None])).astype(jnp.bfloat16)
    return (probs.astype(jnp.bfloat16), grad_scores)


def by_frames(
    inputs,
    lengths,
    infill,
    cotangent,
    w_qkv,
    w_out,
    w_up,
    w_down,
    gain_one,
    shift_one,
    gain_two,
    shift_two,
):
    w_qkv, w_out, w_up, w_down, gain_one, shift_one, gain_two, shift_two = (
        lax.all_gather(w_qkv, ("dp", "seq"), axis=0, tiled=True),
        lax.all_gather(w_out, ("dp", "seq"), axis=0, tiled=True),
        lax.all_gather(w_up, ("dp", "seq"), axis=0, tiled=True),
        lax.all_gather(w_down, ("dp", "seq"), axis=0, tiled=True),
        lax.all_gather(gain_one, ("dp", "seq"), axis=0, tiled=True),
        lax.all_gather(shift_one, ("dp", "seq"), axis=0, tiled=True),
        lax.all_gather(gain_two, ("dp", "seq"), axis=0, tiled=True),
        lax.all_gather(shift_two, ("dp", "seq"), axis=0, tiled=True),
    )
    streams, tok_rows, model_width = inputs.shape
    head_count = HEADS
    head_size = HEAD_DIM
    stream_len = tok_rows * lax.axis_size("seq")
    score_scale = head_size ** (-0.5)
    slopes = slope_table(head_count, stream_len)
    bounds = jnp.cumsum(lengths, axis=1)
    own_pos = lax.axis_index("seq") * tok_rows + jnp.arange(tok_rows, dtype=jnp.int32)
    own_seg = segment_of(bounds, own_pos)
    gain_one_f = gain_one.astype(jnp.float32)
    shift_one_f = shift_one.astype(jnp.float32)
    gain_two_f = gain_two.astype(jnp.float32)
    shift_two_f = shift_two.astype(jnp.float32)
    inputs_f = inputs.astype(jnp.float32)
    normed_one = layer_norm(inputs_f, gain_one_f, shift_one_f).astype(jnp.bfloat16)
    packed = jnp.einsum(
        "std,de->ste", normed_one, w_qkv, preferred_element_type=jnp.float32
    ).astype(jnp.bfloat16)
    query_low = packed[:, :, :model_width]
    key_value = packed[:, :, model_width:]
    query_heads = query_low.reshape(streams, tok_rows, head_count, head_size)
    start_state = (
        jnp.full((streams, head_count, tok_rows), masked_score, jnp.float32),
        jnp.zeros((streams, head_count, tok_rows), jnp.float32),
        jnp.zeros((streams, head_count, tok_rows, head_size), jnp.float32),
    )
    shard_piece = lax.all_gather(key_value, "seq", axis=1, tiled=True)
    key_count = shard_piece.shape[1]
    visit_block_len = 256

    def one_block(carried, offset):
        top_score, weight_sum, weighted = carried
        key_part = lax.dynamic_slice_in_dim(shard_piece, offset, visit_block_len, 1)
        key_pos = offset + jnp.arange(visit_block_len, dtype=jnp.int32)
        key_seg = segment_of(bounds, key_pos)
        key_heads = key_part[:, :, :model_width].reshape(
            streams, visit_block_len, head_count, head_size
        )
        values = key_part[:, :, model_width:].reshape(
            streams, visit_block_len, head_count, head_size
        )
        scores = block_scores(query_heads, key_heads, own_pos, key_pos, own_seg, key_seg, slopes)
        new_top = jnp.maximum(top_score, jnp.max(scores, axis=3))
        rescale = jnp.exp(top_score - new_top)
        weights_blk = jnp.exp(scores - new_top[..., None])
        weight_sum = weight_sum * rescale + jnp.sum(weights_blk, axis=3)
        weighted = weighted * rescale[..., None] + jnp.einsum(
            "shqk,skhc->shqc",
            weights_blk.astype(jnp.bfloat16),
            values,
            preferred_element_type=jnp.float32,
        )
        return ((new_top, weight_sum, weighted), None)

    offsets = jnp.arange(key_count // visit_block_len, dtype=jnp.int32) * visit_block_len
    finished, _ = lax.scan(one_block, start_state, offsets)
    top_score, weight_sum, weighted = finished
    attn_heads = weighted / weight_sum[..., None]
    log_total = top_score + jnp.log(weight_sum)
    attn_rows = jnp.transpose(attn_heads, (0, 2, 1, 3)).reshape(streams, tok_rows, model_width)
    attn_low = attn_rows.astype(jnp.bfloat16)
    hidden = inputs_f + jnp.einsum(
        "std,de->ste", attn_low, w_out, preferred_element_type=jnp.float32
    )
    normed_two_f, ln_two_pull = jax.vjp(layer_norm, hidden, gain_two_f, shift_two_f)
    normed_two = normed_two_f.astype(jnp.bfloat16)
    upward = jnp.einsum("std,df->stf", normed_two, w_up, preferred_element_type=jnp.float32)
    active_f, gelu_pull = jax.vjp(jax.nn.gelu, upward)
    active = active_f.astype(jnp.bfloat16)
    output = (
        hidden + jnp.einsum("stf,fd->std", active, w_down, preferred_element_type=jnp.float32)
    ).astype(jnp.bfloat16)
    grad_output = (cotangent.astype(jnp.float32) * infill.astype(jnp.float32)[:, :, None]).astype(
        jnp.bfloat16
    )
    grad_active = jnp.einsum("ste,fe->stf", grad_output, w_down, preferred_element_type=jnp.float32)
    grad_upward = gelu_pull(grad_active)[0].astype(jnp.bfloat16)
    grad_norm_two = jnp.einsum("stf,df->std", grad_upward, w_up, preferred_element_type=jnp.float32)
    grad_in_two, grad_gain_two, grad_shift_two = ln_two_pull(grad_norm_two)
    grad_hidden = grad_output.astype(jnp.float32) + grad_in_two
    grad_branch = grad_hidden.astype(jnp.bfloat16)
    grad_attn = jnp.einsum(
        "ste,de->std", grad_branch, w_out, preferred_element_type=jnp.float32
    ).astype(jnp.bfloat16)
    grad_heads = grad_attn.reshape(streams, tok_rows, head_count, head_size)
    delta = jnp.einsum("sqhc,shqc->shq", grad_heads.astype(jnp.float32), attn_heads)
    every_kv = lax.all_gather(key_value, "seq", axis=1, tiled=True)
    total_len = every_kv.shape[1]
    block_len = 256
    offsets = jnp.arange(total_len // block_len, dtype=jnp.int32) * block_len
    grad_start = jnp.zeros((streams, tok_rows, head_count, head_size), jnp.float32)

    def key_step(grad_query, offset):
        key_part = lax.dynamic_slice_in_dim(every_kv, offset, block_len, 1)
        key_pos = offset + jnp.arange(block_len, dtype=jnp.int32)
        key_seg = segment_of(bounds, key_pos)
        key_heads = key_part[:, :, :model_width].reshape(streams, block_len, head_count, head_size)
        values = key_part[:, :, model_width:].reshape(streams, block_len, head_count, head_size)
        probs_low, grad_scores = score_grads(
            query_heads,
            grad_heads,
            log_total,
            delta,
            key_heads,
            values,
            own_pos,
            key_pos,
            own_seg,
            key_seg,
            slopes,
        )
        grad_query = (
            grad_query
            + jnp.einsum(
                "shqk,skhc->sqhc", grad_scores, key_heads, preferred_element_type=jnp.float32
            )
            * score_scale
        )
        grad_keys = (
            jnp.einsum(
                "shqk,sqhc->kshc", grad_scores, query_heads, preferred_element_type=jnp.float32
            )
            * score_scale
        )
        grad_values = jnp.einsum(
            "shqk,sqhc->kshc", probs_low, grad_heads, preferred_element_type=jnp.float32
        )
        key_terms = jnp.concatenate(
            [
                grad_keys.reshape(block_len, streams, model_width),
                grad_values.reshape(block_len, streams, model_width),
            ],
            axis=2,
        )
        return (grad_query, key_terms)

    grad_query, key_terms = lax.scan(key_step, grad_start, offsets)
    key_terms = key_terms.reshape(total_len, streams, 2 * model_width)
    own_kv_grad = lax.psum_scatter(
        key_terms.astype(jnp.bfloat16), "seq", scatter_dimension=0, tiled=True
    ).astype(jnp.float32)
    grad_kv = jnp.transpose(own_kv_grad, (1, 0, 2))
    grad_packed = jnp.concatenate(
        [grad_query.reshape(streams, tok_rows, model_width), grad_kv], axis=2
    ).astype(jnp.bfloat16)
    grad_norm_one = jnp.einsum(
        "ste,de->std", grad_packed, w_qkv, preferred_element_type=jnp.float32
    )
    _, ln_one_pull = jax.vjp(layer_norm, inputs_f, gain_one_f, shift_one_f)
    grad_in_one, grad_gain_one, grad_shift_one = ln_one_pull(grad_norm_one)
    input_grad = (grad_hidden + grad_in_one).astype(jnp.bfloat16)
    weight_terms = (
        jnp.einsum("std,ste->de", normed_one, grad_packed, preferred_element_type=jnp.float32),
        jnp.einsum("std,ste->de", attn_low, grad_branch, preferred_element_type=jnp.float32),
        jnp.einsum("std,stf->df", normed_two, grad_upward, preferred_element_type=jnp.float32),
        jnp.einsum("stf,std->fd", active, grad_output, preferred_element_type=jnp.float32),
        grad_gain_one,
        grad_shift_one,
        grad_gain_two,
        grad_shift_two,
    )
    summed = (
        lax.psum_scatter(weight_terms[0], ("dp", "seq"), scatter_dimension=0, tiled=True),
        lax.psum_scatter(weight_terms[1], ("dp", "seq"), scatter_dimension=0, tiled=True),
        lax.psum_scatter(weight_terms[2], ("dp", "seq"), scatter_dimension=0, tiled=True),
        lax.psum_scatter(weight_terms[3], ("dp", "seq"), scatter_dimension=0, tiled=True),
        lax.psum_scatter(weight_terms[4], ("dp", "seq"), scatter_dimension=0, tiled=True),
        lax.psum_scatter(weight_terms[5], ("dp", "seq"), scatter_dimension=0, tiled=True),
        lax.psum_scatter(weight_terms[6], ("dp", "seq"), scatter_dimension=0, tiled=True),
        lax.psum_scatter(weight_terms[7], ("dp", "seq"), scatter_dimension=0, tiled=True),
    )
    return (
        output,
        input_grad,
        summed[0],
        summed[1],
        summed[2],
        summed[3],
        summed[4],
        summed[5],
        summed[6],
        summed[7],
    )


def solution(mesh):
    in_specs = (
        P("dp", "seq", None),
        P("dp", None),
        P("dp", "seq"),
        P("dp", "seq", None),
        P(("dp", "seq"), None),
        P(("dp", "seq"), None),
        P(("dp", "seq"), None),
        P(("dp", "seq"), None),
        P(("dp", "seq")),
        P(("dp", "seq")),
        P(("dp", "seq")),
        P(("dp", "seq")),
    )
    out_specs = (
        P("dp", "seq", None),
        P("dp", "seq", None),
        P(("dp", "seq"), None),
        P(("dp", "seq"), None),
        P(("dp", "seq"), None),
        P(("dp", "seq"), None),
        P(("dp", "seq")),
        P(("dp", "seq")),
        P(("dp", "seq")),
        P(("dp", "seq")),
    )
    grid = (mesh.shape["dp"], mesh.shape["seq"])
    local = by_heads if grid == (4, HEADS // 2) else by_frames
    return jax.shard_map(local, mesh=mesh, in_specs=in_specs, out_specs=out_specs, check_vma=False)
```

```python
import functools

import jax
import jax.numpy as jnp
from jax import lax
from jax.experimental import pallas as pl
from jax.experimental.pallas import tpu as pltpu

from jax.sharding import PartitionSpec as P

HEADS = 16
HEAD_DIM = 64

norm_eps = 1e-05
masked_score = -1e30
MESH_ID = pl.DeviceIdType.MESH
F32 = jnp.float32
BF16 = jnp.bfloat16
far = 1e33
gather_order = (
    "zh02", "xs", "zh11", "x110", "x210", "x100", "xh2", "zh01", "cc10", "x200", "xh1", "x111",
    "seq", "x102", "x211", "zh03", "x202", "wq", "xp2", "x101", "cc00", "xh3", "wt", "xp1", "p0",
    "x103", "p2", "cc11", "p1", "x203", "zh12", "xp3", "x201", "p3", "vt", "a0", "a1", "zh13",
    "a2", "x112", "cc03", "a3", "a4", "o0", "a5", "a6", "x212", "cc02", "x113", "cc01", "a7", "o1",
    "c0", "h0", "x213", "h1", "u0", "cc12", "u1", "cc13", "u2", "u3",
)
scatter_order = (
    "DT0", "c1D0", "pkA", "LN", "DT1", "T0", "c1D1", "DT2", "c2D0", "T1", "T2", "c1D2", "T3",
    "zfD", "LNB", "pkN", "c2D1", "c2D2", "UT0", "c1U0", "UT2", "UT3", "UT1", "ztD", "zsD", "P0",
    "A00", "c2U0", "A01", "A02", "c1U1", "A03", "zfU", "F0", "P1", "A10", "gf0", "c2U1", "A11",
    "A12", "c1U3", "zsU", "A13", "F1", "WG", "c1U2", "gf1", "gs0", "c2U2", "DT3", "W2", "c1D3",
    "ztU", "gs1", "c2D3", "W3", "gl0", "c2U3", "zlD", "gl1", "zlU",
)
q_block = 256


def place():
    dp, sq = lax.axis_index("dp"), lax.axis_index("seq")
    return dp, sq, dp // 2, dp % 2, sq // 2, sq % 2


def planes(z, nz):
    z1 = z + 1 - 2 * (z % 2)
    return z1, (z + 2) % nz, (z1 + 2) % nz


def dot_nt(a, b):
    return lax.dot_general(a, b, (((1,), (1,)), ((), ())), preferred_element_type=F32)


def dot_nn(a, b):
    return lax.dot_general(a, b, (((1,), (0,)), ((), ())), preferred_element_type=F32)


def runs(order, counted):
    out = []
    for name in order:
        kind = name[:-1]
        if kind in counted:
            number = int(name[-1])
            if out and out[-1][0] == kind and out[-1][2] == number:
                out[-1] = (kind, out[-1][1], number + 1)
            else:
                out.append((kind, number, number + 1))
        else:
            out.append((name, 0, 0))
    return out


class Link:
    def __init__(self, src, dst, landing, sems, index, target, when_send=None, when_recv=None):
        self.sems, self.index, self.target = sems, index, target
        self.src, self.dst, self.landing = src, dst, landing
        self.when_send, self.when_recv = when_send, when_recv

    def copy(self, src, dst):
        send, recv = self.sems
        return pltpu.make_async_remote_copy(
            src_ref=src,
            dst_ref=dst,
            send_sem=send.at[self.index],
            recv_sem=recv.at[self.index],
            device_id=self.target,
            device_id_type=MESH_ID,
        )

    def run(self, when, action):
        if when is None:
            action()
        else:
            pl.when(when)(action)

    def start(self):
        self.run(self.when_send, lambda: self.copy(self.src, self.dst).start())

    def wait(self):
        self.run(self.when_recv, lambda: self.copy(self.landing, self.landing).wait_recv())

    def wait_sent(self):
        self.run(self.when_send, lambda: self.copy(self.src, self.dst).wait_send())


def greet(dp, sq, n_seq, n_dp):
    barrier = pltpu.get_barrier_semaphore()
    for k in range(1, n_seq):
        pl.semaphore_signal(
            barrier, inc=1, device_id=(dp, lax.rem(sq + k, n_seq)), device_id_type=MESH_ID
        )
    for m in range(1, n_dp):
        other = lax.rem(dp + m, n_dp)
        pl.semaphore_signal(barrier, inc=1, device_id=(other, sq), device_id_type=MESH_ID)


def all_here(n_seq, n_dp):
    pl.semaphore_wait(pltpu.get_barrier_semaphore(), n_seq - 1 + n_dp - 1)


def distance(len_ref, stream, first_key, keys, first_query, queries):
    key_pos = lax.broadcasted_iota(jnp.int32, (keys, 1), 0) + first_key
    query_pos = lax.broadcasted_iota(jnp.int32, (1, queries), 1) + first_query
    key_seg = jnp.zeros((keys, 1), jnp.int32)
    query_seg = jnp.zeros((1, queries), jnp.int32)
    bound = 0
    for k in range(len_ref.shape[1]):
        bound = bound + len_ref[stream, k]
        key_seg = key_seg + (key_pos >= bound).astype(jnp.int32)
        query_seg = query_seg + (query_pos >= bound).astype(jnp.int32)
    gap = jnp.abs(key_pos - query_pos).astype(F32)
    return jnp.where(key_seg == query_seg, gap, far)


def gelu_both(v):
    square = v * v
    th = jnp.tanh(v * (0.7978845608028654 + 0.7978845608028654 * 0.044715 * square))
    half = 0.5 * (1.0 + th)
    bend = v * (0.5 - 0.5 * th * th)
    return v * half, half + bend * (0.7978845608028654 + 0.7978845608028654 * 0.134145 * square)


def norm_parts(v):
    mean = jnp.mean(v, axis=-1, keepdims=True)
    centered = v - mean
    rstd = lax.rsqrt(jnp.mean(centered * centered, axis=-1, keepdims=True) + norm_eps)
    return centered * rstd, rstd


def norm_back(n, rstd, e):
    return rstd * (
        e - jnp.mean(e, axis=-1, keepdims=True) - n * jnp.mean(e * n, axis=-1, keepdims=True)
    )


def own_slopes(sq, n_seq, total):
    out = []
    for h in range(2):
        value = 0.0
        for q in range(n_seq):
            slope = 2.0 ** (-8.0 * (2 * q + h + 1) / (2 * n_seq)) * (256.0 / total)
            value = jnp.where(sq == q, jnp.float32(slope), value)
        out.append(value)
    return out


def gather_kernel(
    x_ref, w_ref, wo_ref, wu_ref, wd_ref, vec_ref, len_ref,
    wo_all, wu_all, wd_all, par_out, attn, qkv_out, ot_out, lse_out, xh_out, wt_out, hid_out, act_out, bend_out,
    xg, xh, wqb, wt, wq_ref, par_ref, pbuf, pown, par, qkv, vt, obuf, ot, lse, dist, wo_v, wu_t, av, hid, low_two, act_v, bend_v,
    z_send, z_recv, w_send, w_recv, x_send, x_recv, s_send, s_recv, tile_sem, store_sem, loc,
):
    dp, sq, y, x, z, c = place()
    streams, tok_rows, width = x_ref.shape
    n_seq, n_dp = lax.axis_size("seq"), lax.axis_size("dp")
    nz = n_seq // 2
    total = n_seq * tok_rows
    own_rows = w_ref.shape[0]
    slopes = own_slopes(sq, n_seq, total)
    x_nbr, y_nbr = (y * 2 + (1 - x), sq), ((1 - y) * 2 + x, sq)
    sibling = (dp, z * 2 + (1 - c))
    z1, z2, z3 = planes(z, nz)
    near_dev, far_dev = (dp, z1 * 2 + c), (dp, z2 * 2 + c)
    greet(dp, sq, n_seq, n_dp)
    rank = dp * n_seq + sq
    row = lax.broadcasted_iota(jnp.int32, (8, 128), 0)
    lane = lax.broadcasted_iota(jnp.int32, (8, 128), 1)
    mine = (row == rank // 4) & ((lane >> 5) == rank % 4)
    vecs = vec_ref[...].astype(F32)
    par_ref[...] = jnp.concatenate(
        [jnp.where(mine, jnp.broadcast_to(vecs[i:i + 1], (8, 128)), 0.0) for i in range(4)], axis=0
    ).astype(BF16)
    for q in range(n_seq):
        for j in range(3):
            wq_ref[q, :, j * 128:(j + 1) * 128] = w_ref[:, j * width + q * 128:j * width + (q + 1) * 128]
    links = []

    def keep(link):
        link.start()
        links.append(link)
        return link

    locals_ = []

    def local(src, dst):
        copy = pltpu.make_async_copy(src, dst, loc.at[len(locals_)])
        copy.start()
        locals_.append(copy)
        return copy

    cp_x = local(x_ref, xg.at[:, sq])
    cp_wq = local(wq_ref.at[sq], wqb.at[pl.ds(pl.multiple_of(sq * 32 + dp * 32 * n_seq, 32), 32), :])
    cp_w = [
        local(src, dst.at[y, x, z, c])
        for src, dst in ((wo_ref, wo_all), (wu_ref, wu_all), (wd_ref, wd_all))
    ]

    arrays = [(wo_ref, wo_all), (wu_ref, wu_all), (wd_ref, wd_all)]
    groups = [(0, 1), (2,)]
    pending = {}
    every = slice(None)

    arrived = set()

    def wait(*key):
        if key not in arrived:
            arrived.add(key)
            for link in pending[key]:
                link.wait()

    where = [z, z1, z2, z3]

    def z_hop(g, h):
        out = []
        for i in groups[g]:
            own, full = arrays[i]
            there = full.at[y, x, z if h < 3 else z2, c]
            land = full.at[y, x, where[h], c]
            src = own if h < 3 else there
            target = far_dev if h == 2 else near_dev
            out.append(keep(Link(src, there, land, (w_send, w_recv), i * 3 + h - 1, target)))
        pending[("z", g, h)] = out

    def plane(tag, g, h, pairs):
        out = []
        for i in groups[g]:
            own, full = arrays[i]
            for kind, target, src_at, land_at, own_half in pairs(where[h]):
                here = full.at[src_at]
                src = own.at[own_half] if own_half is not None and h == 0 else here
                out.append(keep(Link(
                    src, here, full.at[land_at], (x_send, x_recv), (i * 4 + h) * 5 + kind, target
                )))
        pending[(tag, g, h)] = out

    def cross_one(g, h):
        plane("x1", g, h, lambda b: [
            (0, x_nbr, (y, x, b, c, 0), (y, 1 - x, b, c, 0), 0),
            (1, y_nbr, (y, x, b, c, 1), (1 - y, x, b, c, 1), 1),
        ])

    def cross_two(g, h):
        wait("x1", g, h)
        plane("x2", g, h, lambda b: [
            (2, y_nbr, (y, every, b, c, 0), (1 - y, every, b, c, 0), None),
            (3, x_nbr, (every, x, b, c, 1), (every, 1 - x, b, c, 1), None),
        ])

    def cross_core(g, h):
        wait("x2", g, h)
        plane("c", g, h, lambda b: [
            (4, sibling, (every, every, b, c), (every, every, b, 1 - c), None),
        ])

    def x_hop(h):
        there = xg.at[:, (z if h < 3 else z2) * 2 + c]
        land = xg.at[:, where[h] * 2 + c]
        target = far_dev if h == 2 else near_dev
        pending[("x", h)] = [keep(Link(x_ref if h < 3 else there, there, land, (z_send, z_recv), h - 1, target))]

    def x_pass(h):
        src = xg.at[:, where[h] * 2 + c]
        land = xg.at[:, where[h] * 2 + (1 - c)]
        pending[("xc", h)] = [keep(Link(src, src, land, (z_send, z_recv), 3 + h - 1, sibling))]

    all_here(n_seq, n_dp)
    rows_dp = 32 * n_seq

    def shard_rows(d, q):
        return wqb.at[pl.ds(pl.multiple_of((d * n_seq + q) * 32, 32), 32), :]

    def plane_rows(d):
        return wqb.at[pl.ds(pl.multiple_of(d * rows_dp, 32), rows_dp), :]

    def along_seq():
        small, wide = [], []
        for k in range(1, n_seq):
            other = lax.rem(sq + k, n_seq)
            source = lax.rem(sq + n_seq - k, n_seq)
            slot = pbuf.at[k - 1]
            small.append(keep(Link(par_ref, slot, slot, (s_send, s_recv), k - 1, (dp, other))))
            wide.append(keep(Link(
                wq_ref.at[other], shard_rows(dp, sq), shard_rows(dp, source), (s_send, s_recv), 7 + k - 1, (dp, other)
            )))
        pending["ps",], pending["ws",] = small, wide

    def along_dp():
        wait("ps")
        pown[...] = par_ref[...] + pbuf[0]
        for k in range(1, n_seq - 1):
            pown[...] += pbuf[k]
        pending["pd",] = []
        for m in range(1, n_dp):
            slot = pbuf.at[n_seq - 2 + m]
            pending["pd",].append(
                keep(Link(pown, slot, slot, (s_send, s_recv), 14 + m - 1, (lax.rem(dp + m, n_dp), sq)))
            )
        wait("ws")
        cp_wq.wait()
        pending["wd",] = []
        for m in range(1, n_dp):
            other, source = lax.rem(dp + m, n_dp), lax.rem(dp + n_dp - m, n_dp)
            pending["wd",].append(keep(Link(
                plane_rows(dp), plane_rows(dp), plane_rows(source), (s_send, s_recv), 17 + m - 1, (other, sq)
            )))

    step = 256
    rows_of = {}

    def columns():
        wait("pd")
        par[...] = pown[...] + pbuf[n_seq - 1] + pbuf[n_seq] + pbuf[n_seq + 1]
        wait("wd")
        for r in range(width // step):
            wt[:, r * step:(r + 1) * step] = jnp.transpose(
                wqb[r * step:(r + 1) * step, :].astype(F32)
            ).astype(BF16)
        local(wt, wt_out)
        local(par, par_out)

    def vector(row):
        block = par[row * 8:(row + 1) * 8, :].astype(F32)
        return jnp.concatenate([block[r:r + 1, :] for r in range(8)], axis=1)

    scale = 0.125

    def process(s):
        gain, shift = vector(0), vector(1)

        def one(b, carry):
            v = xg[b, s].astype(F32)
            mean = jnp.mean(v, axis=1, keepdims=True)
            v = v - mean
            spread = jnp.mean(v * v, axis=1, keepdims=True)
            n = v * lax.rsqrt(spread + 1e-5)
            xh[b, s] = n.astype(BF16)
            normed = (n * gain + shift).astype(BF16)
            packed = dot_nt(normed, wt[...])
            row = pl.ds(pl.multiple_of(s * tok_rows, tok_rows), tok_rows)
            qkv[b, row, 0:128] = (packed[:, 0:128] * scale).astype(BF16)
            qkv[b, row, 128:384] = packed[:, 128:384].astype(BF16)
            return carry
        lax.fori_loop(0, streams, one, 0)

    def process_hop(h):
        def one(j, carry):
            process(where[h] * 2 + j)
            return carry
        lax.fori_loop(0, 2, one, 0)

    def turn(j, carry):
        b, r = j // (total // step), j % (total // step)
        row = pl.ds(pl.multiple_of(r * step, step), step)
        vt[b, :, row] = jnp.transpose(qkv[b, row, 256:384].astype(F32)).astype(BF16)
        return carry
    def values():
        local(xh, xh_out)
        local(qkv, qkv_out)
        lax.fori_loop(0, streams * (total // step), turn, 0)

    blocks = total // q_block
    cols = bend_v.shape[2]
    tiles = bend_v.shape[0]

    def tile_copies(i):
        cut = pl.ds(pl.multiple_of(i * cols, cols), cols)
        return [
            pltpu.make_async_copy(
                wu_all.at[part // 2, part % 2, :, :, :, :, cut], wu_t.at[i, part // 2, part % 2], tile_sem.at[i, part]
            )
            for part in range(4)
        ]

    def tile_stores(i):
        return (
            pltpu.make_async_copy(act_v.at[pl.ds(i * 2, 2)], act_out.at[pl.ds(i * 2, 2)], store_sem.at[i, 0]),
            pltpu.make_async_copy(bend_v.at[i], bend_out.at[i], store_sem.at[i, 1]),
        )


    def attend(j, carry):
        b, qb = j // blocks, j % blocks
        row = pl.ds(pl.multiple_of(qb * q_block, q_block), q_block)
        dist[...] = distance(len_ref, b, 0, total, qb * q_block, q_block)
        queries = qkv[b, row, 0:128]
        lane = lax.broadcasted_iota(jnp.int32, (q_block, 128), 1)
        for h in range(2):
            own = jnp.where((lane < 64) == (h == 0), queries, jnp.zeros_like(queries))
            s = dot_nt(qkv[b, :, 128:256], own) - slopes[h] * dist[...]
            top = jnp.max(s, axis=0, keepdims=True)
            p = jnp.exp(s - top)
            weight = jnp.sum(p, axis=0, keepdims=True)
            o = dot_nn(vt[b, h * 64:(h + 1) * 64, :], p.astype(BF16))
            ot[b, h * 64:(h + 1) * 64, row] = o / weight
            lse[b, h:h + 1, row] = top + jnp.log(weight)
        obuf[b, row, :] = jnp.transpose(ot[b, :, row]).astype(BF16)
        return carry

    def send_rows(b):
        out = []
        for k in range(1, n_seq):
            other = lax.rem(sq + k, n_seq)
            source = lax.rem(sq + n_seq - k, n_seq)
            src = obuf.at[b, pl.ds(pl.multiple_of(other * tok_rows, tok_rows), tok_rows), :]
            dst = av.at[b, :, pl.ds(pl.multiple_of(sq * 128, 128), 128)]
            land = av.at[b, :, pl.ds(pl.multiple_of(source * 128, 128), 128)]
            out.append(keep(Link(src, dst, land, (s_send, s_recv), 20 + b * 7 + k - 1, (dp, other))))
        pending[("o", b)] = out
        own_rows.append(local(
            obuf.at[b, pl.ds(pl.multiple_of(sq * tok_rows, tok_rows), tok_rows), :],
            av.at[b, :, pl.ds(pl.multiple_of(sq * 128, 128), 128)],
        ))

    own_rows = []

    def attend_some(first, last):
        lax.fori_loop(first, last, attend, 0)

    tokens = streams * tok_rows
    late = []

    def residual(b):
        wait("o", b)
        own_rows[b].wait()
        if b == 0:
            late[0].wait()
        rows = slice(b * tok_rows, (b + 1) * tok_rows)
        for r in range(0, width, 512):
            hid[rows, r:r + 512] = x_ref[b, :, r:r + 512].astype(F32) + dot_nn(
                av[b], wo_v[:, :, :, :, :, :, r:r + 512].reshape(width, 512)
            )
        n, _ = norm_parts(hid[rows])
        low_two[rows] = (n * vector(2) + vector(3)).astype(BF16)
        if b == streams - 1:
            local(hid, hid_out)
            local(av, attn)

    def one_tile(i, carry):
        for copy in tile_copies(i):
            copy.wait()
        act_f, bend = gelu_both(dot_nn(low_two[...], wu_t[i].reshape(width, cols)))
        act = act_f.astype(BF16)
        for j in range(4):
            act_v[i * 2 + j // 2, j % 2] = act[:, j * 128:(j + 1) * 128]
        bend_v[i] = bend.astype(BF16)
        for copy in tile_stores(i):
            copy.start()
        return carry

    def some_tiles(first, last):
        lax.fori_loop(first * tiles // 4, last * tiles // 4, one_tile, 0)

    def first_group():
        for h in range(4):
            wait("c", 0, h)
        late.append(local(wo_all, wo_v))

        def load(i, carry):
            for copy in tile_copies(i):
                copy.start()
            return carry
        lax.fori_loop(0, tiles, load, 0)

    def x_arrived(h):
        wait("x", h)
        x_pass(h)

    def own_x():
        pending["xc", 0] = [
            keep(Link(x_ref, xg.at[:, sq], xg.at[:, z * 2 + (1 - c)], (z_send, z_recv), 6, sibling))
        ]

    def block_done(h):
        if h == 0:
            cp_x.wait()
        wait("xc", h)
        process_hop(h)

    def hop_x(h):
        if h == 3:
            wait("x", 2)
        x_hop(h)

    def hop(g, h):
        if h == 3:
            wait("z", g, 2)
        z_hop(g, h)

    def cross_begin(g, h):
        if h > 0:
            wait("z", g, h)
        cross_one(g, h)

    def cross_next(g, h):
        if h == 0:
            for i in groups[g]:
                cp_w[i].wait()
        cross_two(g, h)

    def stream_out(b):
        send_rows(b)
        if b == 1:
            local(ot, ot_out)
            local(lse, lse_out)

    steps = {
        "seq": along_seq, "wq": along_dp, "wt": columns, "xs": own_x, "vt": values,
        "c0": first_group,
    }
    for h in range(4):
        steps["p%d" % h] = functools.partial(block_done, h)
        for g in range(2):
            steps["x1%d%d" % (g, h)] = functools.partial(cross_begin, g, h)
            steps["x2%d%d" % (g, h)] = functools.partial(cross_next, g, h)
            steps["cc%d%d" % (g, h)] = functools.partial(cross_core, g, h)
            if h > 0:
                steps["zh%d%d" % (g, h)] = functools.partial(hop, g, h)
        if h > 0:
            steps["xh%d" % h] = functools.partial(hop_x, h)
            steps["xp%d" % h] = functools.partial(x_arrived, h)
    for b in range(streams):
        steps["o%d" % b] = functools.partial(stream_out, b)
        steps["h%d" % b] = functools.partial(residual, b)
    for name, first, last in runs(gather_order, ("a", "u")):
        if name == "a":
            attend_some(first, last)
        elif name == "u":
            some_tiles(first, last)
        else:
            steps[name]()

    def stored(i, carry):
        for copy in tile_stores(i):
            copy.wait()
        return carry
    lax.fori_loop(0, tiles, stored, 0)
    for key in pending:
        wait(*key)
    waited = [cp_x, cp_wq, *cp_w, *own_rows, *late]
    for copy in locals_:
        if not any(copy is other for other in waited):
            copy.wait()
    for link in links:
        link.wait_sent()


def gather_call(inputs, w_qkv, w_out, w_up, w_down, vectors, lengths):
    streams, tok_rows, width = inputs.shape
    n_seq, n_dp = lax.axis_size("seq"), lax.axis_size("dp")
    nz, total = n_seq // 2, n_seq * tok_rows
    any_space = pl.BlockSpec(memory_space=pl.ANY)
    vmem = pl.BlockSpec(memory_space=pltpu.VMEM)
    smem = pl.BlockSpec(memory_space=pltpu.SMEM)

    def halves(w):
        return w.reshape(2, w.shape[0] // 2, w.shape[1])

    own = [halves(w) for w in (w_out, w_up, w_down)]
    full = [jax.ShapeDtypeStruct((2, n_dp // 2, nz, 2) + w.shape, BF16) for w in own]
    cols = w_qkv.shape[1] // n_seq
    outs = full + [
        jax.ShapeDtypeStruct((32, 128), BF16),
        jax.ShapeDtypeStruct((streams, tok_rows, width), BF16),
        jax.ShapeDtypeStruct((streams, total, cols), BF16),
        jax.ShapeDtypeStruct((streams, 128, total), F32),
        jax.ShapeDtypeStruct((streams, 8, total), F32),
        jax.ShapeDtypeStruct((streams, n_seq, tok_rows, width), BF16),
        jax.ShapeDtypeStruct((cols, width), BF16),
        jax.ShapeDtypeStruct((streams * tok_rows, width), F32),
        jax.ShapeDtypeStruct((n_dp * nz, 2, streams * tok_rows, 128), BF16),
        jax.ShapeDtypeStruct((8, streams * tok_rows, w_up.shape[1] // 8), BF16),
    ]
    dma = pltpu.SemaphoreType.DMA
    scratch = [
        pltpu.VMEM((streams, n_seq, tok_rows, width), BF16),
        pltpu.VMEM((streams, n_seq, tok_rows, width), BF16),
        pltpu.VMEM((width, cols), BF16),
        pltpu.VMEM((cols, width), BF16),
        pltpu.VMEM((n_seq, w_qkv.shape[0], cols), BF16),
        pltpu.VMEM((32, 128), BF16),
        pltpu.VMEM((n_seq - 1 + n_dp - 1, 32, 128), BF16),
        pltpu.VMEM((32, 128), BF16),
        pltpu.VMEM((32, 128), BF16),
        pltpu.VMEM((streams, total, cols), BF16),
        pltpu.VMEM((streams, 128, total), BF16),
        pltpu.VMEM((streams, total, 128), BF16),
        pltpu.VMEM((streams, 128, total), F32),
        pltpu.VMEM((streams, 8, total), F32),
        pltpu.VMEM((total, q_block), F32),
        pltpu.VMEM(full[0].shape, BF16),
        pltpu.VMEM((8,) + full[1].shape[:-1] + (w_up.shape[1] // 8,), BF16),
        pltpu.VMEM((streams, tok_rows, width), BF16),
        pltpu.VMEM((streams * tok_rows, width), F32),
        pltpu.VMEM((streams * tok_rows, width), BF16),
        pltpu.VMEM(outs[11].shape, BF16),
        pltpu.VMEM(outs[12].shape, BF16),
        dma((7,)), dma((7,)), dma((9,)), dma((9,)), dma((60,)), dma((60,)), dma((34,)), dma((34,)),
        dma((8, 4)), dma((8, 2)), dma((20,)),
    ]
    return pl.pallas_call(
        gather_kernel,
        out_shape=outs,
        in_specs=[vmem] * 6 + [smem],
        out_specs=[any_space] * len(outs),
        scratch_shapes=scratch,
        compiler_params=pltpu.CompilerParams(
            collective_id=0, has_side_effects=True, vmem_limit_bytes=56 * 2**20
        ),
        name="gather_attend",
    )(inputs, w_qkv, *own, vectors, lengths)


def scatter_kernel(
    x_ref, fill_ref, par_ref, cot_ref, attn_ref, hid_ref, act_ref, bend_ref, wo_ref, wu_ref, wd_ref,
    qkv_ref, ot_ref, lse_ref, xh_ref, wt_ref, len_ref,
    y_out, gx_out, go_out, gu_out, gd_out, gq_out, pg_out,
    hidden, n_two, r_two, low_two, grad_two, yb, gout2, gb2, act_v, act_s, bend_t, n2s2, n2o, at2, ato, wo_v, wu_t, wd_t, gab,
    acc_o, acc_u, acc_d, ra_o, ra_u, ra_d, rb_o, rb_u, rb_d, sa_o, sa_u, sa_d, sb_o, sb_u, sb_d,
    zr_o, zr_u, zr_d, fin_o, fin_u, fin_d,
    do, qkv, ot, lse, xh, wt, kt, delta, dk, dv, dqt, dqkv, dqkvt,
    gp, dqr, dqsum, pgp, pr1, psum, pr2, pgo,
    c_send, c_recv, o_send, o_recv, x_send, x_recv, zw_send, zw_recv, zg_send, zg_recv, s_send, s_recv,
    tile_sem, loc,
):
    dp, sq, y, x, z, c = place()
    streams, tok_rows, width = gab.shape
    tokens = streams * tok_rows
    slopes = own_slopes(lax.axis_index("seq"), lax.axis_size("seq"), qkv.shape[1])
    n_seq, n_dp = lax.axis_size("seq"), lax.axis_size("dp")
    nz = n_seq // 2
    total = n_seq * tok_rows
    x_nbr, y_nbr = (y * 2 + (1 - x), sq), ((1 - y) * 2 + x, sq)
    sibling = (dp, z * 2 + (1 - c))
    z1, z2, z3 = planes(z, nz)
    near_dev, far_dev = (dp, z1 * 2 + c), (dp, z2 * 2 + c)
    greet(dp, sq, n_seq, n_dp)
    links, locals_ = [], []
    every = slice(None)

    def keep(link):
        link.start()
        links.append(link)
        return link

    def local(src, dst):
        copy = pltpu.make_async_copy(src, dst, loc.at[len(locals_)])
        copy.start()
        locals_.append(copy)
        return copy

    def loop(n, body):
        def step(j, carry):
            body(j)
            return carry
        lax.fori_loop(0, n, step, 0)

    pending = {}

    arrived = set()

    def wait(*key):
        if key not in arrived:
            arrived.add(key)
            for link in pending[key]:
                link.wait()

    def f32(v):
        return v.astype(F32)

    def vector(row):
        block = f32(par_ref[row * 8:(row + 1) * 8, :])
        return jnp.concatenate([block[r:r + 1, :] for r in range(8)], axis=1)

    def to_sibling(src, dst, index):
        return keep(Link(src, dst, dst, (c_send, c_recv), index, sibling))

    cols = wu_t.shape[2]
    tiles = wu_ref.shape[1] // cols

    def tile_copies(i):
        slot, first = i % 2, pl.multiple_of(i * cols, cols)
        out = [pltpu.make_async_copy(bend_ref.at[i], bend_t.at[slot], tile_sem.at[8, slot])]
        for part in range(4):
            rows = slice(part * 256, (part + 1) * 256)
            out.append(pltpu.make_async_copy(
                wu_ref.at[rows, pl.ds(first, cols)], wu_t.at[slot, rows], tile_sem.at[part, slot]
            ))
            out.append(pltpu.make_async_copy(
                wd_ref.at[i * 4 + part], wd_t.at[slot, part], tile_sem.at[4 + part, slot]
            ))
        return out

    load_cot, load_act = local(cot_ref, gab), local(act_ref, act_v)
    load_hid = local(hid_ref, hidden)
    for copy in tile_copies(0):
        copy.start()
    load_attn, load_out = local(attn_ref, low_two), local(wo_ref, wo_v)
    load_cot.wait()
    for b in range(streams):
        rows = slice(b * tok_rows, (b + 1) * tok_rows)
        fill = jnp.broadcast_to(f32(fill_ref[b:b + 1, :]), (128, tok_rows))
        gout2[rows] = (f32(gab[b]) * jnp.transpose(fill)[:, 0:1]).astype(BF16)
    all_here(n_seq, n_dp)
    gout_link = to_sibling(gout2.at[0:tokens], gout2.at[tokens:2 * tokens], 0)
    act_link = to_sibling(act_ref.at[:, 1 - c], act_s, 1)

    def chosen(parity):
        j = lax.broadcasted_iota(jnp.int32, (1, width // 2), 1)
        column = ((((j & 127) >> 5) * n_seq + (j >> 7) * 2 + parity) << 5) + (j & 31)
        return (lax.broadcasted_iota(jnp.int32, (width, 1), 0) == column).astype(F32).astype(BF16)

    def pick(v, mine, theirs, index):
        here, there = dot_nn(v, chosen(c)).astype(BF16), dot_nn(v, chosen(1 - c)).astype(BF16)
        for b in range(nz):
            mine[b, 0:tokens] = here[:, b * 128:(b + 1) * 128]
            theirs[b] = there[:, b * 128:(b + 1) * 128]
        return to_sibling(theirs, mine.at[:, tokens:2 * tokens], index)

    gain_two, shift_two = vector(2), vector(3)

    def tile_grad(i):
        cut = pl.ds(pl.multiple_of(i % 2 * cols, cols), cols)
        return gp.at[i // 4, i // 2 % 2 * 2, :, :, cut], gp.at[i // 4, i // 2 % 2 * 2 + 1, :, :, cut]

    def tile_link(i):
        src, dst = tile_grad(i)
        return Link(src, dst, dst, (c_send, c_recv), 4 + i, sibling)

    def one_tile(i, carry):
        slot = i % 2
        for copy in tile_copies(i):
            copy.wait()

        @pl.when(i + 1 < tiles)
        def _():
            for copy in tile_copies(i + 1):
                copy.start()
        down = wd_t[slot].reshape(cols, width)
        act = jnp.concatenate([act_v[i * 2 + j // 2, j % 2] for j in range(4)], axis=1)
        hidden[...] += dot_nn(act, down)
        grad_up = (dot_nt(gout2[0:tokens], down) * f32(bend_t[slot])).astype(BF16)
        tile_grad(i)[0][...] = grad_up.reshape(streams, tok_rows, cols)
        grad_two[...] += dot_nt(grad_up, wu_t[slot])
        tile_link(i).start()
        return carry

    arrays = [
        (acc_o, ra_o, rb_o, sa_o, sb_o, zr_o, fin_o, go_out),
        (acc_u, ra_u, rb_u, sa_u, sb_u, zr_u, fin_u, gu_out),
        (acc_d, ra_d, rb_d, sa_d, sb_d, zr_d, fin_d, gd_out),
    ]
    groups = [(1, 0), (2,)]
    U, D = 0, 1
    plane_of = [z3, z2, z1, z]

    def cross_one(g, p):
        t = plane_of[p]
        out = []
        for i in groups[g]:
            acc, ra, rb = arrays[i][:3]
            out.append(keep(Link(acc.at[1 - y, :, t, 0], ra.at[p], ra.at[p], (x_send, x_recv), (i * 4 + p) * 4, y_nbr)))
            out.append(keep(Link(acc.at[:, 1 - x, t, 1], rb.at[p], rb.at[p], (x_send, x_recv), (i * 4 + p) * 4 + 1, x_nbr)))
        pending[("x1", g, p)] = out

    def cross_two(g, p):
        t = plane_of[p]
        wait("x1", g, p)
        out = []
        for i in groups[g]:
            acc, ra, rb, sa, sb = arrays[i][:5]
            acc[y, 1 - x, t, 0] = (f32(acc[y, 1 - x, t, 0]) + f32(ra[p, 1 - x])).astype(BF16)
            acc[1 - y, x, t, 1] = (f32(acc[1 - y, x, t, 1]) + f32(rb[p, 1 - y])).astype(BF16)
            out.append(keep(Link(acc.at[y, 1 - x, t, 0], sa.at[p], sa.at[p], (x_send, x_recv), (i * 4 + p) * 4 + 2, x_nbr)))
            out.append(keep(Link(acc.at[1 - y, x, t, 1], sb.at[p], sb.at[p], (x_send, x_recv), (i * 4 + p) * 4 + 3, y_nbr)))
        pending[("x2", g, p)] = out

    def cross_three(g, p):
        t = plane_of[p]
        wait("x2", g, p)
        for i in groups[g]:
            acc, ra, rb, sa, sb = arrays[i][:5]
            acc[y, x, t, 0] = (f32(acc[y, x, t, 0]) + f32(ra[p, x]) + f32(sa[p])).astype(BF16)
            acc[y, x, t, 1] = (f32(acc[y, x, t, 1]) + f32(rb[p, y]) + f32(sb[p])).astype(BF16)

    def z_one(g, step, target):
        pending[("z", g, step)] = [
            keep(Link(
                arrays[i][0].at[y, x, plane_of[step]], arrays[i][5].at[step], arrays[i][5].at[step],
                (zw_send, zw_recv), i * 3 + step, target,
            ))
            for i in groups[g]
        ]

    def z_first(g):
        cross_three(g, 0)
        z_one(g, 0, near_dev)

    def z_second(g):
        cross_three(g, 1)
        wait("z", g, 0)
        for i in groups[g]:
            acc, zr = arrays[i][0], arrays[i][5]
            for h in range(2):
                acc[y, x, z2, h] = (f32(acc[y, x, z2, h]) + f32(zr[0, h])).astype(BF16)
        z_one(g, 1, far_dev)

    def z_third(g):
        cross_three(g, 2)
        z_one(g, 2, near_dev)

    def z_last(g):
        cross_three(g, 3)
        wait("z", g, 1)
        wait("z", g, 2)
        for i in groups[g]:
            acc, zr, fin, out = arrays[i][0], *arrays[i][5:]
            fin[...] = f32(acc[y, x, z]) + f32(zr[1]) + f32(zr[2])
            local(fin, out)

    def dot_tn(a, b):
        return lax.dot_general(a, b, (((0,), (0,)), ((), ())), preferred_element_type=F32)

    def down_terms(t):
        def one(d):
            left = jnp.concatenate([act_v[d * 4 + t, c], act_s[d * 4 + t]], axis=0)
            rows = acc_d.shape[4]
            for r in range(0, width, 512):
                terms = dot_tn(left, gout2[:, r:r + 512]).astype(BF16)
                for j in range(2):
                    acc_d[d // 2, d % 2, t, j, :, r:r + 512] = terms[j * rows:(j + 1) * rows]
        loop(n_dp, one)

    def narrow_terms(source, t, acc, right, where):
        terms = dot_tn(source[t], right).astype(BF16)
        for j in range(8):
            acc[j // 4, j // 2 % 2, t, j % 2, :, where] = terms[j * 16:(j + 1) * 16]

    def up_terms(t):
        def one(i):
            d, part = i // 2, i % 2
            cut = pl.ds(pl.multiple_of(part * cols, cols), cols)
            right = gp[d // 2, pl.ds(d % 2 * 2, 2), :, :, cut].reshape(2 * tokens, cols)
            narrow_terms(n2s2, t, acc_u, right, pl.ds(pl.multiple_of(i * cols, cols), cols))
        loop(tiles, one)
        for r in range(0, width, 512):
            narrow_terms(at2, t, acc_o, gb2[:, r:r + 512], slice(r, r + 512))

    copies, copy_xh = [], []

    begun = []

    def opening():
        if not begun:
            begun.append("start")
            for copy in (load_act, load_hid, load_attn):
                copy.wait()
            gout_link.wait()
            act_link.wait()

    def down_plane(p):
        opening()
        down_terms(plane_of[p])
        if not copies:
            copies.extend([local(qkv_ref, qkv), local(ot_ref, ot), local(lse_ref, lse), local(wt_ref, wt)])
            copy_xh.append(local(xh_ref.at[:, :, 0:cols], xh))

    def pick_attn():
        opening()
        pending["attn",] = [pick(low_two[...], at2, ato, 2)]

    def pick_norm():
        pending["norm",] = [pick(low_two[...], n2s2, n2o, 3)]

    def second_norm():
        opening()
        for r in range(0, tokens, 128):
            n, rstd = norm_parts(hidden[r:r + 128])
            n_two[r:r + 128] = n
            r_two[r:r + 128] = jnp.broadcast_to(rstd, (128, 128))
            low_two[r:r + 128] = (n * gain_two + shift_two).astype(BF16)
        grad_two[...] = jnp.zeros_like(grad_two)

    def some_tiles(first, last):
        lax.fori_loop(first * tiles // 4, last * tiles // 4, one_tile, 0)

    grad_links, own_do = [], []

    def branch():
        yb[...] = hidden[...].astype(BF16)
        local(yb, y_out)
        for r in range(0, tokens, 128):
            rows = slice(r, r + 128)
            back = norm_back(n_two[rows], r_two[rows, 0:1], grad_two[rows] * gain_two)
            grad = f32(gout2[rows]) + back
            hidden[rows] = grad
            gb2[rows] = grad.astype(BF16)
        load_out.wait()
        pending["branch",] = [to_sibling(gb2.at[0:tokens], gb2.at[tokens:2 * tokens], 12)]
        for r in range(0, width, 512):
            grad = dot_nt(gb2[0:tokens], wo_v[r // 128:r // 128 + 4].reshape(512, width)).astype(BF16)
            gab[:, :, r:r + 512] = grad.reshape(streams, tok_rows, 512)
        for b in range(streams):
            out = []
            for k in range(1, n_seq):
                other = lax.rem(sq + k, n_seq)
                source = lax.rem(sq + n_seq - k, n_seq)
                src = gab.at[b, :, pl.ds(pl.multiple_of(other * 128, 128), 128)]
                dst = do.at[b, pl.ds(pl.multiple_of(sq * tok_rows, tok_rows), tok_rows), :]
                land = do.at[b, pl.ds(pl.multiple_of(source * tok_rows, tok_rows), tok_rows), :]
                out.append(keep(Link(src, dst, land, (o_send, o_recv), b * 7 + k - 1, (dp, other))))
            grad_links.append(out)
        copy_xh.append(local(xh_ref.at[:, :, cols:width], wu_t))
        own_do.extend(
            local(
                gab.at[b, :, pl.ds(pl.multiple_of(sq * 128, 128), 128)],
                do.at[b, pl.ds(pl.multiple_of(sq * tok_rows, tok_rows), tok_rows), :],
            )
            for b in range(streams)
        )
        pgp[...] = jnp.zeros_like(pgp)
        pgp[2:3, :] = jnp.sum(grad_two[...] * n_two[...], axis=0, keepdims=True)
        pgp[3:4, :] = jnp.sum(grad_two[...], axis=0, keepdims=True)

    def up_plane(p):
        if "up" not in begun:
            begun.append("up")
            for key in ("attn", "norm", "branch"):
                wait(key)

            def wait_tile(i):
                tile_link(i).wait()
            loop(tiles, wait_tile)
        up_terms(plane_of[p])

    step = 256
    blocks = total // q_block

    def turn(j):
        b, r = j // (total // step), j % (total // step)
        row = pl.ds(pl.multiple_of(r * step, step), step)
        kt[b, :, row] = jnp.transpose(f32(qkv[b, row, 128:256])).astype(BF16)
    def keys_turned():
        for copy in copies:
            copy.wait()
        loop(streams * (total // step), turn)


    def prepare(b):
        own_do[b].wait()
        for link in grad_links[b]:
            link.wait()

        def one(r):
            row = pl.ds(pl.multiple_of(r * step, step), step)
            both = jnp.transpose(f32(do[b, row, :])) * ot[b, :, row]
            for h in range(2):
                delta[h:h + 1, row] = jnp.sum(both[h * 64:(h + 1) * 64], axis=0, keepdims=True)
        loop(total // step, one)
        dk[...] = jnp.zeros_like(dk)
        dv[...] = jnp.zeros_like(dv)

    tile = 256

    def attend(b, qb):
        row = pl.ds(pl.multiple_of(qb * q_block, q_block), q_block)
        lane = lax.broadcasted_iota(jnp.int32, (q_block, 128), 1)
        queries, grads = qkv[b, row, 0:128], do[b, row, :]
        none = jnp.zeros_like(queries)
        own = [jnp.where((lane < 64) == (h == 0), queries, none) for h in range(2)]
        own_grad = [jnp.where((lane < 64) == (h == 0), grads, none) for h in range(2)]
        part = [jnp.zeros((64, q_block), F32)] * 2
        for r in range(total // tile):
            keys = slice(r * tile, (r + 1) * tile)
            gap = distance(len_ref, b, r * tile, tile, qb * q_block, q_block)
            grad_v = grad_k = 0
            for h in range(2):
                s = dot_nt(qkv[b, keys, 128:256], own[h]) - slopes[h] * gap
                p = jnp.exp(s - lse[b, h:h + 1, row])
                gp_t = dot_nt(qkv[b, keys, 256:384], own_grad[h])
                ds = (p * (gp_t - delta[h:h + 1, row])).astype(BF16)
                grad_v = grad_v + dot_nn(p.astype(BF16), own_grad[h])
                grad_k = grad_k + dot_nn(ds, own[h])
                part[h] = part[h] + dot_nn(kt[b, h * 64:(h + 1) * 64, keys], ds)
            dv[keys, :] += grad_v
            dk[keys, :] += grad_k
        for h in range(2):
            dqt[h * 64:(h + 1) * 64, row] = part[h] * 0.125

    def attend_some(b, first, last):
        def one(qb, carry):
            attend(b, qb)
            return carry
        lax.fori_loop(first, last, one, 0)

    def gs(b):
        return wo_v.at[b * nz:(b + 1) * nz]

    def gz(b, step):
        return wd_t.at[b, step]

    def finish_stream(b):
        def one(r):
            row = pl.ds(pl.multiple_of(r * step, step), step)
            low = dqt[:, row].astype(BF16)
            dqkvt[b, 0:128, row] = low
            dqkv[row, 0:128] = jnp.transpose(f32(low)).astype(BF16)
            for first, grad in ((128, dk), (256, dv)):
                low = grad[row, :].astype(BF16)
                dqkv[row, first:first + 128] = low
                dqkvt[b, first:first + 128, row] = jnp.transpose(f32(low)).astype(BF16)
        loop(total // step, one)

        def product(s):
            row = pl.ds(pl.multiple_of(s * tok_rows, tok_rows), tok_rows)
            gp[b, s // 2, s % 2] = dot_nn(dqkv[row, :], wt[...]).astype(BF16)
        loop(n_seq, product)
        pending[("gc", b)] = [
            keep(Link(gp.at[b, :, 1 - c], gs(b), gs(b), (zg_send, zg_recv), b * 4, sibling))
        ]

    def g_one(b, step, target):
        pending[("g", b, step)] = [
            keep(Link(gp.at[b, plane_of[step], c], gz(b, step), gz(b, step), (zg_send, zg_recv), b * 4 + 1 + step, target))
        ]

    def g_first(b):
        wait("gc", b)

        def add(j):
            gp[b, j, c] = (f32(gp[b, j, c]) + f32(wo_v[b * nz + j])).astype(BF16)
        loop(nz, add)
        g_one(b, 0, near_dev)
        g_one(b, 2, near_dev)

    def g_second(b):
        wait("g", b, 0)
        gp[b, z2, c] = (f32(gp[b, z2, c]) + f32(gz(b, 0)[...])).astype(BF16)
        g_one(b, 1, far_dev)

    def g_last(b):
        wait("g", b, 1)
        wait("g", b, 2)
        own = f32(gp[b, z, c]) + f32(gz(b, 1)[...]) + f32(gz(b, 2)[...])
        rows = slice(b * tok_rows, (b + 1) * tok_rows)
        n, rstd = norm_parts(f32(x_ref[rows]))
        low_two[rows] = (hidden[rows] + norm_back(n, rstd, own * vector(0))).astype(BF16)
        local(low_two.at[rows], gx_out.at[b])

    rows_dp = 32 * n_seq

    def weight_grad():
        for copy in copy_xh:
            copy.wait()
        sums = jnp.sum(f32(dqkvt[0]), axis=1, keepdims=True)
        for b in range(1, streams):
            sums = sums + jnp.sum(f32(dqkvt[b]), axis=1, keepdims=True)
        gain, shift = vector(0), vector(1)
        for r in range(width // step):
            cols = slice(r * step, (r + 1) * step)
            weight = f32(wt[:, cols])
            n = xh if r < 2 else wu_t
            there = slice(r % 2 * step, (r % 2 + 1) * step)
            raw = dot_nn(dqkvt[0], n[0, :, there])
            for b in range(1, streams):
                raw = raw + dot_nn(dqkvt[b], n[b, :, there])
            pgp[0:1, cols] = jnp.sum(raw * weight, axis=0, keepdims=True)
            pgp[1:2, cols] = jnp.sum(sums * weight, axis=0, keepdims=True)
            grad = raw * gain[:, cols] + sums * shift[:, cols]
            dqkv[cols, :] = jnp.transpose(grad).astype(BF16)
        out = []
        for m in range(1, n_dp):
            other = lax.rem(dp + m, n_dp)
            src = dqkv.at[pl.ds(pl.multiple_of(other * rows_dp, rows_dp), rows_dp), :]
            out.append(keep(Link(src, dqr.at[m - 1], dqr.at[m - 1], (s_send, s_recv), m - 1, (other, sq))))
            src = pgp.at[:, pl.ds(pl.multiple_of(other * rows_dp, rows_dp), rows_dp)]
            out.append(keep(Link(src, pr1.at[m - 1], pr1.at[m - 1], (s_send, s_recv), 3 + m - 1, (other, sq))))
        pending["qd",] = out

    def weight_grad_two():
        wait("qd")
        mine = pl.ds(pl.multiple_of(dp * rows_dp, rows_dp), rows_dp)
        part = f32(dqkv[mine, :])
        small = pgp[:, mine]
        for m in range(n_dp - 1):
            part = part + f32(dqr[m])
            small = small + pr1[m]
        dqsum[...] = part.astype(BF16)
        psum[...] = small
        out = []
        for k in range(1, n_seq):
            other = lax.rem(sq + k, n_seq)
            source = lax.rem(sq + n_seq - k, n_seq)
            src = dqsum.at[pl.ds(pl.multiple_of(other * 32, 32), 32), :]
            out.append(keep(Link(src, gq_out.at[sq], gq_out.at[source], (s_send, s_recv), 6 + k - 1, (dp, other))))
            src = psum.at[:, pl.ds(pl.multiple_of(other // 4 * 128, 128), 128)]
            out.append(keep(Link(src, pr2.at[k - 1], pr2.at[k - 1], (s_send, s_recv), 13 + k - 1, (dp, other))))
        local(dqsum.at[pl.ds(pl.multiple_of(sq * 32, 32), 32), :], gq_out.at[sq])
        pending["qs",] = out

    def weight_grad_last():
        wait("qs")
        small = psum[:, pl.ds(pl.multiple_of(sq // 4 * 128, 128), 128)]
        for k in range(n_seq - 1):
            small = small + pr2[k]
        pgo[...] = small
        local(pgo, pg_out)

    def first_frames():
        keys_turned()
        prepare(0)

    def first_done():
        def sent(i):
            tile_link(i).wait_sent()
        loop(tiles, sent)
        finish_stream(0)

    steps = {
        "pkA": pick_attn, "pkN": pick_norm,
        "LN": second_norm, "LNB": branch,
        "P0": first_frames, "P1": functools.partial(prepare, 1),
        "F0": first_done, "F1": functools.partial(finish_stream, 1),
        "WG": weight_grad, "W2": weight_grad_two, "W3": weight_grad_last,
    }
    for name, action in (("gf", g_first), ("gs", g_second), ("gl", g_last)):
        for b in range(streams):
            steps[name + str(b)] = functools.partial(action, b)
    for p in range(nz):
        steps["DT%d" % p] = functools.partial(down_plane, p)
        steps["UT%d" % p] = functools.partial(up_plane, p)
    for letter, g in (("U", U), ("D", D)):
        for name, action in (("zf", z_first), ("zs", z_second), ("zt", z_third), ("zl", z_last)):
            steps[name + letter] = functools.partial(action, g)
        for p in range(nz):
            steps["c1%s%d" % (letter, p)] = functools.partial(cross_one, g, p)
            steps["c2%s%d" % (letter, p)] = functools.partial(cross_two, g, p)
    for name, first, last in runs(scatter_order, ("A0", "A1", "T")):
        if name in ("A0", "A1"):
            attend_some(int(name[1]), first, last)
        elif name == "T":
            some_tiles(first, last)
        else:
            steps[name]()
    for key in pending:
        wait(*key)
    waited = [load_cot, load_act, load_hid, load_attn, load_out, *copy_xh, *own_do, *copies]
    for copy in locals_:
        if not any(copy is other for other in waited):
            copy.wait()
    for link in links:
        link.wait_sent()


def scatter_call(
    inputs, cotangent, infill, attn, hidden, act, bend, params, weights, qkv, ot, lse, xh, wt, lengths,
):
    streams, total = qkv.shape[:2]
    tokens, width = inputs.shape
    tok_rows = tokens // streams
    n_seq, n_dp = lax.axis_size("seq"), lax.axis_size("dp")
    nz = n_seq // 2
    cols = qkv.shape[2]
    any_space = pl.BlockSpec(memory_space=pl.ANY)
    vmem = pl.BlockSpec(memory_space=pltpu.VMEM)
    smem = pl.BlockSpec(memory_space=pltpu.SMEM)
    dma = pltpu.SemaphoreType.DMA
    sizes = [(w.shape[0] // (2 * n_dp * n_seq), w.shape[1]) for w in weights]
    tile = weights[1].shape[1] // 8

    def buffers(*lead):
        return [pltpu.VMEM(lead + size, BF16) for size in sizes]

    def low(*shape):
        return pltpu.VMEM(shape, BF16)

    def full(*shape):
        return pltpu.VMEM(shape, F32)

    half = width // 2 // nz
    scratch = [
        full(tokens, width), full(tokens, width), full(tokens, 128), low(tokens, width), full(tokens, width),
        low(tokens, width), low(2 * tokens, width), low(2 * tokens, width),
        low(*act.shape), low(act.shape[0], tokens, 128), low(2, *bend.shape[1:]),
        low(nz, 2 * tokens, half), low(nz, tokens, half), low(nz, 2 * tokens, half), low(nz, tokens, half),
        low(width // 128, 128, width), low(2, width, tile), low(2, tile // 128, 128, width), low(streams, tok_rows, width),
    ]
    scratch += buffers(2, 2, nz, 2) + buffers(nz, 2) + buffers(nz, 2) + buffers(nz) + buffers(nz)
    scratch += buffers(nz - 1, 2)
    scratch += [pltpu.VMEM((2,) + size, F32) for size in sizes]
    scratch += [
        low(streams, total, 128), low(*qkv.shape), full(*ot.shape), full(*lse.shape), low(streams, total, tile), low(*wt.shape),
        low(streams, 128, total), full(8, total), full(total, 128), full(total, 128),
        full(128, total), low(total, cols), low(streams, cols, total),
        low(streams, nz, 2, tok_rows, width),
        low(n_dp - 1, width // n_dp, cols), low(width // n_dp, cols),
        full(8, width), full(n_dp - 1, 8, width // n_dp), full(8, width // n_dp), full(n_seq - 1, 8, 128), full(8, 128),
        dma((13,)), dma((13,)), dma((14,)), dma((14,)), dma((48,)), dma((48,)), dma((9,)), dma((9,)),
        dma((8,)), dma((8,)), dma((20,)), dma((20,)), dma((9, 2)), dma((24,)),
    ]
    outs = [
        jax.ShapeDtypeStruct((tokens, width), BF16),
        jax.ShapeDtypeStruct((streams, tok_rows, width), BF16),
        *[jax.ShapeDtypeStruct((2,) + size, F32) for size in sizes],
        jax.ShapeDtypeStruct((n_seq, width // (n_dp * n_seq), cols), BF16),
        jax.ShapeDtypeStruct((8, 128), F32),
    ]
    return pl.pallas_call(
        scatter_kernel,
        out_shape=outs,
        in_specs=[vmem] * 3 + [any_space] * 13 + [smem],
        out_specs=[any_space] * len(outs),
        scratch_shapes=scratch,
        compiler_params=pltpu.CompilerParams(
            collective_id=1, has_side_effects=True, vmem_limit_bytes=63 * 2**20
        ),
        name="scatter_attend",
    )(
        inputs, infill, params, cotangent, attn, hidden, act, bend, weights[0].reshape(-1, 128, width), weights[1],
        weights[2].reshape(-1, 128, width), qkv, ot, lse, xh, wt, lengths,
    )


def finish_kernel(*refs):
    n = 6
    parts, outs, held, wide, sems = refs[:n], refs[n:2 * n], refs[2 * n:3 * n], refs[3 * n], refs[3 * n + 1]
    loads = [pltpu.make_async_copy(src, dst, sems.at[i]) for i, (src, dst) in enumerate(zip(parts, held))]
    sources = (*held[:-1], wide)
    stores = [pltpu.make_async_copy(src, dst, sems.at[n + i]) for i, (src, dst) in enumerate(zip(sources, outs))]
    for load in reversed(loads):
        load.start()
    loads[-1].wait()
    gq = held[-1]
    width = wide.shape[1] // 3
    for q in range(gq.shape[0]):
        for j in range(3):
            wide[:, j * width + q * 128:j * width + (q + 1) * 128] = gq[q, :, j * 128:(j + 1) * 128].astype(F32)
    stores[-1].start()
    for load, store in zip(loads[:-1], stores[:-1]):
        load.wait()
        store.start()
    for store in stores:
        store.wait()


def finish_call(*parts):
    gq = parts[-1]
    hbm = pl.BlockSpec(memory_space=pltpu.HBM)
    outs = [jax.ShapeDtypeStruct(part.shape, part.dtype) for part in parts[:-1]]
    outs.append(jax.ShapeDtypeStruct((gq.shape[1], gq.shape[0] * gq.shape[2]), F32))
    return pl.pallas_call(
        finish_kernel,
        out_shape=outs,
        in_specs=[hbm] * len(parts),
        out_specs=[hbm] * len(outs),
        scratch_shapes=[pltpu.VMEM(part.shape, part.dtype) for part in parts]
        + [pltpu.VMEM(outs[-1].shape, F32), pltpu.SemaphoreType.DMA((2 * len(outs),))],
        compiler_params=pltpu.CompilerParams(vmem_limit_bytes=63 * 2**20),
        name="finish",
    )(*parts)


def by_heads(
    inputs, lengths, infill, cotangent, w_qkv, w_out, w_up, w_down,
    gain_one, shift_one, gain_two, shift_two,
):
    streams, tok_rows, width = inputs.shape
    n_seq = lax.axis_size("seq")
    sq = lax.axis_index("seq")
    stream_len, tokens = tok_rows * n_seq, streams * tok_rows
    own_rows = w_qkv.shape[0]
    vectors = jnp.tile(jnp.stack([gain_one, shift_one, gain_two, shift_two]), (1, 128 // own_rows))
    (
        full_out, full_up, full_down, params, attn, qkv, ot, lse, xh, wt, hidden, act, bend
    ) = gather_call(inputs, w_qkv, w_out, w_up, w_down, vectors, lengths)
    weights = (
        full_out.reshape(width, width), full_up.reshape(width, -1), full_down.reshape(-1, width)
    )
    output, input_grad, grad_out, grad_up, grad_down, grad_qkv, small = scatter_call(
        inputs.reshape(tokens, width), cotangent,
        infill, attn.reshape(tokens, width), hidden, act, bend,
        params, weights,
        qkv, ot, lse, xh.reshape(streams, stream_len, width), wt, lengths,
    )
    output, input_grad, grad_out, grad_up, grad_down, grad_qkv = finish_call(
        output, input_grad, grad_out, grad_up, grad_down, grad_qkv
    )
    small = lax.dynamic_slice(small, (0, sq % (128 // own_rows) * own_rows), (4, own_rows))
    return (
        output.reshape(inputs.shape),
        input_grad,
        grad_qkv,
        grad_out.reshape(w_out.shape),
        grad_up.reshape(w_up.shape),
        grad_down.reshape(w_down.shape),
        small[0], small[1], small[2], small[3],
    )


def layer_norm(features, gain_vec, shift_vec):
    row_mean = jnp.mean(features, axis=-1, keepdims=True)
    centered = features - row_mean
    spread = jnp.mean(centered * centered, axis=-1, keepdims=True)
    return centered * lax.rsqrt(spread + norm_eps) * gain_vec + shift_vec


def segment_of(bounds, positions):
    return jnp.sum((positions[None, :, None] >= bounds[:, None, :]).astype(jnp.int32), axis=2)


def slope_table(head_count, stream_len):
    return 2.0 ** (-8.0 * (jnp.arange(head_count, dtype=jnp.float32) + 1.0) / head_count) * (
        256.0 / stream_len
    )


def block_scores(queries, key_heads, query_pos, key_pos, query_seg, key_seg, slopes):
    raw_scores = jnp.einsum(
        "sqhc,skhc->shqk", queries, key_heads, preferred_element_type=jnp.float32
    )
    distance = jnp.abs(query_pos[:, None] - key_pos[None, :]).astype(jnp.float32)
    scores = (
        raw_scores * queries.shape[3] ** (-0.5) - slopes[None, :, None, None] * distance[None, None]
    )
    same_utt = query_seg[:, None, :, None] == key_seg[:, None, None, :]
    return jnp.where(same_utt, scores, masked_score)


def score_grads(
    queries,
    grad_heads,
    log_total,
    delta,
    key_heads,
    values,
    query_pos,
    key_pos,
    query_seg,
    key_seg,
    slopes,
):
    scores = block_scores(queries, key_heads, query_pos, key_pos, query_seg, key_seg, slopes)
    probs = jnp.exp(scores - log_total[..., None])
    grad_probs = jnp.einsum(
        "sqhc,skhc->shqk", grad_heads, values, preferred_element_type=jnp.float32
    )
    grad_scores = (probs * (grad_probs - delta[..., None])).astype(jnp.bfloat16)
    return (probs.astype(jnp.bfloat16), grad_scores)


def by_frames(
    inputs,
    lengths,
    infill,
    cotangent,
    w_qkv,
    w_out,
    w_up,
    w_down,
    gain_one,
    shift_one,
    gain_two,
    shift_two,
):
    w_qkv, w_out, w_up, w_down, gain_one, shift_one, gain_two, shift_two = (
        lax.all_gather(w_qkv, ("dp", "seq"), axis=0, tiled=True),
        lax.all_gather(w_out, ("dp", "seq"), axis=0, tiled=True),
        lax.all_gather(w_up, ("dp", "seq"), axis=0, tiled=True),
        lax.all_gather(w_down, ("dp", "seq"), axis=0, tiled=True),
        lax.all_gather(gain_one, ("dp", "seq"), axis=0, tiled=True),
        lax.all_gather(shift_one, ("dp", "seq"), axis=0, tiled=True),
        lax.all_gather(gain_two, ("dp", "seq"), axis=0, tiled=True),
        lax.all_gather(shift_two, ("dp", "seq"), axis=0, tiled=True),
    )
    streams, tok_rows, model_width = inputs.shape
    head_count = HEADS
    head_size = HEAD_DIM
    stream_len = tok_rows * lax.axis_size("seq")
    score_scale = head_size ** (-0.5)
    slopes = slope_table(head_count, stream_len)
    bounds = jnp.cumsum(lengths, axis=1)
    own_pos = lax.axis_index("seq") * tok_rows + jnp.arange(tok_rows, dtype=jnp.int32)
    own_seg = segment_of(bounds, own_pos)
    gain_one_f = gain_one.astype(jnp.float32)
    shift_one_f = shift_one.astype(jnp.float32)
    gain_two_f = gain_two.astype(jnp.float32)
    shift_two_f = shift_two.astype(jnp.float32)
    inputs_f = inputs.astype(jnp.float32)
    normed_one = layer_norm(inputs_f, gain_one_f, shift_one_f).astype(jnp.bfloat16)
    packed = jnp.einsum(
        "std,de->ste", normed_one, w_qkv, preferred_element_type=jnp.float32
    ).astype(jnp.bfloat16)
    query_low = packed[:, :, :model_width]
    key_value = packed[:, :, model_width:]
    query_heads = query_low.reshape(streams, tok_rows, head_count, head_size)
    start_state = (
        jnp.full((streams, head_count, tok_rows), masked_score, jnp.float32),
        jnp.zeros((streams, head_count, tok_rows), jnp.float32),
        jnp.zeros((streams, head_count, tok_rows, head_size), jnp.float32),
    )
    shard_piece = lax.all_gather(key_value, "seq", axis=1, tiled=True)
    key_count = shard_piece.shape[1]
    visit_block_len = 256

    def one_block(carried, offset):
        top_score, weight_sum, weighted = carried
        key_part = lax.dynamic_slice_in_dim(shard_piece, offset, visit_block_len, 1)
        key_pos = offset + jnp.arange(visit_block_len, dtype=jnp.int32)
        key_seg = segment_of(bounds, key_pos)
        key_heads = key_part[:, :, :model_width].reshape(
            streams, visit_block_len, head_count, head_size
        )
        values = key_part[:, :, model_width:].reshape(
            streams, visit_block_len, head_count, head_size
        )
        scores = block_scores(query_heads, key_heads, own_pos, key_pos, own_seg, key_seg, slopes)
        new_top = jnp.maximum(top_score, jnp.max(scores, axis=3))
        rescale = jnp.exp(top_score - new_top)
        weights_blk = jnp.exp(scores - new_top[..., None])
        weight_sum = weight_sum * rescale + jnp.sum(weights_blk, axis=3)
        weighted = weighted * rescale[..., None] + jnp.einsum(
            "shqk,skhc->shqc",
            weights_blk.astype(jnp.bfloat16),
            values,
            preferred_element_type=jnp.float32,
        )
        return ((new_top, weight_sum, weighted), None)

    offsets = jnp.arange(key_count // visit_block_len, dtype=jnp.int32) * visit_block_len
    finished, _ = lax.scan(one_block, start_state, offsets)
    top_score, weight_sum, weighted = finished
    attn_heads = weighted / weight_sum[..., None]
    log_total = top_score + jnp.log(weight_sum)
    attn_rows = jnp.transpose(attn_heads, (0, 2, 1, 3)).reshape(streams, tok_rows, model_width)
    attn_low = attn_rows.astype(jnp.bfloat16)
    hidden = inputs_f + jnp.einsum(
        "std,de->ste", attn_low, w_out, preferred_element_type=jnp.float32
    )
    normed_two_f, ln_two_pull = jax.vjp(layer_norm, hidden, gain_two_f, shift_two_f)
    normed_two = normed_two_f.astype(jnp.bfloat16)
    upward = jnp.einsum("std,df->stf", normed_two, w_up, preferred_element_type=jnp.float32)
    active_f, gelu_pull = jax.vjp(jax.nn.gelu, upward)
    active = active_f.astype(jnp.bfloat16)
    output = (
        hidden + jnp.einsum("stf,fd->std", active, w_down, preferred_element_type=jnp.float32)
    ).astype(jnp.bfloat16)
    grad_output = (cotangent.astype(jnp.float32) * infill.astype(jnp.float32)[:, :, None]).astype(
        jnp.bfloat16
    )
    grad_active = jnp.einsum("ste,fe->stf", grad_output, w_down, preferred_element_type=jnp.float32)
    grad_upward = gelu_pull(grad_active)[0].astype(jnp.bfloat16)
    grad_norm_two = jnp.einsum("stf,df->std", grad_upward, w_up, preferred_element_type=jnp.float32)
    grad_in_two, grad_gain_two, grad_shift_two = ln_two_pull(grad_norm_two)
    grad_hidden = grad_output.astype(jnp.float32) + grad_in_two
    grad_branch = grad_hidden.astype(jnp.bfloat16)
    grad_attn = jnp.einsum(
        "ste,de->std", grad_branch, w_out, preferred_element_type=jnp.float32
    ).astype(jnp.bfloat16)
    grad_heads = grad_attn.reshape(streams, tok_rows, head_count, head_size)
    delta = jnp.einsum("sqhc,shqc->shq", grad_heads.astype(jnp.float32), attn_heads)
    every_kv = lax.all_gather(key_value, "seq", axis=1, tiled=True)
    total_len = every_kv.shape[1]
    block_len = 256
    offsets = jnp.arange(total_len // block_len, dtype=jnp.int32) * block_len
    grad_start = jnp.zeros((streams, tok_rows, head_count, head_size), jnp.float32)

    def key_step(grad_query, offset):
        key_part = lax.dynamic_slice_in_dim(every_kv, offset, block_len, 1)
        key_pos = offset + jnp.arange(block_len, dtype=jnp.int32)
        key_seg = segment_of(bounds, key_pos)
        key_heads = key_part[:, :, :model_width].reshape(streams, block_len, head_count, head_size)
        values = key_part[:, :, model_width:].reshape(streams, block_len, head_count, head_size)
        probs_low, grad_scores = score_grads(
            query_heads,
            grad_heads,
            log_total,
            delta,
            key_heads,
            values,
            own_pos,
            key_pos,
            own_seg,
            key_seg,
            slopes,
        )
        grad_query = (
            grad_query
            + jnp.einsum(
                "shqk,skhc->sqhc", grad_scores, key_heads, preferred_element_type=jnp.float32
            )
            * score_scale
        )
        grad_keys = (
            jnp.einsum(
                "shqk,sqhc->kshc", grad_scores, query_heads, preferred_element_type=jnp.float32
            )
            * score_scale
        )
        grad_values = jnp.einsum(
            "shqk,sqhc->kshc", probs_low, grad_heads, preferred_element_type=jnp.float32
        )
        key_terms = jnp.concatenate(
            [
                grad_keys.reshape(block_len, streams, model_width),
                grad_values.reshape(block_len, streams, model_width),
            ],
            axis=2,
        )
        return (grad_query, key_terms)

    grad_query, key_terms = lax.scan(key_step, grad_start, offsets)
    key_terms = key_terms.reshape(total_len, streams, 2 * model_width)
    own_kv_grad = lax.psum_scatter(
        key_terms.astype(jnp.bfloat16), "seq", scatter_dimension=0, tiled=True
    ).astype(jnp.float32)
    grad_kv = jnp.transpose(own_kv_grad, (1, 0, 2))
    grad_packed = jnp.concatenate(
        [grad_query.reshape(streams, tok_rows, model_width), grad_kv], axis=2
    ).astype(jnp.bfloat16)
    grad_norm_one = jnp.einsum(
        "ste,de->std", grad_packed, w_qkv, preferred_element_type=jnp.float32
    )
    _, ln_one_pull = jax.vjp(layer_norm, inputs_f, gain_one_f, shift_one_f)
    grad_in_one, grad_gain_one, grad_shift_one = ln_one_pull(grad_norm_one)
    input_grad = (grad_hidden + grad_in_one).astype(jnp.bfloat16)
    weight_terms = (
        jnp.einsum("std,ste->de", normed_one, grad_packed, preferred_element_type=jnp.float32),
        jnp.einsum("std,ste->de", attn_low, grad_branch, preferred_element_type=jnp.float32),
        jnp.einsum("std,stf->df", normed_two, grad_upward, preferred_element_type=jnp.float32),
        jnp.einsum("stf,std->fd", active, grad_output, preferred_element_type=jnp.float32),
        grad_gain_one,
        grad_shift_one,
        grad_gain_two,
        grad_shift_two,
    )
    summed = (
        lax.psum_scatter(weight_terms[0], ("dp", "seq"), scatter_dimension=0, tiled=True),
        lax.psum_scatter(weight_terms[1], ("dp", "seq"), scatter_dimension=0, tiled=True),
        lax.psum_scatter(weight_terms[2], ("dp", "seq"), scatter_dimension=0, tiled=True),
        lax.psum_scatter(weight_terms[3], ("dp", "seq"), scatter_dimension=0, tiled=True),
        lax.psum_scatter(weight_terms[4], ("dp", "seq"), scatter_dimension=0, tiled=True),
        lax.psum_scatter(weight_terms[5], ("dp", "seq"), scatter_dimension=0, tiled=True),
        lax.psum_scatter(weight_terms[6], ("dp", "seq"), scatter_dimension=0, tiled=True),
        lax.psum_scatter(weight_terms[7], ("dp", "seq"), scatter_dimension=0, tiled=True),
    )
    return (
        output,
        input_grad,
        summed[0],
        summed[1],
        summed[2],
        summed[3],
        summed[4],
        summed[5],
        summed[6],
        summed[7],
    )


def solution(mesh):
    in_specs = (
        P("dp", "seq", None),
        P("dp", None),
        P("dp", "seq"),
        P("dp", "seq", None),
        P(("dp", "seq"), None),
        P(("dp", "seq"), None),
        P(("dp", "seq"), None),
        P(("dp", "seq"), None),
        P(("dp", "seq")),
        P(("dp", "seq")),
        P(("dp", "seq")),
        P(("dp", "seq")),
    )
    out_specs = (
        P("dp", "seq", None),
        P("dp", "seq", None),
        P(("dp", "seq"), None),
        P(("dp", "seq"), None),
        P(("dp", "seq"), None),
        P(("dp", "seq"), None),
        P(("dp", "seq")),
        P(("dp", "seq")),
        P(("dp", "seq")),
        P(("dp", "seq")),
    )
    grid = (mesh.shape["dp"], mesh.shape["seq"])
    local = by_heads if grid == (4, HEADS // 2) else by_frames
    return jax.shard_map(local, mesh=mesh, in_specs=in_specs, out_specs=out_specs, check_vma=False)
```

```python
import functools

import jax
import jax.numpy as jnp
from jax import lax
from jax.experimental import pallas as pl
from jax.experimental.pallas import tpu as pltpu

from jax.sharding import PartitionSpec as P

HEADS = 16
HEAD_DIM = 64

norm_eps = 1e-05
masked_score = -1e30
MESH_ID = pl.DeviceIdType.MESH
F32 = jnp.float32
BF16 = jnp.bfloat16
far = 1e33
gather_order = (
    "zh02", "xs", "zh11", "x110", "x210", "x100", "xh2", "zh01", "cc10", "x200", "xh1", "x111",
    "seq", "x102", "x211", "zh03", "x202", "wq", "xp2", "x101", "cc00", "xh3", "wt", "xp1", "p0",
    "x103", "p2", "cc11", "p1", "x203", "zh12", "xp3", "x201", "p3", "vt", "a0", "a1", "zh13",
    "a2", "x112", "cc03", "a3", "a4", "o0", "a5", "a6", "x212", "cc02", "x113", "cc01", "a7", "o1",
    "c0", "h0", "x213", "h1", "u0", "cc12", "u1", "cc13", "u2", "u3",
)
scatter_order = (
    "DT0", "c1D0", "pkA", "LN", "DT1", "T0", "c1D1", "DT2", "c2D0", "T1", "T2", "c1D2", "T3",
    "zfD", "LNB", "pkN", "c2D1", "c2D2", "UT0", "c1U0", "UT2", "UT3", "UT1", "ztD", "zsD", "P0",
    "A00", "c2U0", "A01", "A02", "c1U1", "A03", "zfU", "F0", "P1", "A10", "gf0", "c2U1", "A11",
    "A12", "c1U3", "zsU", "A13", "F1", "WG", "c1U2", "gf1", "gs0", "c2U2", "DT3", "W2", "c1D3",
    "ztU", "gs1", "c2D3", "W3", "gl0", "c2U3", "zlD", "gl1", "zlU",
)
q_block = 256


def place():
    dp, sq = lax.axis_index("dp"), lax.axis_index("seq")
    return dp, sq, dp // 2, dp % 2, sq // 2, sq % 2


def planes(z, nz):
    z1 = z + 1 - 2 * (z % 2)
    return z1, (z + 2) % nz, (z1 + 2) % nz


def dot_nt(a, b):
    return lax.dot_general(a, b, (((1,), (1,)), ((), ())), preferred_element_type=F32)


def dot_nn(a, b):
    return lax.dot_general(a, b, (((1,), (0,)), ((), ())), preferred_element_type=F32)


def runs(order, counted):
    out = []
    for name in order:
        kind = name[:-1]
        if kind in counted:
            number = int(name[-1])
            if out and out[-1][0] == kind and out[-1][2] == number:
                out[-1] = (kind, out[-1][1], number + 1)
            else:
                out.append((kind, number, number + 1))
        else:
            out.append((name, 0, 0))
    return out


class Link:
    def __init__(self, src, dst, landing, sems, index, target, when_send=None, when_recv=None):
        self.sems, self.index, self.target = sems, index, target
        self.src, self.dst, self.landing = src, dst, landing
        self.when_send, self.when_recv = when_send, when_recv

    def copy(self, src, dst):
        send, recv = self.sems
        return pltpu.make_async_remote_copy(
            src_ref=src,
            dst_ref=dst,
            send_sem=send.at[self.index],
            recv_sem=recv.at[self.index],
            device_id=self.target,
            device_id_type=MESH_ID,
        )

    def run(self, when, action):
        if when is None:
            action()
        else:
            pl.when(when)(action)

    def start(self):
        self.run(self.when_send, lambda: self.copy(self.src, self.dst).start())

    def wait(self):
        self.run(self.when_recv, lambda: self.copy(self.landing, self.landing).wait_recv())

    def wait_sent(self):
        self.run(self.when_send, lambda: self.copy(self.src, self.dst).wait_send())


def greet(dp, sq, n_seq, n_dp):
    barrier = pltpu.get_barrier_semaphore()
    for k in range(1, n_seq):
        pl.semaphore_signal(
            barrier, inc=1, device_id=(dp, lax.rem(sq + k, n_seq)), device_id_type=MESH_ID
        )
    for m in range(1, n_dp):
        other = lax.rem(dp + m, n_dp)
        pl.semaphore_signal(barrier, inc=1, device_id=(other, sq), device_id_type=MESH_ID)


def all_here(n_seq, n_dp):
    pl.semaphore_wait(pltpu.get_barrier_semaphore(), n_seq - 1 + n_dp - 1)


def distance(len_ref, stream, first_key, keys, first_query, queries):
    key_pos = lax.broadcasted_iota(jnp.int32, (keys, 1), 0) + first_key
    query_pos = lax.broadcasted_iota(jnp.int32, (1, queries), 1) + first_query
    key_seg = jnp.zeros((keys, 1), jnp.int32)
    query_seg = jnp.zeros((1, queries), jnp.int32)
    bound = 0
    for k in range(len_ref.shape[1]):
        bound = bound + len_ref[stream, k]
        key_seg = key_seg + (key_pos >= bound).astype(jnp.int32)
        query_seg = query_seg + (query_pos >= bound).astype(jnp.int32)
    gap = jnp.abs(key_pos - query_pos).astype(F32)
    return jnp.where(key_seg == query_seg, gap, far)


def gelu_both(v):
    square = v * v
    th = jnp.tanh(v * (0.7978845608028654 + 0.7978845608028654 * 0.044715 * square))
    half = 0.5 * (1.0 + th)
    bend = v * (0.5 - 0.5 * th * th)
    return v * half, half + bend * (0.7978845608028654 + 0.7978845608028654 * 0.134145 * square)


def norm_parts(v):
    mean = jnp.mean(v, axis=-1, keepdims=True)
    centered = v - mean
    rstd = lax.rsqrt(jnp.mean(centered * centered, axis=-1, keepdims=True) + norm_eps)
    return centered * rstd, rstd


def norm_back(n, rstd, e):
    return rstd * (
        e - jnp.mean(e, axis=-1, keepdims=True) - n * jnp.mean(e * n, axis=-1, keepdims=True)
    )


def own_slopes(sq, n_seq, total):
    out = []
    for h in range(2):
        value = 0.0
        for q in range(n_seq):
            slope = 2.0 ** (-8.0 * (2 * q + h + 1) / (2 * n_seq)) * (256.0 / total)
            value = jnp.where(sq == q, jnp.float32(slope), value)
        out.append(value)
    return out


def gather_kernel(
    x_ref, w_ref, wo_ref, wu_ref, wd_ref, vec_ref, len_ref,
    wo_all, wu_all, wd_all, par_out, attn, qkv_out, ot_out, lse_out, xh_out, wt_out, hid_out, act_out, bend_out,
    xg, xh, wqb, wt, wq_ref, par_ref, pbuf, pown, par, qkv, vt, obuf, ot, lse, dist, wo_v, wu_t, av, hid, low_two, act_v, bend_v,
    z_send, z_recv, w_send, w_recv, x_send, x_recv, s_send, s_recv, tile_sem, store_sem, loc,
):
    dp, sq, y, x, z, c = place()
    streams, tok_rows, width = x_ref.shape
    n_seq, n_dp = lax.axis_size("seq"), lax.axis_size("dp")
    nz = n_seq // 2
    total = n_seq * tok_rows
    own_rows = w_ref.shape[0]
    slopes = own_slopes(sq, n_seq, total)
    x_nbr, y_nbr = (y * 2 + (1 - x), sq), ((1 - y) * 2 + x, sq)
    sibling = (dp, z * 2 + (1 - c))
    z1, z2, z3 = planes(z, nz)
    near_dev, far_dev = (dp, z1 * 2 + c), (dp, z2 * 2 + c)
    greet(dp, sq, n_seq, n_dp)
    rank = dp * n_seq + sq
    row = lax.broadcasted_iota(jnp.int32, (8, 128), 0)
    lane = lax.broadcasted_iota(jnp.int32, (8, 128), 1)
    mine = (row == rank // 4) & ((lane >> 5) == rank % 4)
    spread = lax.broadcasted_iota(jnp.int32, (own_rows, 128), 0) == (
        lax.broadcasted_iota(jnp.int32, (own_rows, 128), 1) & (own_rows - 1)
    )
    vecs = dot_nn(vec_ref[...], spread.astype(F32).astype(BF16))
    par_ref[...] = jnp.concatenate(
        [jnp.where(mine, jnp.broadcast_to(vecs[i:i + 1], (8, 128)), 0.0) for i in range(4)], axis=0
    ).astype(BF16)
    for q in range(n_seq):
        for j in range(3):
            wq_ref[q, :, j * 128:(j + 1) * 128] = w_ref[:, j * width + q * 128:j * width + (q + 1) * 128]
    links = []

    def keep(link):
        link.start()
        links.append(link)
        return link

    locals_ = []

    def local(src, dst):
        copy = pltpu.make_async_copy(src, dst, loc.at[len(locals_)])
        copy.start()
        locals_.append(copy)
        return copy

    cp_x = local(x_ref, xg.at[:, sq])
    cp_wq = local(wq_ref.at[sq], wqb.at[pl.ds(pl.multiple_of(sq * 32 + dp * 32 * n_seq, 32), 32), :])
    cp_w = [
        local(src, dst.at[y, x, z, c])
        for src, dst in ((wo_ref, wo_all), (wu_ref, wu_all), (wd_ref, wd_all))
    ]

    arrays = [(wo_ref, wo_all), (wu_ref, wu_all), (wd_ref, wd_all)]
    groups = [(0, 1), (2,)]
    pending = {}
    every = slice(None)

    arrived = set()

    def wait(*key):
        if key not in arrived:
            arrived.add(key)
            for link in pending[key]:
                link.wait()

    where = [z, z1, z2, z3]

    def z_hop(g, h):
        out = []
        for i in groups[g]:
            own, full = arrays[i]
            there = full.at[y, x, z if h < 3 else z2, c]
            land = full.at[y, x, where[h], c]
            src = own if h < 3 else there
            target = far_dev if h == 2 else near_dev
            out.append(keep(Link(src, there, land, (w_send, w_recv), i * 3 + h - 1, target)))
        pending[("z", g, h)] = out

    def plane(tag, g, h, pairs):
        out = []
        for i in groups[g]:
            own, full = arrays[i]
            for kind, target, src_at, land_at, own_half in pairs(where[h]):
                here = full.at[src_at]
                src = own.at[own_half] if own_half is not None and h == 0 else here
                out.append(keep(Link(
                    src, here, full.at[land_at], (x_send, x_recv), (i * 4 + h) * 5 + kind, target
                )))
        pending[(tag, g, h)] = out

    def cross_one(g, h):
        plane("x1", g, h, lambda b: [
            (0, x_nbr, (y, x, b, c, 0), (y, 1 - x, b, c, 0), 0),
            (1, y_nbr, (y, x, b, c, 1), (1 - y, x, b, c, 1), 1),
        ])

    def cross_two(g, h):
        wait("x1", g, h)
        plane("x2", g, h, lambda b: [
            (2, y_nbr, (y, every, b, c, 0), (1 - y, every, b, c, 0), None),
            (3, x_nbr, (every, x, b, c, 1), (every, 1 - x, b, c, 1), None),
        ])

    def cross_core(g, h):
        wait("x2", g, h)
        plane("c", g, h, lambda b: [
            (4, sibling, (every, every, b, c), (every, every, b, 1 - c), None),
        ])

    def x_hop(h):
        there = xg.at[:, (z if h < 3 else z2) * 2 + c]
        land = xg.at[:, where[h] * 2 + c]
        target = far_dev if h == 2 else near_dev
        pending[("x", h)] = [keep(Link(x_ref if h < 3 else there, there, land, (z_send, z_recv), h - 1, target))]

    def x_pass(h):
        src = xg.at[:, where[h] * 2 + c]
        land = xg.at[:, where[h] * 2 + (1 - c)]
        pending[("xc", h)] = [keep(Link(src, src, land, (z_send, z_recv), 3 + h - 1, sibling))]

    all_here(n_seq, n_dp)
    rows_dp = 32 * n_seq

    def shard_rows(d, q):
        return wqb.at[pl.ds(pl.multiple_of((d * n_seq + q) * 32, 32), 32), :]

    def plane_rows(d):
        return wqb.at[pl.ds(pl.multiple_of(d * rows_dp, 32), rows_dp), :]

    def along_seq():
        small, wide = [], []
        for k in range(1, n_seq):
            other = lax.rem(sq + k, n_seq)
            source = lax.rem(sq + n_seq - k, n_seq)
            slot = pbuf.at[k - 1]
            small.append(keep(Link(par_ref, slot, slot, (s_send, s_recv), k - 1, (dp, other))))
            wide.append(keep(Link(
                wq_ref.at[other], shard_rows(dp, sq), shard_rows(dp, source), (s_send, s_recv), 7 + k - 1, (dp, other)
            )))
        pending["ps",], pending["ws",] = small, wide

    def along_dp():
        wait("ps")
        pown[...] = par_ref[...] + pbuf[0]
        for k in range(1, n_seq - 1):
            pown[...] += pbuf[k]
        pending["pd",] = []
        for m in range(1, n_dp):
            slot = pbuf.at[n_seq - 2 + m]
            pending["pd",].append(
                keep(Link(pown, slot, slot, (s_send, s_recv), 14 + m - 1, (lax.rem(dp + m, n_dp), sq)))
            )
        wait("ws")
        cp_wq.wait()
        pending["wd",] = []
        for m in range(1, n_dp):
            other, source = lax.rem(dp + m, n_dp), lax.rem(dp + n_dp - m, n_dp)
            pending["wd",].append(keep(Link(
                plane_rows(dp), plane_rows(dp), plane_rows(source), (s_send, s_recv), 17 + m - 1, (other, sq)
            )))

    step = 256
    rows_of = {}

    def columns():
        wait("pd")
        par[...] = pown[...] + pbuf[n_seq - 1] + pbuf[n_seq] + pbuf[n_seq + 1]
        wait("wd")
        for r in range(width // step):
            wt[:, r * step:(r + 1) * step] = jnp.transpose(
                wqb[r * step:(r + 1) * step, :].astype(F32)
            ).astype(BF16)
        local(wt, wt_out)
        local(par, par_out)

    def vector(row):
        block = par[row * 8:(row + 1) * 8, :].astype(F32)
        return jnp.concatenate([block[r:r + 1, :] for r in range(8)], axis=1)

    scale = 0.125

    def process(s):
        gain, shift = vector(0), vector(1)

        def one(b, carry):
            v = xg[b, s].astype(F32)
            mean = jnp.mean(v, axis=1, keepdims=True)
            v = v - mean
            spread = jnp.mean(v * v, axis=1, keepdims=True)
            n = v * lax.rsqrt(spread + 1e-5)
            xh[b, s] = n.astype(BF16)
            normed = (n * gain + shift).astype(BF16)
            packed = dot_nt(normed, wt[...])
            row = pl.ds(pl.multiple_of(s * tok_rows, tok_rows), tok_rows)
            qkv[b, row, 0:128] = (packed[:, 0:128] * scale).astype(BF16)
            qkv[b, row, 128:384] = packed[:, 128:384].astype(BF16)
            return carry
        lax.fori_loop(0, streams, one, 0)

    def process_hop(h):
        def one(j, carry):
            process(where[h] * 2 + j)
            return carry
        lax.fori_loop(0, 2, one, 0)

    def turn(j, carry):
        b, r = j // (total // step), j % (total // step)
        row = pl.ds(pl.multiple_of(r * step, step), step)
        vt[b, :, row] = jnp.transpose(qkv[b, row, 256:384].astype(F32)).astype(BF16)
        return carry
    def values():
        local(xh, xh_out)
        local(qkv, qkv_out)
        lax.fori_loop(0, streams * (total // step), turn, 0)

    blocks = total // q_block
    cols = bend_v.shape[2]
    tiles = bend_v.shape[0]

    def tile_copies(i):
        cut = pl.ds(pl.multiple_of(i * cols, cols), cols)
        return [
            pltpu.make_async_copy(
                wu_all.at[part // 2, part % 2, :, :, :, :, cut], wu_t.at[i, part // 2, part % 2], tile_sem.at[i, part]
            )
            for part in range(4)
        ]

    def tile_stores(i):
        return (
            pltpu.make_async_copy(act_v.at[pl.ds(i * 2, 2)], act_out.at[pl.ds(i * 2, 2)], store_sem.at[i, 0]),
            pltpu.make_async_copy(bend_v.at[i], bend_out.at[i], store_sem.at[i, 1]),
        )


    def attend(j, carry):
        b, qb = j // blocks, j % blocks
        row = pl.ds(pl.multiple_of(qb * q_block, q_block), q_block)
        dist[...] = distance(len_ref, b, 0, total, qb * q_block, q_block)
        queries = qkv[b, row, 0:128]
        lane = lax.broadcasted_iota(jnp.int32, (q_block, 128), 1)
        for h in range(2):
            own = jnp.where((lane < 64) == (h == 0), queries, jnp.zeros_like(queries))
            s = dot_nt(qkv[b, :, 128:256], own) - slopes[h] * dist[...]
            top = jnp.max(s, axis=0, keepdims=True)
            p = jnp.exp(s - top)
            weight = jnp.sum(p, axis=0, keepdims=True)
            o = dot_nn(vt[b, h * 64:(h + 1) * 64, :], p.astype(BF16))
            ot[b, h * 64:(h + 1) * 64, row] = o / weight
            lse[b, h:h + 1, row] = top + jnp.log(weight)
        obuf[b, row, :] = jnp.transpose(ot[b, :, row]).astype(BF16)
        return carry

    def send_rows(b):
        out = []
        for k in range(1, n_seq):
            other = lax.rem(sq + k, n_seq)
            source = lax.rem(sq + n_seq - k, n_seq)
            src = obuf.at[b, pl.ds(pl.multiple_of(other * tok_rows, tok_rows), tok_rows), :]
            dst = av.at[b, :, pl.ds(pl.multiple_of(sq * 128, 128), 128)]
            land = av.at[b, :, pl.ds(pl.multiple_of(source * 128, 128), 128)]
            out.append(keep(Link(src, dst, land, (s_send, s_recv), 20 + b * 7 + k - 1, (dp, other))))
        pending[("o", b)] = out
        own_rows.append(local(
            obuf.at[b, pl.ds(pl.multiple_of(sq * tok_rows, tok_rows), tok_rows), :],
            av.at[b, :, pl.ds(pl.multiple_of(sq * 128, 128), 128)],
        ))

    own_rows = []

    def attend_some(first, last):
        lax.fori_loop(first, last, attend, 0)

    tokens = streams * tok_rows
    late = []

    def residual(b):
        wait("o", b)
        own_rows[b].wait()
        if b == 0:
            late[0].wait()
        rows = slice(b * tok_rows, (b + 1) * tok_rows)
        for r in range(0, width, 512):
            hid[rows, r:r + 512] = x_ref[b, :, r:r + 512].astype(F32) + dot_nn(
                av[b], wo_v[:, :, :, :, :, :, r:r + 512].reshape(width, 512)
            )
        n, _ = norm_parts(hid[rows])
        low_two[rows] = (n * vector(2) + vector(3)).astype(BF16)
        if b == streams - 1:
            local(hid, hid_out)
            local(av, attn)

    def one_tile(i, carry):
        for copy in tile_copies(i):
            copy.wait()
        act_f, bend = gelu_both(dot_nn(low_two[...], wu_t[i].reshape(width, cols)))
        act = act_f.astype(BF16)
        for j in range(4):
            act_v[i * 2 + j // 2, j % 2] = act[:, j * 128:(j + 1) * 128]
        bend_v[i] = bend.astype(BF16)
        for copy in tile_stores(i):
            copy.start()
        return carry

    def some_tiles(first, last):
        lax.fori_loop(first * tiles // 4, last * tiles // 4, one_tile, 0)

    def first_group():
        for h in range(4):
            wait("c", 0, h)
        late.append(local(wo_all, wo_v))

        def load(i, carry):
            for copy in tile_copies(i):
                copy.start()
            return carry
        lax.fori_loop(0, tiles, load, 0)

    def x_arrived(h):
        wait("x", h)
        x_pass(h)

    def own_x():
        pending["xc", 0] = [
            keep(Link(x_ref, xg.at[:, sq], xg.at[:, z * 2 + (1 - c)], (z_send, z_recv), 6, sibling))
        ]

    def block_done(h):
        if h == 0:
            cp_x.wait()
        wait("xc", h)
        process_hop(h)

    def hop_x(h):
        if h == 3:
            wait("x", 2)
        x_hop(h)

    def hop(g, h):
        if h == 3:
            wait("z", g, 2)
        z_hop(g, h)

    def cross_begin(g, h):
        if h > 0:
            wait("z", g, h)
        cross_one(g, h)

    def cross_next(g, h):
        if h == 0:
            for i in groups[g]:
                cp_w[i].wait()
        cross_two(g, h)

    def stream_out(b):
        send_rows(b)
        if b == 1:
            local(ot, ot_out)
            local(lse, lse_out)

    steps = {
        "seq": along_seq, "wq": along_dp, "wt": columns, "xs": own_x, "vt": values,
        "c0": first_group,
    }
    for h in range(4):
        steps["p%d" % h] = functools.partial(block_done, h)
        for g in range(2):
            steps["x1%d%d" % (g, h)] = functools.partial(cross_begin, g, h)
            steps["x2%d%d" % (g, h)] = functools.partial(cross_next, g, h)
            steps["cc%d%d" % (g, h)] = functools.partial(cross_core, g, h)
            if h > 0:
                steps["zh%d%d" % (g, h)] = functools.partial(hop, g, h)
        if h > 0:
            steps["xh%d" % h] = functools.partial(hop_x, h)
            steps["xp%d" % h] = functools.partial(x_arrived, h)
    for b in range(streams):
        steps["o%d" % b] = functools.partial(stream_out, b)
        steps["h%d" % b] = functools.partial(residual, b)
    for name, first, last in runs(gather_order, ("a", "u")):
        if name == "a":
            attend_some(first, last)
        elif name == "u":
            some_tiles(first, last)
        else:
            steps[name]()

    def stored(i, carry):
        for copy in tile_stores(i):
            copy.wait()
        return carry
    lax.fori_loop(0, tiles, stored, 0)
    for key in pending:
        wait(*key)
    waited = [cp_x, cp_wq, *cp_w, *own_rows, *late]
    for copy in locals_:
        if not any(copy is other for other in waited):
            copy.wait()
    for link in links:
        link.wait_sent()


def gather_call(inputs, w_qkv, w_out, w_up, w_down, vectors, lengths):
    streams, tok_rows, width = inputs.shape
    n_seq, n_dp = lax.axis_size("seq"), lax.axis_size("dp")
    nz, total = n_seq // 2, n_seq * tok_rows
    any_space = pl.BlockSpec(memory_space=pl.ANY)
    vmem = pl.BlockSpec(memory_space=pltpu.VMEM)
    smem = pl.BlockSpec(memory_space=pltpu.SMEM)

    def halves(w):
        return w.reshape(2, w.shape[0] // 2, w.shape[1])

    own = [halves(w) for w in (w_out, w_up, w_down)]
    full = [jax.ShapeDtypeStruct((2, n_dp // 2, nz, 2) + w.shape, BF16) for w in own]
    cols = w_qkv.shape[1] // n_seq
    outs = full + [
        jax.ShapeDtypeStruct((32, 128), BF16),
        jax.ShapeDtypeStruct((streams, tok_rows, width), BF16),
        jax.ShapeDtypeStruct((streams, total, cols), BF16),
        jax.ShapeDtypeStruct((streams, 128, total), F32),
        jax.ShapeDtypeStruct((streams, 8, total), F32),
        jax.ShapeDtypeStruct((streams, n_seq, tok_rows, width), BF16),
        jax.ShapeDtypeStruct((cols, width), BF16),
        jax.ShapeDtypeStruct((streams * tok_rows, width), F32),
        jax.ShapeDtypeStruct((n_dp * nz, 2, streams * tok_rows, 128), BF16),
        jax.ShapeDtypeStruct((8, streams * tok_rows, w_up.shape[1] // 8), BF16),
    ]
    dma = pltpu.SemaphoreType.DMA
    scratch = [
        pltpu.VMEM((streams, n_seq, tok_rows, width), BF16),
        pltpu.VMEM((streams, n_seq, tok_rows, width), BF16),
        pltpu.VMEM((width, cols), BF16),
        pltpu.VMEM((cols, width), BF16),
        pltpu.VMEM((n_seq, w_qkv.shape[0], cols), BF16),
        pltpu.VMEM((32, 128), BF16),
        pltpu.VMEM((n_seq - 1 + n_dp - 1, 32, 128), BF16),
        pltpu.VMEM((32, 128), BF16),
        pltpu.VMEM((32, 128), BF16),
        pltpu.VMEM((streams, total, cols), BF16),
        pltpu.VMEM((streams, 128, total), BF16),
        pltpu.VMEM((streams, total, 128), BF16),
        pltpu.VMEM((streams, 128, total), F32),
        pltpu.VMEM((streams, 8, total), F32),
        pltpu.VMEM((total, q_block), F32),
        pltpu.VMEM(full[0].shape, BF16),
        pltpu.VMEM((8,) + full[1].shape[:-1] + (w_up.shape[1] // 8,), BF16),
        pltpu.VMEM((streams, tok_rows, width), BF16),
        pltpu.VMEM((streams * tok_rows, width), F32),
        pltpu.VMEM((streams * tok_rows, width), BF16),
        pltpu.VMEM(outs[11].shape, BF16),
        pltpu.VMEM(outs[12].shape, BF16),
        dma((7,)), dma((7,)), dma((9,)), dma((9,)), dma((60,)), dma((60,)), dma((34,)), dma((34,)),
        dma((8, 4)), dma((8, 2)), dma((20,)),
    ]
    return pl.pallas_call(
        gather_kernel,
        out_shape=outs,
        in_specs=[vmem] * 6 + [smem],
        out_specs=[any_space] * len(outs),
        scratch_shapes=scratch,
        compiler_params=pltpu.CompilerParams(
            collective_id=0, has_side_effects=True, vmem_limit_bytes=56 * 2**20
        ),
        name="gather_attend",
    )(inputs, w_qkv, *own, vectors, lengths)


def scatter_kernel(
    x_ref, fill_ref, par_ref, cot_ref, attn_ref, hid_ref, act_ref, bend_ref, wo_ref, wu_ref, wd_ref,
    qkv_ref, ot_ref, lse_ref, xh_ref, wt_ref, len_ref,
    y_out, gx_out, go_out, gu_out, gd_out, gq_out, pg_out,
    hidden, n_two, r_two, low_two, grad_two, yb, gout2, gb2, act_v, act_s, bend_t, n2s2, n2o, at2, ato, wo_v, wu_t, wd_t, gab,
    acc_o, acc_u, acc_d, ra_o, ra_u, ra_d, rb_o, rb_u, rb_d, sa_o, sa_u, sa_d, sb_o, sb_u, sb_d,
    zr_o, zr_u, zr_d, fin_o, fin_u, fin_d,
    do, qkv, ot, lse, xh, wt, kt, delta, dk, dv, dqt, dqkv, dqkvt,
    gp, dqr, dqsum, pgp, pr1, psum, pr2, pgo,
    c_send, c_recv, o_send, o_recv, x_send, x_recv, zw_send, zw_recv, zg_send, zg_recv, s_send, s_recv,
    tile_sem, loc,
):
    dp, sq, y, x, z, c = place()
    streams, tok_rows, width = gab.shape
    tokens = streams * tok_rows
    slopes = own_slopes(lax.axis_index("seq"), lax.axis_size("seq"), qkv.shape[1])
    n_seq, n_dp = lax.axis_size("seq"), lax.axis_size("dp")
    nz = n_seq // 2
    total = n_seq * tok_rows
    x_nbr, y_nbr = (y * 2 + (1 - x), sq), ((1 - y) * 2 + x, sq)
    sibling = (dp, z * 2 + (1 - c))
    z1, z2, z3 = planes(z, nz)
    near_dev, far_dev = (dp, z1 * 2 + c), (dp, z2 * 2 + c)
    greet(dp, sq, n_seq, n_dp)
    links, locals_ = [], []
    every = slice(None)

    def keep(link):
        link.start()
        links.append(link)
        return link

    def local(src, dst):
        copy = pltpu.make_async_copy(src, dst, loc.at[len(locals_)])
        copy.start()
        locals_.append(copy)
        return copy

    def loop(n, body):
        def step(j, carry):
            body(j)
            return carry
        lax.fori_loop(0, n, step, 0)

    pending = {}

    arrived = set()

    def wait(*key):
        if key not in arrived:
            arrived.add(key)
            for link in pending[key]:
                link.wait()

    def f32(v):
        return v.astype(F32)

    def vector(row):
        block = f32(par_ref[row * 8:(row + 1) * 8, :])
        return jnp.concatenate([block[r:r + 1, :] for r in range(8)], axis=1)

    def to_sibling(src, dst, index):
        return keep(Link(src, dst, dst, (c_send, c_recv), index, sibling))

    cols = wu_t.shape[2]
    tiles = wu_ref.shape[1] // cols

    def tile_copies(i):
        slot, first = i % 2, pl.multiple_of(i * cols, cols)
        out = [pltpu.make_async_copy(bend_ref.at[i], bend_t.at[slot], tile_sem.at[8, slot])]
        for part in range(4):
            rows = slice(part * 256, (part + 1) * 256)
            out.append(pltpu.make_async_copy(
                wu_ref.at[rows, pl.ds(first, cols)], wu_t.at[slot, rows], tile_sem.at[part, slot]
            ))
            out.append(pltpu.make_async_copy(
                wd_ref.at[i * 4 + part], wd_t.at[slot, part], tile_sem.at[4 + part, slot]
            ))
        return out

    load_cot, load_act = local(cot_ref, gab), local(act_ref, act_v)
    load_hid = local(hid_ref, hidden)
    for copy in tile_copies(0):
        copy.start()
    load_attn, load_out = local(attn_ref, low_two), local(wo_ref, wo_v)
    load_cot.wait()
    for b in range(streams):
        rows = slice(b * tok_rows, (b + 1) * tok_rows)
        fill = jnp.broadcast_to(f32(fill_ref[b:b + 1, :]), (128, tok_rows))
        gout2[rows] = (f32(gab[b]) * jnp.transpose(fill)[:, 0:1]).astype(BF16)
    all_here(n_seq, n_dp)
    gout_link = to_sibling(gout2.at[0:tokens], gout2.at[tokens:2 * tokens], 0)
    act_link = to_sibling(act_ref.at[:, 1 - c], act_s, 1)

    def chosen(parity):
        j = lax.broadcasted_iota(jnp.int32, (1, width // 2), 1)
        column = ((((j & 127) >> 5) * n_seq + (j >> 7) * 2 + parity) << 5) + (j & 31)
        return (lax.broadcasted_iota(jnp.int32, (width, 1), 0) == column).astype(F32).astype(BF16)

    def pick(v, mine, theirs, index):
        here, there = dot_nn(v, chosen(c)).astype(BF16), dot_nn(v, chosen(1 - c)).astype(BF16)
        for b in range(nz):
            mine[b, 0:tokens] = here[:, b * 128:(b + 1) * 128]
            theirs[b] = there[:, b * 128:(b + 1) * 128]
        return to_sibling(theirs, mine.at[:, tokens:2 * tokens], index)

    gain_two, shift_two = vector(2), vector(3)

    def tile_grad(i):
        cut = pl.ds(pl.multiple_of(i % 2 * cols, cols), cols)
        return gp.at[i // 4, i // 2 % 2 * 2, :, :, cut], gp.at[i // 4, i // 2 % 2 * 2 + 1, :, :, cut]

    def tile_link(i):
        src, dst = tile_grad(i)
        return Link(src, dst, dst, (c_send, c_recv), 4 + i, sibling)

    def one_tile(i, carry):
        slot = i % 2
        for copy in tile_copies(i):
            copy.wait()

        @pl.when(i + 1 < tiles)
        def _():
            for copy in tile_copies(i + 1):
                copy.start()
        down = wd_t[slot].reshape(cols, width)
        act = jnp.concatenate([act_v[i * 2 + j // 2, j % 2] for j in range(4)], axis=1)
        hidden[...] += dot_nn(act, down)
        grad_up = (dot_nt(gout2[0:tokens], down) * f32(bend_t[slot])).astype(BF16)
        tile_grad(i)[0][...] = grad_up.reshape(streams, tok_rows, cols)
        grad_two[...] += dot_nt(grad_up, wu_t[slot])
        tile_link(i).start()
        return carry

    arrays = [
        (acc_o, ra_o, rb_o, sa_o, sb_o, zr_o, fin_o, go_out),
        (acc_u, ra_u, rb_u, sa_u, sb_u, zr_u, fin_u, gu_out),
        (acc_d, ra_d, rb_d, sa_d, sb_d, zr_d, fin_d, gd_out),
    ]
    groups = [(1, 0), (2,)]
    U, D = 0, 1
    plane_of = [z3, z2, z1, z]

    def cross_one(g, p):
        t = plane_of[p]
        out = []
        for i in groups[g]:
            acc, ra, rb = arrays[i][:3]
            out.append(keep(Link(acc.at[1 - y, :, t, 0], ra.at[p], ra.at[p], (x_send, x_recv), (i * 4 + p) * 4, y_nbr)))
            out.append(keep(Link(acc.at[:, 1 - x, t, 1], rb.at[p], rb.at[p], (x_send, x_recv), (i * 4 + p) * 4 + 1, x_nbr)))
        pending[("x1", g, p)] = out

    def cross_two(g, p):
        t = plane_of[p]
        wait("x1", g, p)
        out = []
        for i in groups[g]:
            acc, ra, rb, sa, sb = arrays[i][:5]
            acc[y, 1 - x, t, 0] = (f32(acc[y, 1 - x, t, 0]) + f32(ra[p, 1 - x])).astype(BF16)
            acc[1 - y, x, t, 1] = (f32(acc[1 - y, x, t, 1]) + f32(rb[p, 1 - y])).astype(BF16)
            out.append(keep(Link(acc.at[y, 1 - x, t, 0], sa.at[p], sa.at[p], (x_send, x_recv), (i * 4 + p) * 4 + 2, x_nbr)))
            out.append(keep(Link(acc.at[1 - y, x, t, 1], sb.at[p], sb.at[p], (x_send, x_recv), (i * 4 + p) * 4 + 3, y_nbr)))
        pending[("x2", g, p)] = out

    def cross_three(g, p):
        t = plane_of[p]
        wait("x2", g, p)
        for i in groups[g]:
            acc, ra, rb, sa, sb = arrays[i][:5]
            acc[y, x, t, 0] = (f32(acc[y, x, t, 0]) + f32(ra[p, x]) + f32(sa[p])).astype(BF16)
            acc[y, x, t, 1] = (f32(acc[y, x, t, 1]) + f32(rb[p, y]) + f32(sb[p])).astype(BF16)

    def z_one(g, step, target):
        pending[("z", g, step)] = [
            keep(Link(
                arrays[i][0].at[y, x, plane_of[step]], arrays[i][5].at[step], arrays[i][5].at[step],
                (zw_send, zw_recv), i * 3 + step, target,
            ))
            for i in groups[g]
        ]

    def z_first(g):
        cross_three(g, 0)
        z_one(g, 0, near_dev)

    def z_second(g):
        cross_three(g, 1)
        wait("z", g, 0)
        for i in groups[g]:
            acc, zr = arrays[i][0], arrays[i][5]
            for h in range(2):
                acc[y, x, z2, h] = (f32(acc[y, x, z2, h]) + f32(zr[0, h])).astype(BF16)
        z_one(g, 1, far_dev)

    def z_third(g):
        cross_three(g, 2)
        z_one(g, 2, near_dev)

    def z_last(g):
        cross_three(g, 3)
        wait("z", g, 1)
        wait("z", g, 2)
        for i in groups[g]:
            acc, zr, fin, out = arrays[i][0], *arrays[i][5:]
            fin[...] = f32(acc[y, x, z]) + f32(zr[1]) + f32(zr[2])
            local(fin, out)

    def dot_tn(a, b):
        return lax.dot_general(a, b, (((0,), (0,)), ((), ())), preferred_element_type=F32)

    def down_terms(t):
        def one(d):
            left = jnp.concatenate([act_v[d * 4 + t, c], act_s[d * 4 + t]], axis=0)
            rows = acc_d.shape[4]
            for r in range(0, width, 512):
                terms = dot_tn(left, gout2[:, r:r + 512]).astype(BF16)
                for j in range(2):
                    acc_d[d // 2, d % 2, t, j, :, r:r + 512] = terms[j * rows:(j + 1) * rows]
        loop(n_dp, one)

    def narrow_terms(source, t, acc, right, where):
        terms = dot_tn(source[t], right).astype(BF16)
        for j in range(8):
            acc[j // 4, j // 2 % 2, t, j % 2, :, where] = terms[j * 16:(j + 1) * 16]

    def up_terms(t):
        def one(i):
            d, part = i // 2, i % 2
            cut = pl.ds(pl.multiple_of(part * cols, cols), cols)
            right = gp[d // 2, pl.ds(d % 2 * 2, 2), :, :, cut].reshape(2 * tokens, cols)
            narrow_terms(n2s2, t, acc_u, right, pl.ds(pl.multiple_of(i * cols, cols), cols))
        loop(tiles, one)
        for r in range(0, width, 512):
            narrow_terms(at2, t, acc_o, gb2[:, r:r + 512], slice(r, r + 512))

    copies, copy_xh = [], []

    begun = []

    def opening():
        if not begun:
            begun.append("start")
            for copy in (load_act, load_hid, load_attn):
                copy.wait()
            gout_link.wait()
            act_link.wait()

    def down_plane(p):
        opening()
        down_terms(plane_of[p])
        if not copies:
            copies.extend([local(qkv_ref, qkv), local(ot_ref, ot), local(lse_ref, lse), local(wt_ref, wt)])
            copy_xh.append(local(xh_ref.at[:, :, 0:cols], xh))

    def pick_attn():
        opening()
        pending["attn",] = [pick(low_two[...], at2, ato, 2)]

    def pick_norm():
        pending["norm",] = [pick(low_two[...], n2s2, n2o, 3)]

    def second_norm():
        opening()
        for r in range(0, tokens, 128):
            n, rstd = norm_parts(hidden[r:r + 128])
            n_two[r:r + 128] = n
            r_two[r:r + 128] = jnp.broadcast_to(rstd, (128, 128))
            low_two[r:r + 128] = (n * gain_two + shift_two).astype(BF16)
        grad_two[...] = jnp.zeros_like(grad_two)

    def some_tiles(first, last):
        lax.fori_loop(first * tiles // 4, last * tiles // 4, one_tile, 0)

    grad_links, own_do = [], []

    def branch():
        yb[...] = hidden[...].astype(BF16)
        local(yb, y_out)
        for r in range(0, tokens, 128):
            rows = slice(r, r + 128)
            back = norm_back(n_two[rows], r_two[rows, 0:1], grad_two[rows] * gain_two)
            grad = f32(gout2[rows]) + back
            hidden[rows] = grad
            gb2[rows] = grad.astype(BF16)
        load_out.wait()
        pending["branch",] = [to_sibling(gb2.at[0:tokens], gb2.at[tokens:2 * tokens], 12)]
        for r in range(0, width, 512):
            grad = dot_nt(gb2[0:tokens], wo_v[r // 128:r // 128 + 4].reshape(512, width)).astype(BF16)
            gab[:, :, r:r + 512] = grad.reshape(streams, tok_rows, 512)
        for b in range(streams):
            out = []
            for k in range(1, n_seq):
                other = lax.rem(sq + k, n_seq)
                source = lax.rem(sq + n_seq - k, n_seq)
                src = gab.at[b, :, pl.ds(pl.multiple_of(other * 128, 128), 128)]
                dst = do.at[b, pl.ds(pl.multiple_of(sq * tok_rows, tok_rows), tok_rows), :]
                land = do.at[b, pl.ds(pl.multiple_of(source * tok_rows, tok_rows), tok_rows), :]
                out.append(keep(Link(src, dst, land, (o_send, o_recv), b * 7 + k - 1, (dp, other))))
            grad_links.append(out)
        copy_xh.append(local(xh_ref.at[:, :, cols:width], wu_t))
        own_do.extend(
            local(
                gab.at[b, :, pl.ds(pl.multiple_of(sq * 128, 128), 128)],
                do.at[b, pl.ds(pl.multiple_of(sq * tok_rows, tok_rows), tok_rows), :],
            )
            for b in range(streams)
        )
        pgp[...] = jnp.zeros_like(pgp)
        pgp[2:3, :] = jnp.sum(grad_two[...] * n_two[...], axis=0, keepdims=True)
        pgp[3:4, :] = jnp.sum(grad_two[...], axis=0, keepdims=True)

    def up_plane(p):
        if "up" not in begun:
            begun.append("up")
            for key in ("attn", "norm", "branch"):
                wait(key)

            def wait_tile(i):
                tile_link(i).wait()
            loop(tiles, wait_tile)
        up_terms(plane_of[p])

    step = 256
    blocks = total // q_block

    def turn(j):
        b, r = j // (total // step), j % (total // step)
        row = pl.ds(pl.multiple_of(r * step, step), step)
        kt[b, :, row] = jnp.transpose(f32(qkv[b, row, 128:256])).astype(BF16)
    def keys_turned():
        for copy in copies:
            copy.wait()
        loop(streams * (total // step), turn)


    def prepare(b):
        own_do[b].wait()
        for link in grad_links[b]:
            link.wait()

        def one(r):
            row = pl.ds(pl.multiple_of(r * step, step), step)
            both = jnp.transpose(f32(do[b, row, :])) * ot[b, :, row]
            for h in range(2):
                delta[h:h + 1, row] = jnp.sum(both[h * 64:(h + 1) * 64], axis=0, keepdims=True)
        loop(total // step, one)
        dk[...] = jnp.zeros_like(dk)
        dv[...] = jnp.zeros_like(dv)

    tile = 256

    def attend(b, qb):
        row = pl.ds(pl.multiple_of(qb * q_block, q_block), q_block)
        lane = lax.broadcasted_iota(jnp.int32, (q_block, 128), 1)
        queries, grads = qkv[b, row, 0:128], do[b, row, :]
        none = jnp.zeros_like(queries)
        own = [jnp.where((lane < 64) == (h == 0), queries, none) for h in range(2)]
        own_grad = [jnp.where((lane < 64) == (h == 0), grads, none) for h in range(2)]
        part = [jnp.zeros((64, q_block), F32)] * 2
        for r in range(total // tile):
            keys = slice(r * tile, (r + 1) * tile)
            gap = distance(len_ref, b, r * tile, tile, qb * q_block, q_block)
            grad_v = grad_k = 0
            for h in range(2):
                s = dot_nt(qkv[b, keys, 128:256], own[h]) - slopes[h] * gap
                p = jnp.exp(s - lse[b, h:h + 1, row])
                gp_t = dot_nt(qkv[b, keys, 256:384], own_grad[h])
                ds = (p * (gp_t - delta[h:h + 1, row])).astype(BF16)
                grad_v = grad_v + dot_nn(p.astype(BF16), own_grad[h])
                grad_k = grad_k + dot_nn(ds, own[h])
                part[h] = part[h] + dot_nn(kt[b, h * 64:(h + 1) * 64, keys], ds)
            dv[keys, :] += grad_v
            dk[keys, :] += grad_k
        for h in range(2):
            dqt[h * 64:(h + 1) * 64, row] = part[h] * 0.125

    def attend_some(b, first, last):
        def one(qb, carry):
            attend(b, qb)
            return carry
        lax.fori_loop(first, last, one, 0)

    def gs(b):
        return wo_v.at[b * nz:(b + 1) * nz]

    def gz(b, step):
        return wd_t.at[b, step]

    def finish_stream(b):
        def one(r):
            row = pl.ds(pl.multiple_of(r * step, step), step)
            low = dqt[:, row].astype(BF16)
            dqkvt[b, 0:128, row] = low
            dqkv[row, 0:128] = jnp.transpose(f32(low)).astype(BF16)
            for first, grad in ((128, dk), (256, dv)):
                low = grad[row, :].astype(BF16)
                dqkv[row, first:first + 128] = low
                dqkvt[b, first:first + 128, row] = jnp.transpose(f32(low)).astype(BF16)
        loop(total // step, one)

        def product(s):
            row = pl.ds(pl.multiple_of(s * tok_rows, tok_rows), tok_rows)
            gp[b, s // 2, s % 2] = dot_nn(dqkv[row, :], wt[...]).astype(BF16)
        loop(n_seq, product)
        pending[("gc", b)] = [
            keep(Link(gp.at[b, :, 1 - c], gs(b), gs(b), (zg_send, zg_recv), b * 4, sibling))
        ]

    def g_one(b, step, target):
        pending[("g", b, step)] = [
            keep(Link(gp.at[b, plane_of[step], c], gz(b, step), gz(b, step), (zg_send, zg_recv), b * 4 + 1 + step, target))
        ]

    def g_first(b):
        wait("gc", b)

        def add(j):
            gp[b, j, c] = (f32(gp[b, j, c]) + f32(wo_v[b * nz + j])).astype(BF16)
        loop(nz, add)
        g_one(b, 0, near_dev)
        g_one(b, 2, near_dev)

    def g_second(b):
        wait("g", b, 0)
        gp[b, z2, c] = (f32(gp[b, z2, c]) + f32(gz(b, 0)[...])).astype(BF16)
        g_one(b, 1, far_dev)

    def g_last(b):
        wait("g", b, 1)
        wait("g", b, 2)
        own = f32(gp[b, z, c]) + f32(gz(b, 1)[...]) + f32(gz(b, 2)[...])
        rows = slice(b * tok_rows, (b + 1) * tok_rows)
        n, rstd = norm_parts(f32(x_ref[rows]))
        low_two[rows] = (hidden[rows] + norm_back(n, rstd, own * vector(0))).astype(BF16)
        local(low_two.at[rows], gx_out.at[b])

    rows_dp = 32 * n_seq

    def weight_grad():
        for copy in copy_xh:
            copy.wait()
        sums = jnp.sum(f32(dqkvt[0]), axis=1, keepdims=True)
        for b in range(1, streams):
            sums = sums + jnp.sum(f32(dqkvt[b]), axis=1, keepdims=True)
        gain, shift = vector(0), vector(1)
        for r in range(width // step):
            cols = slice(r * step, (r + 1) * step)
            weight = f32(wt[:, cols])
            n = xh if r < 2 else wu_t
            there = slice(r % 2 * step, (r % 2 + 1) * step)
            raw = dot_nn(dqkvt[0], n[0, :, there])
            for b in range(1, streams):
                raw = raw + dot_nn(dqkvt[b], n[b, :, there])
            pgp[0:1, cols] = jnp.sum(raw * weight, axis=0, keepdims=True)
            pgp[1:2, cols] = jnp.sum(sums * weight, axis=0, keepdims=True)
            grad = raw * gain[:, cols] + sums * shift[:, cols]
            dqkv[cols, :] = jnp.transpose(grad).astype(BF16)
        out = []
        for m in range(1, n_dp):
            other = lax.rem(dp + m, n_dp)
            src = dqkv.at[pl.ds(pl.multiple_of(other * rows_dp, rows_dp), rows_dp), :]
            out.append(keep(Link(src, dqr.at[m - 1], dqr.at[m - 1], (s_send, s_recv), m - 1, (other, sq))))
            src = pgp.at[:, pl.ds(pl.multiple_of(other * rows_dp, rows_dp), rows_dp)]
            out.append(keep(Link(src, pr1.at[m - 1], pr1.at[m - 1], (s_send, s_recv), 3 + m - 1, (other, sq))))
        pending["qd",] = out

    def weight_grad_two():
        wait("qd")
        mine = pl.ds(pl.multiple_of(dp * rows_dp, rows_dp), rows_dp)
        part = f32(dqkv[mine, :])
        small = pgp[:, mine]
        for m in range(n_dp - 1):
            part = part + f32(dqr[m])
            small = small + pr1[m]
        dqsum[...] = part.astype(BF16)
        psum[...] = small
        out = []
        for k in range(1, n_seq):
            other = lax.rem(sq + k, n_seq)
            source = lax.rem(sq + n_seq - k, n_seq)
            src = dqsum.at[pl.ds(pl.multiple_of(other * 32, 32), 32), :]
            out.append(keep(Link(src, gq_out.at[sq], gq_out.at[source], (s_send, s_recv), 6 + k - 1, (dp, other))))
            src = psum.at[:, pl.ds(pl.multiple_of(other // 4 * 128, 128), 128)]
            out.append(keep(Link(src, pr2.at[k - 1], pr2.at[k - 1], (s_send, s_recv), 13 + k - 1, (dp, other))))
        local(dqsum.at[pl.ds(pl.multiple_of(sq * 32, 32), 32), :], gq_out.at[sq])
        pending["qs",] = out

    def weight_grad_last():
        wait("qs")
        small = psum[:, pl.ds(pl.multiple_of(sq // 4 * 128, 128), 128)]
        for k in range(n_seq - 1):
            small = small + pr2[k]
        pgo[...] = small
        local(pgo, pg_out)

    def first_frames():
        keys_turned()
        prepare(0)

    def first_done():
        def sent(i):
            tile_link(i).wait_sent()
        loop(tiles, sent)
        finish_stream(0)

    steps = {
        "pkA": pick_attn, "pkN": pick_norm,
        "LN": second_norm, "LNB": branch,
        "P0": first_frames, "P1": functools.partial(prepare, 1),
        "F0": first_done, "F1": functools.partial(finish_stream, 1),
        "WG": weight_grad, "W2": weight_grad_two, "W3": weight_grad_last,
    }
    for name, action in (("gf", g_first), ("gs", g_second), ("gl", g_last)):
        for b in range(streams):
            steps[name + str(b)] = functools.partial(action, b)
    for p in range(nz):
        steps["DT%d" % p] = functools.partial(down_plane, p)
        steps["UT%d" % p] = functools.partial(up_plane, p)
    for letter, g in (("U", U), ("D", D)):
        for name, action in (("zf", z_first), ("zs", z_second), ("zt", z_third), ("zl", z_last)):
            steps[name + letter] = functools.partial(action, g)
        for p in range(nz):
            steps["c1%s%d" % (letter, p)] = functools.partial(cross_one, g, p)
            steps["c2%s%d" % (letter, p)] = functools.partial(cross_two, g, p)
    for name, first, last in runs(scatter_order, ("A0", "A1", "T")):
        if name in ("A0", "A1"):
            attend_some(int(name[1]), first, last)
        elif name == "T":
            some_tiles(first, last)
        else:
            steps[name]()
    for key in pending:
        wait(*key)
    waited = [load_cot, load_act, load_hid, load_attn, load_out, *copy_xh, *own_do, *copies]
    for copy in locals_:
        if not any(copy is other for other in waited):
            copy.wait()
    for link in links:
        link.wait_sent()


def scatter_call(
    inputs, cotangent, infill, attn, hidden, act, bend, params, weights, qkv, ot, lse, xh, wt, lengths,
):
    streams, total = qkv.shape[:2]
    tokens, width = inputs.shape
    tok_rows = tokens // streams
    n_seq, n_dp = lax.axis_size("seq"), lax.axis_size("dp")
    nz = n_seq // 2
    cols = qkv.shape[2]
    any_space = pl.BlockSpec(memory_space=pl.ANY)
    vmem = pl.BlockSpec(memory_space=pltpu.VMEM)
    smem = pl.BlockSpec(memory_space=pltpu.SMEM)
    dma = pltpu.SemaphoreType.DMA
    sizes = [(w.shape[0] // (2 * n_dp * n_seq), w.shape[1]) for w in weights]
    tile = weights[1].shape[1] // 8

    def buffers(*lead):
        return [pltpu.VMEM(lead + size, BF16) for size in sizes]

    def low(*shape):
        return pltpu.VMEM(shape, BF16)

    def full(*shape):
        return pltpu.VMEM(shape, F32)

    half = width // 2 // nz
    scratch = [
        full(tokens, width), full(tokens, width), full(tokens, 128), low(tokens, width), full(tokens, width),
        low(tokens, width), low(2 * tokens, width), low(2 * tokens, width),
        low(*act.shape), low(act.shape[0], tokens, 128), low(2, *bend.shape[1:]),
        low(nz, 2 * tokens, half), low(nz, tokens, half), low(nz, 2 * tokens, half), low(nz, tokens, half),
        low(width // 128, 128, width), low(2, width, tile), low(2, tile // 128, 128, width), low(streams, tok_rows, width),
    ]
    scratch += buffers(2, 2, nz, 2) + buffers(nz, 2) + buffers(nz, 2) + buffers(nz) + buffers(nz)
    scratch += buffers(nz - 1, 2)
    scratch += [pltpu.VMEM((2,) + size, F32) for size in sizes]
    scratch += [
        low(streams, total, 128), low(*qkv.shape), full(*ot.shape), full(*lse.shape), low(streams, total, tile), low(*wt.shape),
        low(streams, 128, total), full(8, total), full(total, 128), full(total, 128),
        full(128, total), low(total, cols), low(streams, cols, total),
        low(streams, nz, 2, tok_rows, width),
        low(n_dp - 1, width // n_dp, cols), low(width // n_dp, cols),
        full(8, width), full(n_dp - 1, 8, width // n_dp), full(8, width // n_dp), full(n_seq - 1, 8, 128), full(8, 128),
        dma((13,)), dma((13,)), dma((14,)), dma((14,)), dma((48,)), dma((48,)), dma((9,)), dma((9,)),
        dma((8,)), dma((8,)), dma((20,)), dma((20,)), dma((9, 2)), dma((24,)),
    ]
    outs = [
        jax.ShapeDtypeStruct((tokens, width), BF16),
        jax.ShapeDtypeStruct((streams, tok_rows, width), BF16),
        *[jax.ShapeDtypeStruct((2,) + size, F32) for size in sizes],
        jax.ShapeDtypeStruct((n_seq, width // (n_dp * n_seq), cols), BF16),
        jax.ShapeDtypeStruct((8, 128), F32),
    ]
    return pl.pallas_call(
        scatter_kernel,
        out_shape=outs,
        in_specs=[vmem] * 3 + [any_space] * 13 + [smem],
        out_specs=[any_space] * len(outs),
        scratch_shapes=scratch,
        compiler_params=pltpu.CompilerParams(
            collective_id=1, has_side_effects=True, vmem_limit_bytes=63 * 2**20
        ),
        name="scatter_attend",
    )(
        inputs, infill, params, cotangent, attn, hidden, act, bend, weights[0].reshape(-1, 128, width), weights[1],
        weights[2].reshape(-1, 128, width), qkv, ot, lse, xh, wt, lengths,
    )


def finish_kernel(*refs):
    n = 6
    parts, outs, held, wide, sems = refs[:n], refs[n:2 * n], refs[2 * n:3 * n], refs[3 * n], refs[3 * n + 1]
    loads = [pltpu.make_async_copy(src, dst, sems.at[i]) for i, (src, dst) in enumerate(zip(parts, held))]
    sources = (*held[:-1], wide)
    stores = [pltpu.make_async_copy(src, dst, sems.at[n + i]) for i, (src, dst) in enumerate(zip(sources, outs))]
    for load in reversed(loads):
        load.start()
    loads[-1].wait()
    gq = held[-1]
    width = wide.shape[1] // 3
    for q in range(gq.shape[0]):
        for j in range(3):
            wide[:, j * width + q * 128:j * width + (q + 1) * 128] = gq[q, :, j * 128:(j + 1) * 128].astype(F32)
    stores[-1].start()
    for load, store in zip(loads[:-1], stores[:-1]):
        load.wait()
        store.start()
    for store in stores:
        store.wait()


def finish_call(*parts):
    gq = parts[-1]
    hbm = pl.BlockSpec(memory_space=pltpu.HBM)
    outs = [jax.ShapeDtypeStruct(part.shape, part.dtype) for part in parts[:-1]]
    outs.append(jax.ShapeDtypeStruct((gq.shape[1], gq.shape[0] * gq.shape[2]), F32))
    return pl.pallas_call(
        finish_kernel,
        out_shape=outs,
        in_specs=[hbm] * len(parts),
        out_specs=[hbm] * len(outs),
        scratch_shapes=[pltpu.VMEM(part.shape, part.dtype) for part in parts]
        + [pltpu.VMEM(outs[-1].shape, F32), pltpu.SemaphoreType.DMA((2 * len(outs),))],
        compiler_params=pltpu.CompilerParams(vmem_limit_bytes=63 * 2**20),
        name="finish",
    )(*parts)


def by_heads(
    inputs, lengths, infill, cotangent, w_qkv, w_out, w_up, w_down,
    gain_one, shift_one, gain_two, shift_two,
):
    streams, tok_rows, width = inputs.shape
    n_seq = lax.axis_size("seq")
    sq = lax.axis_index("seq")
    stream_len, tokens = tok_rows * n_seq, streams * tok_rows
    own_rows = w_qkv.shape[0]
    vectors = jnp.stack([gain_one, shift_one, gain_two, shift_two])
    (
        full_out, full_up, full_down, params, attn, qkv, ot, lse, xh, wt, hidden, act, bend
    ) = gather_call(inputs, w_qkv, w_out, w_up, w_down, vectors, lengths)
    weights = (
        full_out.reshape(width, width), full_up.reshape(width, -1), full_down.reshape(-1, width)
    )
    output, input_grad, grad_out, grad_up, grad_down, grad_qkv, small = scatter_call(
        inputs.reshape(tokens, width), cotangent,
        infill, attn.reshape(tokens, width), hidden, act, bend,
        params, weights,
        qkv, ot, lse, xh.reshape(streams, stream_len, width), wt, lengths,
    )
    output, input_grad, grad_out, grad_up, grad_down, grad_qkv = finish_call(
        output, input_grad, grad_out, grad_up, grad_down, grad_qkv
    )
    small = lax.dynamic_slice(small, (0, sq % (128 // own_rows) * own_rows), (4, own_rows))
    return (
        output.reshape(inputs.shape),
        input_grad,
        grad_qkv,
        grad_out.reshape(w_out.shape),
        grad_up.reshape(w_up.shape),
        grad_down.reshape(w_down.shape),
        small[0], small[1], small[2], small[3],
    )


def layer_norm(features, gain_vec, shift_vec):
    row_mean = jnp.mean(features, axis=-1, keepdims=True)
    centered = features - row_mean
    spread = jnp.mean(centered * centered, axis=-1, keepdims=True)
    return centered * lax.rsqrt(spread + norm_eps) * gain_vec + shift_vec


def segment_of(bounds, positions):
    return jnp.sum((positions[None, :, None] >= bounds[:, None, :]).astype(jnp.int32), axis=2)


def slope_table(head_count, stream_len):
    return 2.0 ** (-8.0 * (jnp.arange(head_count, dtype=jnp.float32) + 1.0) / head_count) * (
        256.0 / stream_len
    )


def block_scores(queries, key_heads, query_pos, key_pos, query_seg, key_seg, slopes):
    raw_scores = jnp.einsum(
        "sqhc,skhc->shqk", queries, key_heads, preferred_element_type=jnp.float32
    )
    distance = jnp.abs(query_pos[:, None] - key_pos[None, :]).astype(jnp.float32)
    scores = (
        raw_scores * queries.shape[3] ** (-0.5) - slopes[None, :, None, None] * distance[None, None]
    )
    same_utt = query_seg[:, None, :, None] == key_seg[:, None, None, :]
    return jnp.where(same_utt, scores, masked_score)


def score_grads(
    queries,
    grad_heads,
    log_total,
    delta,
    key_heads,
    values,
    query_pos,
    key_pos,
    query_seg,
    key_seg,
    slopes,
):
    scores = block_scores(queries, key_heads, query_pos, key_pos, query_seg, key_seg, slopes)
    probs = jnp.exp(scores - log_total[..., None])
    grad_probs = jnp.einsum(
        "sqhc,skhc->shqk", grad_heads, values, preferred_element_type=jnp.float32
    )
    grad_scores = (probs * (grad_probs - delta[..., None])).astype(jnp.bfloat16)
    return (probs.astype(jnp.bfloat16), grad_scores)


def by_frames(
    inputs,
    lengths,
    infill,
    cotangent,
    w_qkv,
    w_out,
    w_up,
    w_down,
    gain_one,
    shift_one,
    gain_two,
    shift_two,
):
    w_qkv, w_out, w_up, w_down, gain_one, shift_one, gain_two, shift_two = (
        lax.all_gather(w_qkv, ("dp", "seq"), axis=0, tiled=True),
        lax.all_gather(w_out, ("dp", "seq"), axis=0, tiled=True),
        lax.all_gather(w_up, ("dp", "seq"), axis=0, tiled=True),
        lax.all_gather(w_down, ("dp", "seq"), axis=0, tiled=True),
        lax.all_gather(gain_one, ("dp", "seq"), axis=0, tiled=True),
        lax.all_gather(shift_one, ("dp", "seq"), axis=0, tiled=True),
        lax.all_gather(gain_two, ("dp", "seq"), axis=0, tiled=True),
        lax.all_gather(shift_two, ("dp", "seq"), axis=0, tiled=True),
    )
    streams, tok_rows, model_width = inputs.shape
    head_count = HEADS
    head_size = HEAD_DIM
    stream_len = tok_rows * lax.axis_size("seq")
    score_scale = head_size ** (-0.5)
    slopes = slope_table(head_count, stream_len)
    bounds = jnp.cumsum(lengths, axis=1)
    own_pos = lax.axis_index("seq") * tok_rows + jnp.arange(tok_rows, dtype=jnp.int32)
    own_seg = segment_of(bounds, own_pos)
    gain_one_f = gain_one.astype(jnp.float32)
    shift_one_f = shift_one.astype(jnp.float32)
    gain_two_f = gain_two.astype(jnp.float32)
    shift_two_f = shift_two.astype(jnp.float32)
    inputs_f = inputs.astype(jnp.float32)
    normed_one = layer_norm(inputs_f, gain_one_f, shift_one_f).astype(jnp.bfloat16)
    packed = jnp.einsum(
        "std,de->ste", normed_one, w_qkv, preferred_element_type=jnp.float32
    ).astype(jnp.bfloat16)
    query_low = packed[:, :, :model_width]
    key_value = packed[:, :, model_width:]
    query_heads = query_low.reshape(streams, tok_rows, head_count, head_size)
    start_state = (
        jnp.full((streams, head_count, tok_rows), masked_score, jnp.float32),
        jnp.zeros((streams, head_count, tok_rows), jnp.float32),
        jnp.zeros((streams, head_count, tok_rows, head_size), jnp.float32),
    )
    shard_piece = lax.all_gather(key_value, "seq", axis=1, tiled=True)
    key_count = shard_piece.shape[1]
    visit_block_len = 256

    def one_block(carried, offset):
        top_score, weight_sum, weighted = carried
        key_part = lax.dynamic_slice_in_dim(shard_piece, offset, visit_block_len, 1)
        key_pos = offset + jnp.arange(visit_block_len, dtype=jnp.int32)
        key_seg = segment_of(bounds, key_pos)
        key_heads = key_part[:, :, :model_width].reshape(
            streams, visit_block_len, head_count, head_size
        )
        values = key_part[:, :, model_width:].reshape(
            streams, visit_block_len, head_count, head_size
        )
        scores = block_scores(query_heads, key_heads, own_pos, key_pos, own_seg, key_seg, slopes)
        new_top = jnp.maximum(top_score, jnp.max(scores, axis=3))
        rescale = jnp.exp(top_score - new_top)
        weights_blk = jnp.exp(scores - new_top[..., None])
        weight_sum = weight_sum * rescale + jnp.sum(weights_blk, axis=3)
        weighted = weighted * rescale[..., None] + jnp.einsum(
            "shqk,skhc->shqc",
            weights_blk.astype(jnp.bfloat16),
            values,
            preferred_element_type=jnp.float32,
        )
        return ((new_top, weight_sum, weighted), None)

    offsets = jnp.arange(key_count // visit_block_len, dtype=jnp.int32) * visit_block_len
    finished, _ = lax.scan(one_block, start_state, offsets)
    top_score, weight_sum, weighted = finished
    attn_heads = weighted / weight_sum[..., None]
    log_total = top_score + jnp.log(weight_sum)
    attn_rows = jnp.transpose(attn_heads, (0, 2, 1, 3)).reshape(streams, tok_rows, model_width)
    attn_low = attn_rows.astype(jnp.bfloat16)
    hidden = inputs_f + jnp.einsum(
        "std,de->ste", attn_low, w_out, preferred_element_type=jnp.float32
    )
    normed_two_f, ln_two_pull = jax.vjp(layer_norm, hidden, gain_two_f, shift_two_f)
    normed_two = normed_two_f.astype(jnp.bfloat16)
    upward = jnp.einsum("std,df->stf", normed_two, w_up, preferred_element_type=jnp.float32)
    active_f, gelu_pull = jax.vjp(jax.nn.gelu, upward)
    active = active_f.astype(jnp.bfloat16)
    output = (
        hidden + jnp.einsum("stf,fd->std", active, w_down, preferred_element_type=jnp.float32)
    ).astype(jnp.bfloat16)
    grad_output = (cotangent.astype(jnp.float32) * infill.astype(jnp.float32)[:, :, None]).astype(
        jnp.bfloat16
    )
    grad_active = jnp.einsum("ste,fe->stf", grad_output, w_down, preferred_element_type=jnp.float32)
    grad_upward = gelu_pull(grad_active)[0].astype(jnp.bfloat16)
    grad_norm_two = jnp.einsum("stf,df->std", grad_upward, w_up, preferred_element_type=jnp.float32)
    grad_in_two, grad_gain_two, grad_shift_two = ln_two_pull(grad_norm_two)
    grad_hidden = grad_output.astype(jnp.float32) + grad_in_two
    grad_branch = grad_hidden.astype(jnp.bfloat16)
    grad_attn = jnp.einsum(
        "ste,de->std", grad_branch, w_out, preferred_element_type=jnp.float32
    ).astype(jnp.bfloat16)
    grad_heads = grad_attn.reshape(streams, tok_rows, head_count, head_size)
    delta = jnp.einsum("sqhc,shqc->shq", grad_heads.astype(jnp.float32), attn_heads)
    every_kv = lax.all_gather(key_value, "seq", axis=1, tiled=True)
    total_len = every_kv.shape[1]
    block_len = 256
    offsets = jnp.arange(total_len // block_len, dtype=jnp.int32) * block_len
    grad_start = jnp.zeros((streams, tok_rows, head_count, head_size), jnp.float32)

    def key_step(grad_query, offset):
        key_part = lax.dynamic_slice_in_dim(every_kv, offset, block_len, 1)
        key_pos = offset + jnp.arange(block_len, dtype=jnp.int32)
        key_seg = segment_of(bounds, key_pos)
        key_heads = key_part[:, :, :model_width].reshape(streams, block_len, head_count, head_size)
        values = key_part[:, :, model_width:].reshape(streams, block_len, head_count, head_size)
        probs_low, grad_scores = score_grads(
            query_heads,
            grad_heads,
            log_total,
            delta,
            key_heads,
            values,
            own_pos,
            key_pos,
            own_seg,
            key_seg,
            slopes,
        )
        grad_query = (
            grad_query
            + jnp.einsum(
                "shqk,skhc->sqhc", grad_scores, key_heads, preferred_element_type=jnp.float32
            )
            * score_scale
        )
        grad_keys = (
            jnp.einsum(
                "shqk,sqhc->kshc", grad_scores, query_heads, preferred_element_type=jnp.float32
            )
            * score_scale
        )
        grad_values = jnp.einsum(
            "shqk,sqhc->kshc", probs_low, grad_heads, preferred_element_type=jnp.float32
        )
        key_terms = jnp.concatenate(
            [
                grad_keys.reshape(block_len, streams, model_width),
                grad_values.reshape(block_len, streams, model_width),
            ],
            axis=2,
        )
        return (grad_query, key_terms)

    grad_query, key_terms = lax.scan(key_step, grad_start, offsets)
    key_terms = key_terms.reshape(total_len, streams, 2 * model_width)
    own_kv_grad = lax.psum_scatter(
        key_terms.astype(jnp.bfloat16), "seq", scatter_dimension=0, tiled=True
    ).astype(jnp.float32)
    grad_kv = jnp.transpose(own_kv_grad, (1, 0, 2))
    grad_packed = jnp.concatenate(
        [grad_query.reshape(streams, tok_rows, model_width), grad_kv], axis=2
    ).astype(jnp.bfloat16)
    grad_norm_one = jnp.einsum(
        "ste,de->std", grad_packed, w_qkv, preferred_element_type=jnp.float32
    )
    _, ln_one_pull = jax.vjp(layer_norm, inputs_f, gain_one_f, shift_one_f)
    grad_in_one, grad_gain_one, grad_shift_one = ln_one_pull(grad_norm_one)
    input_grad = (grad_hidden + grad_in_one).astype(jnp.bfloat16)
    weight_terms = (
        jnp.einsum("std,ste->de", normed_one, grad_packed, preferred_element_type=jnp.float32),
        jnp.einsum("std,ste->de", attn_low, grad_branch, preferred_element_type=jnp.float32),
        jnp.einsum("std,stf->df", normed_two, grad_upward, preferred_element_type=jnp.float32),
        jnp.einsum("stf,std->fd", active, grad_output, preferred_element_type=jnp.float32),
        grad_gain_one,
        grad_shift_one,
        grad_gain_two,
        grad_shift_two,
    )
    summed = (
        lax.psum_scatter(weight_terms[0], ("dp", "seq"), scatter_dimension=0, tiled=True),
        lax.psum_scatter(weight_terms[1], ("dp", "seq"), scatter_dimension=0, tiled=True),
        lax.psum_scatter(weight_terms[2], ("dp", "seq"), scatter_dimension=0, tiled=True),
        lax.psum_scatter(weight_terms[3], ("dp", "seq"), scatter_dimension=0, tiled=True),
        lax.psum_scatter(weight_terms[4], ("dp", "seq"), scatter_dimension=0, tiled=True),
        lax.psum_scatter(weight_terms[5], ("dp", "seq"), scatter_dimension=0, tiled=True),
        lax.psum_scatter(weight_terms[6], ("dp", "seq"), scatter_dimension=0, tiled=True),
        lax.psum_scatter(weight_terms[7], ("dp", "seq"), scatter_dimension=0, tiled=True),
    )
    return (
        output,
        input_grad,
        summed[0],
        summed[1],
        summed[2],
        summed[3],
        summed[4],
        summed[5],
        summed[6],
        summed[7],
    )


def solution(mesh):
    in_specs = (
        P("dp", "seq", None),
        P("dp", None),
        P("dp", "seq"),
        P("dp", "seq", None),
        P(("dp", "seq"), None),
        P(("dp", "seq"), None),
        P(("dp", "seq"), None),
        P(("dp", "seq"), None),
        P(("dp", "seq")),
        P(("dp", "seq")),
        P(("dp", "seq")),
        P(("dp", "seq")),
    )
    out_specs = (
        P("dp", "seq", None),
        P("dp", "seq", None),
        P(("dp", "seq"), None),
        P(("dp", "seq"), None),
        P(("dp", "seq"), None),
        P(("dp", "seq"), None),
        P(("dp", "seq")),
        P(("dp", "seq")),
        P(("dp", "seq")),
        P(("dp", "seq")),
    )
    grid = (mesh.shape["dp"], mesh.shape["seq"])
    local = by_heads if grid == (4, HEADS // 2) else by_frames
    return jax.shard_map(local, mesh=mesh, in_specs=in_specs, out_specs=out_specs, check_vma=False)
```
